32 devices in a mesh: ctx: 8 (over y, x, core), fsdp: 4 (over z).
Axes of the slice: x: 2, y: 2, z: 4, core: 2. Of those that a mesh axis runs over, the one named last changes fastest.
Arguments:
- tokens: bfloat16 [2048, 2, 1600], P(('ctx', 'fsdp')), may hold values from -6 to 6
- block_pairs: int32 [32], replicated, may hold values from 0 to 31, each once
- out_grad: bfloat16 [2048, 2, 1600], P(('ctx', 'fsdp')), may hold values from -6 to 6
- ln1_gain: bfloat16 [1600], P('fsdp'), may hold values from 0.5 to 1.5
- ln1_bias: bfloat16 [1600], P('fsdp'), may hold values from -4 to 4
- qkv_weight: bfloat16 [1600, 4800], P('fsdp'), may hold values from -0.15625 to 0.15625
- query_bias: bfloat16 [1600], P('fsdp'), may hold values from -4 to 4
- value_bias: bfloat16 [1600], P('fsdp'), may hold values from -4 to 4
- out_weight: bfloat16 [1600, 1600], P('fsdp'), may hold values from -6 to 6
- out_bias: bfloat16 [1600], P('fsdp'), may hold values from -4 to 4
- ln2_gain: bfloat16 [1600], P('fsdp'), may hold values from 0.5 to 1.5
- ln2_bias: bfloat16 [1600], P('fsdp'), may hold values from -4 to 4
- up_weight: bfloat16 [1600, 6400], P('fsdp'), may hold values from -0.15625 to 0.15625
- up_bias: bfloat16 [6400], P('fsdp'), may hold values from -4 to 4
- down_weight: bfloat16 [6400, 1600], P('fsdp'), may hold values from -0.078125 to 0.078125
- down_bias: bfloat16 [1600], P('fsdp'), may hold values from -4 to 4
Outputs:
- block_out: bfloat16 [2048, 2, 1600], P(('ctx', 'fsdp'))
- input_grad: float32 [2048, 2, 1600], P(('ctx', 'fsdp'))
- ln1_gain_grad: float32 [1600], P('fsdp')
- ln1_bias_grad: float32 [1600], P('fsdp')
- qkv_weight_grad: float32 [1600, 4800], P('fsdp')
- query_bias_grad: float32 [1600], P('fsdp')
- value_bias_grad: float32 [1600], P('fsdp')
- out_weight_grad: float32 [1600, 1600], P('fsdp')
- out_bias_grad: float32 [1600], P('fsdp')
- ln2_gain_grad: float32 [1600], P('fsdp')
- ln2_bias_grad: float32 [1600], P('fsdp')
- up_weight_grad: float32 [1600, 6400], P('fsdp')
- up_bias_grad: float32 [6400], P('fsdp')
- down_weight_grad: float32 [6400, 1600], P('fsdp')
- down_bias_grad: float32 [1600], P('fsdp')
The draws below stay inside these ranges and needn't reach their ends.
Inputs may be any that keep to these rules, and one draw needn't show every extreme that they name: A permutation: the device with index e along ctx+fsdp holds the position blocks block_pairs[e] and 63 - block_pairs[e] of every sequence.
All inputs are finite; a program needn't handle non-finite values.
Results may differ from the reference program's by a relative error of at most 0.017.
Values may be sent and summed in bfloat16 or wider, within the bound.
A program may use at most 960 MiB of HBM per device.

```python
from functools import partial
import jax
import jax.numpy as jnp
from jax import lax

D = 1600
HEADS = 25
HD = 64
FF = 6400
BLK = 32
SEQS = 2
LEN = 2048
N_CTX = 8
N_FSDP = 4


def level_of(stream_key, extent, cuts, smallest, high):
    factor_of = 1.0
    for axis_at, shards_of in cuts:
        draws = jax.random.uniform(jax.random.fold_in(jax.random.fold_in(stream_key, 6), axis_at), (shards_of,), jnp.float32, smallest / len(cuts), high / len(cuts))
        factor_of = factor_of * jnp.repeat(jnp.exp(draws), extent[axis_at] // shards_of).reshape((-1,) + (1,) * (len(extent) - 1 - axis_at))
    return factor_of


def centred(stream_key, dims, deviation, reach, split=(), kind=jnp.bfloat16):
    factor_of = level_of(stream_key, dims, split, -0.22, 0.18) if split else 1.0
    values = jax.random.normal(stream_key, dims, jnp.float32) * deviation * factor_of
    return jnp.minimum(jnp.maximum(values, -reach), reach).astype(kind)


def setup_inputs(seed: int = 0) -> dict:
    splits = jax.random.split(jax.random.key(seed), 17)
    return {
        "tokens": centred(splits[0], (LEN, SEQS, D), 1.0, 6.0, ((0, 32),)),
        "block_pairs": jax.random.permutation(splits[1], N_CTX * N_FSDP).astype(jnp.int32),
        "out_grad": centred(splits[2], (LEN, SEQS, D), 1.0, 6.0, ((0, 32),)),
        "ln1_gain": jnp.clip(1.0 + 0.1 * jax.random.normal(splits[3], (D,), jnp.float32), 0.5, 1.5).astype(jnp.bfloat16),
        "ln1_bias": centred(splits[4], (D,), 0.3, 4.0, ((0, 4),)),
        "qkv_weight": centred(splits[5], (D, 3 * D), D ** -0.5, 0.15625, ((0, 4),)),
        "query_bias": centred(splits[6], (D,), 0.3, 4.0, ((0, 4),)),
        "value_bias": centred(splits[7], (D,), 0.3, 4.0, ((0, 4),)),
        "out_weight": centred(splits[8], (D, D), 1.0, 6.0, ((0, 4),)),
        "out_bias": centred(splits[9], (D,), 0.3, 4.0, ((0, 4),)),
        "ln2_gain": jnp.clip(1.0 + 0.1 * jax.random.normal(splits[10], (D,), jnp.float32), 0.5, 1.5).astype(jnp.bfloat16),
        "ln2_bias": centred(splits[11], (D,), 0.3, 4.0, ((0, 4),)),
        "up_weight": centred(splits[12], (D, FF), D ** -0.5, 0.15625, ((0, 4),)),
        "up_bias": centred(splits[13], (FF,), 0.3, 4.0, ((0, 4),)),
        "down_weight": centred(splits[14], (FF, D), FF ** -0.5, 0.078125, ((0, 4),)),
        "down_bias": centred(splits[15], (D,), 0.3, 4.0, ((0, 4),)),
    }


NORM_EPS = 1e-05
NEG_BIG = -1e+30
QUERY_BLOCK = 512

@jax.custom_vjp
def low(v):
    return lax.optimization_barrier(v.astype(jnp.bfloat16)).astype(jnp.float32)

@jax.custom_vjp
def low_back(v):
    return v

def low_keep(v):
    return (low(v), None)

def low_pass(kept, grad):
    return (grad,)

def back_keep(v):
    return (v, None)

def back_low(kept, grad):
    return (low(grad),)
low.defvjp(low_keep, low_pass)
low_back.defvjp(back_keep, back_low)

def layer_norm(values, norm_gain, norm_shift):
    average = lax.optimization_barrier(jnp.mean(values, axis=-1, keepdims=True))
    centered = values - average
    variance = lax.optimization_barrier(jnp.mean(centered * centered, axis=-1, keepdims=True))
    return centered * lax.rsqrt(variance + NORM_EPS) * norm_gain + norm_shift

def gelu_tanh(values):
    return jax.nn.gelu(values, approximate=True)

def block_positions(block_pairs, local_rows, device_count):
    half_rows = local_rows // 2
    owners = jnp.broadcast_to(block_pairs[:, None], (device_count, local_rows)).reshape(-1)
    inside = jnp.tile(jnp.arange(local_rows, dtype=jnp.int32), device_count)
    blocks = jnp.where(inside < half_rows, owners, 2 * device_count - 1 - owners)
    return (blocks * half_rows + inside % half_rows).astype(jnp.int32)

def attend_block(query_piece, pos_piece, key_heads, value_heads, key_pos):
    highest = lax.Precision.HIGHEST
    scaled = jnp.einsum('qhe,khe->hqk', query_piece, key_heads, precision=highest) * HD ** (-0.5)
    scaled = low_back(scaled)
    allowed = key_pos[None, :] <= pos_piece[:, None]
    scaled = jnp.where(allowed[None], scaled, NEG_BIG)
    top_score = lax.optimization_barrier(jnp.max(scaled, axis=-1, keepdims=True))
    shifted = jnp.exp(scaled - top_score)
    soft = shifted / lax.optimization_barrier(jnp.sum(shifted, axis=-1, keepdims=True))
    soft = low(soft)
    return jnp.einsum('hqk,khe->qhe', soft, value_heads, precision=highest)

def forward_pass(params, positions):
    inputs, first_gain, first_shift, joint_weight, query_shift, value_shift, output_weight, output_shift, second_gain, second_shift, upward_weight, upward_shift, downward_weight, downward_shift = params
    highest = lax.Precision.HIGHEST
    normed_one = low(layer_norm(inputs, first_gain, first_shift))
    joint_out = jnp.einsum('rsd,de->rse', normed_one, joint_weight, precision=highest)
    queries = low(low_back(joint_out[..., :D] + query_shift))
    key_flat = low(low_back(joint_out[..., D:2 * D]))
    value_flat = low(low_back(joint_out[..., 2 * D:] + value_shift))
    query_rows = min(QUERY_BLOCK, LEN)
    block_count = LEN // query_rows
    pos_blocks = positions.reshape(block_count, query_rows)
    attend_saved = jax.checkpoint(attend_block)
    results = []
    for sequence in range(SEQS):
        query_blocks = queries[:, sequence].reshape(block_count, query_rows, HEADS, HD)
        key_heads = key_flat[:, sequence].reshape(LEN, HEADS, HD)
        value_heads = value_flat[:, sequence].reshape(LEN, HEADS, HD)

        def scan_step(state_now, current, key_heads=key_heads, value_heads=value_heads):
            return (state_now, attend_saved(current[0], current[1], key_heads, value_heads, positions))
        unused, attended_blocks = lax.scan(scan_step, jnp.zeros((), jnp.float32), (query_blocks, pos_blocks))
        results.append(attended_blocks.reshape(LEN, D))
    attended = low(low_back(jnp.stack(results, axis=1)))
    branch = low_back(jnp.einsum('rse,ed->rsd', attended, output_weight, precision=highest) + output_shift)
    mixed_sum = inputs + branch
    normed_two = low(layer_norm(mixed_sum, second_gain, second_shift))
    upward = low_back(jnp.einsum('rsd,df->rsf', normed_two, upward_weight, precision=highest) + upward_shift)
    activated = low(gelu_tanh(upward))
    return mixed_sum + jnp.einsum('rsf,fd->rsd', activated, downward_weight, precision=highest) + downward_shift

def reference(tokens, block_pairs, out_grad, ln1_gain, ln1_bias, qkv_weight, query_bias, value_bias, out_weight, out_bias, ln2_gain, ln2_bias, up_weight, up_bias, down_weight, down_bias):
    positions = block_positions(block_pairs, 2 * BLK, N_CTX * N_FSDP)
    params = (tokens.astype(jnp.float32), ln1_gain.astype(jnp.float32), ln1_bias.astype(jnp.float32), qkv_weight.astype(jnp.float32), query_bias.astype(jnp.float32), value_bias.astype(jnp.float32), out_weight.astype(jnp.float32), out_bias.astype(jnp.float32), ln2_gain.astype(jnp.float32), ln2_bias.astype(jnp.float32), up_weight.astype(jnp.float32), up_bias.astype(jnp.float32), down_weight.astype(jnp.float32), down_bias.astype(jnp.float32))
    block_out, pull_back = jax.vjp(partial(forward_pass, positions=positions), params)
    grads, = pull_back(out_grad.astype(jnp.float32))
    return (block_out.astype(jnp.bfloat16), grads[0], grads[1], grads[2], grads[3], grads[4], grads[5], grads[6], grads[7], grads[8], grads[9], grads[10], grads[11], grads[12], grads[13])
```

```python
import functools

import jax
import jax.numpy as jnp
from jax import lax
from jax.experimental import pallas as pl
from jax.experimental.pallas import tpu as pltpu
from jax.sharding import PartitionSpec as P

HD = 64
LANES = 128
NORM_EPS = 1e-05
NEG_BIG = -1e30
MESH = pl.DeviceIdType.MESH
F32 = jnp.float32
BF16 = jnp.bfloat16
ANY = pl.BlockSpec(memory_space=pl.ANY)
VMEM = pl.BlockSpec(memory_space=pltpu.VMEM)
DMA = pltpu.SemaphoreType.DMA
VMEM_LIMIT = 56 * 1024 * 1024


def params(cid=None):
    if cid is None:
        return pltpu.CompilerParams(vmem_limit_bytes=VMEM_LIMIT)
    return pltpu.CompilerParams(
        collective_id=cid, has_side_effects=True, vmem_limit_bytes=VMEM_LIMIT
    )


def plane_peers(chips):
    me = lax.axis_index("ctx")
    core = lax.rem(me, 2)
    chip = me // 2
    sibling = chip * 2 + 1 - core
    to = [lax.rem(chip + k, chips) * 2 + core for k in range(1, chips)]
    come = [lax.rem(chip + chips - k, chips) * 2 + core for k in range(1, chips)]
    return me, core, chip, sibling, to, come


def greet(axis, peers):
    barrier = pltpu.get_barrier_semaphore()
    for peer in peers:
        pl.semaphore_signal(barrier, inc=1, device_id={axis: peer}, device_id_type=MESH)
    pl.semaphore_wait(barrier, len(peers))


def send(src, dst, send_sem, recv_sem, axis, peer):
    copy = pltpu.make_async_remote_copy(
        src_ref=src,
        dst_ref=dst,
        send_sem=send_sem,
        recv_sem=recv_sem,
        device_id={axis: peer},
        device_id_type=MESH,
    )
    copy.start()
    return copy


def plane_gather(own_ref, all_ref, sems, chips):
    far_send, far_recv, near_send, near_recv, local_sem = sems
    me, core, chip, sibling, to, come = plane_peers(chips)
    far = [
        send(own_ref, all_ref.at[me], far_send.at[k], far_recv.at[k], "ctx", to[k])
        for k in range(chips - 1)
    ]
    near = [send(own_ref, all_ref.at[me], near_send.at[chips - 1], near_recv.at[chips - 1], "ctx", sibling)]
    local = pltpu.make_async_copy(own_ref, all_ref.at[me], local_sem)
    local.start()
    for k in range(chips - 1):
        far[k].wait_recv()
        block = all_ref.at[come[k]]
        near.append(send(block, block, near_send.at[k], near_recv.at[k], "ctx", sibling))
    for copy in far:
        copy.wait_send()
    for copy in near:
        copy.wait()
    local.wait()


def plane_scatter(part_ref, mine, paired, stage, arrived, sems, chips):
    far_send, far_recv, near_send, near_recv, local_sem = sems
    me, core, chip, sibling, to, come = plane_peers(chips)
    near, local = [None] * chips, [None] * chips
    order = list(range(1, chips)) + [0]
    for k in order:
        base = lax.rem(chip + k, chips) * 2
        near[k] = send(
            part_ref.at[base + 1 - core], paired.at[k], near_send.at[k], near_recv.at[k], "ctx", sibling
        )
        local[k] = pltpu.make_async_copy(part_ref.at[base + core], mine.at[k], local_sem.at[k])
        local[k].start()
    far = []
    for k in range(1, chips):
        local[k].wait()
        near[k].wait_recv()
        stage[k - 1] = (mine[k].astype(F32) + paired[k].astype(F32)).astype(BF16)
        far.append(
            send(stage.at[k - 1], arrived.at[k - 1], far_send.at[k - 1], far_recv.at[k - 1], "ctx", to[k - 1])
        )
    local[0].wait()
    near[0].wait_recv()
    total = mine[0].astype(F32) + paired[0].astype(F32)
    for k in range(chips - 1):
        far[k].wait_recv()
        total = total + arrived[k].astype(F32)
    for copy in far + near:
        copy.wait_send()
    return total


def gather_sems(chips):
    return [DMA((chips - 1,)), DMA((chips - 1,)), DMA((chips,)), DMA((chips,)), DMA]


def scatter_scratch(chips, rows, width):
    return [
        pltpu.VMEM((chips, rows, width), BF16),
        pltpu.VMEM((chips, rows, width), BF16),
        pltpu.VMEM((chips - 1, rows, width), BF16),
        pltpu.VMEM((chips - 1, rows, width), BF16),
        DMA((chips - 1,)),
        DMA((chips - 1,)),
        DMA((chips,)),
        DMA((chips,)),
        DMA((chips,)),
    ]


def normalize(values):
    average = jnp.mean(values, axis=-1, keepdims=True)
    centered = values - average
    variance = jnp.mean(centered * centered, axis=-1, keepdims=True)
    inverse = lax.rsqrt(variance + NORM_EPS)
    return centered * inverse, inverse


def norm_backward(grad, gain, unit, inverse):
    scaled = grad * gain
    first = jnp.mean(scaled, axis=-1, keepdims=True)
    second = jnp.mean(scaled * unit, axis=-1, keepdims=True)
    return (scaled - first - unit * second) * inverse


def first_kernel(chips, tok_ref, vec_ref, all_ref, own, *sems):
    me, core, chip, sibling, to, come = plane_peers(chips)
    unit, inverse = normalize(tok_ref[...].astype(F32))
    own[...] = (unit * vec_ref[0:1, :] + vec_ref[1:2, :]).astype(BF16)
    greet("ctx", to + [sibling])
    plane_gather(own, all_ref, sems, chips)


def first_norm_gather(tok, vecs, n_ctx):
    rows, width = tok.shape
    chips = n_ctx // 2
    return pl.pallas_call(
        functools.partial(first_kernel, chips),
        out_shape=jax.ShapeDtypeStruct((n_ctx, rows, width), BF16),
        in_specs=[VMEM, VMEM],
        out_specs=ANY,
        scratch_shapes=[pltpu.VMEM((rows, width), BF16)] + gather_sems(chips),
        compiler_params=params(0),
        name="norm_gather",
    )(tok, vecs)


def second_kernel(chips, part_ref, tok_ref, vec_ref, mixed_ref, all_ref, own, *scratch):
    me, core, chip, sibling, to, come = plane_peers(chips)
    greet("ctx", to + [sibling])
    total = plane_scatter(part_ref, *scratch[:4], scratch[4:9], chips)
    mixed = tok_ref[...].astype(F32) + total + vec_ref[2:3, :]
    mixed_ref[...] = mixed
    unit, inverse = normalize(mixed)
    own[...] = (unit * vec_ref[0:1, :] + vec_ref[1:2, :]).astype(BF16)
    plane_gather(own, all_ref, scratch[9:], chips)


def second_norm_gather(part, tok, vecs):
    n_ctx, rows, width = part.shape
    chips = n_ctx // 2
    return pl.pallas_call(
        functools.partial(second_kernel, chips),
        out_shape=(
            jax.ShapeDtypeStruct((rows, width), F32),
            jax.ShapeDtypeStruct((n_ctx, rows, width), BF16),
        ),
        in_specs=[ANY, VMEM, VMEM],
        out_specs=(VMEM, ANY),
        scratch_shapes=[pltpu.VMEM((rows, width), BF16)]
        + scatter_scratch(chips, rows, width)
        + gather_sems(chips),
        compiler_params=params(1),
        name="scatter_norm_gather",
    )(part, tok, vecs)


def third_kernel(chips, part_ref, mixed_ref, og_ref, vec_ref, dmixed_ref, sums_ref, all_ref, own, *scratch):
    me, core, chip, sibling, to, come = plane_peers(chips)
    greet("ctx", to + [sibling])
    unit, inverse = normalize(mixed_ref[...])
    grad = plane_scatter(part_ref, *scratch[:4], scratch[4:9], chips)
    out_grad = og_ref[...].astype(F32)
    dmixed = out_grad + norm_backward(grad, vec_ref[0:1, :], unit, inverse)
    dmixed_ref[...] = dmixed
    low = dmixed.astype(BF16)
    own[...] = low
    sums_ref[0:1, :] = jnp.sum(grad * unit, axis=0, keepdims=True)
    sums_ref[1:2, :] = jnp.sum(grad, axis=0, keepdims=True)
    sums_ref[2:3, :] = jnp.sum(low.astype(F32), axis=0, keepdims=True)
    sums_ref[3:4, :] = jnp.sum(out_grad, axis=0, keepdims=True)
    plane_gather(own, all_ref, scratch[9:], chips)


def second_norm_back(part, mixed, og, vecs):
    n_ctx, rows, width = part.shape
    chips = n_ctx // 2
    return pl.pallas_call(
        functools.partial(third_kernel, chips),
        out_shape=(
            jax.ShapeDtypeStruct((rows, width), F32),
            jax.ShapeDtypeStruct((4, width), F32),
            jax.ShapeDtypeStruct((n_ctx, rows, width), BF16),
        ),
        in_specs=[ANY, VMEM, VMEM, VMEM],
        out_specs=(VMEM, VMEM, ANY),
        scratch_shapes=[pltpu.VMEM((rows, width), BF16)]
        + scatter_scratch(chips, rows, width)
        + gather_sems(chips),
        compiler_params=params(2),
        name="scatter_back_gather",
    )(part, mixed, og, vecs)


def fourth_kernel(chips, part_ref, tok_ref, dmixed_ref, vec_ref, grad_ref, sums_ref, *scratch):
    me, core, chip, sibling, to, come = plane_peers(chips)
    greet("ctx", to + [sibling])
    unit, inverse = normalize(tok_ref[...].astype(F32))
    grad = plane_scatter(part_ref, *scratch[:4], scratch[4:9], chips)
    grad_ref[...] = dmixed_ref[...] + norm_backward(grad, vec_ref[0:1, :], unit, inverse)
    sums_ref[0:1, :] = jnp.sum(grad * unit, axis=0, keepdims=True)
    sums_ref[1:2, :] = jnp.sum(grad, axis=0, keepdims=True)


def first_norm_back(part, tok, dmixed, vecs):
    n_ctx, rows, width = part.shape
    chips = n_ctx // 2
    return pl.pallas_call(
        functools.partial(fourth_kernel, chips),
        out_shape=(
            jax.ShapeDtypeStruct((rows, width), F32),
            jax.ShapeDtypeStruct((2, width), F32),
        ),
        in_specs=[ANY, VMEM, VMEM, VMEM],
        out_specs=(VMEM, VMEM),
        scratch_shapes=scatter_scratch(chips, rows, width),
        compiler_params=params(3),
        name="scatter_back",
    )(part, tok, dmixed, vecs)


def out_kernel(chips, part_ref, mixed_ref, vec_ref, out_ref, *scratch):
    me, core, chip, sibling, to, come = plane_peers(chips)
    greet("ctx", to + [sibling])
    total = plane_scatter(part_ref, *scratch[:4], scratch[4:9], chips)
    out_ref[...] = (mixed_ref[...] + total + vec_ref[0:1, :]).astype(BF16)


def block_result(part, mixed, vecs):
    n_ctx, rows, width = part.shape
    chips = n_ctx // 2
    return pl.pallas_call(
        functools.partial(out_kernel, chips),
        out_shape=jax.ShapeDtypeStruct((rows, width), BF16),
        in_specs=[ANY, VMEM, VMEM],
        out_specs=VMEM,
        scratch_shapes=scatter_scratch(chips, rows, width),
        compiler_params=params(4),
        name="scatter_out",
    )(part, mixed, vecs)


def to_heads_kernel(kinds, planes, seqs, tok_ref, head_ref, send_sems, recv_sems, local_sems):
    me = lax.axis_index("fsdp")
    pairs = planes // seqs
    greet("fsdp", [lax.rem(me + k, planes) for k in range(1, planes)])
    width = tok_ref.shape[3] // kinds

    def source(kind, unit):
        start = pl.multiple_of(kind * width + lax.rem(unit, pairs) * LANES, LANES)
        return tok_ref.at[:, unit // pairs, :, pl.ds(start, LANES)]

    copies = []
    for k in range(1, planes):
        unit = lax.rem(me + k, planes)
        for kind in range(kinds):
            copies.append(
                send(
                    source(kind, unit),
                    head_ref.at[kind, :, me],
                    send_sems.at[kind, k - 1],
                    recv_sems.at[kind, k - 1],
                    "fsdp",
                    unit,
                )
            )
    local = []
    for kind in range(kinds):
        copy = pltpu.make_async_copy(source(kind, me), head_ref.at[kind, :, me], local_sems.at[kind])
        copy.start()
        local.append(copy)
    for copy in copies + local:
        copy.wait()


def to_heads(tok, kinds, planes, cid):
    n_ctx, seqs, rows, width = tok.shape
    return pl.pallas_call(
        functools.partial(to_heads_kernel, kinds, planes, seqs),
        out_shape=jax.ShapeDtypeStruct((kinds, n_ctx, planes, rows, LANES), tok.dtype),
        in_specs=[ANY],
        out_specs=ANY,
        scratch_shapes=[DMA((kinds, planes - 1)), DMA((kinds, planes - 1)), DMA((kinds,))],
        compiler_params=params(cid),
        name="to_heads",
    )(tok)


def to_tokens_kernel(kinds, planes, seqs, head_ref, tok_ref, send_sems, recv_sems, local_sems):
    me = lax.axis_index("fsdp")
    pairs = planes // seqs
    greet("fsdp", [lax.rem(me + k, planes) for k in range(1, planes)])
    width = tok_ref.shape[3] // kinds

    def target(kind):
        start = pl.multiple_of(kind * width + lax.rem(me, pairs) * LANES, LANES)
        return tok_ref.at[:, me // pairs, :, pl.ds(start, LANES)]

    copies = []
    for k in range(1, planes):
        peer = lax.rem(me + k, planes)
        for kind in range(kinds):
            copies.append(
                send(
                    head_ref.at[kind, :, peer],
                    target(kind),
                    send_sems.at[kind, k - 1],
                    recv_sems.at[kind, k - 1],
                    "fsdp",
                    peer,
                )
            )
    local = []
    for kind in range(kinds):
        copy = pltpu.make_async_copy(head_ref.at[kind, :, me], target(kind), local_sems.at[kind])
        copy.start()
        local.append(copy)
    for copy in copies + local:
        copy.wait()


def to_tokens(heads, seqs, cid):
    kinds, n_ctx, planes, rows, lanes = heads.shape
    width = kinds * (planes // seqs) * LANES
    return pl.pallas_call(
        functools.partial(to_tokens_kernel, kinds, planes, seqs),
        out_shape=jax.ShapeDtypeStruct((n_ctx, seqs, rows, width), heads.dtype),
        in_specs=[ANY],
        out_specs=ANY,
        scratch_shapes=[DMA((kinds, planes - 1)), DMA((kinds, planes - 1)), DMA((kinds,))],
        compiler_params=params(cid),
        name="to_tokens",
    )(heads)


def nt(left, right):
    return lax.dot_general(left, right, (((1,), (1,)), ((), ())), preferred_element_type=F32)


def nn(left, right):
    return lax.dot_general(left, right, (((1,), (0,)), ((), ())), preferred_element_type=F32)


def sort_blocks(order_ref, source_refs, sorted_refs, blocks, half):
    def body(block, carry):
        place = order_ref[block]
        start = pl.multiple_of(block * half, half)
        for source, target in zip(source_refs, sorted_refs):
            target[pl.ds(start, half), :] = source[place]
        return carry

    lax.fori_loop(0, blocks, body, 0)


def lane_mask(rows, head):
    lane = lax.broadcasted_iota(jnp.int32, (rows, LANES), 1)
    return (lane < HD) if head == 0 else (lane >= HD)


def forward_kernel(tile, order_ref, qkv_ref, out_ref, att_ref, lse_ref, q_s, k_s, v_s, vt_s, o_s):
    blocks, half = out_ref.shape[0], out_ref.shape[1]
    length = blocks * half
    tiles = length // tile
    sort_blocks(order_ref, [qkv_ref.at[0], qkv_ref.at[1], qkv_ref.at[2]], [q_s, k_s, v_s], blocks, half)
    for t in range(tiles):
        span = slice(t * tile, (t + 1) * tile)
        vt_s[:, span] = v_s[span, :].T
    scale = HD ** (-0.5)
    rows_iota = lax.broadcasted_iota(jnp.int32, (tile, tile), 0)
    cols_iota = lax.broadcasted_iota(jnp.int32, (tile, tile), 1)
    allowed = rows_iota <= cols_iota
    masks = [lane_mask(tile, head) for head in range(2)]

    for qt in range(tiles):
        q_span = slice(qt * tile, (qt + 1) * tile)
        query = q_s[q_span, :] * jnp.asarray(scale, BF16)
        queries = [jnp.where(masks[head], query, jnp.zeros_like(query)) for head in range(2)]

        def step(kt, state, masked, queries=queries):
            start = pl.multiple_of(kt * tile, tile)
            keys = k_s[pl.ds(start, tile), :]
            new = []
            for head in range(2):
                top, total, acc = state[head]
                scores = nt(keys, queries[head])
                if masked:
                    scores = jnp.where(allowed, scores, NEG_BIG)
                new_top = jnp.maximum(top, jnp.max(scores, axis=0, keepdims=True))
                soft = jnp.exp(scores - new_top)
                factor = jnp.exp(top - new_top)
                total = total * factor + jnp.sum(soft, axis=0, keepdims=True)
                values = vt_s[head * HD : (head + 1) * HD, pl.ds(start, tile)]
                acc = acc * factor + nn(values, soft.astype(BF16))
                new.append((new_top, total, acc))
            return tuple(new)

        state = tuple(
            (jnp.full((1, tile), NEG_BIG, F32), jnp.zeros((1, tile), F32), jnp.zeros((HD, tile), F32))
            for head in range(2)
        )
        state = step(qt, state, True)
        if qt > 0:
            state = lax.fori_loop(0, qt, lambda kt, s, step=step: step(kt, s, False), state)
        for head in range(2):
            top, total, acc = state[head]
            att_ref[head * HD : (head + 1) * HD, q_span] = acc / total
            lse_ref[head : head + 1, q_span] = top + jnp.log(total)
        o_s[q_span, :] = att_ref[:, q_span].T.astype(BF16)

    def body(block, carry):
        start = pl.multiple_of(block * half, half)
        out_ref[order_ref[block]] = o_s[pl.ds(start, half), :]
        return carry

    lax.fori_loop(0, blocks, body, 0)


SMEM = pl.BlockSpec(memory_space=pltpu.SMEM)


def attend_forward(order, qkv, tile):
    kinds, blocks, half, lanes = qkv.shape
    length = blocks * half
    return pl.pallas_call(
        functools.partial(forward_kernel, tile),
        out_shape=(
            jax.ShapeDtypeStruct((blocks, half, LANES), BF16),
            jax.ShapeDtypeStruct((LANES, length), F32),
            jax.ShapeDtypeStruct((2, length), F32),
        ),
        in_specs=[SMEM, VMEM],
        out_specs=(VMEM, VMEM, VMEM),
        scratch_shapes=[
            pltpu.VMEM((length, LANES), BF16),
            pltpu.VMEM((length, LANES), BF16),
            pltpu.VMEM((length, LANES), BF16),
            pltpu.VMEM((LANES, length), BF16),
            pltpu.VMEM((length, LANES), BF16),
        ],
        compiler_params=params(),
        name="attend_forward",
    )(order, qkv)


def backward_kernel(
    tile, order_ref, qkv_ref, grad_ref, att_ref, lse_ref, out_ref, q_s, k_s, v_s, g_s, kt_s, dq_s, dk_s, dv_s
):
    blocks, half = grad_ref.shape[0], grad_ref.shape[1]
    length = blocks * half
    tiles = length // tile
    sort_blocks(
        order_ref,
        [qkv_ref.at[0], qkv_ref.at[1], qkv_ref.at[2], grad_ref],
        [q_s, k_s, v_s, g_s],
        blocks,
        half,
    )
    for t in range(tiles):
        span = slice(t * tile, (t + 1) * tile)
        kt_s[:, span] = k_s[span, :].T
    scale = HD ** (-0.5)
    rows_iota = lax.broadcasted_iota(jnp.int32, (tile, tile), 0)
    cols_iota = lax.broadcasted_iota(jnp.int32, (tile, tile), 1)
    allowed = rows_iota <= cols_iota
    masks = [lane_mask(tile, head) for head in range(2)]
    dk_s[...] = jnp.zeros_like(dk_s)
    dv_s[...] = jnp.zeros_like(dv_s)

    for qt in range(tiles):
        q_span = slice(qt * tile, (qt + 1) * tile)
        query = q_s[q_span, :] * jnp.asarray(scale, BF16)
        grad = g_s[q_span, :]
        queries = [jnp.where(masks[head], query, jnp.zeros_like(query)) for head in range(2)]
        grads = [jnp.where(masks[head], grad, jnp.zeros_like(grad)) for head in range(2)]
        product = grad.astype(F32).T * att_ref[:, q_span]
        dots = [jnp.sum(product[head * HD : (head + 1) * HD], axis=0, keepdims=True) for head in range(2)]
        totals = [lse_ref[head : head + 1, q_span] for head in range(2)]

        def step(kt, state, masked, queries=queries, grads=grads, dots=dots, totals=totals):
            start = pl.multiple_of(kt * tile, tile)
            rows = pl.ds(start, tile)
            keys = k_s[rows, :]
            values = v_s[rows, :]
            dk = dk_s[rows, :]
            dv = dv_s[rows, :]
            new = []
            for head in range(2):
                scores = nt(keys, queries[head])
                if masked:
                    scores = jnp.where(allowed, scores, NEG_BIG)
                soft = jnp.exp(scores - totals[head])
                dsoft = nt(values, grads[head])
                dscore = (soft * (dsoft - dots[head])).astype(BF16)
                dv = dv + nn(soft.astype(BF16), grads[head])
                dk = dk + nn(dscore, queries[head])
                new.append(state[head] + nn(kt_s[head * HD : (head + 1) * HD, rows], dscore))
            dk_s[rows, :] = dk
            dv_s[rows, :] = dv
            return tuple(new)

        state = (jnp.zeros((HD, tile), F32), jnp.zeros((HD, tile), F32))
        state = step(qt, state, True)
        if qt > 0:
            state = lax.fori_loop(0, qt, lambda kt, s, step=step: step(kt, s, False), state)
        dq = jnp.concatenate(state, axis=0) * scale
        dq_s[q_span, :] = dq.T.astype(BF16)

    def body(block, carry):
        start = pl.multiple_of(block * half, half)
        place = order_ref[block]
        out_ref[0, place] = dq_s[pl.ds(start, half), :]
        out_ref[1, place] = dk_s[pl.ds(start, half), :].astype(BF16)
        out_ref[2, place] = dv_s[pl.ds(start, half), :].astype(BF16)
        return carry

    lax.fori_loop(0, blocks, body, 0)


def attend_backward(order, qkv, grad, att, lse, tile):
    kinds, blocks, half, lanes = qkv.shape
    length = blocks * half
    return pl.pallas_call(
        functools.partial(backward_kernel, tile),
        out_shape=jax.ShapeDtypeStruct((3, blocks, half, LANES), BF16),
        in_specs=[SMEM, VMEM, VMEM, VMEM, VMEM],
        out_specs=VMEM,
        scratch_shapes=[pltpu.VMEM((length, LANES), BF16)] * 4
        + [pltpu.VMEM((LANES, length), BF16), pltpu.VMEM((length, LANES), BF16)]
        + [pltpu.VMEM((length, LANES), F32)] * 2,
        compiler_params=params(),
        name="attend_backward",
    )(order, qkv, grad, att, lse)


def mm(left, right):
    return jnp.matmul(left, right, preferred_element_type=F32)


def mm_nt(left, right):
    return lax.dot_general(left, right, (((1,), (1,)), ((), ())), preferred_element_type=F32)


def mm_tn(left, right):
    return lax.dot_general(left, right, (((0,), (0,)), ((), ())), preferred_element_type=F32)


def gelu_tanh(values):
    return jax.nn.gelu(values, approximate=True)


def local(
    tokens,
    block_pairs,
    out_grad,
    ln1_gain,
    ln1_bias,
    qkv_weight,
    query_bias,
    value_bias,
    out_weight,
    out_bias,
    ln2_gain,
    ln2_bias,
    up_weight,
    up_bias,
    down_weight,
    down_bias,
):
    n_ctx, planes = lax.axis_size("ctx"), lax.axis_size("fsdp")
    c, f = lax.axis_index("ctx"), lax.axis_index("fsdp")
    local_rows, seqs, width = tokens.shape
    half = local_rows // 2
    devices = n_ctx * planes
    blocks = 2 * devices
    length = devices * local_rows
    heads = width // HD
    slots = planes * (-(-heads // devices))
    assert slots == planes and planes % seqs == 0
    span = slots * HD
    rows = local_rows * seqs
    plane_rows = n_ctx * rows
    quarter = width // planes
    ff = up_weight.shape[1]
    ff_quarter = ff // planes
    ff_piece = ff_quarter // n_ctx
    ff_span = ff_piece * planes
    tile = 256

    device_ids = jnp.arange(devices, dtype=jnp.int32)
    device_of_block = jnp.sum(
        jnp.where(block_pairs[None, :] == device_ids[:, None], device_ids[None, :], 0), axis=1
    )
    order = jnp.concatenate([device_of_block * 2, device_of_block[::-1] * 2 + 1]).astype(jnp.int32)

    qkv_padded = jnp.pad(qkv_weight, ((0, 0), (0, n_ctx * span - width)))
    qkv_own = jnp.concatenate(
        [lax.dynamic_slice(qkv_padded, (0, k * width + c * span), (quarter, span)) for k in range(3)], axis=1
    )
    qkv_slice = lax.all_gather(qkv_own, "fsdp", axis=0, tiled=True)
    out_padded = jnp.pad(out_weight, ((span, span), (0, 0)))
    out_start = jnp.clip(c * span - f * quarter + span, 0, quarter + span)
    out_slice = lax.psum(lax.dynamic_slice(out_padded, (out_start, 0), (span, width)), "fsdp")
    up_own = jnp.concatenate(
        [
            lax.dynamic_slice(up_weight, (0, k * ff_quarter + c * ff_piece), (quarter, ff_piece))
            for k in range(planes)
        ],
        axis=1,
    )
    up_slice = lax.all_gather(up_own, "fsdp", axis=0, tiled=True)
    down_own = lax.dynamic_slice(down_weight, (c * ff_piece, 0), (ff_piece, width))
    down_slice = lax.all_gather(down_own, "fsdp", axis=0, tiled=True)

    packed = jnp.concatenate(
        [
            jnp.stack([ln1_gain, ln1_bias, ln2_gain, ln2_bias, query_bias, value_bias, out_bias, down_bias]),
            up_bias.reshape(ff // width, quarter),
        ]
    )
    vectors = lax.all_gather(packed, "fsdp", axis=0).astype(F32)
    gain1, bias1, gain2, bias2, bias_q, bias_v, bias_o, bias_d = [
        vectors[:, k].reshape(width) for k in range(8)
    ]
    bias_up = lax.dynamic_slice(
        vectors[:, 8:].reshape(planes, ff_quarter), (0, c * ff_piece), (planes, ff_piece)
    ).reshape(ff_span)

    def head_part(vector):
        return lax.dynamic_slice(jnp.pad(vector, (0, n_ctx * span - width)), (c * span,), (span,))

    qkv_shift = jnp.concatenate([head_part(bias_q), jnp.zeros((span,), F32), head_part(bias_v)])

    tok = jnp.swapaxes(tokens, 0, 1).reshape(rows, width)
    og = jnp.swapaxes(out_grad, 0, 1).reshape(rows, width)
    og_all = lax.all_gather(og, "ctx", axis=0, tiled=True)

    h1 = first_norm_gather(tok, jnp.stack([gain1, bias1]), n_ctx).reshape(plane_rows, width)
    qkv = (mm(h1, qkv_slice) + qkv_shift).astype(BF16)
    qkv_heads = to_heads(qkv.reshape(n_ctx, seqs, local_rows, 3 * span), 3, planes, 5)
    qkv_heads = qkv_heads.reshape(3, blocks, half, LANES)
    att_heads, att_exact, lse = attend_forward(order, qkv_heads, tile)
    att = to_tokens(att_heads.reshape(1, n_ctx, planes, local_rows, LANES), seqs, 6).reshape(plane_rows, span)
    branch = mm(att, out_slice).astype(BF16).reshape(n_ctx, rows, width)
    mixed, h2 = second_norm_gather(branch, tok, jnp.stack([gain2, bias2, bias_o]))
    h2 = h2.reshape(plane_rows, width)
    up = mm(h2, up_slice) + bias_up
    activated, gelu_back = jax.vjp(gelu_tanh, up)
    act = activated.astype(BF16)
    out_part = mm(act, down_slice).astype(BF16).reshape(n_ctx, rows, width)

    (d_up,) = gelu_back(mm_nt(og_all, down_slice))
    d_up_low = d_up.astype(BF16)
    d_h2 = mm_nt(d_up_low, up_slice).astype(BF16).reshape(n_ctx, rows, width)
    d_mixed, sums2, d_branch = second_norm_back(d_h2, mixed, og, gain2[None, :])
    d_branch = d_branch.reshape(plane_rows, width)
    d_att = mm_nt(d_branch, out_slice).astype(BF16)
    d_att_heads = to_heads(d_att.reshape(n_ctx, seqs, local_rows, span), 1, planes, 7)
    d_heads = attend_backward(order, qkv_heads, d_att_heads.reshape(blocks, half, LANES), att_exact, lse, tile)
    d_qkv = to_tokens(d_heads.reshape(3, n_ctx, planes, local_rows, LANES), seqs, 8)
    d_qkv = d_qkv.reshape(plane_rows, 3 * span)
    d_h1 = mm_nt(d_qkv, qkv_slice).astype(BF16).reshape(n_ctx, rows, width)
    block_out = block_result(out_part, mixed, bias_d[None, :])
    grad_tok, sums1 = first_norm_back(d_h1, tok, d_mixed, gain1[None, :])

    def reduce_own(part):
        return lax.psum_scatter(part.astype(BF16), "fsdp", scatter_dimension=0, tiled=True)

    down_grad = lax.all_gather(reduce_own(mm_tn(act, og_all)), "ctx", axis=0, tiled=True).astype(F32)
    up_parts = lax.all_gather(reduce_own(mm_tn(h2, d_up_low)), "ctx", axis=0)
    up_grad = (
        up_parts.reshape(n_ctx, quarter, planes, ff_piece).transpose(1, 2, 0, 3).reshape(quarter, ff).astype(F32)
    )
    out_parts = lax.all_gather(reduce_own(mm_tn(att, d_branch)), ("ctx", "fsdp"), axis=0, tiled=True)
    out_grad_own = lax.dynamic_slice(out_parts, (f * quarter, 0), (quarter, width)).astype(F32)
    qkv_parts = lax.all_gather(reduce_own(mm_tn(h1, d_qkv)), "ctx", axis=0)
    qkv_grad = jnp.concatenate(
        [
            qkv_parts[:, :, k * span : (k + 1) * span].transpose(1, 0, 2).reshape(quarter, n_ctx * span)[:, :width]
            for k in range(3)
        ],
        axis=1,
    ).astype(F32)

    def spread(values, count):
        return lax.dynamic_update_slice(jnp.zeros((n_ctx * count,), F32), values, (c * count,))

    d_qkv_sum = jnp.sum(d_qkv.astype(F32), axis=0)
    d_up_sum = jnp.sum(d_up_low.astype(F32), axis=0).reshape(planes, ff_piece)
    up_spread = lax.dynamic_update_slice(jnp.zeros((planes, ff_quarter), F32), d_up_sum, (0, c * ff_piece))
    wide = jnp.concatenate([sums1, sums2])
    total_wide, total_q, total_v, total_up = lax.psum(
        (wide, spread(d_qkv_sum[:span], span), spread(d_qkv_sum[2 * span :], span), up_spread), ("ctx", "fsdp")
    )

    def own(vector):
        return lax.dynamic_slice(vector, (f * quarter,), (quarter,))

    up_bias_grad = lax.dynamic_slice(total_up, (f, 0), (1, ff_quarter)).reshape(ff_quarter)

    def back(values):
        return jnp.swapaxes(values.reshape(seqs, local_rows, width), 0, 1)

    return (
        back(block_out),
        back(grad_tok),
        own(total_wide[0]),
        own(total_wide[1]),
        qkv_grad,
        own(total_q),
        own(total_v),
        out_grad_own,
        own(total_wide[4]),
        own(total_wide[2]),
        own(total_wide[3]),
        up_grad,
        up_bias_grad,
        down_grad,
        own(total_wide[5]),
    )


def solution(mesh):
    both, row, vec, mat = P(("ctx", "fsdp"), None, None), P(), P("fsdp"), P("fsdp", None)
    in_specs = (both, row, both, vec, vec, mat, vec, vec, mat, vec, vec, vec, mat, vec, mat, vec)
    out_specs = (both, both, vec, vec, mat, vec, vec, mat, vec, vec, vec, mat, vec, mat, vec)
    return jax.shard_map(local, mesh=mesh, in_specs=in_specs, out_specs=out_specs, check_vma=False)
```

```python
import functools

import jax
import jax.numpy as jnp
from jax import lax
from jax.experimental import pallas as pl
from jax.experimental.pallas import tpu as pltpu
from jax.sharding import PartitionSpec as P

HD = 64
LANES = 128
NORM_EPS = 1e-05
NEG_BIG = -1e30
MESH = pl.DeviceIdType.MESH
F32 = jnp.float32
BF16 = jnp.bfloat16
ANY = pl.BlockSpec(memory_space=pl.ANY)
VMEM = pl.BlockSpec(memory_space=pltpu.VMEM)
DMA = pltpu.SemaphoreType.DMA
VMEM_LIMIT = 56 * 1024 * 1024


def params(cid=None):
    if cid is None:
        return pltpu.CompilerParams(vmem_limit_bytes=VMEM_LIMIT)
    return pltpu.CompilerParams(
        collective_id=cid, has_side_effects=True, vmem_limit_bytes=VMEM_LIMIT
    )


def plane_peers(chips):
    me = lax.axis_index("ctx")
    core = lax.rem(me, 2)
    chip = me // 2
    sibling = chip * 2 + 1 - core
    to = [lax.rem(chip + k, chips) * 2 + core for k in range(1, chips)]
    come = [lax.rem(chip + chips - k, chips) * 2 + core for k in range(1, chips)]
    return me, core, chip, sibling, to, come


def greet(axis, peers):
    barrier = pltpu.get_barrier_semaphore()
    for peer in peers:
        pl.semaphore_signal(barrier, inc=1, device_id={axis: peer}, device_id_type=MESH)
    pl.semaphore_wait(barrier, len(peers))


def send(src, dst, send_sem, recv_sem, axis, peer):
    copy = pltpu.make_async_remote_copy(
        src_ref=src,
        dst_ref=dst,
        send_sem=send_sem,
        recv_sem=recv_sem,
        device_id={axis: peer},
        device_id_type=MESH,
    )
    copy.start()
    return copy


def plane_gather_start(owns, alls, sems, chips):
    far_send, far_recv, near_send, near_recv, local_sem = sems
    me, core, chip, sibling, to, come = plane_peers(chips)
    far, near, local = [], [], []
    for i, (own_ref, all_ref) in enumerate(zip(owns, alls)):
        far.append(
            [
                send(own_ref, all_ref.at[me], far_send.at[i, k], far_recv.at[i, k], "ctx", to[k])
                for k in range(chips - 1)
            ]
        )
        last = chips - 1
        near.append(send(own_ref, all_ref.at[me], near_send.at[i, last], near_recv.at[i, last], "ctx", sibling))
        copy = pltpu.make_async_copy(own_ref, all_ref.at[me], local_sem.at[i])
        copy.start()
        local.append(copy)
    return far, near, local


def plane_gather_finish(started, alls, sems, chips):
    far_send, far_recv, near_send, near_recv, local_sem = sems
    me, core, chip, sibling, to, come = plane_peers(chips)
    far, near, local = started
    near = list(near)
    for i, all_ref in enumerate(alls):
        for k in range(chips - 1):
            far[i][k].wait_recv()
            block = all_ref.at[come[k]]
            near.append(send(block, block, near_send.at[i, k], near_recv.at[i, k], "ctx", sibling))
    for group in far:
        for copy in group:
            copy.wait_send()
    for copy in near + local:
        copy.wait()


def plane_gather(owns, alls, sems, chips):
    plane_gather_finish(plane_gather_start(owns, alls, sems, chips), alls, sems, chips)


def plane_scatter(part_ref, mine, paired, stage, arrived, sems, chips):
    far_send, far_recv, near_send, near_recv, local_sem = sems
    me, core, chip, sibling, to, come = plane_peers(chips)
    near, local = [None] * chips, [None] * chips
    order = list(range(1, chips)) + [0]
    for k in order:
        base = lax.rem(chip + k, chips) * 2
        near[k] = send(
            part_ref.at[base + 1 - core], paired.at[k], near_send.at[k], near_recv.at[k], "ctx", sibling
        )
        local[k] = pltpu.make_async_copy(part_ref.at[base + core], mine.at[k], local_sem.at[k])
        local[k].start()
    far = []
    for k in range(1, chips):
        local[k].wait()
        near[k].wait_recv()
        stage[k - 1] = (mine[k].astype(F32) + paired[k].astype(F32)).astype(BF16)
        far.append(
            send(stage.at[k - 1], arrived.at[k - 1], far_send.at[k - 1], far_recv.at[k - 1], "ctx", to[k - 1])
        )
    local[0].wait()
    near[0].wait_recv()
    total = mine[0].astype(F32) + paired[0].astype(F32)
    for k in range(chips - 1):
        far[k].wait_recv()
        total = total + arrived[k].astype(F32)
    for copy in far + near:
        copy.wait_send()
    return total


def gather_sems(chips, count=1):
    return [DMA((count, chips - 1))] * 2 + [DMA((count, chips))] * 2 + [DMA((count,))]


def scatter_scratch(chips, rows, width):
    return [
        pltpu.VMEM((chips, rows, width), BF16),
        pltpu.VMEM((chips, rows, width), BF16),
        pltpu.VMEM((chips - 1, rows, width), BF16),
        pltpu.VMEM((chips - 1, rows, width), BF16),
        DMA((chips - 1,)),
        DMA((chips - 1,)),
        DMA((chips,)),
        DMA((chips,)),
        DMA((chips,)),
    ]


def normalize(values):
    average = jnp.mean(values, axis=-1, keepdims=True)
    centered = values - average
    variance = jnp.mean(centered * centered, axis=-1, keepdims=True)
    inverse = lax.rsqrt(variance + NORM_EPS)
    return centered * inverse, inverse


def norm_backward(grad, gain, unit, inverse):
    scaled = grad * gain
    first = jnp.mean(scaled, axis=-1, keepdims=True)
    second = jnp.mean(scaled * unit, axis=-1, keepdims=True)
    return (scaled - first - unit * second) * inverse


def first_kernel(
    chips, planes, quarter, tok_ref, og_ref, vec_ref, vecs_ref, h1_ref, ogs_ref, own, v_send, v_recv, v_local, *sems
):
    me, core, chip, sibling, to, come = plane_peers(chips)
    plane = lax.axis_index("fsdp")
    barrier = pltpu.get_barrier_semaphore()
    for peer in to + [sibling]:
        pl.semaphore_signal(barrier, inc=1, device_id={"ctx": peer}, device_id_type=MESH)
    for k in range(1, planes):
        peer = lax.rem(plane + k, planes)
        pl.semaphore_signal(barrier, inc=1, device_id={"fsdp": peer}, device_id_type=MESH)
    pl.semaphore_wait(barrier, chips + planes - 1)
    copies = []
    for k in range(1, planes):
        peer = lax.rem(plane + k, planes)
        copies.append(send(vec_ref, vecs_ref.at[plane], v_send.at[k - 1], v_recv.at[k - 1], "fsdp", peer))
    local = pltpu.make_async_copy(vec_ref, vecs_ref.at[plane], v_local)
    local.start()
    og_sems, h1_sems = sems[:5], sems[5:]
    og_started = plane_gather_start([og_ref], [ogs_ref], og_sems, chips)
    unit, inverse = normalize(tok_ref[...].astype(F32))
    for copy in copies + [local]:
        copy.wait()
    gain, shift = [
        jnp.concatenate([vecs_ref[j, k : k + 1, :quarter].astype(F32) for j in range(planes)], axis=1) for k in range(2)
    ]
    own[...] = (unit * gain + shift).astype(BF16)
    h1_started = plane_gather_start([own], [h1_ref], h1_sems, chips)
    plane_gather_finish(og_started, [ogs_ref], og_sems, chips)
    plane_gather_finish(h1_started, [h1_ref], h1_sems, chips)


def first_norm_gather(tok, og, vec, n_ctx, planes):
    rows, width = tok.shape
    chips = n_ctx // 2
    whole = jax.ShapeDtypeStruct((n_ctx, rows, width), BF16)
    return pl.pallas_call(
        functools.partial(first_kernel, chips, planes, width // planes),
        out_shape=(jax.ShapeDtypeStruct((planes,) + vec.shape, BF16), whole, whole),
        in_specs=[VMEM, ANY, VMEM],
        out_specs=(VMEM, ANY, ANY),
        scratch_shapes=[pltpu.VMEM((rows, width), BF16), DMA((planes - 1,)), DMA((planes - 1,)), DMA]
        + gather_sems(chips)
        + gather_sems(chips),
        compiler_params=params(0),
        name="norm_gather",
    )(tok, og, vec)


def second_kernel(chips, part_ref, tok_ref, vec_ref, mixed_ref, all_ref, own, *scratch):
    me, core, chip, sibling, to, come = plane_peers(chips)
    greet("ctx", to + [sibling])
    total = plane_scatter(part_ref, *scratch[:4], scratch[4:9], chips)
    mixed = tok_ref[...].astype(F32) + total + vec_ref[2:3, :]
    mixed_ref[...] = mixed
    unit, inverse = normalize(mixed)
    own[...] = (unit * vec_ref[0:1, :] + vec_ref[1:2, :]).astype(BF16)
    plane_gather([own], [all_ref], scratch[9:], chips)


def second_norm_gather(part, tok, vecs):
    n_ctx, rows, width = part.shape
    chips = n_ctx // 2
    return pl.pallas_call(
        functools.partial(second_kernel, chips),
        out_shape=(
            jax.ShapeDtypeStruct((rows, width), F32),
            jax.ShapeDtypeStruct((n_ctx, rows, width), BF16),
        ),
        in_specs=[ANY, VMEM, VMEM],
        out_specs=(VMEM, ANY),
        scratch_shapes=[pltpu.VMEM((rows, width), BF16)]
        + scatter_scratch(chips, rows, width)
        + gather_sems(chips),
        compiler_params=params(1),
        name="scatter_norm_gather",
    )(part, tok, vecs)


def third_kernel(chips, part_ref, mixed_ref, og_ref, vec_ref, dmixed_ref, sums_ref, all_ref, own, *scratch):
    me, core, chip, sibling, to, come = plane_peers(chips)
    greet("ctx", to + [sibling])
    unit, inverse = normalize(mixed_ref[...])
    grad = plane_scatter(part_ref, *scratch[:4], scratch[4:9], chips)
    out_grad = og_ref[...].astype(F32)
    dmixed = out_grad + norm_backward(grad, vec_ref[0:1, :], unit, inverse)
    dmixed_ref[...] = dmixed
    low = dmixed.astype(BF16)
    own[...] = low
    sums_ref[0:1, :] = jnp.sum(grad * unit, axis=0, keepdims=True)
    sums_ref[1:2, :] = jnp.sum(grad, axis=0, keepdims=True)
    sums_ref[2:3, :] = jnp.sum(low.astype(F32), axis=0, keepdims=True)
    sums_ref[3:4, :] = jnp.sum(out_grad, axis=0, keepdims=True)
    plane_gather([own], [all_ref], scratch[9:], chips)


def second_norm_back(part, mixed, og, vecs):
    n_ctx, rows, width = part.shape
    chips = n_ctx // 2
    return pl.pallas_call(
        functools.partial(third_kernel, chips),
        out_shape=(
            jax.ShapeDtypeStruct((rows, width), F32),
            jax.ShapeDtypeStruct((4, width), F32),
            jax.ShapeDtypeStruct((n_ctx, rows, width), BF16),
        ),
        in_specs=[ANY, VMEM, VMEM, VMEM],
        out_specs=(VMEM, VMEM, ANY),
        scratch_shapes=[pltpu.VMEM((rows, width), BF16)]
        + scatter_scratch(chips, rows, width)
        + gather_sems(chips),
        compiler_params=params(2),
        name="scatter_back_gather",
    )(part, mixed, og, vecs)


def fourth_kernel(
    chips, part_ref, out_part_ref, tok_ref, dmixed_ref, mixed_ref, vec_ref, grad_ref, out_ref, sums_ref, *scratch
):
    me, core, chip, sibling, to, come = plane_peers(chips)
    greet("ctx", to + [sibling])
    unit, inverse = normalize(tok_ref[...].astype(F32))
    grad = plane_scatter(part_ref, *scratch[:4], scratch[4:9], chips)
    grad_ref[...] = dmixed_ref[...] + norm_backward(grad, vec_ref[0:1, :], unit, inverse)
    sums_ref[0:1, :] = jnp.sum(grad * unit, axis=0, keepdims=True)
    sums_ref[1:2, :] = jnp.sum(grad, axis=0, keepdims=True)
    total = plane_scatter(out_part_ref, *scratch[9:13], scratch[13:], chips)
    out_ref[...] = (mixed_ref[...] + total + vec_ref[1:2, :]).astype(BF16)


def first_norm_back(part, out_part, tok, dmixed, mixed, vecs):
    n_ctx, rows, width = part.shape
    chips = n_ctx // 2
    return pl.pallas_call(
        functools.partial(fourth_kernel, chips),
        out_shape=(
            jax.ShapeDtypeStruct((rows, width), F32),
            jax.ShapeDtypeStruct((rows, width), BF16),
            jax.ShapeDtypeStruct((2, width), F32),
        ),
        in_specs=[ANY, ANY, VMEM, VMEM, VMEM, VMEM],
        out_specs=(VMEM, VMEM, VMEM),
        scratch_shapes=scatter_scratch(chips, rows, width) * 2,
        compiler_params=params(3),
        name="scatter_back",
    )(part, out_part, tok, dmixed, mixed, vecs)


def gather_kernel(chips, count, *refs):
    me, core, chip, sibling, to, come = plane_peers(chips)
    greet("ctx", to + [sibling])
    plane_gather(refs[:count], refs[count : 2 * count], refs[2 * count :], chips)


def gather_plane(arrays, n_ctx, cid):
    chips, count = n_ctx // 2, len(arrays)
    return pl.pallas_call(
        functools.partial(gather_kernel, chips, count),
        out_shape=tuple(jax.ShapeDtypeStruct((n_ctx,) + a.shape, a.dtype) for a in arrays),
        in_specs=[ANY] * count,
        out_specs=(ANY,) * count,
        scratch_shapes=gather_sems(chips, count),
        compiler_params=params(cid),
        name="gather_plane",
    )(*arrays)


def total_kernel(n_ctx, planes, part_ref, out_ref, arrived, own, others, z_send, z_recv, c_send, c_recv):
    me, plane = lax.axis_index("ctx"), lax.axis_index("fsdp")
    barrier = pltpu.get_barrier_semaphore()
    for k in range(1, planes):
        peer = lax.rem(plane + k, planes)
        pl.semaphore_signal(barrier, inc=1, device_id={"fsdp": peer}, device_id_type=MESH)
    for k in range(1, n_ctx):
        peer = lax.rem(me + k, n_ctx)
        pl.semaphore_signal(barrier, inc=1, device_id={"ctx": peer}, device_id_type=MESH)
    pl.semaphore_wait(barrier, planes + n_ctx - 2)
    far = []
    for k in range(1, planes):
        peer = lax.rem(plane + k, planes)
        far.append(send(part_ref.at[peer], arrived.at[k - 1], z_send.at[k - 1], z_recv.at[k - 1], "fsdp", peer))
    total = part_ref[plane]
    for k in range(1, planes):
        far[k - 1].wait()
        total = total + arrived[k - 1]
    own[...] = total
    near = []
    for k in range(1, n_ctx):
        peer = lax.rem(me + k, n_ctx)
        near.append(send(own, others.at[k - 1], c_send.at[k - 1], c_recv.at[k - 1], "ctx", peer))
    for k in range(1, n_ctx):
        near[k - 1].wait()
        total = total + others[k - 1]
    out_ref[...] = total


def total_vectors(part, n_ctx, cid):
    planes, size = part.shape[0], part.shape[1:]
    return pl.pallas_call(
        functools.partial(total_kernel, n_ctx, planes),
        out_shape=jax.ShapeDtypeStruct(size, F32),
        in_specs=[VMEM],
        out_specs=VMEM,
        scratch_shapes=[
            pltpu.VMEM((planes - 1,) + size, F32),
            pltpu.VMEM(size, F32),
            pltpu.VMEM((n_ctx - 1,) + size, F32),
            DMA((planes - 1,)),
            DMA((planes - 1,)),
            DMA((n_ctx - 1,)),
            DMA((n_ctx - 1,)),
        ],
        compiler_params=params(cid),
        name="total_vectors",
    )(part)


def to_heads_kernel(kinds, planes, seqs, tok_ref, head_ref, send_sems, recv_sems, local_sems):
    me = lax.axis_index("fsdp")
    pairs = planes // seqs
    greet("fsdp", [lax.rem(me + k, planes) for k in range(1, planes)])
    width = tok_ref.shape[3] // kinds

    def source(kind, unit):
        start = pl.multiple_of(kind * width + lax.rem(unit, pairs) * LANES, LANES)
        return tok_ref.at[:, unit // pairs, :, pl.ds(start, LANES)]

    copies = []
    for k in range(1, planes):
        unit = lax.rem(me + k, planes)
        for kind in range(kinds):
            copies.append(
                send(
                    source(kind, unit),
                    head_ref.at[kind, :, me],
                    send_sems.at[kind, k - 1],
                    recv_sems.at[kind, k - 1],
                    "fsdp",
                    unit,
                )
            )
    local = []
    for kind in range(kinds):
        copy = pltpu.make_async_copy(source(kind, me), head_ref.at[kind, :, me], local_sems.at[kind])
        copy.start()
        local.append(copy)
    for copy in copies + local:
        copy.wait()


def to_heads(tok, kinds, planes, cid):
    n_ctx, seqs, rows, width = tok.shape
    return pl.pallas_call(
        functools.partial(to_heads_kernel, kinds, planes, seqs),
        out_shape=jax.ShapeDtypeStruct((kinds, n_ctx, planes, rows, LANES), tok.dtype),
        in_specs=[ANY],
        out_specs=ANY,
        scratch_shapes=[DMA((kinds, planes - 1)), DMA((kinds, planes - 1)), DMA((kinds,))],
        compiler_params=params(cid),
        name="to_heads",
    )(tok)


def to_tokens_kernel(kinds, planes, seqs, chips, beside, *refs):
    head_ref, owns = refs[0], refs[1 : 1 + beside]
    tok_ref, alls = refs[1 + beside], refs[2 + beside : 2 + 2 * beside]
    send_sems, recv_sems, local_sems = refs[2 + 2 * beside : 5 + 2 * beside]
    sems = refs[5 + 2 * beside :]
    plane_me, core, chip, sibling, to, come = plane_peers(chips)
    me = lax.axis_index("fsdp")
    pairs = planes // seqs
    barrier = pltpu.get_barrier_semaphore()
    for k in range(1, planes):
        peer = lax.rem(me + k, planes)
        pl.semaphore_signal(barrier, inc=1, device_id={"fsdp": peer}, device_id_type=MESH)
    if beside:
        for peer in to + [sibling]:
            pl.semaphore_signal(barrier, inc=1, device_id={"ctx": peer}, device_id_type=MESH)
    pl.semaphore_wait(barrier, planes - 1 + (chips if beside else 0))
    width = tok_ref.shape[3] // kinds

    def target(kind):
        start = pl.multiple_of(kind * width + lax.rem(me, pairs) * LANES, LANES)
        return tok_ref.at[:, me // pairs, :, pl.ds(start, LANES)]

    copies = []
    for k in range(1, planes):
        peer = lax.rem(me + k, planes)
        for kind in range(kinds):
            copies.append(
                send(
                    head_ref.at[kind, :, peer],
                    target(kind),
                    send_sems.at[kind, k - 1],
                    recv_sems.at[kind, k - 1],
                    "fsdp",
                    peer,
                )
            )
    local = []
    for kind in range(kinds):
        copy = pltpu.make_async_copy(head_ref.at[kind, :, me], target(kind), local_sems.at[kind])
        copy.start()
        local.append(copy)
    if beside:
        plane_gather(owns, alls, sems, chips)
    for copy in copies + local:
        copy.wait()


def to_tokens(heads, seqs, cid, beside=()):
    kinds, n_ctx, planes, rows, lanes = heads.shape
    width = kinds * (planes // seqs) * LANES
    count = len(beside)
    return pl.pallas_call(
        functools.partial(to_tokens_kernel, kinds, planes, seqs, n_ctx // 2, count),
        out_shape=(jax.ShapeDtypeStruct((n_ctx, seqs, rows, width), heads.dtype),)
        + tuple(jax.ShapeDtypeStruct((n_ctx,) + a.shape, a.dtype) for a in beside),
        in_specs=[ANY] * (1 + count),
        out_specs=(ANY,) * (1 + count),
        scratch_shapes=[DMA((kinds, planes - 1)), DMA((kinds, planes - 1)), DMA((kinds,))]
        + (gather_sems(n_ctx // 2, count) if count else []),
        compiler_params=params(cid),
        name="to_tokens",
    )(heads, *beside)


def nt(left, right):
    return lax.dot_general(left, right, (((1,), (1,)), ((), ())), preferred_element_type=F32)


def nn(left, right):
    return lax.dot_general(left, right, (((1,), (0,)), ((), ())), preferred_element_type=F32)


def sort_blocks(order_ref, source_refs, sorted_refs, blocks, half):
    def body(block, carry):
        place = order_ref[block]
        start = pl.multiple_of(block * half, half)
        for source, target in zip(source_refs, sorted_refs):
            target[pl.ds(start, half), :] = source[place]
        return carry

    lax.fori_loop(0, blocks, body, 0)


def lane_mask(rows, head):
    lane = lax.broadcasted_iota(jnp.int32, (rows, LANES), 1)
    return (lane < HD) if head == 0 else (lane >= HD)


def forward_kernel(tile, order_ref, qkv_ref, out_ref, att_ref, lse_ref, q_s, k_s, v_s, vt_s, o_s):
    blocks, half = out_ref.shape[0], out_ref.shape[1]
    length = blocks * half
    tiles = length // tile
    sort_blocks(order_ref, [qkv_ref.at[0], qkv_ref.at[1], qkv_ref.at[2]], [q_s, k_s, v_s], blocks, half)
    for t in range(tiles):
        span = slice(t * tile, (t + 1) * tile)
        vt_s[:, span] = v_s[span, :].T
    scale = HD ** (-0.5)
    rows_iota = lax.broadcasted_iota(jnp.int32, (tile, tile), 0)
    cols_iota = lax.broadcasted_iota(jnp.int32, (tile, tile), 1)
    allowed = rows_iota <= cols_iota
    masks = [lane_mask(tile, head) for head in range(2)]

    for qt in range(tiles):
        q_span = slice(qt * tile, (qt + 1) * tile)
        query = q_s[q_span, :] * jnp.asarray(scale, BF16)
        queries = [jnp.where(masks[head], query, jnp.zeros_like(query)) for head in range(2)]

        def step(kt, state, masked, queries=queries):
            start = pl.multiple_of(kt * tile, tile)
            keys = k_s[pl.ds(start, tile), :]
            new = []
            for head in range(2):
                top, total, acc = state[head]
                scores = nt(keys, queries[head])
                if masked:
                    scores = jnp.where(allowed, scores, NEG_BIG)
                new_top = jnp.maximum(top, jnp.max(scores, axis=0, keepdims=True))
                soft = jnp.exp(scores - new_top)
                factor = jnp.exp(top - new_top)
                total = total * factor + jnp.sum(soft, axis=0, keepdims=True)
                values = vt_s[head * HD : (head + 1) * HD, pl.ds(start, tile)]
                acc = acc * factor + nn(values, soft.astype(BF16))
                new.append((new_top, total, acc))
            return tuple(new)

        state = tuple(
            (jnp.full((1, tile), NEG_BIG, F32), jnp.zeros((1, tile), F32), jnp.zeros((HD, tile), F32))
            for head in range(2)
        )
        state = step(qt, state, True)
        if qt > 0:
            state = lax.fori_loop(0, qt, lambda kt, s, step=step: step(kt, s, False), state)
        for head in range(2):
            top, total, acc = state[head]
            att_ref[head * HD : (head + 1) * HD, q_span] = acc / total
            lse_ref[head : head + 1, q_span] = top + jnp.log(total)
        o_s[q_span, :] = att_ref[:, q_span].T.astype(BF16)

    def body(block, carry):
        start = pl.multiple_of(block * half, half)
        out_ref[order_ref[block]] = o_s[pl.ds(start, half), :]
        return carry

    lax.fori_loop(0, blocks, body, 0)


SMEM = pl.BlockSpec(memory_space=pltpu.SMEM)


def attend_forward(order, qkv, tile):
    kinds, blocks, half, lanes = qkv.shape
    length = blocks * half
    return pl.pallas_call(
        functools.partial(forward_kernel, tile),
        out_shape=(
            jax.ShapeDtypeStruct((blocks, half, LANES), BF16),
            jax.ShapeDtypeStruct((LANES, length), F32),
            jax.ShapeDtypeStruct((2, length), F32),
        ),
        in_specs=[SMEM, VMEM],
        out_specs=(VMEM, VMEM, VMEM),
        scratch_shapes=[
            pltpu.VMEM((length, LANES), BF16),
            pltpu.VMEM((length, LANES), BF16),
            pltpu.VMEM((length, LANES), BF16),
            pltpu.VMEM((LANES, length), BF16),
            pltpu.VMEM((length, LANES), BF16),
        ],
        compiler_params=params(),
        name="attend_forward",
    )(order, qkv)


def backward_kernel(
    tile, order_ref, qkv_ref, grad_ref, att_ref, lse_ref, out_ref, q_s, k_s, v_s, g_s, kt_s, dq_s, dk_s, dv_s
):
    blocks, half = grad_ref.shape[0], grad_ref.shape[1]
    length = blocks * half
    tiles = length // tile
    sort_blocks(
        order_ref,
        [qkv_ref.at[0], qkv_ref.at[1], qkv_ref.at[2], grad_ref],
        [q_s, k_s, v_s, g_s],
        blocks,
        half,
    )
    for t in range(tiles):
        span = slice(t * tile, (t + 1) * tile)
        kt_s[:, span] = k_s[span, :].T
    scale = HD ** (-0.5)
    rows_iota = lax.broadcasted_iota(jnp.int32, (tile, tile), 0)
    cols_iota = lax.broadcasted_iota(jnp.int32, (tile, tile), 1)
    allowed = rows_iota <= cols_iota
    masks = [lane_mask(tile, head) for head in range(2)]
    dk_s[...] = jnp.zeros_like(dk_s)
    dv_s[...] = jnp.zeros_like(dv_s)

    for qt in range(tiles):
        q_span = slice(qt * tile, (qt + 1) * tile)
        query = q_s[q_span, :] * jnp.asarray(scale, BF16)
        grad = g_s[q_span, :]
        queries = [jnp.where(masks[head], query, jnp.zeros_like(query)) for head in range(2)]
        grads = [jnp.where(masks[head], grad, jnp.zeros_like(grad)) for head in range(2)]
        product = grad.astype(F32).T * att_ref[:, q_span]
        dots = [jnp.sum(product[head * HD : (head + 1) * HD], axis=0, keepdims=True) for head in range(2)]
        totals = [lse_ref[head : head + 1, q_span] for head in range(2)]

        def step(kt, state, masked, queries=queries, grads=grads, dots=dots, totals=totals):
            start = pl.multiple_of(kt * tile, tile)
            rows = pl.ds(start, tile)
            keys = k_s[rows, :]
            values = v_s[rows, :]
            dk = dk_s[rows, :]
            dv = dv_s[rows, :]
            new = []
            for head in range(2):
                scores = nt(keys, queries[head])
                if masked:
                    scores = jnp.where(allowed, scores, NEG_BIG)
                soft = jnp.exp(scores - totals[head])
                dsoft = nt(values, grads[head])
                dscore = (soft * (dsoft - dots[head])).astype(BF16)
                dv = dv + nn(soft.astype(BF16), grads[head])
                dk = dk + nn(dscore, queries[head])
                new.append(state[head] + nn(kt_s[head * HD : (head + 1) * HD, rows], dscore))
            dk_s[rows, :] = dk
            dv_s[rows, :] = dv
            return tuple(new)

        state = (jnp.zeros((HD, tile), F32), jnp.zeros((HD, tile), F32))
        state = step(qt, state, True)
        if qt > 0:
            state = lax.fori_loop(0, qt, lambda kt, s, step=step: step(kt, s, False), state)
        dq = jnp.concatenate(state, axis=0) * scale
        dq_s[q_span, :] = dq.T.astype(BF16)

    def body(block, carry):
        start = pl.multiple_of(block * half, half)
        place = order_ref[block]
        out_ref[0, place] = dq_s[pl.ds(start, half), :]
        out_ref[1, place] = dk_s[pl.ds(start, half), :].astype(BF16)
        out_ref[2, place] = dv_s[pl.ds(start, half), :].astype(BF16)
        return carry

    lax.fori_loop(0, blocks, body, 0)


def attend_backward(order, qkv, grad, att, lse, tile):
    kinds, blocks, half, lanes = qkv.shape
    length = blocks * half
    return pl.pallas_call(
        functools.partial(backward_kernel, tile),
        out_shape=jax.ShapeDtypeStruct((3, blocks, half, LANES), BF16),
        in_specs=[SMEM, VMEM, VMEM, VMEM, VMEM],
        out_specs=VMEM,
        scratch_shapes=[pltpu.VMEM((length, LANES), BF16)] * 4
        + [pltpu.VMEM((LANES, length), BF16), pltpu.VMEM((length, LANES), BF16)]
        + [pltpu.VMEM((length, LANES), F32)] * 2,
        compiler_params=params(),
        name="attend_backward",
    )(order, qkv, grad, att, lse)


def assemble_kernel(pieces, part_ref, out_ref):
    for start, source, first, size in pieces:
        out_ref[:, start : start + size] = part_ref[source, :, first : first + size].astype(F32)


def assemble(parts, pieces, width, block):
    n_ctx, rows, columns = parts.shape
    return pl.pallas_call(
        functools.partial(assemble_kernel, pieces),
        grid=(rows // block,),
        out_shape=jax.ShapeDtypeStruct((rows, width), F32),
        in_specs=[pl.BlockSpec((n_ctx, block, columns), lambda i: (0, i, 0))],
        out_specs=pl.BlockSpec((block, width), lambda i: (i, 0)),
        compiler_params=params(),
        name="assemble",
    )(parts)


def mm(left, right):
    return jnp.matmul(left, right, preferred_element_type=F32)


def mm_nt(left, right):
    return lax.dot_general(left, right, (((1,), (1,)), ((), ())), preferred_element_type=F32)


def mm_tn(left, right):
    return lax.dot_general(left, right, (((0,), (0,)), ((), ())), preferred_element_type=F32)


def gelu_tanh(values):
    return jax.nn.gelu(values, approximate=True)


def local(
    tokens,
    block_pairs,
    out_grad,
    ln1_gain,
    ln1_bias,
    qkv_weight,
    query_bias,
    value_bias,
    out_weight,
    out_bias,
    ln2_gain,
    ln2_bias,
    up_weight,
    up_bias,
    down_weight,
    down_bias,
):
    n_ctx, planes = lax.axis_size("ctx"), lax.axis_size("fsdp")
    c, f = lax.axis_index("ctx"), lax.axis_index("fsdp")
    local_rows, seqs, width = tokens.shape
    half = local_rows // 2
    devices = n_ctx * planes
    blocks = 2 * devices
    length = devices * local_rows
    heads = width // HD
    slots = planes * (-(-heads // devices))
    assert slots == planes and planes % seqs == 0
    span = slots * HD
    rows = local_rows * seqs
    plane_rows = n_ctx * rows
    quarter = width // planes
    ff = up_weight.shape[1]
    ff_quarter = ff // planes
    ff_piece = ff_quarter // n_ctx
    ff_span = ff_piece * planes
    tile = 256

    device_ids = jnp.arange(devices, dtype=jnp.int32)
    device_of_block = jnp.sum(
        jnp.where(block_pairs[None, :] == device_ids[:, None], device_ids[None, :], 0), axis=1
    )
    order = jnp.concatenate([device_of_block * 2, device_of_block[::-1] * 2 + 1]).astype(jnp.int32)

    first = [-(-quarter * j // HD) for j in range(planes)] + [heads]
    counts = [first[j + 1] - first[j] for j in range(planes)]
    assert max(counts) <= n_ctx
    slot_head = [jnp.minimum(first[j] + c, heads - 1) for j in range(planes)]
    first_own = jnp.asarray(first, jnp.int32)[f]
    count_own = jnp.asarray(counts, jnp.int32)[f]

    qkv_own = jnp.concatenate(
        [
            lax.dynamic_slice(qkv_weight, (0, k * width + slot_head[j] * HD), (quarter, HD))
            for k in range(3)
            for j in range(planes)
        ],
        axis=1,
    )
    qkv_slice = lax.all_gather(qkv_own, "fsdp", axis=0, tiled=True)
    next_rows = lax.ppermute(out_weight[:HD], "fsdp", [(j + 1, j) for j in range(planes - 1)])
    out_own = lax.dynamic_slice(
        jnp.concatenate([out_weight, next_rows]), ((first_own + c) * HD - f * quarter, 0), (HD, width)
    )
    out_own = jnp.where(c < count_own, out_own, jnp.zeros_like(out_own))
    out_slice = lax.all_gather(out_own, "fsdp", axis=0, tiled=True)
    up_own = jnp.concatenate(
        [
            lax.dynamic_slice(up_weight, (0, k * ff_quarter + c * ff_piece), (quarter, ff_piece))
            for k in range(planes)
        ],
        axis=1,
    )
    up_slice = lax.all_gather(up_own, "fsdp", axis=0, tiled=True)
    down_own = lax.dynamic_slice(down_weight, (c * ff_piece, 0), (ff_piece, width))
    down_slice = lax.all_gather(down_own, "fsdp", axis=0, tiled=True)

    tok = jnp.swapaxes(tokens, 0, 1).reshape(rows, width)
    og = jnp.swapaxes(out_grad, 0, 1).reshape(rows, width)

    packed = jnp.concatenate(
        [
            jnp.stack([ln1_gain, ln1_bias, ln2_gain, ln2_bias, query_bias, value_bias, out_bias, down_bias]),
            up_bias.reshape(ff // width, quarter),
        ]
    )
    packed = jnp.pad(packed, ((0, -packed.shape[0] % 16), (0, -quarter % LANES)))
    vectors, h1, og_all = first_norm_gather(tok, og, packed, n_ctx, planes)
    h1 = h1.reshape(plane_rows, width)
    og_all = og_all.reshape(plane_rows, width)
    vectors = vectors[:, :, :quarter].astype(F32)
    gain1, bias1, gain2, bias2, bias_q, bias_v, bias_o, bias_d = [
        vectors[:, k].reshape(width) for k in range(8)
    ]
    bias_up = lax.dynamic_slice(
        vectors[:, 8 : 8 + ff // width].reshape(planes, ff_quarter), (0, c * ff_piece), (planes, ff_piece)
    ).reshape(ff_span)

    def head_part(vector):
        return [lax.dynamic_slice(vector, (slot_head[j] * HD,), (HD,)) for j in range(planes)]

    qkv_shift = jnp.concatenate(head_part(bias_q) + [jnp.zeros((span,), F32)] + head_part(bias_v))

    qkv = (mm(h1, qkv_slice) + qkv_shift).astype(BF16)
    qkv_heads = to_heads(qkv.reshape(n_ctx, seqs, local_rows, 3 * span), 3, planes, 5)
    qkv_heads = qkv_heads.reshape(3, blocks, half, LANES)
    att_heads, att_exact, lse = attend_forward(order, qkv_heads, tile)
    (att,) = to_tokens(att_heads.reshape(1, n_ctx, planes, local_rows, LANES), seqs, 6)
    att = att.reshape(plane_rows, span)
    branch = mm(att, out_slice).astype(BF16).reshape(n_ctx, rows, width)
    mixed, h2 = second_norm_gather(branch, tok, jnp.stack([gain2, bias2, bias_o]))
    h2 = h2.reshape(plane_rows, width)
    up = mm(h2, up_slice) + bias_up
    activated, gelu_back = jax.vjp(gelu_tanh, up)
    act = activated.astype(BF16)
    out_part = mm(act, down_slice).astype(BF16).reshape(n_ctx, rows, width)

    def reduce_own(part):
        return lax.psum_scatter(part, "fsdp", scatter_dimension=0, tiled=True)

    (d_up,) = gelu_back(mm_nt(og_all, down_slice))
    d_up_low = d_up.astype(BF16)
    down_part = mm_tn(act, og_all).astype(BF16)
    d_h2 = mm_nt(d_up_low, up_slice).astype(BF16).reshape(n_ctx, rows, width)
    up_part = mm_tn(h2, d_up_low).astype(BF16)
    d_h2, down_part, up_part = lax.optimization_barrier((d_h2, down_part, up_part))
    down_own_grad, up_own_grad = reduce_own(down_part), reduce_own(up_part)
    d_mixed, sums2, d_branch = second_norm_back(d_h2, mixed, og, gain2[None, :])
    d_branch = d_branch.reshape(plane_rows, width)
    d_att = mm_nt(d_branch, out_slice).astype(BF16)
    d_att_heads = to_heads(d_att.reshape(n_ctx, seqs, local_rows, span), 1, planes, 7)
    out_w_part = mm_tn(att, d_branch).astype(BF16)
    d_att_heads, out_w_part = lax.optimization_barrier((d_att_heads, out_w_part))
    out_own_grad = reduce_own(out_w_part)
    d_heads = attend_backward(order, qkv_heads, d_att_heads.reshape(blocks, half, LANES), att_exact, lse, tile)
    d_qkv, down_parts = to_tokens(
        d_heads.reshape(3, n_ctx, planes, local_rows, LANES), seqs, 8, (down_own_grad,)
    )
    d_qkv = d_qkv.reshape(plane_rows, 3 * span)
    qkv_part = mm_tn(h1, d_qkv).astype(BF16)
    d_h1 = mm_nt(d_qkv, qkv_slice).astype(BF16).reshape(n_ctx, rows, width)
    d_h1, qkv_part = lax.optimization_barrier((d_h1, qkv_part))
    qkv_own_grad = reduce_own(qkv_part)
    grad_tok, block_out, sums1 = first_norm_back(
        d_h1, out_part, tok, d_mixed, mixed, jnp.stack([gain1, bias_d])
    )

    d_qkv_sum = jnp.sum(d_qkv.astype(F32), axis=0)
    d_up_sum = jnp.sum(d_up_low.astype(F32), axis=0).reshape(planes, ff_piece)
    up_spread = lax.dynamic_update_slice(jnp.zeros((planes, ff_quarter), F32), d_up_sum, (0, c * ff_piece))

    def spread(values):
        full = jnp.zeros((width + HD,), F32)
        for j in range(planes):
            place = jnp.where(c < counts[j], (first[j] + c) * HD, width)
            full = lax.dynamic_update_slice(full, values[j * HD : (j + 1) * HD], (place,))
        return full[None, :width]

    wide = jnp.concatenate([sums1, sums2, spread(d_qkv_sum[:span]), spread(d_qkv_sum[2 * span :])])
    wide = wide.reshape(8, planes, quarter).transpose(1, 0, 2).reshape(planes, 8 * quarter)
    flat = jnp.concatenate([wide, up_spread], axis=1)
    size = flat.shape[1]
    flat = jnp.pad(flat, ((0, 0), (0, -size % (8 * LANES))))
    totals = total_vectors(flat.reshape(planes, -1, LANES), n_ctx, 9).reshape(-1)
    sums = totals[: 8 * quarter].reshape(8, quarter)
    up_bias_grad = totals[8 * quarter : size]

    up_parts, out_parts = gather_plane([up_own_grad, out_own_grad], n_ctx, 10)
    (qkv_parts,) = gather_plane([qkv_own_grad], n_ctx, 11)
    down_grad = down_parts.reshape(ff_quarter, width).astype(F32)
    block = quarter // 5
    up_pieces = [
        (j * ff_quarter + d * ff_piece, d, j * ff_piece, ff_piece) for j in range(planes) for d in range(n_ctx)
    ]
    up_grad = assemble(up_parts, up_pieces, ff, block)
    qkv_pieces = [
        (k * width + (first[j] + d) * HD, d, k * span + j * HD, HD)
        for k in range(3)
        for j in range(planes)
        for d in range(counts[j])
    ]
    qkv_grad = assemble(qkv_parts, qkv_pieces, 3 * width, block)
    out_rows = out_parts.reshape(n_ctx * HD, width)
    tail = (f + 1) * quarter - first_own * HD
    tail_rows = lax.dynamic_slice(out_rows, (tail, 0), (HD, width))
    tail_rows = lax.ppermute(tail_rows, "fsdp", [(j, j + 1) for j in range(planes - 1)])
    lead = first_own * HD - f * quarter
    shifted = lax.dynamic_slice(
        jnp.concatenate([jnp.zeros((HD, width), BF16), out_rows]), (HD - lead, 0), (quarter, width)
    )
    from_tail = jnp.concatenate([tail_rows, jnp.zeros((quarter - HD, width), BF16)])
    row_ids = lax.broadcasted_iota(jnp.int32, (quarter, width), 0)
    out_grad_own = jnp.where(row_ids < lead, from_tail, shifted).astype(F32)

    def back(values):
        return jnp.swapaxes(values.reshape(seqs, local_rows, width), 0, 1)

    return (
        back(block_out),
        back(grad_tok),
        sums[0],
        sums[1],
        qkv_grad,
        sums[6],
        sums[7],
        out_grad_own,
        sums[4],
        sums[2],
        sums[3],
        up_grad,
        up_bias_grad,
        down_grad,
        sums[5],
    )


def solution(mesh):
    both, row, vec, mat = P(("ctx", "fsdp"), None, None), P(), P("fsdp"), P("fsdp", None)
    in_specs = (both, row, both, vec, vec, mat, vec, vec, mat, vec, vec, vec, mat, vec, mat, vec)
    out_specs = (both, both, vec, vec, mat, vec, vec, mat, vec, vec, vec, mat, vec, mat, vec)
    return jax.shard_map(local, mesh=mesh, in_specs=in_specs, out_specs=out_specs, check_vma=False)
```

```python
import functools

import jax
import jax.numpy as jnp
from jax import lax
from jax.experimental import pallas as pl
from jax.experimental.pallas import tpu as pltpu
from jax.sharding import PartitionSpec as P

HD = 64
LANES = 128
NORM_EPS = 1e-05
NEG_BIG = -1e30
MESH = pl.DeviceIdType.MESH
F32 = jnp.float32
BF16 = jnp.bfloat16
ANY = pl.BlockSpec(memory_space=pl.ANY)
VMEM = pl.BlockSpec(memory_space=pltpu.VMEM)
DMA = pltpu.SemaphoreType.DMA
VMEM_LIMIT = 56 * 1024 * 1024
SMALL = pl.CostEstimate(flops=1, bytes_accessed=1, transcendentals=0)


def params(cid=None):
    if cid is None:
        return pltpu.CompilerParams(vmem_limit_bytes=VMEM_LIMIT)
    return pltpu.CompilerParams(
        collective_id=cid, has_side_effects=True, vmem_limit_bytes=VMEM_LIMIT
    )


def plane_peers(chips):
    me = lax.axis_index("ctx")
    core = lax.rem(me, 2)
    chip = me // 2
    sibling = chip * 2 + 1 - core
    if chips == 4:
        across_x = chip + 1 - 2 * lax.rem(chip, 2)
        across_y = lax.rem(chip + 2, 4)
        corner = lax.rem(across_x + 2, 4)
        first = across_x * (1 - core) + across_y * core
        second = across_y * (1 - core) + across_x * core
        to = come = [first * 2 + core, second * 2 + core, corner * 2 + core]
    else:
        to = [lax.rem(chip + k, chips) * 2 + core for k in range(1, chips)]
        come = [lax.rem(chip + chips - k, chips) * 2 + core for k in range(1, chips)]
    return me, core, chip, sibling, to, come


def greet(plane=(), across=()):
    barrier = pltpu.get_barrier_semaphore()
    for peer in plane:
        pl.semaphore_signal(barrier, inc=1, device_id={"ctx": peer}, device_id_type=MESH)
    for peer in across:
        pl.semaphore_signal(barrier, inc=1, device_id={"fsdp": peer}, device_id_type=MESH)
    pl.semaphore_wait(barrier, len(plane) + len(across))


def other_planes(planes):
    me = lax.axis_index("fsdp")
    return me, [lax.rem(me + k, planes) for k in range(1, planes)]


def send(src, dst, send_sem, recv_sem, axis, peer):
    copy = pltpu.make_async_remote_copy(
        src_ref=src,
        dst_ref=dst,
        send_sem=send_sem,
        recv_sem=recv_sem,
        device_id={axis: peer},
        device_id_type=MESH,
    )
    copy.start()
    return copy


def plane_gather_start(owns, alls, sems, chips):
    far_send, far_recv, near_send, near_recv, local_sem = sems
    me, core, chip, sibling, to, come = plane_peers(chips)
    direct = 2 if chips == 4 else chips - 1
    last = chips - 1
    far, near, local = [], [], []
    for i, (own_ref, all_ref) in enumerate(zip(owns, alls)):
        far.append(
            [
                send(own_ref, all_ref.at[me], far_send.at[i, k], far_recv.at[i, k], "ctx", to[k])
                for k in range(direct)
            ]
        )
        near.append(send(own_ref, all_ref.at[me], near_send.at[i, last], near_recv.at[i, last], "ctx", sibling))
        copy = pltpu.make_async_copy(own_ref, all_ref.at[me], local_sem.at[i])
        copy.start()
        local.append(copy)
    return far, near, local


def plane_gather_finish(started, alls, sems, chips):
    far_send, far_recv, near_send, near_recv, local_sem = sems
    me, core, chip, sibling, to, come = plane_peers(chips)
    far, near, local = started
    near = list(near)

    def pass_on(i, all_ref, k):
        far[i][k].wait_recv()
        block = all_ref.at[come[k]]
        if chips == 4 and k == 0:
            far[i].append(send(block, block, far_send.at[i, 2], far_recv.at[i, 2], "ctx", to[1]))
        near.append(send(block, block, near_send.at[i, k], near_recv.at[i, k], "ctx", sibling))

    direct = 2 if chips == 4 else chips - 1
    for i, all_ref in enumerate(alls):
        for k in range(direct):
            pass_on(i, all_ref, k)
    for i, all_ref in enumerate(alls):
        for k in range(direct, chips - 1):
            pass_on(i, all_ref, k)
    for group in far:
        for copy in group:
            copy.wait_send()
    for copy in near + local:
        copy.wait()


def plane_gather(owns, alls, sems, chips):
    plane_gather_finish(plane_gather_start(owns, alls, sems, chips), alls, sems, chips)


def plane_scatter(part_ref, mine, paired, stage, arrived, sems, chips):
    far_send, far_recv, near_send, near_recv, local_sem = sems
    me, core, chip, sibling, to, come = plane_peers(chips)
    targets = to + [me]
    order = [2, 1, 0, 3] if chips == 4 else list(range(chips))
    near, local = [None] * chips, [None] * chips
    crossed = [1, 0, 2, 3] if chips == 4 else list(range(chips))
    for k in order:
        other = targets[crossed[k]] + 1 - 2 * core
        near[k] = send(part_ref.at[other], paired.at[k], near_send.at[k], near_recv.at[k], "ctx", sibling)
        local[k] = pltpu.make_async_copy(part_ref.at[targets[k]], mine.at[k], local_sem.at[k])
        local[k].start()

    def both(k):
        local[k].wait()
        near[k].wait_recv()
        return mine[k].astype(F32) + paired[k].astype(F32)

    def dispatch(k, target):
        return send(stage.at[k], arrived.at[k], far_send.at[k], far_recv.at[k], "ctx", target)

    far = [None] * (chips - 1)
    if chips == 4:
        stage[2] = both(2).astype(BF16)
        far[2] = dispatch(2, to[0])
        stage[0] = both(0).astype(BF16)
        far[0] = dispatch(0, to[0])
        partial = both(1)
        far[2].wait_recv()
        stage[1] = (partial + arrived[2].astype(F32)).astype(BF16)
        far[1] = dispatch(1, to[1])
        total = both(3)
        arriving = [0, 1]
    else:
        for k in range(chips - 1):
            stage[k] = both(k).astype(BF16)
            far[k] = dispatch(k, to[k])
        total = both(chips - 1)
        arriving = range(chips - 1)
    for k in arriving:
        far[k].wait_recv()
        total = total + arrived[k].astype(F32)
    for copy in far + near:
        copy.wait_send()
    return total


def gather_sems(chips, count=1):
    return [DMA((count, chips - 1))] * 2 + [DMA((count, chips))] * 2 + [DMA((count,))]


def scatter_scratch(chips, rows, width):
    return [
        pltpu.VMEM((chips, rows, width), BF16),
        pltpu.VMEM((chips, rows, width), BF16),
        pltpu.VMEM((chips - 1, rows, width), BF16),
        pltpu.VMEM((chips - 1, rows, width), BF16),
        DMA((chips - 1,)),
        DMA((chips - 1,)),
        DMA((chips,)),
        DMA((chips,)),
        DMA((chips,)),
    ]


def normalize(values):
    average = jnp.mean(values, axis=-1, keepdims=True)
    centered = values - average
    variance = jnp.mean(centered * centered, axis=-1, keepdims=True)
    inverse = lax.rsqrt(variance + NORM_EPS)
    return centered * inverse, inverse


def norm_backward(grad, gain, unit, inverse):
    scaled = grad * gain
    first = jnp.mean(scaled, axis=-1, keepdims=True)
    second = jnp.mean(scaled * unit, axis=-1, keepdims=True)
    return (scaled - first - unit * second) * inverse


def first_kernel(
    chips, planes, quarter, tok_ref, og_ref, vec_ref, vecs_ref, h1_ref, ogs_ref, own, v_send, v_recv, v_local, *sems
):
    me, core, chip, sibling, to, come = plane_peers(chips)
    plane, others = other_planes(planes)
    greet(to + [sibling], others)
    copies = [
        send(vec_ref, vecs_ref.at[plane], v_send.at[k], v_recv.at[k], "fsdp", peer) for k, peer in enumerate(others)
    ]
    local = pltpu.make_async_copy(vec_ref, vecs_ref.at[plane], v_local)
    local.start()
    og_sems, h1_sems = sems[:5], sems[5:]
    og_started = plane_gather_start([og_ref], [ogs_ref], og_sems, chips)
    unit, inverse = normalize(tok_ref[...].astype(F32))
    for copy in copies + [local]:
        copy.wait()
    gain, shift = [
        jnp.concatenate([vecs_ref[j, k : k + 1, :quarter].astype(F32) for j in range(planes)], axis=1) for k in range(2)
    ]
    own[...] = (unit * gain + shift).astype(BF16)
    h1_started = plane_gather_start([own], [h1_ref], h1_sems, chips)
    plane_gather_finish(og_started, [ogs_ref], og_sems, chips)
    plane_gather_finish(h1_started, [h1_ref], h1_sems, chips)


def first_norm_gather(tok, og, vec, n_ctx, planes):
    rows, width = tok.shape
    chips = n_ctx // 2
    whole = jax.ShapeDtypeStruct((n_ctx, rows, width), BF16)
    return pl.pallas_call(
        functools.partial(first_kernel, chips, planes, width // planes),
        out_shape=(jax.ShapeDtypeStruct((planes,) + vec.shape, BF16), whole, whole),
        in_specs=[VMEM, ANY, VMEM],
        out_specs=(VMEM, ANY, ANY),
        scratch_shapes=[pltpu.VMEM((rows, width), BF16), DMA((planes - 1,)), DMA((planes - 1,)), DMA]
        + gather_sems(chips)
        + gather_sems(chips),
        compiler_params=params(0),
        name="norm_gather",
    )(tok, og, vec)


def second_kernel(chips, part_ref, tok_ref, vec_ref, mixed_ref, all_ref, own, *scratch):
    me, core, chip, sibling, to, come = plane_peers(chips)
    greet(to + [sibling])
    total = plane_scatter(part_ref, *scratch[:4], scratch[4:9], chips)
    mixed = tok_ref[...].astype(F32) + total + vec_ref[2:3, :]
    mixed_ref[...] = mixed
    unit, inverse = normalize(mixed)
    own[...] = (unit * vec_ref[0:1, :] + vec_ref[1:2, :]).astype(BF16)
    plane_gather([own], [all_ref], scratch[9:], chips)


def second_norm_gather(part, tok, vecs):
    n_ctx, rows, width = part.shape
    chips = n_ctx // 2
    return pl.pallas_call(
        functools.partial(second_kernel, chips),
        out_shape=(
            jax.ShapeDtypeStruct((rows, width), F32),
            jax.ShapeDtypeStruct((n_ctx, rows, width), BF16),
        ),
        in_specs=[ANY, VMEM, VMEM],
        out_specs=(VMEM, ANY),
        scratch_shapes=[pltpu.VMEM((rows, width), BF16)]
        + scatter_scratch(chips, rows, width)
        + gather_sems(chips),
        compiler_params=params(1),
        cost_estimate=SMALL,
        name="scatter_norm_gather",
    )(part, tok, vecs)


def third_kernel(chips, part_ref, mixed_ref, og_ref, vec_ref, dmixed_ref, sums_ref, all_ref, own, *scratch):
    me, core, chip, sibling, to, come = plane_peers(chips)
    greet(to + [sibling])
    unit, inverse = normalize(mixed_ref[...])
    grad = plane_scatter(part_ref, *scratch[:4], scratch[4:9], chips)
    out_grad = og_ref[...].astype(F32)
    dmixed = out_grad + norm_backward(grad, vec_ref[0:1, :], unit, inverse)
    dmixed_ref[...] = dmixed
    low = dmixed.astype(BF16)
    own[...] = low
    sums_ref[0:1, :] = jnp.sum(grad * unit, axis=0, keepdims=True)
    sums_ref[1:2, :] = jnp.sum(grad, axis=0, keepdims=True)
    sums_ref[2:3, :] = jnp.sum(low.astype(F32), axis=0, keepdims=True)
    sums_ref[3:4, :] = jnp.sum(out_grad, axis=0, keepdims=True)
    plane_gather([own], [all_ref], scratch[9:], chips)


def second_norm_back(part, mixed, og, vecs):
    n_ctx, rows, width = part.shape
    chips = n_ctx // 2
    return pl.pallas_call(
        functools.partial(third_kernel, chips),
        out_shape=(
            jax.ShapeDtypeStruct((rows, width), F32),
            jax.ShapeDtypeStruct((4, width), F32),
            jax.ShapeDtypeStruct((n_ctx, rows, width), BF16),
        ),
        in_specs=[ANY, VMEM, VMEM, VMEM],
        out_specs=(VMEM, VMEM, ANY),
        scratch_shapes=[pltpu.VMEM((rows, width), BF16)]
        + scatter_scratch(chips, rows, width)
        + gather_sems(chips),
        compiler_params=params(2),
        cost_estimate=SMALL,
        name="scatter_back_gather",
    )(part, mixed, og, vecs)


def fourth_kernel(
    chips,
    planes,
    part_ref,
    outw_ref,
    flat_ref,
    tok_ref,
    dmixed_ref,
    vec_ref,
    grad_ref,
    outw_all,
    sums_ref,
    flat_out,
    small,
    small_own,
    small_z,
    small_c,
    flat_own,
    flat_z,
    flat_c,
    z_send,
    z_recv,
    c_send,
    c_recv,
    *scratch,
):
    n_ctx = 2 * chips
    me, core, chip, sibling, to, come = plane_peers(chips)
    plane, others = other_planes(planes)
    around = [lax.rem(me + k, n_ctx) for k in range(1, n_ctx)]
    greet(around, others)
    scatter, outw_sems = scratch[:9], scratch[9:]
    flat_sent = [
        send(flat_ref.at[peer], flat_z.at[k], z_send.at[0, k], z_recv.at[0, k], "fsdp", peer)
        for k, peer in enumerate(others)
    ]
    unit, inverse = normalize(tok_ref[...].astype(F32))
    grad = plane_scatter(part_ref, *scatter[:4], scatter[4:9], chips)
    outw_started = plane_gather_start([outw_ref], [outw_all], outw_sems, chips)
    sums = jnp.concatenate(
        [jnp.sum(grad * unit, axis=0, keepdims=True), jnp.sum(grad, axis=0, keepdims=True)], axis=0
    )
    quarter = sums.shape[1] // planes
    small[...] = jnp.zeros_like(small)
    for j in range(planes):
        small[j, 0:2, 0:quarter] = sums[:, j * quarter : (j + 1) * quarter]
    small_sent = [
        send(small.at[peer], small_z.at[k], z_send.at[1, k], z_recv.at[1, k], "fsdp", peer)
        for k, peer in enumerate(others)
    ]
    grad_ref[...] = dmixed_ref[...] + norm_backward(grad, vec_ref[0:1, :], unit, inverse)
    small_total = small[plane]
    flat_total = flat_ref[plane]
    for k in range(planes - 1):
        flat_sent[k].wait()
        small_sent[k].wait()
        small_total = small_total + small_z[k]
        flat_total = flat_total + flat_z[k]
    small_own[...] = small_total
    flat_own[...] = flat_total
    sent = []
    for k, peer in enumerate(around):
        sent.append(send(small_own, small_c.at[k], c_send.at[0, k], c_recv.at[0, k], "ctx", peer))
        sent.append(send(flat_own, flat_c.at[k], c_send.at[1, k], c_recv.at[1, k], "ctx", peer))
    plane_gather_finish(outw_started, [outw_all], outw_sems, chips)
    for copy in sent:
        copy.wait()
    for k in range(n_ctx - 1):
        small_total = small_total + small_c[k]
        flat_total = flat_total + flat_c[k]
    sums_ref[...] = small_total
    flat_out[...] = flat_total


def first_norm_back(part, outw_own, flat, tok, dmixed, vecs):
    n_ctx, rows, width = part.shape
    planes = flat.shape[0]
    quarter = width // planes
    chips = n_ctx // 2
    size = (8, quarter + -quarter % LANES)
    return pl.pallas_call(
        functools.partial(fourth_kernel, chips, planes),
        out_shape=(
            jax.ShapeDtypeStruct((rows, width), F32),
            jax.ShapeDtypeStruct((n_ctx,) + outw_own.shape, BF16),
            jax.ShapeDtypeStruct(size, F32),
            jax.ShapeDtypeStruct(flat.shape[1:], F32),
        ),
        in_specs=[ANY, ANY, VMEM, VMEM, VMEM, VMEM],
        out_specs=(VMEM, ANY, VMEM, VMEM),
        scratch_shapes=[
            pltpu.VMEM((planes,) + size, F32),
            pltpu.VMEM(size, F32),
            pltpu.VMEM((planes - 1,) + size, F32),
            pltpu.VMEM((n_ctx - 1,) + size, F32),
            pltpu.VMEM(flat.shape[1:], F32),
            pltpu.VMEM((planes - 1,) + flat.shape[1:], F32),
            pltpu.VMEM((n_ctx - 1,) + flat.shape[1:], F32),
            DMA((2, planes - 1)),
            DMA((2, planes - 1)),
            DMA((2, n_ctx - 1)),
            DMA((2, n_ctx - 1)),
        ]
        + scatter_scratch(chips, rows, width)
        + gather_sems(chips),
        compiler_params=params(3),
        cost_estimate=SMALL,
        name="scatter_back",
    )(part, outw_own, flat, tok, dmixed, vecs)


def gather_kernel(chips, count, *refs):
    me, core, chip, sibling, to, come = plane_peers(chips)
    greet(to + [sibling])
    plane_gather(refs[:count], refs[count : 2 * count], refs[2 * count :], chips)


def gather_plane(arrays, n_ctx, cid):
    chips, count = n_ctx // 2, len(arrays)
    return pl.pallas_call(
        functools.partial(gather_kernel, chips, count),
        out_shape=tuple(jax.ShapeDtypeStruct((n_ctx,) + a.shape, a.dtype) for a in arrays),
        in_specs=[ANY] * count,
        out_specs=(ANY,) * count,
        scratch_shapes=gather_sems(chips, count),
        compiler_params=params(cid),
        cost_estimate=SMALL,
        name="gather_plane",
    )(*arrays)


def to_heads_kernel(kinds, planes, seqs, chips, beside, *refs):
    inputs = 4 if beside else 1
    outputs = 2 if beside else 1
    tok_ref, head_ref = refs[0], refs[inputs]
    send_sems, recv_sems, local_sems = refs[inputs + outputs : inputs + outputs + 3]
    scratch = refs[inputs + outputs + 3 :]
    plane_me, core, chip, sibling, to, come = plane_peers(chips)
    me, others = other_planes(planes)
    pairs = planes // seqs
    greet(to + [sibling] if beside else [], others)
    width = tok_ref.shape[3] // kinds

    def source(kind, unit):
        start = pl.multiple_of(kind * width + lax.rem(unit, pairs) * LANES, LANES)
        return tok_ref.at[:, unit // pairs, :, pl.ds(start, LANES)]

    copies = []
    for k, unit in enumerate(others):
        for kind in range(kinds):
            copies.append(
                send(
                    source(kind, unit),
                    head_ref.at[kind, :, me],
                    send_sems.at[kind, k],
                    recv_sems.at[kind, k],
                    "fsdp",
                    unit,
                )
            )
    for kind in range(kinds):
        copy = pltpu.make_async_copy(source(kind, me), head_ref.at[kind, :, me], local_sems.at[kind])
        copy.start()
        copies.append(copy)
    if beside:
        part_ref, mixed_ref, vec_ref, out_ref = refs[1], refs[2], refs[3], refs[inputs + 1]
        total = plane_scatter(part_ref, *scratch[:4], scratch[4:], chips)
        out_ref[...] = (mixed_ref[...] + total + vec_ref[...]).astype(BF16)
    for copy in copies:
        copy.wait()


def to_heads(tok, kinds, planes, cid, beside=()):
    n_ctx, seqs, local_rows, width = tok.shape
    chips = n_ctx // 2
    out_shape = (jax.ShapeDtypeStruct((kinds, n_ctx, planes, local_rows, LANES), tok.dtype),)
    in_specs, out_specs = [ANY], (ANY,)
    scratch = [DMA((kinds, planes - 1)), DMA((kinds, planes - 1)), DMA((kinds,))]
    if beside:
        rows, model = beside[1].shape
        out_shape += (jax.ShapeDtypeStruct((rows, model), BF16),)
        in_specs, out_specs = [ANY, ANY, VMEM, VMEM], (ANY, VMEM)
        scratch += scatter_scratch(chips, rows, model)
    return pl.pallas_call(
        functools.partial(to_heads_kernel, kinds, planes, seqs, chips, bool(beside)),
        out_shape=out_shape,
        in_specs=in_specs,
        out_specs=out_specs,
        scratch_shapes=scratch,
        compiler_params=params(cid),
        cost_estimate=SMALL,
        name="to_heads",
    )(tok, *beside)


def to_tokens_kernel(kinds, planes, seqs, chips, beside, *refs):
    head_ref, owns = refs[0], refs[1 : 1 + beside]
    tok_ref, alls = refs[1 + beside], refs[2 + beside : 2 + 2 * beside]
    send_sems, recv_sems, local_sems = refs[2 + 2 * beside : 5 + 2 * beside]
    sems = refs[5 + 2 * beside :]
    plane_me, core, chip, sibling, to, come = plane_peers(chips)
    me, others = other_planes(planes)
    pairs = planes // seqs
    greet(to + [sibling] if beside else [], others)
    width = tok_ref.shape[3] // kinds

    def target(kind):
        start = pl.multiple_of(kind * width + lax.rem(me, pairs) * LANES, LANES)
        return tok_ref.at[:, me // pairs, :, pl.ds(start, LANES)]

    copies = []
    for k in range(1, planes):
        peer = lax.rem(me + k, planes)
        for kind in range(kinds):
            copies.append(
                send(
                    head_ref.at[kind, :, peer],
                    target(kind),
                    send_sems.at[kind, k - 1],
                    recv_sems.at[kind, k - 1],
                    "fsdp",
                    peer,
                )
            )
    local = []
    for kind in range(kinds):
        copy = pltpu.make_async_copy(head_ref.at[kind, :, me], target(kind), local_sems.at[kind])
        copy.start()
        local.append(copy)
    if beside:
        plane_gather(owns, alls, sems, chips)
    for copy in copies + local:
        copy.wait()


def to_tokens(heads, seqs, cid, beside=()):
    kinds, n_ctx, planes, rows, lanes = heads.shape
    width = kinds * (planes // seqs) * LANES
    count = len(beside)
    return pl.pallas_call(
        functools.partial(to_tokens_kernel, kinds, planes, seqs, n_ctx // 2, count),
        out_shape=(jax.ShapeDtypeStruct((n_ctx, seqs, rows, width), heads.dtype),)
        + tuple(jax.ShapeDtypeStruct((n_ctx,) + a.shape, a.dtype) for a in beside),
        in_specs=[ANY] * (1 + count),
        out_specs=(ANY,) * (1 + count),
        scratch_shapes=[DMA((kinds, planes - 1)), DMA((kinds, planes - 1)), DMA((kinds,))]
        + (gather_sems(n_ctx // 2, count) if count else []),
        compiler_params=params(cid),
        cost_estimate=SMALL,
        name="to_tokens",
    )(heads, *beside)


def nt(left, right):
    return lax.dot_general(left, right, (((1,), (1,)), ((), ())), preferred_element_type=F32)


def nn(left, right):
    return lax.dot_general(left, right, (((1,), (0,)), ((), ())), preferred_element_type=F32)


def sort_blocks(order_ref, source_refs, sorted_refs, blocks, half):
    def body(block, carry):
        place = order_ref[block]
        start = pl.multiple_of(block * half, half)
        for source, target in zip(source_refs, sorted_refs):
            target[pl.ds(start, half), :] = source[place]
        return carry

    lax.fori_loop(0, blocks, body, 0)


def lane_mask(rows, head):
    lane = lax.broadcasted_iota(jnp.int32, (rows, LANES), 1)
    return (lane < HD) if head == 0 else (lane >= HD)


def forward_kernel(tile, order_ref, qkv_ref, out_ref, att_ref, lse_ref, q_s, k_s, v_s, vt_s, o_s):
    blocks, half = out_ref.shape[0], out_ref.shape[1]
    length = blocks * half
    tiles = length // tile
    sort_blocks(order_ref, [qkv_ref.at[0], qkv_ref.at[1], qkv_ref.at[2]], [q_s, k_s, v_s], blocks, half)
    for t in range(tiles):
        span = slice(t * tile, (t + 1) * tile)
        vt_s[:, span] = v_s[span, :].T
    scale = HD ** (-0.5)
    rows_iota = lax.broadcasted_iota(jnp.int32, (tile, tile), 0)
    cols_iota = lax.broadcasted_iota(jnp.int32, (tile, tile), 1)
    allowed = rows_iota <= cols_iota
    masks = [lane_mask(tile, head) for head in range(2)]

    for qt in range(tiles):
        q_span = slice(qt * tile, (qt + 1) * tile)
        query = q_s[q_span, :] * jnp.asarray(scale, BF16)
        queries = [jnp.where(masks[head], query, jnp.zeros_like(query)) for head in range(2)]

        def step(kt, state, masked, queries=queries):
            start = pl.multiple_of(kt * tile, tile)
            keys = k_s[pl.ds(start, tile), :]
            new = []
            for head in range(2):
                top, total, acc = state[head]
                scores = nt(keys, queries[head])
                if masked:
                    scores = jnp.where(allowed, scores, NEG_BIG)
                new_top = jnp.maximum(top, jnp.max(scores, axis=0, keepdims=True))
                soft = jnp.exp(scores - new_top)
                factor = jnp.exp(top - new_top)
                total = total * factor + jnp.sum(soft, axis=0, keepdims=True)
                values = vt_s[head * HD : (head + 1) * HD, pl.ds(start, tile)]
                acc = acc * factor + nn(values, soft.astype(BF16))
                new.append((new_top, total, acc))
            return tuple(new)

        state = tuple(
            (jnp.full((1, tile), NEG_BIG, F32), jnp.zeros((1, tile), F32), jnp.zeros((HD, tile), F32))
            for head in range(2)
        )
        state = step(qt, state, True)
        if qt > 0:
            state = lax.fori_loop(0, qt, lambda kt, s, step=step: step(kt, s, False), state)
        for head in range(2):
            top, total, acc = state[head]
            att_ref[head * HD : (head + 1) * HD, q_span] = acc / total
            lse_ref[head : head + 1, q_span] = top + jnp.log(total)
        o_s[q_span, :] = att_ref[:, q_span].T.astype(BF16)

    def body(block, carry):
        start = pl.multiple_of(block * half, half)
        out_ref[order_ref[block]] = o_s[pl.ds(start, half), :]
        return carry

    lax.fori_loop(0, blocks, body, 0)


SMEM = pl.BlockSpec(memory_space=pltpu.SMEM)


def attend_forward(order, qkv, tile):
    kinds, blocks, half, lanes = qkv.shape
    length = blocks * half
    return pl.pallas_call(
        functools.partial(forward_kernel, tile),
        out_shape=(
            jax.ShapeDtypeStruct((blocks, half, LANES), BF16),
            jax.ShapeDtypeStruct((LANES, length), F32),
            jax.ShapeDtypeStruct((2, length), F32),
        ),
        in_specs=[SMEM, VMEM],
        out_specs=(VMEM, VMEM, VMEM),
        scratch_shapes=[
            pltpu.VMEM((length, LANES), BF16),
            pltpu.VMEM((length, LANES), BF16),
            pltpu.VMEM((length, LANES), BF16),
            pltpu.VMEM((LANES, length), BF16),
            pltpu.VMEM((length, LANES), BF16),
        ],
        compiler_params=params(),
        cost_estimate=SMALL,
        name="attend_forward",
    )(order, qkv)


def backward_kernel(
    tile, order_ref, qkv_ref, grad_ref, att_ref, lse_ref, out_ref, q_s, k_s, v_s, g_s, kt_s, dq_s, dk_s, dv_s
):
    blocks, half = grad_ref.shape[0], grad_ref.shape[1]
    length = blocks * half
    tiles = length // tile
    sort_blocks(
        order_ref,
        [qkv_ref.at[0], qkv_ref.at[1], qkv_ref.at[2], grad_ref],
        [q_s, k_s, v_s, g_s],
        blocks,
        half,
    )
    for t in range(tiles):
        span = slice(t * tile, (t + 1) * tile)
        kt_s[:, span] = k_s[span, :].T
    scale = HD ** (-0.5)
    rows_iota = lax.broadcasted_iota(jnp.int32, (tile, tile), 0)
    cols_iota = lax.broadcasted_iota(jnp.int32, (tile, tile), 1)
    allowed = rows_iota <= cols_iota
    masks = [lane_mask(tile, head) for head in range(2)]
    dk_s[...] = jnp.zeros_like(dk_s)
    dv_s[...] = jnp.zeros_like(dv_s)

    for qt in range(tiles):
        q_span = slice(qt * tile, (qt + 1) * tile)
        query = q_s[q_span, :] * jnp.asarray(scale, BF16)
        grad = g_s[q_span, :]
        queries = [jnp.where(masks[head], query, jnp.zeros_like(query)) for head in range(2)]
        grads = [jnp.where(masks[head], grad, jnp.zeros_like(grad)) for head in range(2)]
        product = grad.astype(F32).T * att_ref[:, q_span]
        dots = [jnp.sum(product[head * HD : (head + 1) * HD], axis=0, keepdims=True) for head in range(2)]
        totals = [lse_ref[head : head + 1, q_span] for head in range(2)]

        def step(kt, state, masked, queries=queries, grads=grads, dots=dots, totals=totals):
            start = pl.multiple_of(kt * tile, tile)
            rows = pl.ds(start, tile)
            keys = k_s[rows, :]
            values = v_s[rows, :]
            dk = dk_s[rows, :]
            dv = dv_s[rows, :]
            new = []
            for head in range(2):
                scores = nt(keys, queries[head])
                if masked:
                    scores = jnp.where(allowed, scores, NEG_BIG)
                soft = jnp.exp(scores - totals[head])
                dsoft = nt(values, grads[head])
                dscore = (soft * (dsoft - dots[head])).astype(BF16)
                dv = dv + nn(soft.astype(BF16), grads[head])
                dk = dk + nn(dscore, queries[head])
                new.append(state[head] + nn(kt_s[head * HD : (head + 1) * HD, rows], dscore))
            dk_s[rows, :] = dk
            dv_s[rows, :] = dv
            return tuple(new)

        state = (jnp.zeros((HD, tile), F32), jnp.zeros((HD, tile), F32))
        state = step(qt, state, True)
        if qt > 0:
            state = lax.fori_loop(0, qt, lambda kt, s, step=step: step(kt, s, False), state)
        dq = jnp.concatenate(state, axis=0) * scale
        dq_s[q_span, :] = dq.T.astype(BF16)

    def body(block, carry):
        start = pl.multiple_of(block * half, half)
        place = order_ref[block]
        out_ref[0, place] = dq_s[pl.ds(start, half), :]
        out_ref[1, place] = dk_s[pl.ds(start, half), :].astype(BF16)
        out_ref[2, place] = dv_s[pl.ds(start, half), :].astype(BF16)
        return carry

    lax.fori_loop(0, blocks, body, 0)


def attend_backward(order, qkv, grad, att, lse, tile):
    kinds, blocks, half, lanes = qkv.shape
    length = blocks * half
    return pl.pallas_call(
        functools.partial(backward_kernel, tile),
        out_shape=jax.ShapeDtypeStruct((3, blocks, half, LANES), BF16),
        in_specs=[SMEM, VMEM, VMEM, VMEM, VMEM],
        out_specs=VMEM,
        scratch_shapes=[pltpu.VMEM((length, LANES), BF16)] * 4
        + [pltpu.VMEM((LANES, length), BF16), pltpu.VMEM((length, LANES), BF16)]
        + [pltpu.VMEM((length, LANES), F32)] * 2,
        compiler_params=params(),
        cost_estimate=SMALL,
        name="attend_backward",
    )(order, qkv, grad, att, lse)


def assemble_kernel(pieces, part_ref, out_ref):
    for start, source, first, size in pieces:
        out_ref[:, start : start + size] = part_ref[source, :, first : first + size].astype(F32)


def assemble(parts, pieces, width, block):
    n_ctx, rows, columns = parts.shape
    return pl.pallas_call(
        functools.partial(assemble_kernel, pieces),
        grid=(rows // block,),
        out_shape=jax.ShapeDtypeStruct((rows, width), F32),
        in_specs=[pl.BlockSpec((n_ctx, block, columns), lambda i: (0, i, 0))],
        out_specs=pl.BlockSpec((block, width), lambda i: (i, 0)),
        compiler_params=params(),
        name="assemble",
    )(parts)


def mm(left, right):
    return jnp.matmul(left, right, preferred_element_type=F32)


def mm_nt(left, right):
    return lax.dot_general(left, right, (((1,), (1,)), ((), ())), preferred_element_type=F32)


def mm_tn(left, right):
    return lax.dot_general(left, right, (((0,), (0,)), ((), ())), preferred_element_type=F32)


def gelu_tanh(values):
    return jax.nn.gelu(values, approximate=True)


def local(
    tokens,
    block_pairs,
    out_grad,
    ln1_gain,
    ln1_bias,
    qkv_weight,
    query_bias,
    value_bias,
    out_weight,
    out_bias,
    ln2_gain,
    ln2_bias,
    up_weight,
    up_bias,
    down_weight,
    down_bias,
):
    n_ctx, planes = lax.axis_size("ctx"), lax.axis_size("fsdp")
    c, f = lax.axis_index("ctx"), lax.axis_index("fsdp")
    local_rows, seqs, width = tokens.shape
    half = local_rows // 2
    devices = n_ctx * planes
    blocks = 2 * devices
    length = devices * local_rows
    heads = width // HD
    slots = planes * (-(-heads // devices))
    assert slots == planes and planes % seqs == 0
    span = slots * HD
    rows = local_rows * seqs
    plane_rows = n_ctx * rows
    quarter = width // planes
    ff = up_weight.shape[1]
    ff_quarter = ff // planes
    ff_piece = ff_quarter // n_ctx
    ff_span = ff_piece * planes
    tile = 256

    device_ids = jnp.arange(devices, dtype=jnp.int32)
    device_of_block = jnp.sum(
        jnp.where(block_pairs[None, :] == device_ids[:, None], device_ids[None, :], 0), axis=1
    )
    order = jnp.concatenate([device_of_block * 2, device_of_block[::-1] * 2 + 1]).astype(jnp.int32)

    first = [-(-quarter * j // HD) for j in range(planes)] + [heads]
    counts = [first[j + 1] - first[j] for j in range(planes)]
    assert max(counts) <= n_ctx
    slot_head = [jnp.minimum(first[j] + c, heads - 1) for j in range(planes)]
    first_own = jnp.asarray(first, jnp.int32)[f]
    count_own = jnp.asarray(counts, jnp.int32)[f]

    qkv_own = jnp.concatenate(
        [
            lax.dynamic_slice(qkv_weight, (0, k * width + slot_head[j] * HD), (quarter, HD))
            for k in range(3)
            for j in range(planes)
        ],
        axis=1,
    )
    qkv_slice = lax.all_gather(qkv_own, "fsdp", axis=0, tiled=True)
    next_rows = lax.ppermute(out_weight[:HD], "fsdp", [(j + 1, j) for j in range(planes - 1)])
    out_own = lax.dynamic_slice(
        jnp.concatenate([out_weight, next_rows]), ((first_own + c) * HD - f * quarter, 0), (HD, width)
    )
    out_own = jnp.where(c < count_own, out_own, jnp.zeros_like(out_own))
    down_own = lax.dynamic_slice(down_weight, (c * ff_piece, 0), (ff_piece, width))

    tok = jnp.swapaxes(tokens, 0, 1).reshape(rows, width)
    og = jnp.swapaxes(out_grad, 0, 1).reshape(rows, width)

    packed = jnp.concatenate(
        [
            jnp.stack([ln1_gain, ln1_bias, ln2_gain, ln2_bias, query_bias, value_bias, out_bias, down_bias]),
            up_bias.reshape(ff // width, quarter),
        ]
    )
    packed = jnp.pad(packed, ((0, -packed.shape[0] % 16), (0, -quarter % LANES)))
    vectors, h1, og_all = first_norm_gather(tok, og, packed, n_ctx, planes)
    up_own = jnp.concatenate(
        [
            lax.dynamic_slice(up_weight, (0, k * ff_quarter + c * ff_piece), (quarter, ff_piece))
            for k in range(planes)
        ],
        axis=1,
    )
    rows_own = jnp.concatenate([out_own, down_own])
    h1 = h1.reshape(plane_rows, width)
    og_all = og_all.reshape(plane_rows, width)
    vectors = vectors[:, :, :quarter].astype(F32)
    gain1, bias1, gain2, bias2, bias_q, bias_v, bias_o, bias_d = [
        vectors[:, k].reshape(width) for k in range(8)
    ]
    bias_up = lax.dynamic_slice(
        vectors[:, 8 : 8 + ff // width].reshape(planes, ff_quarter), (0, c * ff_piece), (planes, ff_piece)
    ).reshape(ff_span)

    def head_part(vector):
        return [lax.dynamic_slice(vector, (slot_head[j] * HD,), (HD,)) for j in range(planes)]

    qkv_shift = jnp.concatenate(head_part(bias_q) + [jnp.zeros((span,), F32)] + head_part(bias_v))

    qkv = (mm(h1, qkv_slice) + qkv_shift).astype(BF16)
    (qkv_heads,) = to_heads(qkv.reshape(n_ctx, seqs, local_rows, 3 * span), 3, planes, 5)
    qkv_heads, rows_own = lax.optimization_barrier((qkv_heads, rows_own))
    mixed_rows = lax.all_gather(rows_own, "fsdp", axis=0)
    out_slice = mixed_rows[:, :HD].reshape(span, width)
    down_slice = mixed_rows[:, HD:].reshape(ff_span, width)
    qkv_heads = qkv_heads.reshape(3, blocks, half, LANES)
    att_heads, att_exact, lse = attend_forward(order, qkv_heads, tile)
    att_heads, up_own = lax.optimization_barrier((att_heads, up_own))
    up_slice = lax.all_gather(up_own, "fsdp", axis=0, tiled=True)
    (att,) = to_tokens(att_heads.reshape(1, n_ctx, planes, local_rows, LANES), seqs, 6)
    att = att.reshape(plane_rows, span)
    branch = mm(att, out_slice).astype(BF16).reshape(n_ctx, rows, width)
    mixed, h2 = second_norm_gather(branch, tok, jnp.stack([gain2, bias2, bias_o]))
    h2 = h2.reshape(plane_rows, width)
    up = mm(h2, up_slice) + bias_up
    activated, gelu_back = jax.vjp(gelu_tanh, up)
    act = activated.astype(BF16)
    out_part = mm(act, down_slice).astype(BF16).reshape(n_ctx, rows, width)

    def reduce_own(part):
        return lax.psum_scatter(part, "fsdp", scatter_dimension=0, tiled=True)

    down_part = mm_tn(act, og_all).astype(BF16)
    og_all, unused = lax.optimization_barrier((og_all, down_part))
    (d_up,) = gelu_back(mm_nt(og_all, down_slice))
    d_up_low = d_up.astype(BF16)
    d_h2 = mm_nt(d_up_low, up_slice).astype(BF16).reshape(n_ctx, rows, width)
    up_part = mm_tn(h2, d_up_low).astype(BF16)
    d_h2, unused = lax.optimization_barrier((d_h2, up_part))
    down_own_grad, up_own_grad = reduce_own(down_part), reduce_own(up_part)
    d_mixed, sums2, d_branch = second_norm_back(d_h2, mixed, og, gain2[None, :])
    d_branch = d_branch.reshape(plane_rows, width)
    d_att = mm_nt(d_branch, out_slice).astype(BF16)
    out_w_part = mm_tn(att, d_branch).astype(BF16)
    d_att, unused = lax.optimization_barrier((d_att, out_w_part))
    out_own_grad = reduce_own(out_w_part)
    d_att_heads, block_out = to_heads(
        d_att.reshape(n_ctx, seqs, local_rows, span), 1, planes, 7, (out_part, mixed, bias_d[None, :])
    )
    d_heads = attend_backward(order, qkv_heads, d_att_heads.reshape(blocks, half, LANES), att_exact, lse, tile)
    d_qkv, down_parts, up_parts = to_tokens(
        d_heads.reshape(3, n_ctx, planes, local_rows, LANES), seqs, 8, (down_own_grad, up_own_grad)
    )
    d_qkv = d_qkv.reshape(plane_rows, 3 * span)
    qkv_part = mm_tn(h1, d_qkv).astype(BF16)
    qkv_part, d_qkv = lax.optimization_barrier((qkv_part, d_qkv))
    qkv_own_grad = reduce_own(qkv_part)
    d_h1 = mm_nt(d_qkv, qkv_slice).astype(BF16).reshape(n_ctx, rows, width)

    d_qkv_sum = jnp.sum(d_qkv.astype(F32), axis=0)
    d_up_sum = jnp.sum(d_up_low.astype(F32), axis=0).reshape(planes, ff_piece)
    up_spread = lax.dynamic_update_slice(jnp.zeros((planes, ff_quarter), F32), d_up_sum, (0, c * ff_piece))

    def spread(values):
        full = jnp.zeros((width + HD,), F32)
        for j in range(planes):
            place = jnp.where(c < counts[j], (first[j] + c) * HD, width)
            full = lax.dynamic_update_slice(full, values[j * HD : (j + 1) * HD], (place,))
        return full[None, :width]

    wide = jnp.concatenate([sums2, spread(d_qkv_sum[:span]), spread(d_qkv_sum[2 * span :])])
    wide = wide.reshape(6, planes, quarter).transpose(1, 0, 2).reshape(planes, 6 * quarter)
    flat = jnp.concatenate([wide, up_spread], axis=1)
    size = flat.shape[1]
    flat = jnp.pad(flat, ((0, 0), (0, -size % (8 * LANES)))).reshape(planes, -1, LANES)

    grad_tok, out_parts, sums1, totals = first_norm_back(
        d_h1, out_own_grad, flat, tok, d_mixed, gain1[None, :]
    )
    sums1 = sums1[:2, :quarter]
    totals = totals.reshape(-1)
    sums = totals[: 6 * quarter].reshape(6, quarter)
    up_bias_grad = totals[6 * quarter : size]

    down_grad = down_parts.reshape(ff_quarter, width).astype(F32)
    block = quarter // 5
    up_pieces = [
        (j * ff_quarter + d * ff_piece, d, j * ff_piece, ff_piece) for j in range(planes) for d in range(n_ctx)
    ]
    up_grad = assemble(up_parts, up_pieces, ff, block)
    out_parts, up_grad, qkv_own_grad = lax.optimization_barrier((out_parts, up_grad, qkv_own_grad))
    (qkv_parts,) = gather_plane([qkv_own_grad], n_ctx, 9)
    qkv_pieces = [
        (k * width + (first[j] + d) * HD, d, k * span + j * HD, HD)
        for k in range(3)
        for j in range(planes)
        for d in range(counts[j])
    ]
    qkv_grad = assemble(qkv_parts, qkv_pieces, 3 * width, block)
    out_rows = out_parts.reshape(n_ctx * HD, width)
    tail = (f + 1) * quarter - first_own * HD
    tail_rows = lax.dynamic_slice(out_rows, (tail, 0), (HD, width))
    tail_rows = lax.ppermute(tail_rows, "fsdp", [(j, j + 1) for j in range(planes - 1)])
    lead = first_own * HD - f * quarter
    shifted = lax.dynamic_slice(
        jnp.concatenate([jnp.zeros((HD, width), BF16), out_rows]), (HD - lead, 0), (quarter, width)
    )
    from_tail = jnp.concatenate([tail_rows, jnp.zeros((quarter - HD, width), BF16)])
    row_ids = lax.broadcasted_iota(jnp.int32, (quarter, width), 0)
    out_grad_own = jnp.where(row_ids < lead, from_tail, shifted).astype(F32)

    def back(values):
        return jnp.swapaxes(values.reshape(seqs, local_rows, width), 0, 1)

    return (
        back(block_out),
        back(grad_tok),
        sums1[0],
        sums1[1],
        qkv_grad,
        sums[4],
        sums[5],
        out_grad_own,
        sums[2],
        sums[0],
        sums[1],
        up_grad,
        up_bias_grad,
        down_grad,
        sums[3],
    )


def solution(mesh):
    both, row, vec, mat = P(("ctx", "fsdp"), None, None), P(), P("fsdp"), P("fsdp", None)
    in_specs = (both, row, both, vec, vec, mat, vec, vec, mat, vec, vec, vec, mat, vec, mat, vec)
    out_specs = (both, both, vec, vec, mat, vec, vec, mat, vec, vec, vec, mat, vec, mat, vec)
    return jax.shard_map(local, mesh=mesh, in_specs=in_specs, out_specs=out_specs, check_vma=False)
```

```python
import functools
import math

import jax
import jax.numpy as jnp
from jax import lax
from jax.experimental import pallas as pl
from jax.experimental.pallas import tpu as pltpu
from jax.sharding import PartitionSpec as P

HD = 64
LANES = 128
NORM_EPS = 1e-05
NEG_BIG = -1e30
MESH = pl.DeviceIdType.MESH
F32 = jnp.float32
BF16 = jnp.bfloat16
ANY = pl.BlockSpec(memory_space=pl.ANY)
VMEM = pl.BlockSpec(memory_space=pltpu.VMEM)
DMA = pltpu.SemaphoreType.DMA
VMEM_LIMIT = 56 * 1024 * 1024
SMALL = pl.CostEstimate(flops=1, bytes_accessed=1, transcendentals=0)


def params(cid=None):
    if cid is None:
        return pltpu.CompilerParams(vmem_limit_bytes=VMEM_LIMIT)
    return pltpu.CompilerParams(
        collective_id=cid, has_side_effects=True, vmem_limit_bytes=VMEM_LIMIT
    )


def plane_peers(chips):
    me = lax.axis_index("ctx")
    core = lax.rem(me, 2)
    chip = me // 2
    sibling = chip * 2 + 1 - core
    if chips == 4:
        across_x = chip + 1 - 2 * lax.rem(chip, 2)
        across_y = lax.rem(chip + 2, 4)
        corner = lax.rem(across_x + 2, 4)
        first = across_x * (1 - core) + across_y * core
        second = across_y * (1 - core) + across_x * core
        to = come = [first * 2 + core, second * 2 + core, corner * 2 + core]
    else:
        to = [lax.rem(chip + k, chips) * 2 + core for k in range(1, chips)]
        come = [lax.rem(chip + chips - k, chips) * 2 + core for k in range(1, chips)]
    return me, core, chip, sibling, to, come


def greet(plane=(), across=()):
    barrier = pltpu.get_barrier_semaphore()
    for peer in plane:
        pl.semaphore_signal(barrier, inc=1, device_id={"ctx": peer}, device_id_type=MESH)
    for peer in across:
        pl.semaphore_signal(barrier, inc=1, device_id={"fsdp": peer}, device_id_type=MESH)
    pl.semaphore_wait(barrier, len(plane) + len(across))


def other_planes(planes):
    me = lax.axis_index("fsdp")
    return me, [lax.rem(me + k, planes) for k in range(1, planes)]


def send(src, dst, send_sem, recv_sem, axis, peer):
    copy = pltpu.make_async_remote_copy(
        src_ref=src,
        dst_ref=dst,
        send_sem=send_sem,
        recv_sem=recv_sem,
        device_id={axis: peer},
        device_id_type=MESH,
    )
    copy.start()
    return copy


def plane_gather_start(owns, alls, sems, chips):
    far_send, far_recv, near_send, near_recv, local_sem = sems
    me, core, chip, sibling, to, come = plane_peers(chips)
    direct = 2 if chips == 4 else chips - 1
    last = chips - 1
    far, near, local = [], [], []
    for i, (own_ref, all_ref) in enumerate(zip(owns, alls)):
        far.append(
            [
                send(own_ref, all_ref.at[me], far_send.at[i, k], far_recv.at[i, k], "ctx", to[k])
                for k in range(direct)
            ]
        )
        near.append(send(own_ref, all_ref.at[me], near_send.at[i, last], near_recv.at[i, last], "ctx", sibling))
        copy = pltpu.make_async_copy(own_ref, all_ref.at[me], local_sem.at[i])
        copy.start()
        local.append(copy)
    return far, near, local


def plane_gather_finish(started, alls, sems, chips):
    far_send, far_recv, near_send, near_recv, local_sem = sems
    me, core, chip, sibling, to, come = plane_peers(chips)
    far, near, local = started
    near = list(near)

    def pass_on(i, all_ref, k):
        far[i][k].wait_recv()
        block = all_ref.at[come[k]]
        if chips == 4 and k == 0:
            far[i].append(send(block, block, far_send.at[i, 2], far_recv.at[i, 2], "ctx", to[1]))
        near.append(send(block, block, near_send.at[i, k], near_recv.at[i, k], "ctx", sibling))

    direct = 2 if chips == 4 else chips - 1
    for i, all_ref in enumerate(alls):
        for k in range(direct):
            pass_on(i, all_ref, k)
    for i, all_ref in enumerate(alls):
        for k in range(direct, chips - 1):
            pass_on(i, all_ref, k)
    for group in far:
        for copy in group:
            copy.wait_send()
    for copy in near + local:
        copy.wait()


def plane_gather(owns, alls, sems, chips):
    plane_gather_finish(plane_gather_start(owns, alls, sems, chips), alls, sems, chips)


def plane_scatter(block_of, mine, paired, arrived, sems, chips):
    far_send, far_recv, near_send, near_recv, local_sem = sems
    me, core, chip, sibling, to, come = plane_peers(chips)
    targets = to + [me]
    order = [2, 1, 0, 3] if chips == 4 else list(range(chips))
    near, local = [None] * chips, [None] * chips
    crossed = [1, 0, 2, 3] if chips == 4 else list(range(chips))
    for k in order:
        other = targets[crossed[k]] + 1 - 2 * core
        near[k] = send(block_of(other), paired.at[k], near_send.at[k], near_recv.at[k], "ctx", sibling)
        local[k] = pltpu.make_async_copy(block_of(targets[k]), mine.at[k], local_sem.at[k])
        local[k].start()

    def both(k):
        local[k].wait()
        near[k].wait_recv()
        return mine[k].astype(F32) + paired[k].astype(F32)

    def dispatch(k, target):
        return send(mine.at[k], arrived.at[k], far_send.at[k], far_recv.at[k], "ctx", target)

    far = [None] * (chips - 1)
    if chips == 4:
        mine[2] = both(2).astype(BF16)
        far[2] = dispatch(2, to[0])
        mine[0] = both(0).astype(BF16)
        far[0] = dispatch(0, to[0])
        partial = both(1)
        far[2].wait_recv()
        mine[1] = (partial + arrived[2].astype(F32)).astype(BF16)
        far[1] = dispatch(1, to[1])
        total = both(3)
        arriving = [0, 1]
    else:
        for k in range(chips - 1):
            mine[k] = both(k).astype(BF16)
            far[k] = dispatch(k, to[k])
        total = both(chips - 1)
        arriving = range(chips - 1)
    for k in arriving:
        far[k].wait_recv()
        total = total + arrived[k].astype(F32)
    for copy in far + near:
        copy.wait_send()
    return total


def gather_sems(chips, count=1):
    return [DMA((count, chips - 1))] * 2 + [DMA((count, chips))] * 2 + [DMA((count,))]


def scatter_scratch(chips, *block):
    return [
        pltpu.VMEM((chips,) + block, BF16),
        pltpu.VMEM((chips,) + block, BF16),
        pltpu.VMEM((chips - 1,) + block, BF16),
        DMA((chips - 1,)),
        DMA((chips - 1,)),
        DMA((chips,)),
        DMA((chips,)),
        DMA((chips,)),
    ]


def normalize(values):
    average = jnp.mean(values, axis=-1, keepdims=True)
    centered = values - average
    variance = jnp.mean(centered * centered, axis=-1, keepdims=True)
    inverse = lax.rsqrt(variance + NORM_EPS)
    return centered * inverse, inverse


def norm_backward(grad, gain, unit, inverse):
    scaled = grad * gain
    first = jnp.mean(scaled, axis=-1, keepdims=True)
    second = jnp.mean(scaled * unit, axis=-1, keepdims=True)
    return (scaled - first - unit * second) * inverse


def first_kernel(
    chips,
    planes,
    seqs,
    quarter,
    tok_ref,
    og_ref,
    vec_ref,
    weight_ref,
    vecs_ref,
    ogs_ref,
    h1_ref,
    weights_ref,
    own,
    column,
    v_send,
    v_recv,
    v_local,
    h_send,
    h_recv,
    w_send,
    w_recv,
    w_local,
    *sems,
):
    me, core, chip, sibling, to, come = plane_peers(chips)
    plane, others = other_planes(planes)
    pairs = planes // seqs
    rows = own.shape[0] // seqs
    greet(to + [sibling], others)
    og_sems, h1_sems = sems[:5], [sems[5 + 5 * k : 10 + 5 * k] for k in range(planes)]
    copies = [
        send(vec_ref, vecs_ref.at[plane], v_send.at[k], v_recv.at[k], "fsdp", peer) for k, peer in enumerate(others)
    ]
    local = pltpu.make_async_copy(vec_ref, vecs_ref.at[plane], v_local)
    local.start()
    og_started = plane_gather_start([og_ref], [ogs_ref], og_sems, chips)
    unit, inverse = normalize(tok_ref[...].astype(F32))
    for copy in copies + [local]:
        copy.wait()
    lines = quarter // LANES + 1

    def vector(k):
        pieces = []
        for j in range(planes):
            for line in range(lines):
                size = min(LANES, quarter - line * LANES)
                if size:
                    row = k * lines + line
                    pieces.append(vecs_ref[j, row : row + 1, :size].astype(F32))
        return jnp.concatenate(pieces, axis=1)

    own[...] = (unit * vector(0) + vector(1)).astype(BF16)

    def half_of(peer):
        return own.at[pl.ds(pl.multiple_of(peer // pairs * rows, rows), rows)]

    halves = [
        send(half_of(peer), column.at[k], h_send.at[k], h_recv.at[k], "fsdp", peer) for k, peer in enumerate(others)
    ]
    weights = [
        send(weight_ref.at[lax.rem(peer, pairs)], weights_ref.at[plane], w_send.at[k], w_recv.at[k], "fsdp", peer)
        for k, peer in enumerate(others)
    ]
    weights.append(pltpu.make_async_copy(weight_ref.at[lax.rem(plane, pairs)], weights_ref.at[plane], w_local))
    weights[-1].start()
    sources = [plane] + [lax.rem(plane + planes - k, planes) for k in range(1, planes)]
    blocks = [half_of(plane)] + [column.at[k] for k in range(planes - 1)]
    started = [plane_gather_start([blocks[0]], [h1_ref.at[sources[0]]], h1_sems[0], chips)]
    plane_gather_finish(og_started, [ogs_ref], og_sems, chips)
    for k in range(1, planes):
        halves[k - 1].wait_recv()
        started.append(plane_gather_start([blocks[k]], [h1_ref.at[sources[k]]], h1_sems[k], chips))
    for k in range(planes):
        plane_gather_finish(started[k], [h1_ref.at[sources[k]]], h1_sems[k], chips)
    for copy in halves:
        copy.wait_send()
    for copy in weights:
        copy.wait()


def first_norm_gather(tok, og, vec, weight, n_ctx, planes, seqs):
    rows, width = tok.shape
    chips, half = n_ctx // 2, rows // seqs
    return pl.pallas_call(
        functools.partial(first_kernel, chips, planes, seqs, width // planes),
        out_shape=(
            jax.ShapeDtypeStruct((planes,) + vec.shape, BF16),
            jax.ShapeDtypeStruct((n_ctx, rows, width), BF16),
            jax.ShapeDtypeStruct((planes, n_ctx, half, width), BF16),
            jax.ShapeDtypeStruct((planes,) + weight.shape[1:], BF16),
        ),
        in_specs=[VMEM, ANY, VMEM, ANY],
        out_specs=(VMEM, ANY, ANY, ANY),
        scratch_shapes=[
            pltpu.VMEM((rows, width), BF16),
            pltpu.VMEM((planes - 1, half, width), BF16),
            DMA((planes - 1,)),
            DMA((planes - 1,)),
            DMA,
            DMA((planes - 1,)),
            DMA((planes - 1,)),
            DMA((planes - 1,)),
            DMA((planes - 1,)),
            DMA,
        ]
        + gather_sems(chips)
        + gather_sems(chips) * planes,
        compiler_params=params(0),
        cost_estimate=SMALL,
        name="norm_gather",
    )(tok, og, vec, weight)


def second_kernel(chips, part_ref, tok_ref, vec_ref, mixed_ref, all_ref, own, *scratch):
    me, core, chip, sibling, to, come = plane_peers(chips)
    greet(to + [sibling])
    total = plane_scatter(lambda c: part_ref.at[c], *scratch[:3], scratch[3:8], chips)
    mixed = tok_ref[...].astype(F32) + total + vec_ref[2:3, :]
    mixed_ref[...] = mixed
    unit, inverse = normalize(mixed)
    own[...] = (unit * vec_ref[0:1, :] + vec_ref[1:2, :]).astype(BF16)
    plane_gather([own], [all_ref], scratch[8:], chips)


def second_norm_gather(part, tok, vecs):
    n_ctx, rows, width = part.shape
    chips = n_ctx // 2
    return pl.pallas_call(
        functools.partial(second_kernel, chips),
        out_shape=(
            jax.ShapeDtypeStruct((rows, width), F32),
            jax.ShapeDtypeStruct((n_ctx, rows, width), BF16),
        ),
        in_specs=[ANY, VMEM, VMEM],
        out_specs=(VMEM, ANY),
        scratch_shapes=[pltpu.VMEM((rows, width), BF16)]
        + scatter_scratch(chips, rows, width)
        + gather_sems(chips),
        compiler_params=params(1),
        cost_estimate=SMALL,
        name="scatter_norm_gather",
    )(part, tok, vecs)


def third_kernel(chips, part_ref, mixed_ref, og_ref, vec_ref, dmixed_ref, sums_ref, all_ref, own, *scratch):
    me, core, chip, sibling, to, come = plane_peers(chips)
    greet(to + [sibling])
    unit, inverse = normalize(mixed_ref[...])
    grad = plane_scatter(lambda c: part_ref.at[c], *scratch[:3], scratch[3:8], chips)
    out_grad = og_ref[...].astype(F32)
    dmixed = out_grad + norm_backward(grad, vec_ref[0:1, :], unit, inverse)
    dmixed_ref[...] = dmixed
    low = dmixed.astype(BF16)
    own[...] = low
    sums_ref[0:1, :] = jnp.sum(grad * unit, axis=0, keepdims=True)
    sums_ref[1:2, :] = jnp.sum(grad, axis=0, keepdims=True)
    sums_ref[2:3, :] = jnp.sum(low.astype(F32), axis=0, keepdims=True)
    sums_ref[3:4, :] = jnp.sum(out_grad, axis=0, keepdims=True)
    plane_gather([own], [all_ref], scratch[8:], chips)


def second_norm_back(part, mixed, og, vecs):
    n_ctx, rows, width = part.shape
    chips = n_ctx // 2
    return pl.pallas_call(
        functools.partial(third_kernel, chips),
        out_shape=(
            jax.ShapeDtypeStruct((rows, width), F32),
            jax.ShapeDtypeStruct((4, width), F32),
            jax.ShapeDtypeStruct((n_ctx, rows, width), BF16),
        ),
        in_specs=[ANY, VMEM, VMEM, VMEM],
        out_specs=(VMEM, VMEM, ANY),
        scratch_shapes=[pltpu.VMEM((rows, width), BF16)]
        + scatter_scratch(chips, rows, width)
        + gather_sems(chips),
        compiler_params=params(2),
        cost_estimate=SMALL,
        name="scatter_back_gather",
    )(part, mixed, og, vecs)


def fourth_kernel(
    chips,
    planes,
    seqs,
    part_ref,
    qkv_ref,
    outw_ref,
    flat_ref,
    tok_ref,
    dmixed_ref,
    vec_ref,
    grad_ref,
    qkv_all,
    outw_all,
    sums_ref,
    flat_out,
    q_arrived,
    q_own,
    q_send,
    q_recv,
    q_local,
    rows_own,
    rows_arrived,
    r_send,
    r_recv,
    small,
    small_own,
    small_z,
    small_c,
    flat_own,
    flat_z,
    flat_c,
    z_send,
    z_recv,
    c_send,
    c_recv,
    *scratch,
):
    n_ctx = 2 * chips
    pairs = planes // seqs
    me, core, chip, sibling, to, come = plane_peers(chips)
    plane, others = other_planes(planes)
    around = [lax.rem(me + k, n_ctx) for k in range(1, n_ctx)]
    greet(around, others)
    scatter, rest_sems, qkv_sems = scratch[:8], scratch[8:13], scratch[13:]

    pushed = [
        send(qkv_ref.at[peer], q_arrived.at[plane], q_send.at[k], q_recv.at[k], "fsdp", peer)
        for k, peer in enumerate(others)
    ]
    held = pltpu.make_async_copy(qkv_ref.at[plane], q_arrived.at[plane], q_local)
    held.start()
    flat_sent = [
        send(flat_ref.at[peer], flat_z.at[k], z_send.at[0, k], z_recv.at[0, k], "fsdp", peer)
        for k, peer in enumerate(others)
    ]
    unit, inverse = normalize(tok_ref[...].astype(F32))
    total = plane_scatter(lambda c: part_ref.at[:, c], *scatter[:3], scatter[3:], chips)
    rows_own[...] = total.astype(BF16)
    rows_sent = [
        send(rows_own.at[peer], rows_arrived.at[plane], r_send.at[k], r_recv.at[k], "fsdp", peer)
        for k, peer in enumerate(others)
    ]
    rows_arrived[plane] = rows_own[plane]
    rest_started = plane_gather_start([outw_ref], [outw_all], rest_sems, chips)
    for copy in pushed + [held]:
        copy.wait()
    for pair in range(pairs):
        terms = [q_arrived[seq * pairs + pair].astype(F32) for seq in range(seqs)]
        q_own[pair] = sum(terms[1:], terms[0]).astype(BF16)
    qkv_started = plane_gather_start([q_own], [qkv_all], qkv_sems, chips)
    plane_gather_finish(rest_started, [outw_all], rest_sems, chips)

    for copy in rows_sent:
        copy.wait()
    halves = []
    for seq in range(seqs):
        terms = [rows_arrived[seq * pairs + pair].astype(F32) for pair in range(pairs)]
        halves.append(sum(terms[1:], terms[0]))
    grad = jnp.concatenate(halves, axis=0)
    sums = jnp.concatenate(
        [jnp.sum(grad * unit, axis=0, keepdims=True), jnp.sum(grad, axis=0, keepdims=True)], axis=0
    )
    quarter = sums.shape[1] // planes
    small[...] = jnp.zeros_like(small)
    for j in range(planes):
        small[j, 0:2, 0:quarter] = sums[:, j * quarter : (j + 1) * quarter]
    small_sent = [
        send(small.at[peer], small_z.at[k], z_send.at[1, k], z_recv.at[1, k], "fsdp", peer)
        for k, peer in enumerate(others)
    ]
    grad_ref[...] = dmixed_ref[...] + norm_backward(grad, vec_ref[0:1, :], unit, inverse)
    small_total = small[plane]
    flat_total = flat_ref[plane]
    for k in range(planes - 1):
        flat_sent[k].wait()
        small_sent[k].wait()
        small_total = small_total + small_z[k]
        flat_total = flat_total + flat_z[k]
    small_own[...] = small_total
    flat_own[...] = flat_total
    sent = []
    for k, peer in enumerate(around):
        sent.append(send(small_own, small_c.at[k], c_send.at[0, k], c_recv.at[0, k], "ctx", peer))
        sent.append(send(flat_own, flat_c.at[k], c_send.at[1, k], c_recv.at[1, k], "ctx", peer))
    plane_gather_finish(qkv_started, [qkv_all], qkv_sems, chips)
    for copy in sent:
        copy.wait()
    for k in range(n_ctx - 1):
        small_total = small_total + small_c[k]
        flat_total = flat_total + flat_c[k]
    sums_ref[...] = small_total
    flat_out[...] = flat_total


def first_norm_back(part, qkv_part, outw_own, flat, tok, dmixed, vecs):
    planes, n_ctx, half, width = part.shape
    rows = tok.shape[0]
    seqs = rows // half
    quarter, columns = qkv_part.shape[1:]
    chips, pairs = n_ctx // 2, planes // seqs
    size = (8, quarter + -quarter % LANES)
    return pl.pallas_call(
        functools.partial(fourth_kernel, chips, planes, seqs),
        out_shape=(
            jax.ShapeDtypeStruct((rows, width), F32),
            jax.ShapeDtypeStruct((n_ctx, pairs, quarter, columns), BF16),
            jax.ShapeDtypeStruct((n_ctx,) + outw_own.shape, BF16),
            jax.ShapeDtypeStruct(size, F32),
            jax.ShapeDtypeStruct(flat.shape[1:], F32),
        ),
        in_specs=[ANY, ANY, ANY, VMEM, VMEM, VMEM, VMEM],
        out_specs=(VMEM, ANY, ANY, VMEM, VMEM),
        scratch_shapes=[
            pltpu.VMEM((planes, quarter, columns), BF16),
            pltpu.VMEM((pairs, quarter, columns), BF16),
            DMA((planes - 1,)),
            DMA((planes - 1,)),
            DMA,
            pltpu.VMEM((planes, half, width), BF16),
            pltpu.VMEM((planes, half, width), BF16),
            DMA((planes - 1,)),
            DMA((planes - 1,)),
            pltpu.VMEM((planes,) + size, F32),
            pltpu.VMEM(size, F32),
            pltpu.VMEM((planes - 1,) + size, F32),
            pltpu.VMEM((n_ctx - 1,) + size, F32),
            pltpu.VMEM(flat.shape[1:], F32),
            pltpu.VMEM((planes - 1,) + flat.shape[1:], F32),
            pltpu.VMEM((n_ctx - 1,) + flat.shape[1:], F32),
            DMA((2, planes - 1)),
            DMA((2, planes - 1)),
            DMA((2, n_ctx - 1)),
            DMA((2, n_ctx - 1)),
        ]
        + scatter_scratch(chips, planes, half, width)
        + gather_sems(chips)
        + gather_sems(chips),
        compiler_params=params(3),
        cost_estimate=SMALL,
        name="scatter_back",
    )(part, qkv_part, outw_own, flat, tok, dmixed, vecs)


def to_heads_kernel(
    planes,
    seqs,
    chips,
    tok_ref,
    part_ref,
    mixed_ref,
    vec_ref,
    down_ref,
    head_ref,
    out_ref,
    down_all,
    send_sems,
    recv_sems,
    local_sem,
    *scratch,
):
    ctx_me, core, chip, sibling, to, come = plane_peers(chips)
    me, others = other_planes(planes)
    pairs = planes // seqs
    greet(to + [sibling], others)

    def source(unit):
        start = pl.multiple_of(lax.rem(unit, pairs) * LANES, LANES)
        return tok_ref.at[:, unit // pairs, :, pl.ds(start, LANES)]

    copies = [
        send(source(unit), head_ref.at[me], send_sems.at[k], recv_sems.at[k], "fsdp", unit)
        for k, unit in enumerate(others)
    ]
    copies.append(pltpu.make_async_copy(source(me), head_ref.at[me], local_sem))
    copies[-1].start()
    total = plane_scatter(lambda c: part_ref.at[c], *scratch[:3], scratch[3:8], chips)
    gathered = plane_gather_start([down_ref], [down_all], scratch[8:], chips)
    out_ref[...] = (mixed_ref[...] + total + vec_ref[...]).astype(BF16)
    plane_gather_finish(gathered, [down_all], scratch[8:], chips)
    for copy in copies:
        copy.wait()


def to_heads(tok, planes, cid, part, mixed, vec, down_own):
    n_ctx, seqs, local_rows, width = tok.shape
    chips = n_ctx // 2
    rows, model = mixed.shape
    return pl.pallas_call(
        functools.partial(to_heads_kernel, planes, seqs, chips),
        out_shape=(
            jax.ShapeDtypeStruct((planes, n_ctx, local_rows, LANES), BF16),
            jax.ShapeDtypeStruct((rows, model), BF16),
            jax.ShapeDtypeStruct((n_ctx,) + down_own.shape, BF16),
        ),
        in_specs=[ANY, ANY, VMEM, VMEM, ANY],
        out_specs=(ANY, VMEM, ANY),
        scratch_shapes=[DMA((planes - 1,)), DMA((planes - 1,)), DMA]
        + scatter_scratch(chips, rows, model)
        + gather_sems(chips),
        compiler_params=params(cid),
        cost_estimate=SMALL,
        name="to_heads",
    )(tok, part, mixed, vec, down_own)


def to_tokens_kernel(
    planes, seqs, head_ref, weight_ref, tok_ref, weights_ref, send_sems, recv_sems, local_sem, w_send, w_recv, w_local
):
    me, others = other_planes(planes)
    pairs = planes // seqs
    greet((), others)
    start = pl.multiple_of(lax.rem(me, pairs) * LANES, LANES)
    target = tok_ref.at[:, me // pairs, :, pl.ds(start, LANES)]
    copies = [
        send(head_ref.at[peer], target, send_sems.at[k], recv_sems.at[k], "fsdp", peer) for k, peer in enumerate(others)
    ]
    copies += [
        send(weight_ref, weights_ref.at[me], w_send.at[k], w_recv.at[k], "fsdp", peer) for k, peer in enumerate(others)
    ]
    for copy in (
        pltpu.make_async_copy(head_ref.at[me], target, local_sem),
        pltpu.make_async_copy(weight_ref, weights_ref.at[me], w_local),
    ):
        copy.start()
        copies.append(copy)
    for copy in copies:
        copy.wait()


def to_tokens(heads, seqs, cid, weight):
    planes, n_ctx, rows, lanes = heads.shape
    width = (planes // seqs) * LANES
    return pl.pallas_call(
        functools.partial(to_tokens_kernel, planes, seqs),
        out_shape=(
            jax.ShapeDtypeStruct((n_ctx, seqs, rows, width), heads.dtype),
            jax.ShapeDtypeStruct((planes,) + weight.shape, BF16),
        ),
        in_specs=[ANY] * 2,
        out_specs=(ANY,) * 2,
        scratch_shapes=[DMA((planes - 1,)), DMA((planes - 1,)), DMA] * 2,
        compiler_params=params(cid),
        cost_estimate=SMALL,
        name="to_tokens",
    )(heads, weight)


def nt(left, right):
    return lax.dot_general(left, right, (((1,), (1,)), ((), ())), preferred_element_type=F32)


def nn(left, right):
    return lax.dot_general(left, right, (((1,), (0,)), ((), ())), preferred_element_type=F32)


def sort_blocks(order_ref, qkv_ref, targets, blocks, half):
    def body(block, carry):
        row = qkv_ref[order_ref[block]]
        start = pl.multiple_of(block * half, half)
        for k, target in enumerate(targets):
            target[pl.ds(start, half), :] = row[:, k * LANES : (k + 1) * LANES]
        return carry

    lax.fori_loop(0, blocks, body, 0)


def lane_mask(rows, head):
    lane = lax.broadcasted_iota(jnp.int32, (rows, LANES), 1)
    return (lane < HD) if head == 0 else (lane >= HD)


def unsort_blocks(order_ref, sorted_refs, target_ref, blocks, half):
    def body(block, carry):
        start = pl.multiple_of(block * half, half)
        place = order_ref[block]
        for k, source in enumerate(sorted_refs):
            target_ref[place, :, k * LANES : (k + 1) * LANES] = source[pl.ds(start, half), :].astype(BF16)
        return carry

    lax.fori_loop(0, blocks, body, 0)


def long_forward_kernel(tile, order_ref, qkv_ref, out_ref, att_ref, lse_ref, q_s, k_s, v_s, vt_s, o_s):
    blocks, half = out_ref.shape[0], out_ref.shape[1]
    length = blocks * half
    tiles = length // tile
    sort_blocks(order_ref, qkv_ref, [q_s, k_s, v_s], blocks, half)
    for t in range(tiles):
        span = slice(t * tile, (t + 1) * tile)
        vt_s[:, span] = v_s[span, :].T
    scale = HD ** (-0.5)
    rows_iota = lax.broadcasted_iota(jnp.int32, (tile, tile), 0)
    cols_iota = lax.broadcasted_iota(jnp.int32, (tile, tile), 1)
    allowed = rows_iota <= cols_iota
    masks = [lane_mask(tile, head) for head in range(2)]

    for qt in range(tiles):
        q_span = slice(qt * tile, (qt + 1) * tile)
        query = q_s[q_span, :] * jnp.asarray(scale, BF16)
        queries = [jnp.where(masks[head], query, jnp.zeros_like(query)) for head in range(2)]

        def step(kt, state, masked, queries=queries):
            start = pl.multiple_of(kt * tile, tile)
            keys = k_s[pl.ds(start, tile), :]
            new = []
            for head in range(2):
                top, total, acc = state[head]
                scores = nt(keys, queries[head])
                if masked:
                    scores = jnp.where(allowed, scores, NEG_BIG)
                new_top = jnp.maximum(top, jnp.max(scores, axis=0, keepdims=True))
                soft = jnp.exp(scores - new_top)
                factor = jnp.exp(top - new_top)
                total = total * factor + jnp.sum(soft, axis=0, keepdims=True)
                values = vt_s[head * HD : (head + 1) * HD, pl.ds(start, tile)]
                acc = acc * factor + nn(values, soft.astype(BF16))
                new.append((new_top, total, acc))
            return tuple(new)

        state = tuple(
            (jnp.full((1, tile), NEG_BIG, F32), jnp.zeros((1, tile), F32), jnp.zeros((HD, tile), F32))
            for head in range(2)
        )
        state = step(qt, state, True)
        if qt > 0:
            state = lax.fori_loop(0, qt, lambda kt, s, step=step: step(kt, s, False), state)
        parts = []
        for head in range(2):
            top, total, acc = state[head]
            parts.append(acc / total)
            lse_ref[head : head + 1, q_span] = top + jnp.log(total)
        att = jnp.concatenate(parts, axis=0).T
        att_ref[q_span, :] = att
        o_s[q_span, :] = att.astype(BF16)

    unsort_blocks(order_ref, [o_s], out_ref, blocks, half)


def forward_kernel(tile, order_ref, qkv_ref, out_ref, att_ref, lse_ref, q_s, k_s, v_s, o_s, s_s, p_s):
    blocks, half = out_ref.shape[0], out_ref.shape[1]
    length = blocks * half
    tiles = length // tile
    sort_blocks(order_ref, qkv_ref, [q_s, k_s, v_s], blocks, half)
    scale = HD ** (-0.5)
    rows_iota = lax.broadcasted_iota(jnp.int32, (tile, tile), 0)
    cols_iota = lax.broadcasted_iota(jnp.int32, (tile, tile), 1)
    allowed = cols_iota <= rows_iota
    masks = [lane_mask(tile, head) for head in range(2)]

    for qt in range(tiles):
        q_span = slice(qt * tile, (qt + 1) * tile)
        query = q_s[q_span, :] * jnp.asarray(scale, BF16)
        parts = []
        for head in range(2):
            one = jnp.where(masks[head], query, jnp.zeros_like(query))
            top = jnp.full((tile, LANES), NEG_BIG, F32)
            for kt in range(qt + 1):
                k_span = slice(kt * tile, (kt + 1) * tile)
                scores = nt(one, k_s[k_span, :])
                if kt == qt:
                    scores = jnp.where(allowed, scores, NEG_BIG)
                s_s[head, :, k_span] = scores
                for lane in range(0, tile, LANES):
                    top = jnp.maximum(top, scores[:, lane : lane + LANES])
            top = jnp.max(top, axis=1, keepdims=True)
            total = jnp.zeros((tile, LANES), F32)
            for kt in range(qt + 1):
                k_span = slice(kt * tile, (kt + 1) * tile)
                soft = jnp.exp(s_s[head, :, k_span] - top)
                for lane in range(0, tile, LANES):
                    total = total + soft[:, lane : lane + LANES]
                p_s[head, :, k_span] = soft.astype(BF16)
            total = jnp.sum(total, axis=1, keepdims=True)
            span = slice(0, (qt + 1) * tile)
            parts.append(nn(p_s[head, :, span], v_s[span, :]) / total)
            lse = jnp.broadcast_to(top + jnp.log(total), (tile, LANES))
            lse_ref[head : head + 1, q_span] = lse.T[0:1, :]
        att = jnp.where(masks[0], parts[0], parts[1])
        att_ref[q_span, :] = att
        o_s[q_span, :] = att.astype(BF16)
    unsort_blocks(order_ref, [o_s], out_ref, blocks, half)


SMEM = pl.BlockSpec(memory_space=pltpu.SMEM)
SHORT = 2048


def attend_forward(order, qkv, tile):
    blocks, half, lanes = qkv.shape
    length = blocks * half
    rows, short = pltpu.VMEM((length, LANES), BF16), length <= SHORT
    return pl.pallas_call(
        functools.partial(forward_kernel if short else long_forward_kernel, tile),
        out_shape=(
            jax.ShapeDtypeStruct((blocks, half, LANES), BF16),
            jax.ShapeDtypeStruct((length, LANES), F32),
            jax.ShapeDtypeStruct((2, length), F32),
        ),
        in_specs=[SMEM, VMEM],
        out_specs=(VMEM, VMEM, VMEM),
        scratch_shapes=[rows, rows, rows, rows, pltpu.VMEM((2, tile, length), F32), pltpu.VMEM((2, tile, length), BF16)]
        if short
        else [rows, rows, rows, pltpu.VMEM((LANES, length), BF16), rows],
        compiler_params=params(),
        cost_estimate=SMALL,
        name="attend_forward",
    )(order, qkv)


def long_backward_kernel(
    tile, order_ref, qkv_ref, grad_ref, att_ref, lse_ref, out_ref, q_s, k_s, v_s, g_s, kt_s, dq_s, dk_s, dv_s
):
    blocks, half = grad_ref.shape[0], grad_ref.shape[1]
    length = blocks * half
    tiles = length // tile
    sort_blocks(order_ref, qkv_ref, [q_s, k_s, v_s], blocks, half)
    sort_blocks(order_ref, grad_ref, [g_s], blocks, half)
    for t in range(tiles):
        span = slice(t * tile, (t + 1) * tile)
        kt_s[:, span] = k_s[span, :].T
    scale = HD ** (-0.5)
    rows_iota = lax.broadcasted_iota(jnp.int32, (tile, tile), 0)
    cols_iota = lax.broadcasted_iota(jnp.int32, (tile, tile), 1)
    allowed = rows_iota <= cols_iota
    masks = [lane_mask(tile, head) for head in range(2)]
    dk_s[...] = jnp.zeros_like(dk_s)
    dv_s[...] = jnp.zeros_like(dv_s)

    for qt in range(tiles):
        q_span = slice(qt * tile, (qt + 1) * tile)
        query = q_s[q_span, :] * jnp.asarray(scale, BF16)
        grad = g_s[q_span, :]
        queries = [jnp.where(masks[head], query, jnp.zeros_like(query)) for head in range(2)]
        grads = [jnp.where(masks[head], grad, jnp.zeros_like(grad)) for head in range(2)]
        product = (grad.astype(F32) * att_ref[q_span, :]).T
        dots = [jnp.sum(product[head * HD : (head + 1) * HD], axis=0, keepdims=True) for head in range(2)]
        totals = [lse_ref[head : head + 1, q_span] for head in range(2)]

        def step(kt, state, masked, queries=queries, grads=grads, dots=dots, totals=totals):
            start = pl.multiple_of(kt * tile, tile)
            rows = pl.ds(start, tile)
            keys = k_s[rows, :]
            values = v_s[rows, :]
            dk = dk_s[rows, :]
            dv = dv_s[rows, :]
            new = []
            for head in range(2):
                scores = nt(keys, queries[head])
                if masked:
                    scores = jnp.where(allowed, scores, NEG_BIG)
                soft = jnp.exp(scores - totals[head])
                dsoft = nt(values, grads[head])
                dscore = (soft * (dsoft - dots[head])).astype(BF16)
                dv = dv + nn(soft.astype(BF16), grads[head])
                dk = dk + nn(dscore, queries[head])
                new.append(state[head] + nn(kt_s[head * HD : (head + 1) * HD, rows], dscore))
            dk_s[rows, :] = dk
            dv_s[rows, :] = dv
            return tuple(new)

        state = (jnp.zeros((HD, tile), F32), jnp.zeros((HD, tile), F32))
        state = step(qt, state, True)
        if qt > 0:
            state = lax.fori_loop(0, qt, lambda kt, s, step=step: step(kt, s, False), state)
        dq = jnp.concatenate(state, axis=0) * scale
        dq_s[q_span, :] = dq.T.astype(BF16)

    unsort_blocks(order_ref, [dq_s, dk_s, dv_s], out_ref, blocks, half)


def backward_kernel(
    tile, order_ref, qkv_ref, grad_ref, att_ref, lse_ref, out_ref, q_s, k_s, v_s, g_s, kt_s, dq_s, dk_s, dv_s, qh_s, gh_s, dot_s, p_s, ds_s
):
    blocks, half = grad_ref.shape[0], grad_ref.shape[1]
    length = blocks * half
    tiles = length // tile
    sort_blocks(order_ref, qkv_ref, [q_s, k_s, v_s], blocks, half)
    sort_blocks(order_ref, grad_ref, [g_s], blocks, half)
    scale = HD ** (-0.5)
    rows_iota = lax.broadcasted_iota(jnp.int32, (tile, tile), 0)
    cols_iota = lax.broadcasted_iota(jnp.int32, (tile, tile), 1)
    allowed = rows_iota <= cols_iota
    masks = [lane_mask(tile, head) for head in range(2)]
    for t in range(tiles):
        span = slice(t * tile, (t + 1) * tile)
        kt_s[:, span] = k_s[span, :].T
        query = q_s[span, :] * jnp.asarray(scale, BF16)
        grad = g_s[span, :]
        product = (grad.astype(F32) * att_ref[span, :]).T
        for head in range(2):
            qh_s[head, span, :] = jnp.where(masks[head], query, jnp.zeros_like(query))
            gh_s[head, span, :] = jnp.where(masks[head], grad, jnp.zeros_like(grad))
            dot_s[head : head + 1, span] = jnp.sum(product[head * HD : (head + 1) * HD], axis=0, keepdims=True)

    for kt in range(tiles):
        k_span = slice(kt * tile, (kt + 1) * tile)
        rest = slice(kt * tile, length)
        keys, values = k_s[k_span, :], v_s[k_span, :]
        dk, dv = None, None
        for head in range(2):
            for qt in range(kt, tiles):
                span = slice(qt * tile, (qt + 1) * tile)
                scores = nt(keys, qh_s[head, span, :])
                if kt == qt:
                    scores = jnp.where(allowed, scores, NEG_BIG)
                soft = jnp.exp(scores - lse_ref[head : head + 1, span])
                p_s[head, :, span] = soft.astype(BF16)
                dsoft = nt(values, gh_s[head, span, :])
                ds_s[head, k_span, span] = (soft * (dsoft - dot_s[head : head + 1, span])).astype(BF16)
            dv_one = nn(p_s[head, :, rest], gh_s[head, rest, :])
            dk_one = nn(ds_s[head, k_span, rest], qh_s[head, rest, :])
            dv = dv_one if dv is None else dv + dv_one
            dk = dk_one if dk is None else dk + dk_one
        dk_s[k_span, :] = dk.astype(BF16)
        dv_s[k_span, :] = dv.astype(BF16)
    for qt in range(tiles):
        span = slice(qt * tile, (qt + 1) * tile)
        upto = slice(0, (qt + 1) * tile)
        dq = [nn(kt_s[head * HD : (head + 1) * HD, upto], ds_s[head, upto, span]) for head in range(2)]
        dq_s[span, :] = (jnp.concatenate(dq, axis=0) * scale).T.astype(BF16)
    unsort_blocks(order_ref, [dq_s, dk_s, dv_s], out_ref, blocks, half)


def attend_backward(order, qkv, grad, att, lse, tile):
    blocks, half, lanes = qkv.shape
    length = blocks * half
    rows, short = pltpu.VMEM((length, LANES), BF16), length <= SHORT
    flipped = pltpu.VMEM((LANES, length), BF16)
    return pl.pallas_call(
        functools.partial(backward_kernel if short else long_backward_kernel, tile),
        out_shape=jax.ShapeDtypeStruct((blocks, half, 3 * LANES), BF16),
        in_specs=[SMEM, VMEM, VMEM, VMEM, VMEM],
        out_specs=VMEM,
        scratch_shapes=[rows, rows, rows, rows, flipped, rows, rows, rows]
        + [pltpu.VMEM((2, length, LANES), BF16)] * 2
        + [pltpu.VMEM((2, length), F32), pltpu.VMEM((2, tile, length), BF16), pltpu.VMEM((2, length, length), BF16)]
        if short
        else [rows, rows, rows, rows, flipped, rows] + [pltpu.VMEM((length, LANES), F32)] * 2,
        compiler_params=params(),
        cost_estimate=SMALL,
        name="attend_backward",
    )(order, qkv, grad, att, lse)


def assemble_kernel(pieces, part_ref, out_ref):
    for start, source, first, size in pieces:
        out_ref[:, start : start + size] = part_ref[source, :, first : first + size].astype(F32)


def assemble(parts, pieces, width, block):
    n_ctx, rows, columns = parts.shape
    return pl.pallas_call(
        functools.partial(assemble_kernel, pieces),
        grid=(rows // block,),
        out_shape=jax.ShapeDtypeStruct((rows, width), F32),
        in_specs=[pl.BlockSpec((n_ctx, block, columns), lambda i: (0, i, 0))],
        out_specs=pl.BlockSpec((block, width), lambda i: (i, 0)),
        compiler_params=params(),
        name="assemble",
    )(parts)


def tn(left, right):
    return nn(left.T, right)


def rows_block(rows, most):
    return math.gcd(rows, most)


def whole_block(shape):
    return pl.BlockSpec(shape, lambda i: (0,) * len(shape), pipeline_mode=pl.Buffered(1))


def row_spec(block, width):
    return pl.BlockSpec((block, width), lambda i: (i, 0))


def product_kernel(left_ref, right_ref, shift_ref, out_ref):
    out_ref[...] = (nn(left_ref[...], right_ref[...]) + shift_ref[...]).astype(BF16)


def product(left, right, shift=None):
    rows, depth = left.shape
    width = right.shape[1]
    block = rows_block(rows, 512)
    if shift is None:
        shift = jnp.zeros((width,), F32)
    return pl.pallas_call(
        product_kernel,
        grid=(rows // block,),
        out_shape=jax.ShapeDtypeStruct((rows, width), BF16),
        in_specs=[row_spec(block, depth), whole_block((depth, width)), whole_block((1, width))],
        out_specs=row_spec(block, width),
        compiler_params=params(),
        cost_estimate=SMALL,
        name="product",
    )(left, right, shift[None, :])


def back_kernel(left_ref, grad_ref, weight_ref, grad_left_ref, grad_weight_ref, sum_ref, total):
    step = pl.program_id(0)
    grad = grad_ref[...]
    grad_left_ref[...] = nt(grad, weight_ref[...]).astype(BF16)
    term = tn(grad, left_ref[...])
    sums = jnp.sum(grad.astype(F32), axis=0, keepdims=True)

    @pl.when(step == 0)
    def _():
        total[...] = term
        sum_ref[...] = sums

    @pl.when(step > 0)
    def _():
        total[...] += term
        sum_ref[...] += sums

    @pl.when(step == pl.num_programs(0) - 1)
    def _():
        grad_weight_ref[...] = total[...].T.astype(BF16)


def product_back(left, grad, weight):
    rows, depth = left.shape
    width = grad.shape[1]
    block = rows_block(rows, 512)
    return pl.pallas_call(
        back_kernel,
        grid=(rows // block,),
        out_shape=(
            jax.ShapeDtypeStruct((rows, depth), BF16),
            jax.ShapeDtypeStruct((depth, width), BF16),
            jax.ShapeDtypeStruct((1, width), F32),
        ),
        in_specs=[row_spec(block, depth), row_spec(block, width), whole_block((depth, width))],
        out_specs=(
            row_spec(block, depth),
            pl.BlockSpec((depth, width), lambda i: (0, 0)),
            pl.BlockSpec((1, width), lambda i: (0, 0)),
        ),
        scratch_shapes=[pltpu.VMEM((width, depth), F32)],
        compiler_params=params(),
        cost_estimate=SMALL,
        name="product_back",
    )(left, grad, weight)


def out_back_kernel(att_ref, grad_ref, weight_ref, grad_att_ref, grad_weight_ref, total):
    step = pl.program_id(0)
    grad = grad_ref[...]
    grad_att_ref[...] = nt(grad, weight_ref[...]).astype(BF16)
    term = tn(att_ref[...], grad)

    @pl.when(step == 0)
    def _():
        total[...] = term

    @pl.when(step > 0)
    def _():
        total[...] += term

    @pl.when(step == pl.num_programs(0) - 1)
    def _():
        grad_weight_ref[...] = total[...].astype(BF16)


def out_back(att, grad, weight):
    rows, depth = att.shape
    width = grad.shape[1]
    block = rows_block(rows, 512)
    return pl.pallas_call(
        out_back_kernel,
        grid=(rows // block,),
        out_shape=(jax.ShapeDtypeStruct((rows, depth), BF16), jax.ShapeDtypeStruct((depth, width), BF16)),
        in_specs=[row_spec(block, depth), row_spec(block, width), whole_block((depth, width))],
        out_specs=(row_spec(block, depth), pl.BlockSpec((depth, width), lambda i: (0, 0))),
        scratch_shapes=[pltpu.VMEM((depth, width), F32)],
        compiler_params=params(),
        cost_estimate=SMALL,
        name="out_back",
    )(att, grad, weight)


GELU_A = math.sqrt(2.0 / math.pi)
GELU_B = 0.044715


def up_kernel(h_ref, og_ref, weight_ref, shift_ref, act_ref, slope_ref, grad_ref, total):
    step = pl.program_id(0)
    up = nn(h_ref[...], weight_ref[...]) + shift_ref[...]
    square = up * up
    soft = jnp.tanh(GELU_A * up * (1.0 + GELU_B * square))
    half = 0.5 * (1.0 + soft)
    act = (up * half).astype(BF16)
    act_ref[...] = act
    slope_ref[...] = half + 0.5 * up * (1.0 - soft * soft) * (GELU_A * (1.0 + 3.0 * GELU_B * square))
    term = tn(act, og_ref[...])

    @pl.when(step == 0)
    def _():
        total[...] = term

    @pl.when(step > 0)
    def _():
        total[...] += term

    @pl.when(step == pl.num_programs(0) - 1)
    def _():
        grad_ref[...] = total[...].astype(BF16)


def feed_up(values, out_grad, weight, shift):
    rows, width = values.shape
    hidden = weight.shape[1]
    block = rows_block(rows, 512)
    return pl.pallas_call(
        up_kernel,
        grid=(rows // block,),
        out_shape=(
            jax.ShapeDtypeStruct((rows, hidden), BF16),
            jax.ShapeDtypeStruct((rows, hidden), F32),
            jax.ShapeDtypeStruct((hidden, width), BF16),
        ),
        in_specs=[
            row_spec(block, width),
            row_spec(block, width),
            whole_block((width, hidden)),
            whole_block((1, hidden)),
        ],
        out_specs=(
            row_spec(block, hidden),
            row_spec(block, hidden),
            pl.BlockSpec((hidden, width), lambda i: (0, 0)),
        ),
        scratch_shapes=[pltpu.VMEM((hidden, width), F32)],
        compiler_params=params(),
        cost_estimate=SMALL,
        name="feed_up",
    )(values, out_grad, weight, shift[None, :])


def down_kernel(
    h_ref, og_ref, act_ref, slope_ref, up_w_ref, down_w_ref, out_ref, d_h_ref, grad_ref, sum_ref, total
):
    step = pl.program_id(0)
    d_up = (nt(og_ref[...], down_w_ref[...]) * slope_ref[...]).astype(BF16)
    d_h_ref[...] = nt(d_up, up_w_ref[...]).astype(BF16)
    sums = jnp.sum(d_up.astype(F32), axis=0, keepdims=True)
    term = tn(d_up, h_ref[...])
    out_ref[...] = nn(act_ref[...], down_w_ref[...]).astype(BF16)

    @pl.when(step == 0)
    def _():
        total[...] = term
        sum_ref[...] = sums

    @pl.when(step > 0)
    def _():
        total[...] += term
        sum_ref[...] += sums

    @pl.when(step == pl.num_programs(0) - 1)
    def _():
        grad_ref[...] = total[...].T.astype(BF16)


def feed_down(values, out_grad, act, slope, up_weight, down_weight):
    rows, width = values.shape
    hidden = up_weight.shape[1]
    block = rows_block(rows, 512)
    return pl.pallas_call(
        down_kernel,
        grid=(rows // block,),
        out_shape=(
            jax.ShapeDtypeStruct((rows, width), BF16),
            jax.ShapeDtypeStruct((rows, width), BF16),
            jax.ShapeDtypeStruct((width, hidden), BF16),
            jax.ShapeDtypeStruct((1, hidden), F32),
        ),
        in_specs=[
            row_spec(block, width),
            row_spec(block, width),
            row_spec(block, hidden),
            row_spec(block, hidden),
            whole_block((width, hidden)),
            whole_block((hidden, width)),
        ],
        out_specs=(
            row_spec(block, width),
            row_spec(block, width),
            pl.BlockSpec((width, hidden), lambda i: (0, 0)),
            pl.BlockSpec((1, hidden), lambda i: (0, 0)),
        ),
        scratch_shapes=[pltpu.VMEM((hidden, width), F32)],
        compiler_params=params(),
        cost_estimate=SMALL,
        name="feed_down",
    )(values, out_grad, act, slope, up_weight, down_weight)


def local(
    tokens,
    block_pairs,
    out_grad,
    ln1_gain,
    ln1_bias,
    qkv_weight,
    query_bias,
    value_bias,
    out_weight,
    out_bias,
    ln2_gain,
    ln2_bias,
    up_weight,
    up_bias,
    down_weight,
    down_bias,
):
    n_ctx, planes = lax.axis_size("ctx"), lax.axis_size("fsdp")
    c, f = lax.axis_index("ctx"), lax.axis_index("fsdp")
    local_rows, seqs, width = tokens.shape
    half = local_rows // 2
    devices = n_ctx * planes
    blocks = 2 * devices
    length = devices * local_rows
    heads = width // HD
    slots = planes * (-(-heads // devices))
    assert slots == planes and planes % seqs == 0
    span = slots * HD
    rows = local_rows * seqs
    plane_rows = n_ctx * rows
    quarter = width // planes
    ff = up_weight.shape[1]
    ff_quarter = ff // planes
    ff_piece = ff_quarter // n_ctx
    ff_span = ff_piece * planes
    tile = 256

    device_ids = jnp.arange(devices, dtype=jnp.int32)
    device_of_block = jnp.sum(
        jnp.where(block_pairs[None, :] == device_ids[:, None], device_ids[None, :], 0), axis=1
    )
    place_of_block = lax.rem(device_of_block, planes) * n_ctx + device_of_block // planes
    order = jnp.concatenate([place_of_block * 2, place_of_block[::-1] * 2 + 1]).astype(jnp.int32)

    first = [-(-quarter * j // HD) for j in range(planes)] + [heads]
    counts = [first[j + 1] - first[j] for j in range(planes)]
    assert max(counts) <= n_ctx
    slot_head = [jnp.minimum(first[j] + c, heads - 1) for j in range(planes)]
    first_own = jnp.asarray(first, jnp.int32)[f]
    count_own = jnp.asarray(counts, jnp.int32)[f]

    pairs = planes // seqs
    pair, pair_span = lax.rem(f, pairs), 2 * HD
    qkv_own = jnp.stack(
        [
            jnp.concatenate(
                [
                    lax.dynamic_slice(qkv_weight, (0, k * width + slot_head[j] * HD), (quarter, HD))
                    for k in range(3)
                    for j in (2 * p, 2 * p + 1)
                ],
                axis=1,
            )
            for p in range(pairs)
        ]
    )
    next_rows = lax.ppermute(out_weight[:HD], "fsdp", [(j + 1, j) for j in range(planes - 1)])
    out_own = lax.dynamic_slice(
        jnp.concatenate([out_weight, next_rows]), ((first_own + c) * HD - f * quarter, 0), (HD, width)
    )
    out_own = jnp.where(c < count_own, out_own, jnp.zeros_like(out_own))
    down_own = lax.dynamic_slice(down_weight, (c * ff_piece, 0), (ff_piece, width))


    tok = jnp.swapaxes(tokens, 0, 1).reshape(rows, width)
    og = jnp.swapaxes(out_grad, 0, 1).reshape(rows, width)

    short = -quarter % LANES
    vector_list = [ln1_gain, ln1_bias, ln2_gain, ln2_bias, query_bias, value_bias, out_bias, down_bias]
    vector_list += [up_bias[k * quarter : (k + 1) * quarter] for k in range(ff // width)]
    packed = jnp.concatenate([jnp.pad(v, (0, short)) for v in vector_list])
    packed = jnp.pad(packed, (0, -packed.size % (16 * LANES))).reshape(-1, LANES)
    vectors, og_all, h1, qkv_slice = first_norm_gather(tok, og, packed, qkv_own, n_ctx, planes, seqs)
    h1 = h1.reshape(length, width)
    qkv_slice = qkv_slice.reshape(width, 3 * pair_span)
    h1, up_weight, down_own = lax.optimization_barrier((h1, up_weight, down_own))
    down_slice = lax.all_gather(down_own, "fsdp", axis=0, tiled=True)
    up_own = jnp.concatenate(
        [
            lax.dynamic_slice(up_weight, (0, k * ff_quarter + c * ff_piece), (quarter, ff_piece))
            for k in range(planes)
        ],
        axis=1,
    )
    up_slice = lax.all_gather(up_own, "fsdp", axis=0, tiled=True)
    og_all = og_all.reshape(plane_rows, width)
    vectors = vectors.reshape(planes, -1)[:, : len(vector_list) * (quarter + short)]
    vectors = vectors.reshape(planes, len(vector_list), quarter + short)[:, :, :quarter].astype(F32)
    gain1, bias1, gain2, bias2, bias_q, bias_v, bias_o, bias_d = [
        vectors[:, k].reshape(width) for k in range(8)
    ]
    bias_up = lax.dynamic_slice(
        vectors[:, 8 : 8 + ff // width].reshape(planes, ff_quarter), (0, c * ff_piece), (planes, ff_piece)
    ).reshape(ff_span)

    pair_heads = [jnp.minimum(jnp.asarray(first, jnp.int32)[2 * pair + i] + c, heads - 1) for i in range(2)]

    def head_part(vector):
        return [lax.dynamic_slice(vector, (head * HD,), (HD,)) for head in pair_heads]

    qkv_shift = jnp.concatenate(head_part(bias_q) + [jnp.zeros((pair_span,), F32)] + head_part(bias_v))

    qkv = product(h1, qkv_slice, qkv_shift).reshape(blocks, half, 3 * pair_span)
    att_heads, att_exact, lse = attend_forward(order, qkv, tile)
    att, out_slice = to_tokens(att_heads.reshape(planes, n_ctx, local_rows, LANES), seqs, 6, out_own)
    out_slice = out_slice.reshape(span, width)
    att = att.reshape(plane_rows, span)
    branch = product(att, out_slice).reshape(n_ctx, rows, width)
    mixed, h2 = second_norm_gather(branch, tok, jnp.stack([gain2, bias2, bias_o]))
    h2 = h2.reshape(plane_rows, width)
    def reduce_own(part):
        return lax.psum_scatter(part, "fsdp", scatter_dimension=0, tiled=True)

    act, slope, down_part = feed_up(h2, og_all, up_slice, bias_up)
    down_own_grad = reduce_own(down_part)
    out_part, d_h2, up_part, d_up_sum = feed_down(h2, og_all, act, slope, up_slice, down_slice)
    up_own_grad = reduce_own(up_part)
    out_part, d_h2 = [part.reshape(n_ctx, rows, width) for part in (out_part, d_h2)]
    d_mixed, sums2, d_branch = second_norm_back(d_h2, mixed, og, gain2[None, :])
    d_branch = d_branch.reshape(plane_rows, width)
    d_att, out_w_part = out_back(att, d_branch, out_slice)
    d_att_heads, block_out, down_parts = to_heads(
        d_att.reshape(n_ctx, seqs, local_rows, span), planes, 7, out_part, mixed, bias_d[None, :], down_own_grad
    )
    d_att_heads, out_w_part = lax.optimization_barrier((d_att_heads, out_w_part))
    out_own_grad = reduce_own(out_w_part)
    up_parts = lax.all_gather(up_own_grad, "ctx", axis=0)
    d_qkv = attend_backward(order, qkv, d_att_heads.reshape(blocks, half, LANES), att_exact, lse, tile)
    d_qkv = d_qkv.reshape(length, 3 * pair_span)
    d_h1, qkv_part, d_qkv_sum = product_back(h1, d_qkv, qkv_slice)
    qkv_part = qkv_part.reshape(planes, quarter, 3 * pair_span)
    d_h1 = d_h1.reshape(planes, n_ctx, local_rows, width)
    d_qkv_sum = d_qkv_sum[0]

    d_up_sum = d_up_sum.reshape(planes, ff_piece)
    up_spread = lax.dynamic_update_slice(jnp.zeros((planes, ff_quarter), F32), d_up_sum, (0, c * ff_piece))

    def spread(values):
        full = jnp.zeros((width + HD,), F32)
        for i in range(2):
            slot = 2 * pair + i
            real = c < jnp.asarray(counts, jnp.int32)[slot]
            place = jnp.where(real, pair_heads[i] * HD, width)
            full = lax.dynamic_update_slice(full, values[i * HD : (i + 1) * HD], (place,))
        return full[None, :width]

    wide = jnp.concatenate([sums2, spread(d_qkv_sum[:pair_span]), spread(d_qkv_sum[2 * pair_span :])])
    wide = wide.reshape(6, planes, quarter).transpose(1, 0, 2).reshape(planes, 6 * quarter)
    flat = jnp.concatenate([wide, up_spread], axis=1)
    size = flat.shape[1]
    flat = jnp.pad(flat, ((0, 0), (0, -size % (8 * LANES)))).reshape(planes, -1, LANES)

    grad_tok, qkv_parts, out_parts, sums1, totals = first_norm_back(
        d_h1, qkv_part, out_own_grad, flat, tok, d_mixed, gain1[None, :]
    )
    sums1 = sums1[:2, :quarter]
    totals = totals.reshape(-1)
    sums = totals[: 6 * quarter].reshape(6, quarter)
    up_bias_grad = totals[6 * quarter : size]

    down_grad = down_parts.reshape(ff_quarter, width).astype(F32)
    block = quarter // 5
    up_pieces = [
        (j * ff_quarter + d * ff_piece, d, j * ff_piece, ff_piece) for j in range(planes) for d in range(n_ctx)
    ]
    up_grad = assemble(up_parts, up_pieces, ff, block)
    qkv_pieces = [
        (k * width + (first[j] + d) * HD, d * pairs + j // 2, k * pair_span + j % 2 * HD, HD)
        for k in range(3)
        for j in range(planes)
        for d in range(counts[j])
    ]
    qkv_grad = assemble(qkv_parts.reshape(n_ctx * pairs, quarter, 3 * pair_span), qkv_pieces, 3 * width, block)
    out_rows = out_parts.reshape(n_ctx * HD, width)
    tail = (f + 1) * quarter - first_own * HD
    tail_rows = lax.dynamic_slice(out_rows, (tail, 0), (HD, width))
    tail_rows = lax.ppermute(tail_rows, "fsdp", [(j, j + 1) for j in range(planes - 1)])
    lead = first_own * HD - f * quarter
    shifted = lax.dynamic_slice(
        jnp.concatenate([jnp.zeros((HD, width), BF16), out_rows]), (HD - lead, 0), (quarter, width)
    )
    from_tail = jnp.concatenate([tail_rows, jnp.zeros((quarter - HD, width), BF16)])
    row_ids = lax.broadcasted_iota(jnp.int32, (quarter, width), 0)
    out_grad_own = jnp.where(row_ids < lead, from_tail, shifted).astype(F32)

    def back(values):
        return jnp.swapaxes(values.reshape(seqs, local_rows, width), 0, 1)

    return (
        back(block_out),
        back(grad_tok),
        sums1[0],
        sums1[1],
        qkv_grad,
        sums[4],
        sums[5],
        out_grad_own,
        sums[2],
        sums[0],
        sums[1],
        up_grad,
        up_bias_grad,
        down_grad,
        sums[3],
    )


def solution(mesh):
    both, row, vec, mat = P(("ctx", "fsdp"), None, None), P(), P("fsdp"), P("fsdp", None)
    in_specs = (both, row, both, vec, vec, mat, vec, vec, mat, vec, vec, vec, mat, vec, mat, vec)
    out_specs = (both, both, vec, vec, mat, vec, vec, mat, vec, vec, vec, mat, vec, mat, vec)
    return jax.shard_map(local, mesh=mesh, in_specs=in_specs, out_specs=out_specs, check_vma=False)
```

```python
import functools
import math

import jax
import jax.numpy as jnp
from jax import lax
from jax.experimental import pallas as pl
from jax.experimental.pallas import tpu as pltpu
from jax.sharding import PartitionSpec as P

HD = 64
LANES = 128
NORM_EPS = 1e-05
NEG_BIG = -1e30
MESH = pl.DeviceIdType.MESH
F32 = jnp.float32
BF16 = jnp.bfloat16
ANY = pl.BlockSpec(memory_space=pl.ANY)
VMEM = pl.BlockSpec(memory_space=pltpu.VMEM)
DMA = pltpu.SemaphoreType.DMA
VMEM_LIMIT = 56 * 1024 * 1024
SMALL = pl.CostEstimate(flops=1, bytes_accessed=1, transcendentals=0)


def params(cid=None):
    if cid is None:
        return pltpu.CompilerParams(vmem_limit_bytes=VMEM_LIMIT)
    return pltpu.CompilerParams(
        collective_id=cid, has_side_effects=True, vmem_limit_bytes=VMEM_LIMIT
    )


def plane_peers(chips):
    me = lax.axis_index("ctx")
    core = lax.rem(me, 2)
    chip = me // 2
    sibling = chip * 2 + 1 - core
    if chips == 4:
        across_x = chip + 1 - 2 * lax.rem(chip, 2)
        across_y = lax.rem(chip + 2, 4)
        corner = lax.rem(across_x + 2, 4)
        first = across_x * (1 - core) + across_y * core
        second = across_y * (1 - core) + across_x * core
        to = come = [first * 2 + core, second * 2 + core, corner * 2 + core]
    else:
        to = [lax.rem(chip + k, chips) * 2 + core for k in range(1, chips)]
        come = [lax.rem(chip + chips - k, chips) * 2 + core for k in range(1, chips)]
    return me, core, chip, sibling, to, come


def greet(plane=(), across=()):
    barrier = pltpu.get_barrier_semaphore()
    for peer in plane:
        pl.semaphore_signal(barrier, inc=1, device_id={"ctx": peer}, device_id_type=MESH)
    for peer in across:
        pl.semaphore_signal(barrier, inc=1, device_id={"fsdp": peer}, device_id_type=MESH)
    pl.semaphore_wait(barrier, len(plane) + len(across))


def other_planes(planes):
    me = lax.axis_index("fsdp")
    return me, [lax.rem(me + k, planes) for k in range(1, planes)]


def send(src, dst, send_sem, recv_sem, axis, peer):
    copy = pltpu.make_async_remote_copy(
        src_ref=src,
        dst_ref=dst,
        send_sem=send_sem,
        recv_sem=recv_sem,
        device_id={axis: peer},
        device_id_type=MESH,
    )
    copy.start()
    return copy


def plane_gather_start(owns, alls, sems, chips):
    far_send, far_recv, near_send, near_recv, local_sem = sems
    me, core, chip, sibling, to, come = plane_peers(chips)
    direct = 2 if chips == 4 else chips - 1
    last = chips - 1
    far, near, local = [], [], []
    for i, (own_ref, all_ref) in enumerate(zip(owns, alls)):
        far.append(
            [
                send(own_ref, all_ref.at[me], far_send.at[i, k], far_recv.at[i, k], "ctx", to[k])
                for k in range(direct)
            ]
        )
        near.append(send(own_ref, all_ref.at[me], near_send.at[i, last], near_recv.at[i, last], "ctx", sibling))
        copy = pltpu.make_async_copy(own_ref, all_ref.at[me], local_sem.at[i])
        copy.start()
        local.append(copy)
    return far, near, local


def plane_gather_pass(started, alls, sems, chips, turns):
    far_send, far_recv, near_send, near_recv, local_sem = sems
    me, core, chip, sibling, to, come = plane_peers(chips)
    far, near, local = started
    for i, all_ref in enumerate(alls):
        for k in turns:
            far[i][k].wait_recv()
            block = all_ref.at[come[k]]
            if chips == 4 and k == 0:
                far[i].append(send(block, block, far_send.at[i, 2], far_recv.at[i, 2], "ctx", to[1]))
            near.append(send(block, block, near_send.at[i, k], near_recv.at[i, k], "ctx", sibling))


def plane_gather_middle(started, alls, sems, chips):
    plane_gather_pass(started, alls, sems, chips, range(2 if chips == 4 else chips - 1))


def plane_gather_end(started, alls, sems, chips):
    plane_gather_pass(started, alls, sems, chips, range(2, chips - 1) if chips == 4 else ())
    far, near, local = started
    for group in far:
        for copy in group:
            copy.wait_send()
    for copy in near + local:
        copy.wait()


def plane_gather_finish(started, alls, sems, chips):
    plane_gather_middle(started, alls, sems, chips)
    plane_gather_end(started, alls, sems, chips)


def plane_gather(owns, alls, sems, chips):
    plane_gather_finish(plane_gather_start(owns, alls, sems, chips), alls, sems, chips)


def plane_scatter_stages(block_of, mine, paired, arrived, sems, chips, result):
    far_send, far_recv, near_send, near_recv, local_sem = sems
    me, core, chip, sibling, to, come = plane_peers(chips)
    targets = to + [me]
    order = [2, 1, 0, 3] if chips == 4 else list(range(chips))
    near, local = [None] * chips, [None] * chips
    crossed = [1, 0, 2, 3] if chips == 4 else list(range(chips))
    for k in order:
        other = targets[crossed[k]] + 1 - 2 * core
        near[k] = send(block_of(other), paired.at[k], near_send.at[k], near_recv.at[k], "ctx", sibling)
        local[k] = pltpu.make_async_copy(block_of(targets[k]), mine.at[k], local_sem.at[k])
        local[k].start()
    yield

    def both(k):
        local[k].wait()
        near[k].wait_recv()
        return mine[k].astype(F32) + paired[k].astype(F32)

    def dispatch(k, target):
        return send(mine.at[k], arrived.at[k], far_send.at[k], far_recv.at[k], "ctx", target)

    far = [None] * (chips - 1)
    if chips == 4:
        mine[2] = both(2).astype(BF16)
        far[2] = dispatch(2, to[0])
        mine[0] = both(0).astype(BF16)
        far[0] = dispatch(0, to[0])
        partial = both(1)
        yield
        far[2].wait_recv()
        mine[1] = (partial + arrived[2].astype(F32)).astype(BF16)
        far[1] = dispatch(1, to[1])
        total = both(3)
        arriving = [0, 1]
    else:
        for k in range(chips - 1):
            mine[k] = both(k).astype(BF16)
            far[k] = dispatch(k, to[k])
        total = both(chips - 1)
        arriving = range(chips - 1)
    yield
    for k in arriving:
        far[k].wait_recv()
        total = total + arrived[k].astype(F32)
    for copy in far + near:
        copy.wait_send()
    result.append(total)


def plane_scatter(block_of, mine, paired, arrived, sems, chips):
    result = []
    for unused in plane_scatter_stages(block_of, mine, paired, arrived, sems, chips, result):
        pass
    return result[0]


def gather_sems(chips, count=1):
    return [DMA((count, chips - 1))] * 2 + [DMA((count, chips))] * 2 + [DMA((count,))]


def scatter_orders(chips):
    if chips == 4:
        return [2, 0, 1, 3], [1, 0, 2, 3]
    return list(range(chips)), list(range(chips))


def plane_scatter_made(make, part, paired, arrived, sems, chips, meanwhile):
    far_send, far_recv, near_send, near_recv = sems
    me, core, chip, sibling, to, come = plane_peers(chips)
    targets = to + [me]
    order, crossed = scatter_orders(chips)
    near, far = [None] * chips, [None] * (chips - 1)

    def produce(k):
        make(k, targets[k] // 2)
        place = crossed[k]
        near[place] = send(
            part.at[k, 1 - core], paired.at[place], near_send.at[place], near_recv.at[place], "ctx", sibling
        )

    def both(k):
        near[k].wait_recv()
        return part[k, core].astype(F32) + paired[k].astype(F32)

    def dispatch(k, values, target):
        paired[k] = values.astype(BF16)
        far[k] = send(paired.at[k], arrived.at[k], far_send.at[k], far_recv.at[k], "ctx", target)

    if chips == 4:
        produce(2)
        produce(0)
        dispatch(2, both(2), to[0])
        produce(1)
        dispatch(0, both(0), to[0])
        produce(3)
        partial = both(1)
        far[2].wait_recv()
        dispatch(1, partial + arrived[2].astype(F32), to[1])
        arriving = [0, 1]
    else:
        for k in order:
            produce(k)
        for k in range(chips - 1):
            dispatch(k, both(k), to[k])
        arriving = range(chips - 1)
    meanwhile()
    total = both(chips - 1)
    for k in arriving:
        far[k].wait_recv()
        total = total + arrived[k].astype(F32)
    for copy in far + near:
        copy.wait_send()
    return total


def made_scratch(chips, *block):
    return [
        pltpu.VMEM((chips, 2) + block, BF16),
        pltpu.VMEM((chips,) + block, BF16),
        pltpu.VMEM((chips - 1,) + block, BF16),
        DMA((chips - 1,)),
        DMA((chips - 1,)),
        DMA((chips,)),
        DMA((chips,)),
    ]


def scatter_scratch(chips, *block):
    return [
        pltpu.VMEM((chips,) + block, BF16),
        pltpu.VMEM((chips,) + block, BF16),
        pltpu.VMEM((chips - 1,) + block, BF16),
        DMA((chips - 1,)),
        DMA((chips - 1,)),
        DMA((chips,)),
        DMA((chips,)),
        DMA((chips,)),
    ]


def normalize(values):
    average = jnp.mean(values, axis=-1, keepdims=True)
    centered = values - average
    variance = jnp.mean(centered * centered, axis=-1, keepdims=True)
    inverse = lax.rsqrt(variance + NORM_EPS)
    return centered * inverse, inverse


def norm_backward(grad, gain, unit, inverse):
    scaled = grad * gain
    first = jnp.mean(scaled, axis=-1, keepdims=True)
    second = jnp.mean(scaled * unit, axis=-1, keepdims=True)
    return (scaled - first - unit * second) * inverse


def first_kernel(
    chips,
    planes,
    seqs,
    quarter,
    tok_ref,
    og_ref,
    vec_ref,
    weight_ref,
    vecs_ref,
    ogs_ref,
    h1_ref,
    weights_ref,
    own,
    column,
    v_send,
    v_recv,
    v_local,
    h_send,
    h_recv,
    w_send,
    w_recv,
    w_local,
    *sems,
):
    me, core, chip, sibling, to, come = plane_peers(chips)
    plane, others = other_planes(planes)
    pairs = planes // seqs
    rows = own.shape[0] // seqs
    greet(to + [sibling], others)
    og_sems, h1_sems = sems[:5], [sems[5 + 5 * k : 10 + 5 * k] for k in range(planes)]
    copies = [
        send(vec_ref, vecs_ref.at[plane], v_send.at[k], v_recv.at[k], "fsdp", peer) for k, peer in enumerate(others)
    ]
    local = pltpu.make_async_copy(vec_ref, vecs_ref.at[plane], v_local)
    local.start()
    og_started = plane_gather_start([og_ref], [ogs_ref], og_sems, chips)
    unit, inverse = normalize(tok_ref[...].astype(F32))
    for copy in copies + [local]:
        copy.wait()
    lines = quarter // LANES + 1

    def vector(k):
        pieces = []
        for j in range(planes):
            for line in range(lines):
                size = min(LANES, quarter - line * LANES)
                if size:
                    row = k * lines + line
                    pieces.append(vecs_ref[j, row : row + 1, :size].astype(F32))
        return jnp.concatenate(pieces, axis=1)

    own[...] = (unit * vector(0) + vector(1)).astype(BF16)

    def half_of(peer):
        return own.at[pl.ds(pl.multiple_of(peer // pairs * rows, rows), rows)]

    halves = [
        send(half_of(peer), column.at[k], h_send.at[k], h_recv.at[k], "fsdp", peer) for k, peer in enumerate(others)
    ]
    weights = [
        send(weight_ref.at[lax.rem(peer, pairs)], weights_ref.at[plane], w_send.at[k], w_recv.at[k], "fsdp", peer)
        for k, peer in enumerate(others)
    ]
    weights.append(pltpu.make_async_copy(weight_ref.at[lax.rem(plane, pairs)], weights_ref.at[plane], w_local))
    weights[-1].start()
    sources = [plane] + [lax.rem(plane + planes - k, planes) for k in range(1, planes)]
    blocks = [half_of(plane)] + [column.at[k] for k in range(planes - 1)]
    started = [plane_gather_start([blocks[0]], [h1_ref.at[sources[0]]], h1_sems[0], chips)]
    plane_gather_finish(og_started, [ogs_ref], og_sems, chips)
    for k in range(1, planes):
        halves[k - 1].wait_recv()
        started.append(plane_gather_start([blocks[k]], [h1_ref.at[sources[k]]], h1_sems[k], chips))
    for k in range(planes):
        plane_gather_finish(started[k], [h1_ref.at[sources[k]]], h1_sems[k], chips)
    for copy in halves:
        copy.wait_send()
    for copy in weights:
        copy.wait()


def first_norm_gather(tok, og, vec, weight, n_ctx, planes, seqs):
    rows, width = tok.shape
    chips, half = n_ctx // 2, rows // seqs
    return pl.pallas_call(
        functools.partial(first_kernel, chips, planes, seqs, width // planes),
        out_shape=(
            jax.ShapeDtypeStruct((planes,) + vec.shape, BF16),
            jax.ShapeDtypeStruct((n_ctx, rows, width), BF16),
            jax.ShapeDtypeStruct((planes, n_ctx, half, width), BF16),
            jax.ShapeDtypeStruct((planes,) + weight.shape[1:], BF16),
        ),
        in_specs=[VMEM, ANY, VMEM, ANY],
        out_specs=(VMEM, ANY, ANY, ANY),
        scratch_shapes=[
            pltpu.VMEM((rows, width), BF16),
            pltpu.VMEM((planes - 1, half, width), BF16),
            DMA((planes - 1,)),
            DMA((planes - 1,)),
            DMA,
            DMA((planes - 1,)),
            DMA((planes - 1,)),
            DMA((planes - 1,)),
            DMA((planes - 1,)),
            DMA,
        ]
        + gather_sems(chips)
        + gather_sems(chips) * planes,
        compiler_params=params(0),
        cost_estimate=SMALL,
        name="norm_gather",
    )(tok, og, vec, weight)


def second_kernel(chips, part_ref, tok_ref, vec_ref, mixed_ref, all_ref, own, *scratch):
    me, core, chip, sibling, to, come = plane_peers(chips)
    greet(to + [sibling])
    total = plane_scatter(lambda c: part_ref.at[c], *scratch[:3], scratch[3:8], chips)
    mixed = tok_ref[...].astype(F32) + total + vec_ref[2:3, :]
    mixed_ref[...] = mixed
    unit, inverse = normalize(mixed)
    own[...] = (unit * vec_ref[0:1, :] + vec_ref[1:2, :]).astype(BF16)
    plane_gather([own], [all_ref], scratch[8:], chips)


def second_norm_gather(part, tok, vecs):
    n_ctx, rows, width = part.shape
    chips = n_ctx // 2
    return pl.pallas_call(
        functools.partial(second_kernel, chips),
        out_shape=(
            jax.ShapeDtypeStruct((rows, width), F32),
            jax.ShapeDtypeStruct((n_ctx, rows, width), BF16),
        ),
        in_specs=[ANY, VMEM, VMEM],
        out_specs=(VMEM, ANY),
        scratch_shapes=[pltpu.VMEM((rows, width), BF16)]
        + scatter_scratch(chips, rows, width)
        + gather_sems(chips),
        compiler_params=params(1),
        cost_estimate=SMALL,
        name="scatter_norm_gather",
    )(part, tok, vecs)


def third_kernel(
    chips,
    h_hbm,
    og_hbm,
    act_hbm,
    slope_hbm,
    up_w_hbm,
    down_w_hbm,
    mixed_ref,
    og_ref,
    vec_ref,
    dmixed_ref,
    sums_ref,
    all_ref,
    out_hbm,
    up_grad_ref,
    up_sum_ref,
    h_ref,
    ogs_ref,
    act_ref,
    slope_ref,
    up_w_ref,
    down_w_ref,
    d_up_ref,
    out_ref,
    load_sem,
    out_sem,
    own,
    *scratch,
):
    me, core, chip, sibling, to, come = plane_peers(chips)
    made, gather = scratch[:7], scratch[7:]
    loads = [
        pltpu.make_async_copy(source, target, load_sem.at[k])
        for k, (source, target) in enumerate(
            [
                (down_w_hbm, down_w_ref),
                (og_hbm, ogs_ref),
                (slope_hbm, slope_ref),
                (up_w_hbm, up_w_ref),
                (h_hbm, h_ref),
                (act_hbm, act_ref),
            ]
        )
    ]
    for load in loads:
        load.start()
    greet(to + [sibling])
    unit, inverse = normalize(mixed_ref[...])
    rows = mixed_ref.shape[0]
    for load in loads[:4]:
        load.wait()
    part = made[0]

    def make(k, target):
        span = pl.ds(pl.multiple_of(target * 2 * rows, 2 * rows), 2 * rows)
        d_up = (nt(ogs_ref[span, :], down_w_ref[...]) * slope_ref[span, :]).astype(BF16)
        d_up_ref[span, :] = d_up
        d_h = nt(d_up, up_w_ref[...]).astype(BF16)
        part[k, 0] = d_h[:rows]
        part[k, 1] = d_h[rows:]

    def meanwhile():
        for load in loads[4:]:
            load.wait()
        d_up = d_up_ref[...]
        up_sum_ref[...] = jnp.sum(d_up.astype(F32), axis=0, keepdims=True)
        up_grad_ref[...] = tn(d_up, h_ref[...]).T.astype(BF16)
        out_ref[...] = nn(act_ref[...], down_w_ref[...]).astype(BF16)
        pltpu.make_async_copy(out_ref, out_hbm, out_sem).start()

    grad = plane_scatter_made(make, *made[:3], made[3:], chips, meanwhile)
    out_grad = og_ref[...].astype(F32)
    dmixed = out_grad + norm_backward(grad, vec_ref[0:1, :], unit, inverse)
    low = dmixed.astype(BF16)
    own[...] = low
    started = plane_gather_start([own], [all_ref], gather, chips)
    dmixed_ref[...] = dmixed
    sums_ref[0:1, :] = jnp.sum(grad * unit, axis=0, keepdims=True)
    sums_ref[1:2, :] = jnp.sum(grad, axis=0, keepdims=True)
    sums_ref[2:3, :] = jnp.sum(low.astype(F32), axis=0, keepdims=True)
    sums_ref[3:4, :] = jnp.sum(out_grad, axis=0, keepdims=True)
    plane_gather_finish(started, [all_ref], gather, chips)
    pltpu.make_async_copy(out_ref, out_hbm, out_sem).wait()


def feed_back(values, out_grads, act, slope, up_weight, down_weight, mixed, og, vecs):
    rows, width = mixed.shape
    total_rows, hidden = act.shape
    n_ctx = total_rows // rows
    chips = n_ctx // 2
    return pl.pallas_call(
        functools.partial(third_kernel, chips),
        out_shape=(
            jax.ShapeDtypeStruct((rows, width), F32),
            jax.ShapeDtypeStruct((4, width), F32),
            jax.ShapeDtypeStruct((n_ctx, rows, width), BF16),
            jax.ShapeDtypeStruct((total_rows, width), BF16),
            jax.ShapeDtypeStruct((width, hidden), BF16),
            jax.ShapeDtypeStruct((1, hidden), F32),
        ),
        in_specs=[ANY] * 6 + [VMEM] * 3,
        out_specs=(VMEM, VMEM, ANY, ANY, VMEM, VMEM),
        scratch_shapes=[
            pltpu.VMEM((total_rows, width), BF16),
            pltpu.VMEM((total_rows, width), BF16),
            pltpu.VMEM((total_rows, hidden), BF16),
            pltpu.VMEM((total_rows, hidden), F32),
            pltpu.VMEM((width, hidden), BF16),
            pltpu.VMEM((hidden, width), BF16),
            pltpu.VMEM((total_rows, hidden), BF16),
            pltpu.VMEM((total_rows, width), BF16),
            DMA((6,)),
            DMA,
            pltpu.VMEM((rows, width), BF16),
        ]
        + made_scratch(chips, rows, width)
        + gather_sems(chips),
        compiler_params=params(2),
        cost_estimate=SMALL,
        name="feed_back",
    )(values, out_grads, act, slope, up_weight, down_weight, mixed, og, vecs)


def fourth_kernel(
    chips,
    planes,
    seqs,
    part_ref,
    qkv_ref,
    outw_ref,
    flat_ref,
    tok_ref,
    dmixed_ref,
    vec_ref,
    grad_ref,
    qkv_all,
    outw_all,
    sums_ref,
    flat_out,
    q_arrived,
    q_own,
    q_send,
    q_recv,
    q_local,
    rows_own,
    rows_arrived,
    r_send,
    r_recv,
    small,
    small_own,
    small_z,
    small_c,
    flat_own,
    flat_z,
    flat_c,
    z_send,
    z_recv,
    c_send,
    c_recv,
    *scratch,
):
    n_ctx = 2 * chips
    pairs = planes // seqs
    me, core, chip, sibling, to, come = plane_peers(chips)
    plane, others = other_planes(planes)
    around = [lax.rem(me + k, n_ctx) for k in range(1, n_ctx)]
    greet(around, others)
    scatter, rest_sems, qkv_sems = scratch[:8], scratch[8:13], scratch[13:]

    pushed = [
        send(qkv_ref.at[peer], q_arrived.at[plane], q_send.at[k], q_recv.at[k], "fsdp", peer)
        for k, peer in enumerate(others)
    ]
    held = pltpu.make_async_copy(qkv_ref.at[plane], q_arrived.at[plane], q_local)
    held.start()
    flat_sent = [
        send(flat_ref.at[peer], flat_z.at[k], z_send.at[0, k], z_recv.at[0, k], "fsdp", peer)
        for k, peer in enumerate(others)
    ]
    unit, inverse = normalize(tok_ref[...].astype(F32))
    total = plane_scatter(lambda c: part_ref.at[:, c], *scatter[:3], scatter[3:], chips)
    rows_own[...] = total.astype(BF16)
    rows_sent = [
        send(rows_own.at[peer], rows_arrived.at[plane], r_send.at[k], r_recv.at[k], "fsdp", peer)
        for k, peer in enumerate(others)
    ]
    rows_arrived[plane] = rows_own[plane]
    rest_started = plane_gather_start([outw_ref], [outw_all], rest_sems, chips)
    for copy in pushed + [held]:
        copy.wait()
    for pair in range(pairs):
        terms = [q_arrived[seq * pairs + pair].astype(F32) for seq in range(seqs)]
        q_own[pair] = sum(terms[1:], terms[0]).astype(BF16)
    qkv_started = plane_gather_start([q_own], [qkv_all], qkv_sems, chips)
    plane_gather_finish(rest_started, [outw_all], rest_sems, chips)

    for copy in rows_sent:
        copy.wait()
    halves = []
    for seq in range(seqs):
        terms = [rows_arrived[seq * pairs + pair].astype(F32) for pair in range(pairs)]
        halves.append(sum(terms[1:], terms[0]))
    grad = jnp.concatenate(halves, axis=0)
    sums = jnp.concatenate(
        [jnp.sum(grad * unit, axis=0, keepdims=True), jnp.sum(grad, axis=0, keepdims=True)], axis=0
    )
    quarter = sums.shape[1] // planes
    small[...] = jnp.zeros_like(small)
    for j in range(planes):
        small[j, 0:2, 0:quarter] = sums[:, j * quarter : (j + 1) * quarter]
    small_sent = [
        send(small.at[peer], small_z.at[k], z_send.at[1, k], z_recv.at[1, k], "fsdp", peer)
        for k, peer in enumerate(others)
    ]
    grad_ref[...] = dmixed_ref[...] + norm_backward(grad, vec_ref[0:1, :], unit, inverse)
    small_total = small[plane]
    flat_total = flat_ref[plane]
    for k in range(planes - 1):
        flat_sent[k].wait()
        small_sent[k].wait()
        small_total = small_total + small_z[k]
        flat_total = flat_total + flat_z[k]
    small_own[...] = small_total
    flat_own[...] = flat_total
    sent = []
    for k, peer in enumerate(around):
        sent.append(send(small_own, small_c.at[k], c_send.at[0, k], c_recv.at[0, k], "ctx", peer))
        sent.append(send(flat_own, flat_c.at[k], c_send.at[1, k], c_recv.at[1, k], "ctx", peer))
    plane_gather_finish(qkv_started, [qkv_all], qkv_sems, chips)
    for copy in sent:
        copy.wait()
    for k in range(n_ctx - 1):
        small_total = small_total + small_c[k]
        flat_total = flat_total + flat_c[k]
    sums_ref[...] = small_total
    flat_out[...] = flat_total


def first_norm_back(part, qkv_part, outw_own, flat, tok, dmixed, vecs):
    planes, n_ctx, half, width = part.shape
    rows = tok.shape[0]
    seqs = rows // half
    quarter, columns = qkv_part.shape[1:]
    chips, pairs = n_ctx // 2, planes // seqs
    size = (8, quarter + -quarter % LANES)
    return pl.pallas_call(
        functools.partial(fourth_kernel, chips, planes, seqs),
        out_shape=(
            jax.ShapeDtypeStruct((rows, width), F32),
            jax.ShapeDtypeStruct((n_ctx, pairs, quarter, columns), BF16),
            jax.ShapeDtypeStruct((n_ctx,) + outw_own.shape, BF16),
            jax.ShapeDtypeStruct(size, F32),
            jax.ShapeDtypeStruct(flat.shape[1:], F32),
        ),
        in_specs=[ANY, ANY, ANY, VMEM, VMEM, VMEM, VMEM],
        out_specs=(VMEM, ANY, ANY, VMEM, VMEM),
        scratch_shapes=[
            pltpu.VMEM((planes, quarter, columns), BF16),
            pltpu.VMEM((pairs, quarter, columns), BF16),
            DMA((planes - 1,)),
            DMA((planes - 1,)),
            DMA,
            pltpu.VMEM((planes, half, width), BF16),
            pltpu.VMEM((planes, half, width), BF16),
            DMA((planes - 1,)),
            DMA((planes - 1,)),
            pltpu.VMEM((planes,) + size, F32),
            pltpu.VMEM(size, F32),
            pltpu.VMEM((planes - 1,) + size, F32),
            pltpu.VMEM((n_ctx - 1,) + size, F32),
            pltpu.VMEM(flat.shape[1:], F32),
            pltpu.VMEM((planes - 1,) + flat.shape[1:], F32),
            pltpu.VMEM((n_ctx - 1,) + flat.shape[1:], F32),
            DMA((2, planes - 1)),
            DMA((2, planes - 1)),
            DMA((2, n_ctx - 1)),
            DMA((2, n_ctx - 1)),
        ]
        + scatter_scratch(chips, planes, half, width)
        + gather_sems(chips)
        + gather_sems(chips),
        compiler_params=params(3),
        cost_estimate=SMALL,
        name="scatter_back",
    )(part, qkv_part, outw_own, flat, tok, dmixed, vecs)


def finish_kernel(
    chips,
    planes,
    seqs,
    h1_hbm,
    d_hbm,
    w_hbm,
    out_part_ref,
    outw_ref,
    flat_ref,
    tok_ref,
    dmixed_ref,
    mixed_ref,
    vec_ref,
    grad_ref,
    out_ref,
    qkv_all,
    outw_all,
    sums_ref,
    flat_out,
    h1_ref,
    d_ref,
    w_ref,
    load_sem,
    dw_ref,
    q_arrived,
    q_own,
    q_send,
    q_recv,
    outw_arrived,
    outw_own,
    o_send,
    o_recv,
    rows_own,
    rows_arrived,
    r_send,
    r_recv,
    small,
    small_own,
    small_z,
    small_c,
    flat_own,
    flat_z,
    flat_c,
    z_send,
    z_recv,
    c_send,
    c_recv,
    *scratch,
):
    n_ctx = 2 * chips
    pairs = planes // seqs
    me, core, chip, sibling, to, come = plane_peers(chips)
    plane, others = other_planes(planes)
    around = [lax.rem(me + k, n_ctx) for k in range(1, n_ctx)]
    made, out_scatter, outw_sems, qkv_sems = scratch[:7], scratch[7:15], scratch[15:20], scratch[20:]
    loads = [
        pltpu.make_async_copy(source, target, load_sem.at[k])
        for k, (source, target) in enumerate([(d_hbm, d_ref), (h1_hbm, h1_ref), (w_hbm, w_ref)])
    ]
    for load in loads:
        load.start()
    greet(around, others)
    outw_sent = [
        send(outw_ref.at[peer], outw_arrived.at[k], o_send.at[k], o_recv.at[k], "fsdp", peer)
        for k, peer in enumerate(others)
    ]
    flat_sent = [
        send(flat_ref.at[peer], flat_z.at[k], z_send.at[0, k], z_recv.at[0, k], "fsdp", peer)
        for k, peer in enumerate(others)
    ]
    unit, inverse = normalize(tok_ref[...].astype(F32))

    for load in loads:
        load.wait()
    quarter = dw_ref.shape[1]
    dw = tn(d_ref[...], h1_ref[...]).T.astype(BF16)
    for j in range(planes):
        dw_ref[j] = dw[j * quarter : (j + 1) * quarter]
    pushed = [
        send(dw_ref.at[peer], q_arrived.at[plane], q_send.at[k], q_recv.at[k], "fsdp", peer)
        for k, peer in enumerate(others)
    ]
    q_arrived[plane] = dw_ref[plane]

    part = made[0]
    half = part.shape[3]

    def make(k, target):
        blocks = []
        for j in range(planes):
            start = pl.multiple_of(j * n_ctx * half + target * 2 * half, 2 * half)
            blocks.append(d_ref[pl.ds(start, 2 * half), :])
        d_h = nt(jnp.concatenate(blocks, axis=0), w_ref[...]).astype(BF16)
        for j in range(planes):
            for side in range(2):
                start = (2 * j + side) * half
                part[k, side, j] = d_h[start : start + half]

    total = plane_scatter_made(make, *made[:3], made[3:], chips, lambda: None)
    rows_own[...] = total.astype(BF16)
    rows_sent = [
        send(rows_own.at[peer], rows_arrived.at[plane], r_send.at[k], r_recv.at[k], "fsdp", peer)
        for k, peer in enumerate(others)
    ]
    rows_arrived[plane] = rows_own[plane]

    total = outw_ref[plane].astype(F32)
    for k, copy in enumerate(outw_sent):
        copy.wait()
        total = total + outw_arrived[k].astype(F32)
    outw_own[...] = total.astype(BF16)
    outw_started = plane_gather_start([outw_own], [outw_all], outw_sems, chips)
    out_total = []
    out_stages = plane_scatter_stages(
        lambda c: out_part_ref.at[c], *out_scatter[:3], out_scatter[3:], chips, out_total
    )
    next(out_stages)
    next(out_stages)
    for copy in pushed:
        copy.wait()
    for pair in range(pairs):
        terms = [q_arrived[seq * pairs + pair].astype(F32) for seq in range(seqs)]
        q_own[pair] = sum(terms[1:], terms[0]).astype(BF16)
    qkv_started = plane_gather_start([q_own], [qkv_all], qkv_sems, chips)
    plane_gather_middle(outw_started, [outw_all], outw_sems, chips)
    next(out_stages, None)
    plane_gather_middle(qkv_started, [qkv_all], qkv_sems, chips)

    for copy in rows_sent:
        copy.wait()
    halves = []
    for seq in range(seqs):
        terms = [rows_arrived[seq * pairs + pair].astype(F32) for pair in range(pairs)]
        halves.append(sum(terms[1:], terms[0]))
    grad = jnp.concatenate(halves, axis=0)
    sums = jnp.concatenate(
        [jnp.sum(grad * unit, axis=0, keepdims=True), jnp.sum(grad, axis=0, keepdims=True)], axis=0
    )
    small[...] = jnp.zeros_like(small)
    for j in range(planes):
        small[j, 0:2, 0:quarter] = sums[:, j * quarter : (j + 1) * quarter]
    small_sent = [
        send(small.at[peer], small_z.at[k], z_send.at[1, k], z_recv.at[1, k], "fsdp", peer)
        for k, peer in enumerate(others)
    ]
    grad_ref[...] = dmixed_ref[...] + norm_backward(grad, vec_ref[0:1, :], unit, inverse)
    small_total = small[plane]
    flat_total = flat_ref[plane]
    for k in range(planes - 1):
        flat_sent[k].wait()
        small_sent[k].wait()
        small_total = small_total + small_z[k]
        flat_total = flat_total + flat_z[k]
    small_own[...] = small_total
    flat_own[...] = flat_total
    sent = []
    for k, peer in enumerate(around):
        sent.append(send(small_own, small_c.at[k], c_send.at[0, k], c_recv.at[0, k], "ctx", peer))
        sent.append(send(flat_own, flat_c.at[k], c_send.at[1, k], c_recv.at[1, k], "ctx", peer))
    for unused in out_stages:
        pass
    out_ref[...] = (mixed_ref[...] + out_total[0] + vec_ref[1:2, :]).astype(BF16)
    plane_gather_end(outw_started, [outw_all], outw_sems, chips)
    plane_gather_end(qkv_started, [qkv_all], qkv_sems, chips)
    for copy in sent:
        copy.wait()
    for k in range(n_ctx - 1):
        small_total = small_total + small_c[k]
        flat_total = flat_total + flat_c[k]
    sums_ref[...] = small_total
    flat_out[...] = flat_total


def finish(h1, d_qkv, weight, out_part, outw_part, flat, tok, dmixed, mixed, vecs):
    n_ctx, rows, width = out_part.shape
    planes, half = outw_part.shape[0], h1.shape[0] // (outw_part.shape[0] * n_ctx)
    seqs = rows // half
    quarter, columns = width // planes, weight.shape[1]
    chips, pairs = n_ctx // 2, planes // seqs
    size = (8, quarter + -quarter % LANES)
    piece = outw_part.shape[1:]
    return pl.pallas_call(
        functools.partial(finish_kernel, chips, planes, seqs),
        out_shape=(
            jax.ShapeDtypeStruct((rows, width), F32),
            jax.ShapeDtypeStruct((rows, width), BF16),
            jax.ShapeDtypeStruct((n_ctx, pairs, quarter, columns), BF16),
            jax.ShapeDtypeStruct((n_ctx,) + piece, BF16),
            jax.ShapeDtypeStruct(size, F32),
            jax.ShapeDtypeStruct(flat.shape[1:], F32),
        ),
        in_specs=[ANY] * 4 + [VMEM] * 6,
        out_specs=(VMEM, VMEM, ANY, ANY, VMEM, VMEM),
        scratch_shapes=[
            pltpu.VMEM(h1.shape, BF16),
            pltpu.VMEM(d_qkv.shape, BF16),
            pltpu.VMEM(weight.shape, BF16),
            DMA((3,)),
            pltpu.VMEM((planes, quarter, columns), BF16),
            pltpu.VMEM((planes, quarter, columns), BF16),
            pltpu.VMEM((pairs, quarter, columns), BF16),
            DMA((planes - 1,)),
            DMA((planes - 1,)),
            pltpu.VMEM((planes - 1,) + piece, BF16),
            pltpu.VMEM(piece, BF16),
            DMA((planes - 1,)),
            DMA((planes - 1,)),
            pltpu.VMEM((planes, half, width), BF16),
            pltpu.VMEM((planes, half, width), BF16),
            DMA((planes - 1,)),
            DMA((planes - 1,)),
            pltpu.VMEM((planes,) + size, F32),
            pltpu.VMEM(size, F32),
            pltpu.VMEM((planes - 1,) + size, F32),
            pltpu.VMEM((n_ctx - 1,) + size, F32),
            pltpu.VMEM(flat.shape[1:], F32),
            pltpu.VMEM((planes - 1,) + flat.shape[1:], F32),
            pltpu.VMEM((n_ctx - 1,) + flat.shape[1:], F32),
            DMA((2, planes - 1)),
            DMA((2, planes - 1)),
            DMA((2, n_ctx - 1)),
            DMA((2, n_ctx - 1)),
        ]
        + made_scratch(chips, planes, half, width)
        + scatter_scratch(chips, rows, width)
        + gather_sems(chips)
        + gather_sems(chips),
        compiler_params=params(9),
        cost_estimate=SMALL,
        name="finish",
    )(h1, d_qkv, weight, out_part, outw_part, flat, tok, dmixed, mixed, vecs)


def to_heads_kernel(
    planes, seqs, chips, tok_ref, down_ref, head_ref, down_all, send_sems, recv_sems, local_sem, *sems
):
    ctx_me, core, chip, sibling, to, come = plane_peers(chips)
    me, others = other_planes(planes)
    pairs = planes // seqs
    greet(to + [sibling], others)

    def source(unit):
        start = pl.multiple_of(lax.rem(unit, pairs) * LANES, LANES)
        return tok_ref.at[:, unit // pairs, :, pl.ds(start, LANES)]

    copies = [
        send(source(unit), head_ref.at[me], send_sems.at[k], recv_sems.at[k], "fsdp", unit)
        for k, unit in enumerate(others)
    ]
    copies.append(pltpu.make_async_copy(source(me), head_ref.at[me], local_sem))
    copies[-1].start()
    plane_gather([down_ref], [down_all], sems, chips)
    for copy in copies:
        copy.wait()


def to_heads(tok, planes, cid, down_own):
    n_ctx, seqs, local_rows, width = tok.shape
    chips = n_ctx // 2
    return pl.pallas_call(
        functools.partial(to_heads_kernel, planes, seqs, chips),
        out_shape=(
            jax.ShapeDtypeStruct((planes, n_ctx, local_rows, LANES), BF16),
            jax.ShapeDtypeStruct((n_ctx,) + down_own.shape, BF16),
        ),
        in_specs=[ANY, ANY],
        out_specs=(ANY, ANY),
        scratch_shapes=[DMA((planes - 1,)), DMA((planes - 1,)), DMA] + gather_sems(chips),
        compiler_params=params(cid),
        cost_estimate=SMALL,
        name="to_heads",
    )(tok, down_own)


def to_tokens_kernel(
    planes, seqs, head_ref, weight_ref, tok_ref, weights_ref, send_sems, recv_sems, local_sem, w_send, w_recv, w_local
):
    me, others = other_planes(planes)
    pairs = planes // seqs
    greet((), others)
    start = pl.multiple_of(lax.rem(me, pairs) * LANES, LANES)
    target = tok_ref.at[:, me // pairs, :, pl.ds(start, LANES)]
    copies = [
        send(head_ref.at[peer], target, send_sems.at[k], recv_sems.at[k], "fsdp", peer) for k, peer in enumerate(others)
    ]
    copies += [
        send(weight_ref, weights_ref.at[me], w_send.at[k], w_recv.at[k], "fsdp", peer) for k, peer in enumerate(others)
    ]
    for copy in (
        pltpu.make_async_copy(head_ref.at[me], target, local_sem),
        pltpu.make_async_copy(weight_ref, weights_ref.at[me], w_local),
    ):
        copy.start()
        copies.append(copy)
    for copy in copies:
        copy.wait()


def to_tokens(heads, seqs, cid, weight):
    planes, n_ctx, rows, lanes = heads.shape
    width = (planes // seqs) * LANES
    return pl.pallas_call(
        functools.partial(to_tokens_kernel, planes, seqs),
        out_shape=(
            jax.ShapeDtypeStruct((n_ctx, seqs, rows, width), heads.dtype),
            jax.ShapeDtypeStruct((planes,) + weight.shape, BF16),
        ),
        in_specs=[ANY] * 2,
        out_specs=(ANY,) * 2,
        scratch_shapes=[DMA((planes - 1,)), DMA((planes - 1,)), DMA] * 2,
        compiler_params=params(cid),
        cost_estimate=SMALL,
        name="to_tokens",
    )(heads, weight)


def nt(left, right):
    return lax.dot_general(left, right, (((1,), (1,)), ((), ())), preferred_element_type=F32)


def nn(left, right):
    return lax.dot_general(left, right, (((1,), (0,)), ((), ())), preferred_element_type=F32)


def sort_blocks(order_ref, qkv_ref, targets, blocks, half):
    def body(block, carry):
        row = qkv_ref[order_ref[block]]
        start = pl.multiple_of(block * half, half)
        for k, target in enumerate(targets):
            target[pl.ds(start, half), :] = row[:, k * LANES : (k + 1) * LANES]
        return carry

    lax.fori_loop(0, blocks, body, 0)


def lane_mask(rows, head):
    lane = lax.broadcasted_iota(jnp.int32, (rows, LANES), 1)
    return (lane < HD) if head == 0 else (lane >= HD)


def unsort_blocks(order_ref, sorted_refs, target_ref, blocks, half):
    def body(block, carry):
        start = pl.multiple_of(block * half, half)
        place = order_ref[block]
        for k, source in enumerate(sorted_refs):
            target_ref[place, :, k * LANES : (k + 1) * LANES] = source[pl.ds(start, half), :].astype(BF16)
        return carry

    lax.fori_loop(0, blocks, body, 0)


def long_forward_kernel(tile, order_ref, qkv_ref, out_ref, att_ref, lse_ref, q_s, k_s, v_s, vt_s, o_s):
    blocks, half = out_ref.shape[0], out_ref.shape[1]
    length = blocks * half
    tiles = length // tile
    sort_blocks(order_ref, qkv_ref, [q_s, k_s, v_s], blocks, half)
    for t in range(tiles):
        span = slice(t * tile, (t + 1) * tile)
        vt_s[:, span] = v_s[span, :].T
    scale = HD ** (-0.5)
    rows_iota = lax.broadcasted_iota(jnp.int32, (tile, tile), 0)
    cols_iota = lax.broadcasted_iota(jnp.int32, (tile, tile), 1)
    allowed = rows_iota <= cols_iota
    masks = [lane_mask(tile, head) for head in range(2)]

    for qt in range(tiles):
        q_span = slice(qt * tile, (qt + 1) * tile)
        query = q_s[q_span, :] * jnp.asarray(scale, BF16)
        queries = [jnp.where(masks[head], query, jnp.zeros_like(query)) for head in range(2)]

        def step(kt, state, masked, queries=queries):
            start = pl.multiple_of(kt * tile, tile)
            keys = k_s[pl.ds(start, tile), :]
            new = []
            for head in range(2):
                top, total, acc = state[head]
                scores = nt(keys, queries[head])
                if masked:
                    scores = jnp.where(allowed, scores, NEG_BIG)
                new_top = jnp.maximum(top, jnp.max(scores, axis=0, keepdims=True))
                soft = jnp.exp(scores - new_top)
                factor = jnp.exp(top - new_top)
                total = total * factor + jnp.sum(soft, axis=0, keepdims=True)
                values = vt_s[head * HD : (head + 1) * HD, pl.ds(start, tile)]
                acc = acc * factor + nn(values, soft.astype(BF16))
                new.append((new_top, total, acc))
            return tuple(new)

        state = tuple(
            (jnp.full((1, tile), NEG_BIG, F32), jnp.zeros((1, tile), F32), jnp.zeros((HD, tile), F32))
            for head in range(2)
        )
        state = step(qt, state, True)
        if qt > 0:
            state = lax.fori_loop(0, qt, lambda kt, s, step=step: step(kt, s, False), state)
        parts = []
        for head in range(2):
            top, total, acc = state[head]
            parts.append(acc / total)
            lse_ref[head : head + 1, q_span] = top + jnp.log(total)
        att = jnp.concatenate(parts, axis=0).T
        att_ref[q_span, :] = att
        o_s[q_span, :] = att.astype(BF16)

    unsort_blocks(order_ref, [o_s], out_ref, blocks, half)


def forward_kernel(tile, order_ref, qkv_ref, out_ref, att_ref, lse_ref, q_s, k_s, v_s, o_s, s_s, p_s):
    blocks, half = out_ref.shape[0], out_ref.shape[1]
    length = blocks * half
    tiles = length // tile
    sort_blocks(order_ref, qkv_ref, [q_s, k_s, v_s], blocks, half)
    scale = HD ** (-0.5)
    rows_iota = lax.broadcasted_iota(jnp.int32, (tile, tile), 0)
    cols_iota = lax.broadcasted_iota(jnp.int32, (tile, tile), 1)
    allowed = cols_iota <= rows_iota
    masks = [lane_mask(tile, head) for head in range(2)]

    for qt in range(tiles):
        q_span = slice(qt * tile, (qt + 1) * tile)
        query = q_s[q_span, :] * jnp.asarray(scale, BF16)
        parts = []
        for head in range(2):
            one = jnp.where(masks[head], query, jnp.zeros_like(query))
            top = jnp.full((tile, LANES), NEG_BIG, F32)
            for kt in range(qt + 1):
                k_span = slice(kt * tile, (kt + 1) * tile)
                scores = nt(one, k_s[k_span, :])
                if kt == qt:
                    scores = jnp.where(allowed, scores, NEG_BIG)
                s_s[head, :, k_span] = scores
                for lane in range(0, tile, LANES):
                    top = jnp.maximum(top, scores[:, lane : lane + LANES])
            top = jnp.max(top, axis=1, keepdims=True)
            total = jnp.zeros((tile, LANES), F32)
            for kt in range(qt + 1):
                k_span = slice(kt * tile, (kt + 1) * tile)
                soft = jnp.exp(s_s[head, :, k_span] - top)
                for lane in range(0, tile, LANES):
                    total = total + soft[:, lane : lane + LANES]
                p_s[head, :, k_span] = soft.astype(BF16)
            total = jnp.sum(total, axis=1, keepdims=True)
            span = slice(0, (qt + 1) * tile)
            parts.append(nn(p_s[head, :, span], v_s[span, :]) / total)
            lse = jnp.broadcast_to(top + jnp.log(total), (tile, LANES))
            lse_ref[head : head + 1, q_span] = lse.T[0:1, :]
        att = jnp.where(masks[0], parts[0], parts[1])
        att_ref[q_span, :] = att
        o_s[q_span, :] = att.astype(BF16)
    unsort_blocks(order_ref, [o_s], out_ref, blocks, half)


SMEM = pl.BlockSpec(memory_space=pltpu.SMEM)
SHORT = 2048


def attend_forward(order, qkv, tile):
    blocks, half, lanes = qkv.shape
    length = blocks * half
    rows, short = pltpu.VMEM((length, LANES), BF16), length <= SHORT
    return pl.pallas_call(
        functools.partial(forward_kernel if short else long_forward_kernel, tile),
        out_shape=(
            jax.ShapeDtypeStruct((blocks, half, LANES), BF16),
            jax.ShapeDtypeStruct((length, LANES), F32),
            jax.ShapeDtypeStruct((2, length), F32),
        ),
        in_specs=[SMEM, VMEM],
        out_specs=(VMEM, VMEM, VMEM),
        scratch_shapes=[rows, rows, rows, rows, pltpu.VMEM((2, tile, length), F32), pltpu.VMEM((2, tile, length), BF16)]
        if short
        else [rows, rows, rows, pltpu.VMEM((LANES, length), BF16), rows],
        compiler_params=params(),
        cost_estimate=SMALL,
        name="attend_forward",
    )(order, qkv)


def long_backward_kernel(
    tile, order_ref, qkv_ref, grad_ref, att_ref, lse_ref, out_ref, sum_ref, q_s, k_s, v_s, g_s, kt_s, dq_s, dk_s, dv_s
):
    blocks, half = grad_ref.shape[0], grad_ref.shape[1]
    length = blocks * half
    tiles = length // tile
    sort_blocks(order_ref, qkv_ref, [q_s, k_s, v_s], blocks, half)
    sort_blocks(order_ref, grad_ref, [g_s], blocks, half)
    for t in range(tiles):
        span = slice(t * tile, (t + 1) * tile)
        kt_s[:, span] = k_s[span, :].T
    scale = HD ** (-0.5)
    rows_iota = lax.broadcasted_iota(jnp.int32, (tile, tile), 0)
    cols_iota = lax.broadcasted_iota(jnp.int32, (tile, tile), 1)
    allowed = rows_iota <= cols_iota
    masks = [lane_mask(tile, head) for head in range(2)]
    dk_s[...] = jnp.zeros_like(dk_s)
    dv_s[...] = jnp.zeros_like(dv_s)

    for qt in range(tiles):
        q_span = slice(qt * tile, (qt + 1) * tile)
        query = q_s[q_span, :] * jnp.asarray(scale, BF16)
        grad = g_s[q_span, :]
        queries = [jnp.where(masks[head], query, jnp.zeros_like(query)) for head in range(2)]
        grads = [jnp.where(masks[head], grad, jnp.zeros_like(grad)) for head in range(2)]
        product = (grad.astype(F32) * att_ref[q_span, :]).T
        dots = [jnp.sum(product[head * HD : (head + 1) * HD], axis=0, keepdims=True) for head in range(2)]
        totals = [lse_ref[head : head + 1, q_span] for head in range(2)]

        def step(kt, state, masked, queries=queries, grads=grads, dots=dots, totals=totals):
            start = pl.multiple_of(kt * tile, tile)
            rows = pl.ds(start, tile)
            keys = k_s[rows, :]
            values = v_s[rows, :]
            dk = dk_s[rows, :]
            dv = dv_s[rows, :]
            new = []
            for head in range(2):
                scores = nt(keys, queries[head])
                if masked:
                    scores = jnp.where(allowed, scores, NEG_BIG)
                soft = jnp.exp(scores - totals[head])
                dsoft = nt(values, grads[head])
                dscore = (soft * (dsoft - dots[head])).astype(BF16)
                dv = dv + nn(soft.astype(BF16), grads[head])
                dk = dk + nn(dscore, queries[head])
                new.append(state[head] + nn(kt_s[head * HD : (head + 1) * HD, rows], dscore))
            dk_s[rows, :] = dk
            dv_s[rows, :] = dv
            return tuple(new)

        state = (jnp.zeros((HD, tile), F32), jnp.zeros((HD, tile), F32))
        state = step(qt, state, True)
        if qt > 0:
            state = lax.fori_loop(0, qt, lambda kt, s, step=step: step(kt, s, False), state)
        dq = jnp.concatenate(state, axis=0) * scale
        dq_s[q_span, :] = dq.T.astype(BF16)

    unsort_blocks(order_ref, [dq_s, dk_s, dv_s], out_ref, blocks, half)
    for k, source in enumerate([dq_s, dk_s, dv_s]):
        values = source[...].astype(BF16).astype(F32)
        sum_ref[:, k * LANES : (k + 1) * LANES] = jnp.sum(values, axis=0, keepdims=True)


def backward_kernel(
    tile, order_ref, qkv_ref, grad_ref, att_ref, lse_ref, out_ref, sum_ref, q_s, k_s, v_s, g_s, kt_s, dq_s, dk_s, dv_s, qh_s, gh_s, dot_s, p_s, ds_s
):
    blocks, half = grad_ref.shape[0], grad_ref.shape[1]
    length = blocks * half
    tiles = length // tile
    sort_blocks(order_ref, qkv_ref, [q_s, k_s, v_s], blocks, half)
    sort_blocks(order_ref, grad_ref, [g_s], blocks, half)
    scale = HD ** (-0.5)
    rows_iota = lax.broadcasted_iota(jnp.int32, (tile, tile), 0)
    cols_iota = lax.broadcasted_iota(jnp.int32, (tile, tile), 1)
    allowed = rows_iota <= cols_iota
    masks = [lane_mask(tile, head) for head in range(2)]
    for t in range(tiles):
        span = slice(t * tile, (t + 1) * tile)
        kt_s[:, span] = k_s[span, :].T
        query = q_s[span, :] * jnp.asarray(scale, BF16)
        grad = g_s[span, :]
        product = (grad.astype(F32) * att_ref[span, :]).T
        for head in range(2):
            qh_s[head, span, :] = jnp.where(masks[head], query, jnp.zeros_like(query))
            gh_s[head, span, :] = jnp.where(masks[head], grad, jnp.zeros_like(grad))
            dot_s[head : head + 1, span] = jnp.sum(product[head * HD : (head + 1) * HD], axis=0, keepdims=True)

    for kt in range(tiles):
        k_span = slice(kt * tile, (kt + 1) * tile)
        rest = slice(kt * tile, length)
        keys, values = k_s[k_span, :], v_s[k_span, :]
        dk, dv = None, None
        for head in range(2):
            for qt in range(kt, tiles):
                span = slice(qt * tile, (qt + 1) * tile)
                scores = nt(keys, qh_s[head, span, :])
                if kt == qt:
                    scores = jnp.where(allowed, scores, NEG_BIG)
                soft = jnp.exp(scores - lse_ref[head : head + 1, span])
                p_s[head, :, span] = soft.astype(BF16)
                dsoft = nt(values, gh_s[head, span, :])
                ds_s[head, k_span, span] = (soft * (dsoft - dot_s[head : head + 1, span])).astype(BF16)
            dv_one = nn(p_s[head, :, rest], gh_s[head, rest, :])
            dk_one = nn(ds_s[head, k_span, rest], qh_s[head, rest, :])
            dv = dv_one if dv is None else dv + dv_one
            dk = dk_one if dk is None else dk + dk_one
        dk_s[k_span, :] = dk.astype(BF16)
        dv_s[k_span, :] = dv.astype(BF16)
    for qt in range(tiles):
        span = slice(qt * tile, (qt + 1) * tile)
        upto = slice(0, (qt + 1) * tile)
        dq = [nn(kt_s[head * HD : (head + 1) * HD, upto], ds_s[head, upto, span]) for head in range(2)]
        dq_s[span, :] = (jnp.concatenate(dq, axis=0) * scale).T.astype(BF16)
    unsort_blocks(order_ref, [dq_s, dk_s, dv_s], out_ref, blocks, half)
    for k, source in enumerate([dq_s, dk_s, dv_s]):
        values = source[...].astype(BF16).astype(F32)
        sum_ref[:, k * LANES : (k + 1) * LANES] = jnp.sum(values, axis=0, keepdims=True)


def attend_backward(order, qkv, grad, att, lse, tile):
    blocks, half, lanes = qkv.shape
    length = blocks * half
    rows, short = pltpu.VMEM((length, LANES), BF16), length <= SHORT
    flipped = pltpu.VMEM((LANES, length), BF16)
    return pl.pallas_call(
        functools.partial(backward_kernel if short else long_backward_kernel, tile),
        out_shape=(
            jax.ShapeDtypeStruct((blocks, half, 3 * LANES), BF16),
            jax.ShapeDtypeStruct((1, 3 * LANES), F32),
        ),
        in_specs=[SMEM, VMEM, VMEM, VMEM, VMEM],
        out_specs=(VMEM, VMEM),
        scratch_shapes=[rows, rows, rows, rows, flipped, rows, rows, rows]
        + [pltpu.VMEM((2, length, LANES), BF16)] * 2
        + [pltpu.VMEM((2, length), F32), pltpu.VMEM((2, tile, length), BF16), pltpu.VMEM((2, length, length), BF16)]
        if short
        else [rows, rows, rows, rows, flipped, rows] + [pltpu.VMEM((length, LANES), F32)] * 2,
        compiler_params=params(),
        cost_estimate=SMALL,
        name="attend_backward",
    )(order, qkv, grad, att, lse)


def assemble_kernel(pieces, part_ref, out_ref):
    for start, source, first, size in pieces:
        out_ref[:, start : start + size] = part_ref[source, :, first : first + size].astype(F32)


def assemble(parts, pieces, width, block):
    n_ctx, rows, columns = parts.shape
    return pl.pallas_call(
        functools.partial(assemble_kernel, pieces),
        grid=(rows // block,),
        out_shape=jax.ShapeDtypeStruct((rows, width), F32),
        in_specs=[pl.BlockSpec((n_ctx, block, columns), lambda i: (0, i, 0))],
        out_specs=pl.BlockSpec((block, width), lambda i: (i, 0)),
        compiler_params=params(),
        name="assemble",
    )(parts)


def tn(left, right):
    return nn(left.T, right)


def rows_block(rows, most):
    return math.gcd(rows, most)


def whole_block(shape):
    return pl.BlockSpec(shape, lambda i: (0,) * len(shape), pipeline_mode=pl.Buffered(1))


def row_spec(block, width):
    return pl.BlockSpec((block, width), lambda i: (i, 0))


def product_kernel(left_ref, right_ref, shift_ref, out_ref):
    out_ref[...] = (nn(left_ref[...], right_ref[...]) + shift_ref[...]).astype(BF16)


def product(left, right, shift=None):
    rows, depth = left.shape
    width = right.shape[1]
    block = rows_block(rows, 512)
    if shift is None:
        shift = jnp.zeros((width,), F32)
    return pl.pallas_call(
        product_kernel,
        grid=(rows // block,),
        out_shape=jax.ShapeDtypeStruct((rows, width), BF16),
        in_specs=[row_spec(block, depth), whole_block((depth, width)), whole_block((1, width))],
        out_specs=row_spec(block, width),
        compiler_params=params(),
        cost_estimate=SMALL,
        name="product",
    )(left, right, shift[None, :])


def back_kernel(left_ref, grad_ref, weight_ref, grad_left_ref, grad_weight_ref, sum_ref, total):
    step = pl.program_id(0)
    grad = grad_ref[...]
    grad_left_ref[...] = nt(grad, weight_ref[...]).astype(BF16)
    term = tn(grad, left_ref[...])
    sums = jnp.sum(grad.astype(F32), axis=0, keepdims=True)

    @pl.when(step == 0)
    def _():
        total[...] = term
        sum_ref[...] = sums

    @pl.when(step > 0)
    def _():
        total[...] += term
        sum_ref[...] += sums

    @pl.when(step == pl.num_programs(0) - 1)
    def _():
        grad_weight_ref[...] = total[...].T.astype(BF16)


def product_back(left, grad, weight):
    rows, depth = left.shape
    width = grad.shape[1]
    block = rows_block(rows, 512)
    return pl.pallas_call(
        back_kernel,
        grid=(rows // block,),
        out_shape=(
            jax.ShapeDtypeStruct((rows, depth), BF16),
            jax.ShapeDtypeStruct((depth, width), BF16),
            jax.ShapeDtypeStruct((1, width), F32),
        ),
        in_specs=[row_spec(block, depth), row_spec(block, width), whole_block((depth, width))],
        out_specs=(
            row_spec(block, depth),
            pl.BlockSpec((depth, width), lambda i: (0, 0)),
            pl.BlockSpec((1, width), lambda i: (0, 0)),
        ),
        scratch_shapes=[pltpu.VMEM((width, depth), F32)],
        compiler_params=params(),
        cost_estimate=SMALL,
        name="product_back",
    )(left, grad, weight)


def out_back_kernel(att_ref, grad_ref, weight_ref, grad_att_ref, grad_weight_ref, total):
    step = pl.program_id(0)
    grad = grad_ref[...]
    grad_att_ref[...] = nt(grad, weight_ref[...]).astype(BF16)
    term = tn(att_ref[...], grad)

    @pl.when(step == 0)
    def _():
        total[...] = term

    @pl.when(step > 0)
    def _():
        total[...] += term

    @pl.when(step == pl.num_programs(0) - 1)
    def _():
        grad_weight_ref[...] = total[...].astype(BF16)


def out_back(att, grad, weight):
    rows, depth = att.shape
    width = grad.shape[1]
    block = rows_block(rows, 512)
    return pl.pallas_call(
        out_back_kernel,
        grid=(rows // block,),
        out_shape=(jax.ShapeDtypeStruct((rows, depth), BF16), jax.ShapeDtypeStruct((depth, width), BF16)),
        in_specs=[row_spec(block, depth), row_spec(block, width), whole_block((depth, width))],
        out_specs=(row_spec(block, depth), pl.BlockSpec((depth, width), lambda i: (0, 0))),
        scratch_shapes=[pltpu.VMEM((depth, width), F32)],
        compiler_params=params(),
        cost_estimate=SMALL,
        name="out_back",
    )(att, grad, weight)


GELU_A = math.sqrt(2.0 / math.pi)
GELU_B = 0.044715


def up_kernel(h_ref, og_ref, weight_ref, shift_ref, act_ref, slope_ref, grad_ref, total):
    step = pl.program_id(0)
    up = nn(h_ref[...], weight_ref[...]) + shift_ref[...]
    square = up * up
    soft = jnp.tanh(GELU_A * up * (1.0 + GELU_B * square))
    half = 0.5 * (1.0 + soft)
    act = (up * half).astype(BF16)
    act_ref[...] = act
    slope_ref[...] = half + 0.5 * up * (1.0 - soft * soft) * (GELU_A * (1.0 + 3.0 * GELU_B * square))
    term = tn(act, og_ref[...])

    @pl.when(step == 0)
    def _():
        total[...] = term

    @pl.when(step > 0)
    def _():
        total[...] += term

    @pl.when(step == pl.num_programs(0) - 1)
    def _():
        grad_ref[...] = total[...].astype(BF16)


def feed_up(values, out_grad, weight, shift):
    rows, width = values.shape
    hidden = weight.shape[1]
    block = rows_block(rows, 512)
    return pl.pallas_call(
        up_kernel,
        grid=(rows // block,),
        out_shape=(
            jax.ShapeDtypeStruct((rows, hidden), BF16),
            jax.ShapeDtypeStruct((rows, hidden), F32),
            jax.ShapeDtypeStruct((hidden, width), BF16),
        ),
        in_specs=[
            row_spec(block, width),
            row_spec(block, width),
            whole_block((width, hidden)),
            whole_block((1, hidden)),
        ],
        out_specs=(
            row_spec(block, hidden),
            row_spec(block, hidden),
            pl.BlockSpec((hidden, width), lambda i: (0, 0)),
        ),
        scratch_shapes=[pltpu.VMEM((hidden, width), F32)],
        compiler_params=params(),
        cost_estimate=SMALL,
        name="feed_up",
    )(values, out_grad, weight, shift[None, :])


def local(
    tokens,
    block_pairs,
    out_grad,
    ln1_gain,
    ln1_bias,
    qkv_weight,
    query_bias,
    value_bias,
    out_weight,
    out_bias,
    ln2_gain,
    ln2_bias,
    up_weight,
    up_bias,
    down_weight,
    down_bias,
):
    n_ctx, planes = lax.axis_size("ctx"), lax.axis_size("fsdp")
    c, f = lax.axis_index("ctx"), lax.axis_index("fsdp")
    local_rows, seqs, width = tokens.shape
    half = local_rows // 2
    devices = n_ctx * planes
    blocks = 2 * devices
    length = devices * local_rows
    heads = width // HD
    slots = planes * (-(-heads // devices))
    assert slots == planes and planes % seqs == 0
    span = slots * HD
    rows = local_rows * seqs
    plane_rows = n_ctx * rows
    quarter = width // planes
    ff = up_weight.shape[1]
    ff_quarter = ff // planes
    ff_piece = ff_quarter // n_ctx
    ff_span = ff_piece * planes
    tile = 256

    device_ids = jnp.arange(devices, dtype=jnp.int32)
    device_of_block = jnp.sum(
        jnp.where(block_pairs[None, :] == device_ids[:, None], device_ids[None, :], 0), axis=1
    )
    place_of_block = lax.rem(device_of_block, planes) * n_ctx + device_of_block // planes
    order = jnp.concatenate([place_of_block * 2, place_of_block[::-1] * 2 + 1]).astype(jnp.int32)

    first = [-(-quarter * j // HD) for j in range(planes)] + [heads]
    counts = [first[j + 1] - first[j] for j in range(planes)]
    assert max(counts) <= n_ctx
    slot_head = [jnp.minimum(first[j] + c, heads - 1) for j in range(planes)]
    first_own = jnp.asarray(first, jnp.int32)[f]
    count_own = jnp.asarray(counts, jnp.int32)[f]

    pairs = planes // seqs
    pair, pair_span = lax.rem(f, pairs), 2 * HD
    qkv_own = jnp.stack(
        [
            jnp.concatenate(
                [
                    lax.dynamic_slice(qkv_weight, (0, k * width + slot_head[j] * HD), (quarter, HD))
                    for k in range(3)
                    for j in (2 * p, 2 * p + 1)
                ],
                axis=1,
            )
            for p in range(pairs)
        ]
    )
    next_rows = lax.ppermute(out_weight[:HD], "fsdp", [(j + 1, j) for j in range(planes - 1)])
    out_own = lax.dynamic_slice(
        jnp.concatenate([out_weight, next_rows]), ((first_own + c) * HD - f * quarter, 0), (HD, width)
    )
    out_own = jnp.where(c < count_own, out_own, jnp.zeros_like(out_own))
    down_own = lax.dynamic_slice(down_weight, (c * ff_piece, 0), (ff_piece, width))


    tok = jnp.swapaxes(tokens, 0, 1).reshape(rows, width)
    og = jnp.swapaxes(out_grad, 0, 1).reshape(rows, width)

    short = -quarter % LANES
    vector_list = [ln1_gain, ln1_bias, ln2_gain, ln2_bias, query_bias, value_bias, out_bias, down_bias]
    vector_list += [up_bias[k * quarter : (k + 1) * quarter] for k in range(ff // width)]
    packed = jnp.concatenate([jnp.pad(v, (0, short)) for v in vector_list])
    packed = jnp.pad(packed, (0, -packed.size % (16 * LANES))).reshape(-1, LANES)
    vectors, og_all, h1, qkv_slice = first_norm_gather(tok, og, packed, qkv_own, n_ctx, planes, seqs)
    h1 = h1.reshape(length, width)
    qkv_slice = qkv_slice.reshape(width, 3 * pair_span)
    h1, up_weight, down_own = lax.optimization_barrier((h1, up_weight, down_own))
    down_slice = lax.all_gather(down_own, "fsdp", axis=0, tiled=True)
    up_own = jnp.concatenate(
        [
            lax.dynamic_slice(up_weight, (0, k * ff_quarter + c * ff_piece), (quarter, ff_piece))
            for k in range(planes)
        ],
        axis=1,
    )
    up_slice = lax.all_gather(up_own, "fsdp", axis=0, tiled=True)
    og_all = og_all.reshape(plane_rows, width)
    vectors = vectors.reshape(planes, -1)[:, : len(vector_list) * (quarter + short)]
    vectors = vectors.reshape(planes, len(vector_list), quarter + short)[:, :, :quarter].astype(F32)
    gain1, bias1, gain2, bias2, bias_q, bias_v, bias_o, bias_d = [
        vectors[:, k].reshape(width) for k in range(8)
    ]
    bias_up = lax.dynamic_slice(
        vectors[:, 8 : 8 + ff // width].reshape(planes, ff_quarter), (0, c * ff_piece), (planes, ff_piece)
    ).reshape(ff_span)

    pair_heads = [jnp.minimum(jnp.asarray(first, jnp.int32)[2 * pair + i] + c, heads - 1) for i in range(2)]

    def head_part(vector):
        return [lax.dynamic_slice(vector, (head * HD,), (HD,)) for head in pair_heads]

    qkv_shift = jnp.concatenate(head_part(bias_q) + [jnp.zeros((pair_span,), F32)] + head_part(bias_v))

    qkv = product(h1, qkv_slice, qkv_shift).reshape(blocks, half, 3 * pair_span)
    att_heads, att_exact, lse = attend_forward(order, qkv, tile)
    att, out_slice = to_tokens(att_heads.reshape(planes, n_ctx, local_rows, LANES), seqs, 6, out_own)
    out_slice = out_slice.reshape(span, width)
    att = att.reshape(plane_rows, span)
    branch = product(att, out_slice).reshape(n_ctx, rows, width)
    mixed, h2 = second_norm_gather(branch, tok, jnp.stack([gain2, bias2, bias_o]))
    h2 = h2.reshape(plane_rows, width)
    def reduce_own(part):
        return lax.psum_scatter(part, "fsdp", scatter_dimension=0, tiled=True)

    act, slope, down_part = feed_up(h2, og_all, up_slice, bias_up)
    down_own_grad = reduce_own(down_part)
    d_mixed, sums2, d_branch, out_part, up_part, d_up_sum = feed_back(
        h2, og_all, act, slope, up_slice, down_slice, mixed, og, gain2[None, :]
    )
    up_own_grad = reduce_own(up_part)
    out_part = out_part.reshape(n_ctx, rows, width)
    d_branch = d_branch.reshape(plane_rows, width)
    d_att, out_w_part = out_back(att, d_branch, out_slice)
    d_att_heads, down_parts = to_heads(d_att.reshape(n_ctx, seqs, local_rows, span), planes, 7, down_own_grad)
    d_qkv, d_qkv_sum = attend_backward(
        order, qkv, d_att_heads.reshape(blocks, half, LANES), att_exact, lse, tile
    )
    d_qkv, d_qkv_sum = d_qkv.reshape(length, 3 * pair_span), d_qkv_sum[0]
    down_parts, unused = lax.optimization_barrier((down_parts, d_qkv))
    down_grad = down_parts.reshape(ff_quarter, width).astype(F32)

    d_up_sum = d_up_sum.reshape(planes, ff_piece)
    up_spread = lax.dynamic_update_slice(jnp.zeros((planes, ff_quarter), F32), d_up_sum, (0, c * ff_piece))

    def spread(values):
        full = jnp.zeros((width + HD,), F32)
        for i in range(2):
            slot = 2 * pair + i
            real = c < jnp.asarray(counts, jnp.int32)[slot]
            place = jnp.where(real, pair_heads[i] * HD, width)
            full = lax.dynamic_update_slice(full, values[i * HD : (i + 1) * HD], (place,))
        return full[None, :width]

    wide = jnp.concatenate([sums2, spread(d_qkv_sum[:pair_span]), spread(d_qkv_sum[2 * pair_span :])])
    wide = wide.reshape(6, planes, quarter).transpose(1, 0, 2).reshape(planes, 6 * quarter)
    flat = jnp.concatenate([wide, up_spread], axis=1)
    size = flat.shape[1]
    flat = jnp.pad(flat, ((0, 0), (0, -size % (8 * LANES)))).reshape(planes, -1, LANES)

    if length <= SHORT:
        grad_tok, block_out, qkv_parts, out_parts, sums1, totals = finish(
            h1,
            d_qkv,
            qkv_slice,
            out_part,
            out_w_part.reshape(planes, HD, width),
            flat,
            tok,
            d_mixed,
            mixed,
            jnp.stack([gain1, bias_d]),
        )
    else:
        d_h1, qkv_part, unused = product_back(h1, d_qkv, qkv_slice)
        grad_tok, qkv_parts, out_parts, sums1, totals = first_norm_back(
            d_h1.reshape(planes, n_ctx, local_rows, width),
            qkv_part.reshape(planes, quarter, 3 * pair_span),
            reduce_own(out_w_part),
            flat,
            tok,
            d_mixed,
            gain1[None, :],
        )
        total = lax.psum_scatter(out_part.reshape(plane_rows, width), "ctx", scatter_dimension=0, tiled=True)
        block_out = (mixed + total.astype(F32) + bias_d).astype(BF16)
    qkv_parts, up_own_grad = lax.optimization_barrier((qkv_parts, up_own_grad))
    up_parts = lax.all_gather(up_own_grad, "ctx", axis=0)
    sums1 = sums1[:2, :quarter]
    totals = totals.reshape(-1)
    sums = totals[: 6 * quarter].reshape(6, quarter)
    up_bias_grad = totals[6 * quarter : size]

    block = quarter // 5
    up_pieces = [
        (j * ff_quarter + d * ff_piece, d, j * ff_piece, ff_piece) for j in range(planes) for d in range(n_ctx)
    ]
    up_grad = assemble(up_parts, up_pieces, ff, block)
    qkv_pieces = [
        (k * width + (first[j] + d) * HD, d * pairs + j // 2, k * pair_span + j % 2 * HD, HD)
        for k in range(3)
        for j in range(planes)
        for d in range(counts[j])
    ]
    qkv_grad = assemble(qkv_parts.reshape(n_ctx * pairs, quarter, 3 * pair_span), qkv_pieces, 3 * width, block)
    out_rows = out_parts.reshape(n_ctx * HD, width)
    tail = (f + 1) * quarter - first_own * HD
    tail_rows = lax.dynamic_slice(out_rows, (tail, 0), (HD, width))
    tail_rows = lax.ppermute(tail_rows, "fsdp", [(j, j + 1) for j in range(planes - 1)])
    lead = first_own * HD - f * quarter
    shifted = lax.dynamic_slice(
        jnp.concatenate([jnp.zeros((HD, width), BF16), out_rows]), (HD - lead, 0), (quarter, width)
    )
    from_tail = jnp.concatenate([tail_rows, jnp.zeros((quarter - HD, width), BF16)])
    row_ids = lax.broadcasted_iota(jnp.int32, (quarter, width), 0)
    out_grad_own = jnp.where(row_ids < lead, from_tail, shifted).astype(F32)

    def back(values):
        return jnp.swapaxes(values.reshape(seqs, local_rows, width), 0, 1)

    return (
        back(block_out),
        back(grad_tok),
        sums1[0],
        sums1[1],
        qkv_grad,
        sums[4],
        sums[5],
        out_grad_own,
        sums[2],
        sums[0],
        sums[1],
        up_grad,
        up_bias_grad,
        down_grad,
        sums[3],
    )


def solution(mesh):
    both, row, vec, mat = P(("ctx", "fsdp"), None, None), P(), P("fsdp"), P("fsdp", None)
    in_specs = (both, row, both, vec, vec, mat, vec, vec, mat, vec, vec, vec, mat, vec, mat, vec)
    out_specs = (both, both, vec, vec, mat, vec, vec, mat, vec, vec, vec, mat, vec, mat, vec)
    return jax.shard_map(local, mesh=mesh, in_specs=in_specs, out_specs=out_specs, check_vma=False)
```

```python
import functools
import math

import jax
import jax.numpy as jnp
from jax import lax
from jax.experimental import pallas as pl
from jax.experimental.pallas import tpu as pltpu
from jax.sharding import PartitionSpec as P

HD = 64
LANES = 128
NORM_EPS = 1e-05
NEG_BIG = -1e30
MESH = pl.DeviceIdType.MESH
F32 = jnp.float32
BF16 = jnp.bfloat16
ANY = pl.BlockSpec(memory_space=pl.ANY)
VMEM = pl.BlockSpec(memory_space=pltpu.VMEM)
DMA = pltpu.SemaphoreType.DMA
VMEM_LIMIT = 56 * 1024 * 1024
SMALL = pl.CostEstimate(flops=1, bytes_accessed=1, transcendentals=0)


def params(cid=None):
    if cid is None:
        return pltpu.CompilerParams(vmem_limit_bytes=VMEM_LIMIT)
    return pltpu.CompilerParams(
        collective_id=cid, has_side_effects=True, vmem_limit_bytes=VMEM_LIMIT
    )


def plane_peers(chips):
    me = lax.axis_index("ctx")
    core = lax.rem(me, 2)
    chip = me // 2
    sibling = chip * 2 + 1 - core
    if chips == 4:
        across_x = chip + 1 - 2 * lax.rem(chip, 2)
        across_y = lax.rem(chip + 2, 4)
        corner = lax.rem(across_x + 2, 4)
        first = across_x * (1 - core) + across_y * core
        second = across_y * (1 - core) + across_x * core
        to = come = [first * 2 + core, second * 2 + core, corner * 2 + core]
    else:
        to = [lax.rem(chip + k, chips) * 2 + core for k in range(1, chips)]
        come = [lax.rem(chip + chips - k, chips) * 2 + core for k in range(1, chips)]
    return me, core, chip, sibling, to, come


def greet(plane=(), across=()):
    barrier = pltpu.get_barrier_semaphore()
    for peer in plane:
        pl.semaphore_signal(barrier, inc=1, device_id={"ctx": peer}, device_id_type=MESH)
    for peer in across:
        pl.semaphore_signal(barrier, inc=1, device_id={"fsdp": peer}, device_id_type=MESH)
    pl.semaphore_wait(barrier, len(plane) + len(across))


def other_planes(planes):
    me = lax.axis_index("fsdp")
    return me, [lax.rem(me + k, planes) for k in range(1, planes)]


def send(src, dst, send_sem, recv_sem, axis, peer):
    copy = pltpu.make_async_remote_copy(
        src_ref=src,
        dst_ref=dst,
        send_sem=send_sem,
        recv_sem=recv_sem,
        device_id={axis: peer},
        device_id_type=MESH,
    )
    copy.start()
    return copy


def plane_gather_start(owns, alls, sems, chips):
    far_send, far_recv, near_send, near_recv, local_sem = sems
    me, core, chip, sibling, to, come = plane_peers(chips)
    direct = 2 if chips == 4 else chips - 1
    last = chips - 1
    far, near, local = [], [], []
    for i, (own_ref, all_ref) in enumerate(zip(owns, alls)):
        far.append(
            [
                send(own_ref, all_ref.at[me], far_send.at[i, k], far_recv.at[i, k], "ctx", to[k])
                for k in range(direct)
            ]
        )
        near.append(send(own_ref, all_ref.at[me], near_send.at[i, last], near_recv.at[i, last], "ctx", sibling))
        copy = pltpu.make_async_copy(own_ref, all_ref.at[me], local_sem.at[i])
        copy.start()
        local.append(copy)
    return far, near, local


def plane_gather_pass(started, alls, sems, chips, turns):
    far_send, far_recv, near_send, near_recv, local_sem = sems
    me, core, chip, sibling, to, come = plane_peers(chips)
    far, near, local = started
    for i, all_ref in enumerate(alls):
        for k in turns:
            far[i][k].wait_recv()
            block = all_ref.at[come[k]]
            if chips == 4 and k == 0:
                far[i].append(send(block, block, far_send.at[i, 2], far_recv.at[i, 2], "ctx", to[1]))
            near.append(send(block, block, near_send.at[i, k], near_recv.at[i, k], "ctx", sibling))


def plane_gather_middle(started, alls, sems, chips):
    plane_gather_pass(started, alls, sems, chips, range(2 if chips == 4 else chips - 1))


def plane_gather_end(started, alls, sems, chips):
    plane_gather_pass(started, alls, sems, chips, range(2, chips - 1) if chips == 4 else ())
    far, near, local = started
    for group in far:
        for copy in group:
            copy.wait_send()
    for copy in near + local:
        copy.wait()


def plane_gather_finish(started, alls, sems, chips):
    plane_gather_middle(started, alls, sems, chips)
    plane_gather_end(started, alls, sems, chips)


def plane_gather(owns, alls, sems, chips):
    plane_gather_finish(plane_gather_start(owns, alls, sems, chips), alls, sems, chips)


def plane_scatter_stages(block_of, mine, paired, arrived, sems, chips, result):
    far_send, far_recv, near_send, near_recv, local_sem = sems
    me, core, chip, sibling, to, come = plane_peers(chips)
    targets = to + [me]
    order = [2, 1, 0, 3] if chips == 4 else list(range(chips))
    near, local = [None] * chips, [None] * chips
    crossed = [1, 0, 2, 3] if chips == 4 else list(range(chips))
    for k in order:
        other = targets[crossed[k]] + 1 - 2 * core
        near[k] = send(block_of(other), paired.at[k], near_send.at[k], near_recv.at[k], "ctx", sibling)
        local[k] = pltpu.make_async_copy(block_of(targets[k]), mine.at[k], local_sem.at[k])
        local[k].start()
    yield

    def both(k):
        local[k].wait()
        near[k].wait_recv()
        return mine[k].astype(F32) + paired[k].astype(F32)

    def dispatch(k, target):
        return send(mine.at[k], arrived.at[k], far_send.at[k], far_recv.at[k], "ctx", target)

    far = [None] * (chips - 1)
    if chips == 4:
        mine[2] = both(2).astype(BF16)
        far[2] = dispatch(2, to[0])
        mine[0] = both(0).astype(BF16)
        far[0] = dispatch(0, to[0])
        partial = both(1)
        yield
        far[2].wait_recv()
        mine[1] = (partial + arrived[2].astype(F32)).astype(BF16)
        far[1] = dispatch(1, to[1])
        total = both(3)
        arriving = [0, 1]
    else:
        for k in range(chips - 1):
            mine[k] = both(k).astype(BF16)
            far[k] = dispatch(k, to[k])
        total = both(chips - 1)
        arriving = range(chips - 1)
    yield
    for k in arriving:
        far[k].wait_recv()
        total = total + arrived[k].astype(F32)
    for copy in far + near:
        copy.wait_send()
    result.append(total)


def plane_scatter(block_of, mine, paired, arrived, sems, chips):
    result = []
    for unused in plane_scatter_stages(block_of, mine, paired, arrived, sems, chips, result):
        pass
    return result[0]


def gather_sems(chips, count=1):
    return [DMA((count, chips - 1))] * 2 + [DMA((count, chips))] * 2 + [DMA((count,))]


def scatter_orders(chips):
    if chips == 4:
        return [2, 0, 1, 3], [1, 0, 2, 3]
    return list(range(chips)), list(range(chips))


def plane_scatter_made(make, part, paired, arrived, sems, chips, meanwhile):
    far_send, far_recv, near_send, near_recv = sems
    me, core, chip, sibling, to, come = plane_peers(chips)
    targets = to + [me]
    order, crossed = scatter_orders(chips)
    near, far = [None] * chips, [None] * (chips - 1)

    def produce(k):
        make(k, targets[k] // 2)
        place = crossed[k]
        near[place] = send(
            part.at[k, 1 - core], paired.at[place], near_send.at[place], near_recv.at[place], "ctx", sibling
        )

    def both(k):
        near[k].wait_recv()
        return part[k, core].astype(F32) + paired[k].astype(F32)

    def dispatch(k, values, target):
        paired[k] = values.astype(BF16)
        far[k] = send(paired.at[k], arrived.at[k], far_send.at[k], far_recv.at[k], "ctx", target)

    if chips == 4:
        produce(2)
        produce(0)
        dispatch(2, both(2), to[0])
        produce(1)
        dispatch(0, both(0), to[0])
        produce(3)
        partial = both(1)
        far[2].wait_recv()
        dispatch(1, partial + arrived[2].astype(F32), to[1])
        arriving = [0, 1]
    else:
        for k in order:
            produce(k)
        for k in range(chips - 1):
            dispatch(k, both(k), to[k])
        arriving = range(chips - 1)
    meanwhile()
    total = both(chips - 1)
    for k in arriving:
        far[k].wait_recv()
        total = total + arrived[k].astype(F32)
    for copy in far + near:
        copy.wait_send()
    return total


def made_scratch(chips, *block):
    return [
        pltpu.VMEM((chips, 2) + block, BF16),
        pltpu.VMEM((chips,) + block, BF16),
        pltpu.VMEM((chips - 1,) + block, BF16),
        DMA((chips - 1,)),
        DMA((chips - 1,)),
        DMA((chips,)),
        DMA((chips,)),
    ]


def scatter_scratch(chips, *block):
    return [
        pltpu.VMEM((chips,) + block, BF16),
        pltpu.VMEM((chips,) + block, BF16),
        pltpu.VMEM((chips - 1,) + block, BF16),
        DMA((chips - 1,)),
        DMA((chips - 1,)),
        DMA((chips,)),
        DMA((chips,)),
        DMA((chips,)),
    ]


def normalize(values):
    average = jnp.mean(values, axis=-1, keepdims=True)
    centered = values - average
    variance = jnp.mean(centered * centered, axis=-1, keepdims=True)
    inverse = lax.rsqrt(variance + NORM_EPS)
    return centered * inverse, inverse


def norm_backward(grad, gain, unit, inverse):
    scaled = grad * gain
    first = jnp.mean(scaled, axis=-1, keepdims=True)
    second = jnp.mean(scaled * unit, axis=-1, keepdims=True)
    return (scaled - first - unit * second) * inverse


def first_kernel(
    chips,
    planes,
    seqs,
    quarter,
    tok_ref,
    og_ref,
    vec_ref,
    weight_ref,
    out_w_ref,
    vecs_ref,
    ogs_ref,
    h1_ref,
    weights_ref,
    next_ref,
    own,
    column,
    v_send,
    v_recv,
    v_local,
    h_send,
    h_recv,
    w_send,
    w_recv,
    w_local,
    n_send,
    n_recv,
    n_local,
    *sems,
):
    me, core, chip, sibling, to, come = plane_peers(chips)
    plane, others = other_planes(planes)
    pairs = planes // seqs
    rows = own.shape[0] // seqs
    greet(to + [sibling], others)
    og_sems, h1_sems = sems[:5], [sems[5 + 5 * k : 10 + 5 * k] for k in range(planes)]
    copies = [
        send(vec_ref, vecs_ref.at[plane], v_send.at[k], v_recv.at[k], "fsdp", peer) for k, peer in enumerate(others)
    ]
    local = pltpu.make_async_copy(vec_ref, vecs_ref.at[plane], v_local)
    local.start()
    lead = out_w_ref.at[pl.ds(0, HD)]
    last = plane == planes - 1

    def lead_copy():
        return pltpu.make_async_remote_copy(
            src_ref=lead,
            dst_ref=next_ref,
            send_sem=n_send,
            recv_sem=n_recv,
            device_id={"fsdp": lax.rem(plane + planes - 1, planes)},
            device_id_type=MESH,
        )

    @pl.when(plane > 0)
    def _():
        lead_copy().start()

    @pl.when(last)
    def _():
        pltpu.make_async_copy(lead, next_ref, n_local).start()

    og_started = plane_gather_start([og_ref], [ogs_ref], og_sems, chips)
    unit, inverse = normalize(tok_ref[...].astype(F32))
    for copy in copies + [local]:
        copy.wait()
    lines = quarter // LANES + 1

    def vector(k):
        pieces = []
        for j in range(planes):
            for line in range(lines):
                size = min(LANES, quarter - line * LANES)
                if size:
                    row = k * lines + line
                    pieces.append(vecs_ref[j, row : row + 1, :size].astype(F32))
        return jnp.concatenate(pieces, axis=1)

    own[...] = (unit * vector(0) + vector(1)).astype(BF16)

    def half_of(peer):
        return own.at[pl.ds(pl.multiple_of(peer // pairs * rows, rows), rows)]

    halves = [
        send(half_of(peer), column.at[k], h_send.at[k], h_recv.at[k], "fsdp", peer) for k, peer in enumerate(others)
    ]
    weights = [
        send(weight_ref.at[lax.rem(peer, pairs)], weights_ref.at[plane], w_send.at[k], w_recv.at[k], "fsdp", peer)
        for k, peer in enumerate(others)
    ]
    weights.append(pltpu.make_async_copy(weight_ref.at[lax.rem(plane, pairs)], weights_ref.at[plane], w_local))
    weights[-1].start()
    sources = [plane] + [lax.rem(plane + planes - k, planes) for k in range(1, planes)]
    blocks = [half_of(plane)] + [column.at[k] for k in range(planes - 1)]
    started = [plane_gather_start([blocks[0]], [h1_ref.at[sources[0]]], h1_sems[0], chips)]
    plane_gather_middle(og_started, [ogs_ref], og_sems, chips)
    for k in range(1, planes):
        halves[k - 1].wait_recv()
        started.append(plane_gather_start([blocks[k]], [h1_ref.at[sources[k]]], h1_sems[k], chips))
        plane_gather_middle(started[k - 1], [h1_ref.at[sources[k - 1]]], h1_sems[k - 1], chips)
    plane_gather_middle(started[-1], [h1_ref.at[sources[-1]]], h1_sems[-1], chips)
    plane_gather_end(og_started, [ogs_ref], og_sems, chips)
    for k in range(planes):
        plane_gather_end(started[k], [h1_ref.at[sources[k]]], h1_sems[k], chips)
    @pl.when(plane > 0)
    def _():
        lead_copy().wait_send()

    @pl.when(last)
    def _():
        pltpu.make_async_copy(lead, next_ref, n_local).wait()

    @pl.when(plane < planes - 1)
    def _():
        lead_copy().wait_recv()

    for copy in halves:
        copy.wait_send()
    for copy in weights:
        copy.wait()


def first_norm_gather(tok, og, vec, weight, out_weight, n_ctx, planes, seqs):
    rows, width = tok.shape
    chips, half = n_ctx // 2, rows // seqs
    return pl.pallas_call(
        functools.partial(first_kernel, chips, planes, seqs, width // planes),
        out_shape=(
            jax.ShapeDtypeStruct((planes,) + vec.shape, BF16),
            jax.ShapeDtypeStruct((n_ctx, rows, width), BF16),
            jax.ShapeDtypeStruct((planes, n_ctx, half, width), BF16),
            jax.ShapeDtypeStruct((planes,) + weight.shape[1:], BF16),
            jax.ShapeDtypeStruct((HD, width), BF16),
        ),
        in_specs=[VMEM, ANY, VMEM, ANY, ANY],
        out_specs=(VMEM, ANY, ANY, ANY, ANY),
        scratch_shapes=[
            pltpu.VMEM((rows, width), BF16),
            pltpu.VMEM((planes - 1, half, width), BF16),
            DMA((planes - 1,)),
            DMA((planes - 1,)),
            DMA,
            DMA((planes - 1,)),
            DMA((planes - 1,)),
            DMA((planes - 1,)),
            DMA((planes - 1,)),
            DMA,
            DMA,
            DMA,
            DMA,
        ]
        + gather_sems(chips)
        + gather_sems(chips) * planes,
        compiler_params=params(0),
        cost_estimate=SMALL,
        name="norm_gather",
    )(tok, og, vec, weight, out_weight)


def second_kernel(chips, att_ref, weight_ref, tok_ref, vec_ref, mixed_ref, all_ref, own, *scratch):
    me, core, chip, sibling, to, come = plane_peers(chips)
    greet(to + [sibling])
    rows = tok_ref.shape[0]
    part = scratch[0]

    def make(k, target):
        span = pl.ds(pl.multiple_of(target * 2 * rows, 2 * rows), 2 * rows)
        branch = nn(att_ref[span, :], weight_ref[...]).astype(BF16)
        part[k, 0] = branch[:rows]
        part[k, 1] = branch[rows:]

    total = plane_scatter_made(make, *scratch[:3], scratch[3:7], chips, lambda: None)
    mixed = tok_ref[...].astype(F32) + total + vec_ref[2:3, :]
    mixed_ref[...] = mixed
    unit, inverse = normalize(mixed)
    own[...] = (unit * vec_ref[0:1, :] + vec_ref[1:2, :]).astype(BF16)
    plane_gather([own], [all_ref], scratch[7:], chips)


def second_norm_gather(att, weight, tok, vecs, n_ctx):
    rows, width = tok.shape
    chips = n_ctx // 2
    return pl.pallas_call(
        functools.partial(second_kernel, chips),
        out_shape=(
            jax.ShapeDtypeStruct((rows, width), F32),
            jax.ShapeDtypeStruct((n_ctx, rows, width), BF16),
        ),
        in_specs=[VMEM] * 4,
        out_specs=(VMEM, ANY),
        scratch_shapes=[pltpu.VMEM((rows, width), BF16)]
        + made_scratch(chips, rows, width)
        + gather_sems(chips),
        compiler_params=params(1),
        cost_estimate=SMALL,
        name="scatter_norm_gather",
    )(att, weight, tok, vecs)


def third_kernel(
    chips,
    h_hbm,
    og_hbm,
    act_hbm,
    slope_hbm,
    up_w_hbm,
    down_w_hbm,
    mixed_ref,
    og_ref,
    vec_ref,
    dmixed_ref,
    sums_ref,
    all_ref,
    out_hbm,
    up_grad_ref,
    up_sum_ref,
    h_ref,
    ogs_ref,
    act_ref,
    slope_ref,
    up_w_ref,
    down_w_ref,
    d_up_ref,
    out_ref,
    load_sem,
    out_sem,
    own,
    *scratch,
):
    me, core, chip, sibling, to, come = plane_peers(chips)
    made, gather = scratch[:7], scratch[7:]
    loads = [
        pltpu.make_async_copy(source, target, load_sem.at[k])
        for k, (source, target) in enumerate(
            [
                (down_w_hbm, down_w_ref),
                (og_hbm, ogs_ref),
                (slope_hbm, slope_ref),
                (up_w_hbm, up_w_ref),
                (h_hbm, h_ref),
                (act_hbm, act_ref),
            ]
        )
    ]
    for load in loads:
        load.start()
    greet(to + [sibling])
    unit, inverse = normalize(mixed_ref[...])
    rows = mixed_ref.shape[0]
    for load in loads[:4]:
        load.wait()
    part = made[0]

    def make(k, target):
        span = pl.ds(pl.multiple_of(target * 2 * rows, 2 * rows), 2 * rows)
        d_up = (nt(ogs_ref[span, :], down_w_ref[...]) * slope_ref[span, :]).astype(BF16)
        d_up_ref[span, :] = d_up
        d_h = nt(d_up, up_w_ref[...]).astype(BF16)
        part[k, 0] = d_h[:rows]
        part[k, 1] = d_h[rows:]

    def meanwhile():
        for load in loads[4:]:
            load.wait()
        d_up = d_up_ref[...]
        up_sum_ref[...] = jnp.sum(d_up.astype(F32), axis=0, keepdims=True)
        up_grad_ref[...] = tn(d_up, h_ref[...]).T.astype(BF16)
        out_ref[...] = nn(act_ref[...], down_w_ref[...]).astype(BF16)
        pltpu.make_async_copy(out_ref, out_hbm, out_sem).start()

    grad = plane_scatter_made(make, *made[:3], made[3:], chips, meanwhile)
    out_grad = og_ref[...].astype(F32)
    dmixed = out_grad + norm_backward(grad, vec_ref[0:1, :], unit, inverse)
    low = dmixed.astype(BF16)
    own[...] = low
    started = plane_gather_start([own], [all_ref], gather, chips)
    dmixed_ref[...] = dmixed
    sums_ref[0:1, :] = jnp.sum(grad * unit, axis=0, keepdims=True)
    sums_ref[1:2, :] = jnp.sum(grad, axis=0, keepdims=True)
    sums_ref[2:3, :] = jnp.sum(low.astype(F32), axis=0, keepdims=True)
    sums_ref[3:4, :] = jnp.sum(out_grad, axis=0, keepdims=True)
    plane_gather_finish(started, [all_ref], gather, chips)
    pltpu.make_async_copy(out_ref, out_hbm, out_sem).wait()


def feed_back(values, out_grads, act, slope, up_weight, down_weight, mixed, og, vecs):
    rows, width = mixed.shape
    total_rows, hidden = act.shape
    n_ctx = total_rows // rows
    chips = n_ctx // 2
    return pl.pallas_call(
        functools.partial(third_kernel, chips),
        out_shape=(
            jax.ShapeDtypeStruct((rows, width), F32),
            jax.ShapeDtypeStruct((4, width), F32),
            jax.ShapeDtypeStruct((n_ctx, rows, width), BF16),
            jax.ShapeDtypeStruct((total_rows, width), BF16),
            jax.ShapeDtypeStruct((width, hidden), BF16),
            jax.ShapeDtypeStruct((1, hidden), F32),
        ),
        in_specs=[ANY] * 6 + [VMEM] * 3,
        out_specs=(VMEM, VMEM, ANY, ANY, VMEM, VMEM),
        scratch_shapes=[
            pltpu.VMEM((total_rows, width), BF16),
            pltpu.VMEM((total_rows, width), BF16),
            pltpu.VMEM((total_rows, hidden), BF16),
            pltpu.VMEM((total_rows, hidden), F32),
            pltpu.VMEM((width, hidden), BF16),
            pltpu.VMEM((hidden, width), BF16),
            pltpu.VMEM((total_rows, hidden), BF16),
            pltpu.VMEM((total_rows, width), BF16),
            DMA((6,)),
            DMA,
            pltpu.VMEM((rows, width), BF16),
        ]
        + made_scratch(chips, rows, width)
        + gather_sems(chips),
        compiler_params=params(2),
        cost_estimate=SMALL,
        name="feed_back",
    )(values, out_grads, act, slope, up_weight, down_weight, mixed, og, vecs)


def fourth_kernel(
    chips,
    planes,
    seqs,
    part_ref,
    qkv_ref,
    outw_ref,
    flat_ref,
    tok_ref,
    dmixed_ref,
    vec_ref,
    grad_ref,
    qkv_all,
    outw_all,
    sums_ref,
    flat_out,
    q_arrived,
    q_own,
    q_send,
    q_recv,
    q_local,
    rows_own,
    rows_arrived,
    r_send,
    r_recv,
    small,
    small_own,
    small_z,
    small_c,
    flat_own,
    flat_z,
    flat_c,
    z_send,
    z_recv,
    c_send,
    c_recv,
    *scratch,
):
    n_ctx = 2 * chips
    pairs = planes // seqs
    me, core, chip, sibling, to, come = plane_peers(chips)
    plane, others = other_planes(planes)
    around = [lax.rem(me + k, n_ctx) for k in range(1, n_ctx)]
    greet(around, others)
    scatter, rest_sems, qkv_sems = scratch[:8], scratch[8:13], scratch[13:]

    pushed = [
        send(qkv_ref.at[peer], q_arrived.at[plane], q_send.at[k], q_recv.at[k], "fsdp", peer)
        for k, peer in enumerate(others)
    ]
    held = pltpu.make_async_copy(qkv_ref.at[plane], q_arrived.at[plane], q_local)
    held.start()
    flat_sent = [
        send(flat_ref.at[peer], flat_z.at[k], z_send.at[0, k], z_recv.at[0, k], "fsdp", peer)
        for k, peer in enumerate(others)
    ]
    unit, inverse = normalize(tok_ref[...].astype(F32))
    total = plane_scatter(lambda c: part_ref.at[:, c], *scatter[:3], scatter[3:], chips)
    rows_own[...] = total.astype(BF16)
    rows_sent = [
        send(rows_own.at[peer], rows_arrived.at[plane], r_send.at[k], r_recv.at[k], "fsdp", peer)
        for k, peer in enumerate(others)
    ]
    rows_arrived[plane] = rows_own[plane]
    rest_started = plane_gather_start([outw_ref], [outw_all], rest_sems, chips)
    for copy in pushed + [held]:
        copy.wait()
    for pair in range(pairs):
        terms = [q_arrived[seq * pairs + pair].astype(F32) for seq in range(seqs)]
        q_own[pair] = sum(terms[1:], terms[0]).astype(BF16)
    qkv_started = plane_gather_start([q_own], [qkv_all], qkv_sems, chips)
    plane_gather_finish(rest_started, [outw_all], rest_sems, chips)

    for copy in rows_sent:
        copy.wait()
    halves = []
    for seq in range(seqs):
        terms = [rows_arrived[seq * pairs + pair].astype(F32) for pair in range(pairs)]
        halves.append(sum(terms[1:], terms[0]))
    grad = jnp.concatenate(halves, axis=0)
    sums = jnp.concatenate(
        [jnp.sum(grad * unit, axis=0, keepdims=True), jnp.sum(grad, axis=0, keepdims=True)], axis=0
    )
    quarter = sums.shape[1] // planes
    small[...] = jnp.zeros_like(small)
    for j in range(planes):
        small[j, 0:2, 0:quarter] = sums[:, j * quarter : (j + 1) * quarter]
    small_sent = [
        send(small.at[peer], small_z.at[k], z_send.at[1, k], z_recv.at[1, k], "fsdp", peer)
        for k, peer in enumerate(others)
    ]
    grad_ref[...] = dmixed_ref[...] + norm_backward(grad, vec_ref[0:1, :], unit, inverse)
    small_total = small[plane]
    flat_total = flat_ref[plane]
    for k in range(planes - 1):
        flat_sent[k].wait()
        small_sent[k].wait()
        small_total = small_total + small_z[k]
        flat_total = flat_total + flat_z[k]
    small_own[...] = small_total
    flat_own[...] = flat_total
    sent = []
    for k, peer in enumerate(around):
        sent.append(send(small_own, small_c.at[k], c_send.at[0, k], c_recv.at[0, k], "ctx", peer))
        sent.append(send(flat_own, flat_c.at[k], c_send.at[1, k], c_recv.at[1, k], "ctx", peer))
    plane_gather_finish(qkv_started, [qkv_all], qkv_sems, chips)
    for copy in sent:
        copy.wait()
    for k in range(n_ctx - 1):
        small_total = small_total + small_c[k]
        flat_total = flat_total + flat_c[k]
    sums_ref[...] = small_total
    flat_out[...] = flat_total


def first_norm_back(part, qkv_part, outw_own, flat, tok, dmixed, vecs):
    planes, n_ctx, half, width = part.shape
    rows = tok.shape[0]
    seqs = rows // half
    quarter, columns = qkv_part.shape[1:]
    chips, pairs = n_ctx // 2, planes // seqs
    size = (8, quarter + -quarter % LANES)
    return pl.pallas_call(
        functools.partial(fourth_kernel, chips, planes, seqs),
        out_shape=(
            jax.ShapeDtypeStruct((rows, width), F32),
            jax.ShapeDtypeStruct((n_ctx, pairs, quarter, columns), BF16),
            jax.ShapeDtypeStruct((n_ctx,) + outw_own.shape, BF16),
            jax.ShapeDtypeStruct(size, F32),
            jax.ShapeDtypeStruct(flat.shape[1:], F32),
        ),
        in_specs=[ANY, ANY, ANY, VMEM, VMEM, VMEM, VMEM],
        out_specs=(VMEM, ANY, ANY, VMEM, VMEM),
        scratch_shapes=[
            pltpu.VMEM((planes, quarter, columns), BF16),
            pltpu.VMEM((pairs, quarter, columns), BF16),
            DMA((planes - 1,)),
            DMA((planes - 1,)),
            DMA,
            pltpu.VMEM((planes, half, width), BF16),
            pltpu.VMEM((planes, half, width), BF16),
            DMA((planes - 1,)),
            DMA((planes - 1,)),
            pltpu.VMEM((planes,) + size, F32),
            pltpu.VMEM(size, F32),
            pltpu.VMEM((planes - 1,) + size, F32),
            pltpu.VMEM((n_ctx - 1,) + size, F32),
            pltpu.VMEM(flat.shape[1:], F32),
            pltpu.VMEM((planes - 1,) + flat.shape[1:], F32),
            pltpu.VMEM((n_ctx - 1,) + flat.shape[1:], F32),
            DMA((2, planes - 1)),
            DMA((2, planes - 1)),
            DMA((2, n_ctx - 1)),
            DMA((2, n_ctx - 1)),
        ]
        + scatter_scratch(chips, planes, half, width)
        + gather_sems(chips)
        + gather_sems(chips),
        compiler_params=params(3),
        cost_estimate=SMALL,
        name="scatter_back",
    )(part, qkv_part, outw_own, flat, tok, dmixed, vecs)


def finish_kernel(
    chips,
    planes,
    seqs,
    h1_hbm,
    d_hbm,
    w_hbm,
    up_ref,
    outw_ref,
    flat_ref,
    tok_ref,
    dmixed_ref,
    vec_ref,
    grad_ref,
    qkv_all,
    up_all,
    outw_all,
    sums_ref,
    flat_out,
    h1_ref,
    d_ref,
    w_ref,
    load_sem,
    dw_ref,
    q_arrived,
    q_own,
    q_send,
    q_recv,
    outw_arrived,
    outw_own,
    o_send,
    o_recv,
    rows_own,
    rows_arrived,
    r_send,
    r_recv,
    small,
    small_own,
    small_z,
    small_c,
    flat_own,
    flat_z,
    flat_c,
    z_send,
    z_recv,
    c_send,
    c_recv,
    *scratch,
):
    n_ctx = 2 * chips
    pairs = planes // seqs
    me, core, chip, sibling, to, come = plane_peers(chips)
    plane, others = other_planes(planes)
    around = [lax.rem(me + k, n_ctx) for k in range(1, n_ctx)]
    made, outw_sems, qkv_sems, up_sems = scratch[:7], scratch[7:12], scratch[12:17], scratch[17:]
    loads = [
        pltpu.make_async_copy(source, target, load_sem.at[k])
        for k, (source, target) in enumerate([(d_hbm, d_ref), (h1_hbm, h1_ref), (w_hbm, w_ref)])
    ]
    for load in loads:
        load.start()
    greet(around, others)
    outw_sent = [
        send(outw_ref.at[peer], outw_arrived.at[k], o_send.at[k], o_recv.at[k], "fsdp", peer)
        for k, peer in enumerate(others)
    ]
    flat_sent = [
        send(flat_ref.at[peer], flat_z.at[k], z_send.at[0, k], z_recv.at[0, k], "fsdp", peer)
        for k, peer in enumerate(others)
    ]
    unit, inverse = normalize(tok_ref[...].astype(F32))

    for load in loads:
        load.wait()
    quarter = dw_ref.shape[1]
    dw = tn(d_ref[...], h1_ref[...]).T.astype(BF16)
    for j in range(planes):
        dw_ref[j] = dw[j * quarter : (j + 1) * quarter]
    pushed = [
        send(dw_ref.at[peer], q_arrived.at[plane], q_send.at[k], q_recv.at[k], "fsdp", peer)
        for k, peer in enumerate(others)
    ]
    q_arrived[plane] = dw_ref[plane]

    part = made[0]
    half = part.shape[3]

    def make(k, target):
        blocks = []
        for j in range(planes):
            start = pl.multiple_of(j * n_ctx * half + target * 2 * half, 2 * half)
            blocks.append(d_ref[pl.ds(start, 2 * half), :])
        d_h = nt(jnp.concatenate(blocks, axis=0), w_ref[...]).astype(BF16)
        for j in range(planes):
            for side in range(2):
                start = (2 * j + side) * half
                part[k, side, j] = d_h[start : start + half]

    total = plane_scatter_made(make, *made[:3], made[3:], chips, lambda: None)
    rows_own[...] = total.astype(BF16)
    rows_sent = [
        send(rows_own.at[peer], rows_arrived.at[plane], r_send.at[k], r_recv.at[k], "fsdp", peer)
        for k, peer in enumerate(others)
    ]
    rows_arrived[plane] = rows_own[plane]

    up_started = plane_gather_start([up_ref], [up_all], up_sems, chips)
    total = outw_ref[plane].astype(F32)
    for k, copy in enumerate(outw_sent):
        copy.wait()
        total = total + outw_arrived[k].astype(F32)
    outw_own[...] = total.astype(BF16)
    outw_started = plane_gather_start([outw_own], [outw_all], outw_sems, chips)
    for copy in pushed:
        copy.wait()
    for pair in range(pairs):
        terms = [q_arrived[seq * pairs + pair].astype(F32) for seq in range(seqs)]
        q_own[pair] = sum(terms[1:], terms[0]).astype(BF16)
    qkv_started = plane_gather_start([q_own], [qkv_all], qkv_sems, chips)
    plane_gather_middle(up_started, [up_all], up_sems, chips)
    plane_gather_middle(outw_started, [outw_all], outw_sems, chips)
    plane_gather_middle(qkv_started, [qkv_all], qkv_sems, chips)

    for copy in rows_sent:
        copy.wait()
    halves = []
    for seq in range(seqs):
        terms = [rows_arrived[seq * pairs + pair].astype(F32) for pair in range(pairs)]
        halves.append(sum(terms[1:], terms[0]))
    grad = jnp.concatenate(halves, axis=0)
    sums = jnp.concatenate(
        [jnp.sum(grad * unit, axis=0, keepdims=True), jnp.sum(grad, axis=0, keepdims=True)], axis=0
    )
    small[...] = jnp.zeros_like(small)
    for j in range(planes):
        small[j, 0:2, 0:quarter] = sums[:, j * quarter : (j + 1) * quarter]
    small_sent = [
        send(small.at[peer], small_z.at[k], z_send.at[1, k], z_recv.at[1, k], "fsdp", peer)
        for k, peer in enumerate(others)
    ]
    grad_ref[...] = dmixed_ref[...] + norm_backward(grad, vec_ref[0:1, :], unit, inverse)
    small_total = small[plane]
    flat_total = flat_ref[plane]
    for k in range(planes - 1):
        flat_sent[k].wait()
        small_sent[k].wait()
        small_total = small_total + small_z[k]
        flat_total = flat_total + flat_z[k]
    small_own[...] = small_total
    flat_own[...] = flat_total
    sent = []
    for k, peer in enumerate(around):
        sent.append(send(small_own, small_c.at[k], c_send.at[0, k], c_recv.at[0, k], "ctx", peer))
        sent.append(send(flat_own, flat_c.at[k], c_send.at[1, k], c_recv.at[1, k], "ctx", peer))
    plane_gather_end(outw_started, [outw_all], outw_sems, chips)
    plane_gather_end(qkv_started, [qkv_all], qkv_sems, chips)
    plane_gather_end(up_started, [up_all], up_sems, chips)
    for copy in sent:
        copy.wait()
    for k in range(n_ctx - 1):
        small_total = small_total + small_c[k]
        flat_total = flat_total + flat_c[k]
    sums_ref[...] = small_total
    flat_out[...] = flat_total


def finish(h1, d_qkv, weight, up_own, outw_part, flat, tok, dmixed, vecs):
    rows, width = tok.shape
    planes = outw_part.shape[0]
    n_ctx = lax.axis_size("ctx")
    half = h1.shape[0] // (planes * n_ctx)
    seqs = rows // half
    quarter, columns = width // planes, weight.shape[1]
    chips, pairs = n_ctx // 2, planes // seqs
    size = (8, quarter + -quarter % LANES)
    piece = outw_part.shape[1:]
    return pl.pallas_call(
        functools.partial(finish_kernel, chips, planes, seqs),
        out_shape=(
            jax.ShapeDtypeStruct((rows, width), F32),
            jax.ShapeDtypeStruct((n_ctx, pairs, quarter, columns), BF16),
            jax.ShapeDtypeStruct((n_ctx,) + up_own.shape, BF16),
            jax.ShapeDtypeStruct((n_ctx,) + piece, BF16),
            jax.ShapeDtypeStruct(size, F32),
            jax.ShapeDtypeStruct(flat.shape[1:], F32),
        ),
        in_specs=[ANY] * 4 + [VMEM] * 5,
        out_specs=(VMEM, ANY, ANY, ANY, VMEM, VMEM),
        scratch_shapes=[
            pltpu.VMEM(h1.shape, BF16),
            pltpu.VMEM(d_qkv.shape, BF16),
            pltpu.VMEM(weight.shape, BF16),
            DMA((3,)),
            pltpu.VMEM((planes, quarter, columns), BF16),
            pltpu.VMEM((planes, quarter, columns), BF16),
            pltpu.VMEM((pairs, quarter, columns), BF16),
            DMA((planes - 1,)),
            DMA((planes - 1,)),
            pltpu.VMEM((planes - 1,) + piece, BF16),
            pltpu.VMEM(piece, BF16),
            DMA((planes - 1,)),
            DMA((planes - 1,)),
            pltpu.VMEM((planes, half, width), BF16),
            pltpu.VMEM((planes, half, width), BF16),
            DMA((planes - 1,)),
            DMA((planes - 1,)),
            pltpu.VMEM((planes,) + size, F32),
            pltpu.VMEM(size, F32),
            pltpu.VMEM((planes - 1,) + size, F32),
            pltpu.VMEM((n_ctx - 1,) + size, F32),
            pltpu.VMEM(flat.shape[1:], F32),
            pltpu.VMEM((planes - 1,) + flat.shape[1:], F32),
            pltpu.VMEM((n_ctx - 1,) + flat.shape[1:], F32),
            DMA((2, planes - 1)),
            DMA((2, planes - 1)),
            DMA((2, n_ctx - 1)),
            DMA((2, n_ctx - 1)),
        ]
        + made_scratch(chips, planes, half, width)
        + gather_sems(chips)
        + gather_sems(chips)
        + gather_sems(chips),
        compiler_params=params(9),
        cost_estimate=SMALL,
        name="finish",
    )(h1, d_qkv, weight, up_own, outw_part, flat, tok, dmixed, vecs)


def to_heads_kernel(
    planes, seqs, chips, tok_ref, down_ref, head_ref, down_all, send_sems, recv_sems, local_sem, *sems
):
    ctx_me, core, chip, sibling, to, come = plane_peers(chips)
    me, others = other_planes(planes)
    pairs = planes // seqs
    greet(to + [sibling], others)

    def source(unit):
        start = pl.multiple_of(lax.rem(unit, pairs) * LANES, LANES)
        return tok_ref.at[:, unit // pairs, :, pl.ds(start, LANES)]

    copies = [
        send(source(unit), head_ref.at[me], send_sems.at[k], recv_sems.at[k], "fsdp", unit)
        for k, unit in enumerate(others)
    ]
    copies.append(pltpu.make_async_copy(source(me), head_ref.at[me], local_sem))
    copies[-1].start()
    plane_gather([down_ref], [down_all], sems, chips)
    for copy in copies:
        copy.wait()


def to_heads(tok, planes, cid, down_own):
    n_ctx, seqs, local_rows, width = tok.shape
    chips = n_ctx // 2
    return pl.pallas_call(
        functools.partial(to_heads_kernel, planes, seqs, chips),
        out_shape=(
            jax.ShapeDtypeStruct((planes, n_ctx, local_rows, LANES), BF16),
            jax.ShapeDtypeStruct((n_ctx,) + down_own.shape, BF16),
        ),
        in_specs=[ANY, ANY],
        out_specs=(ANY, ANY),
        scratch_shapes=[DMA((planes - 1,)), DMA((planes - 1,)), DMA] + gather_sems(chips),
        compiler_params=params(cid),
        cost_estimate=SMALL,
        name="to_heads",
    )(tok, down_own)


def to_tokens_kernel(
    planes, seqs, head_ref, weight_ref, tok_ref, weights_ref, send_sems, recv_sems, local_sem, w_send, w_recv, w_local
):
    me, others = other_planes(planes)
    pairs = planes // seqs
    greet((), others)
    start = pl.multiple_of(lax.rem(me, pairs) * LANES, LANES)
    target = tok_ref.at[:, me // pairs, :, pl.ds(start, LANES)]
    copies = [
        send(head_ref.at[peer], target, send_sems.at[k], recv_sems.at[k], "fsdp", peer) for k, peer in enumerate(others)
    ]
    copies += [
        send(weight_ref, weights_ref.at[me], w_send.at[k], w_recv.at[k], "fsdp", peer) for k, peer in enumerate(others)
    ]
    for copy in (
        pltpu.make_async_copy(head_ref.at[me], target, local_sem),
        pltpu.make_async_copy(weight_ref, weights_ref.at[me], w_local),
    ):
        copy.start()
        copies.append(copy)
    for copy in copies:
        copy.wait()


def to_tokens(heads, seqs, cid, weight):
    planes, n_ctx, rows, lanes = heads.shape
    width = (planes // seqs) * LANES
    return pl.pallas_call(
        functools.partial(to_tokens_kernel, planes, seqs),
        out_shape=(
            jax.ShapeDtypeStruct((n_ctx, seqs, rows, width), heads.dtype),
            jax.ShapeDtypeStruct((planes,) + weight.shape, BF16),
        ),
        in_specs=[ANY] * 2,
        out_specs=(ANY,) * 2,
        scratch_shapes=[DMA((planes - 1,)), DMA((planes - 1,)), DMA] * 2,
        compiler_params=params(cid),
        cost_estimate=SMALL,
        name="to_tokens",
    )(heads, weight)


def nt(left, right):
    return lax.dot_general(left, right, (((1,), (1,)), ((), ())), preferred_element_type=F32)


def nn(left, right):
    return lax.dot_general(left, right, (((1,), (0,)), ((), ())), preferred_element_type=F32)


def sort_blocks(order_ref, qkv_ref, targets, blocks, half):
    def body(block, carry):
        row = qkv_ref[order_ref[block]]
        start = pl.multiple_of(block * half, half)
        for k, target in enumerate(targets):
            target[pl.ds(start, half), :] = row[:, k * LANES : (k + 1) * LANES]
        return carry

    lax.fori_loop(0, blocks, body, 0)


def lane_mask(rows, head):
    lane = lax.broadcasted_iota(jnp.int32, (rows, LANES), 1)
    return (lane < HD) if head == 0 else (lane >= HD)


def unsort_blocks(order_ref, sorted_refs, target_ref, blocks, half):
    def body(block, carry):
        start = pl.multiple_of(block * half, half)
        place = order_ref[block]
        for k, source in enumerate(sorted_refs):
            target_ref[place, :, k * LANES : (k + 1) * LANES] = source[pl.ds(start, half), :].astype(BF16)
        return carry

    lax.fori_loop(0, blocks, body, 0)


def long_forward_kernel(tile, order_ref, qkv_ref, out_ref, att_ref, lse_ref, q_s, k_s, v_s, vt_s, o_s):
    blocks, half = out_ref.shape[0], out_ref.shape[1]
    length = blocks * half
    tiles = length // tile
    sort_blocks(order_ref, qkv_ref, [q_s, k_s, v_s], blocks, half)
    for t in range(tiles):
        span = slice(t * tile, (t + 1) * tile)
        vt_s[:, span] = v_s[span, :].T
    scale = HD ** (-0.5)
    rows_iota = lax.broadcasted_iota(jnp.int32, (tile, tile), 0)
    cols_iota = lax.broadcasted_iota(jnp.int32, (tile, tile), 1)
    allowed = rows_iota <= cols_iota
    masks = [lane_mask(tile, head) for head in range(2)]

    for qt in range(tiles):
        q_span = slice(qt * tile, (qt + 1) * tile)
        query = q_s[q_span, :] * jnp.asarray(scale, BF16)
        queries = [jnp.where(masks[head], query, jnp.zeros_like(query)) for head in range(2)]

        def step(kt, state, masked, queries=queries):
            start = pl.multiple_of(kt * tile, tile)
            keys = k_s[pl.ds(start, tile), :]
            new = []
            for head in range(2):
                top, total, acc = state[head]
                scores = nt(keys, queries[head])
                if masked:
                    scores = jnp.where(allowed, scores, NEG_BIG)
                new_top = jnp.maximum(top, jnp.max(scores, axis=0, keepdims=True))
                soft = jnp.exp(scores - new_top)
                factor = jnp.exp(top - new_top)
                total = total * factor + jnp.sum(soft, axis=0, keepdims=True)
                values = vt_s[head * HD : (head + 1) * HD, pl.ds(start, tile)]
                acc = acc * factor + nn(values, soft.astype(BF16))
                new.append((new_top, total, acc))
            return tuple(new)

        state = tuple(
            (jnp.full((1, tile), NEG_BIG, F32), jnp.zeros((1, tile), F32), jnp.zeros((HD, tile), F32))
            for head in range(2)
        )
        state = step(qt, state, True)
        if qt > 0:
            state = lax.fori_loop(0, qt, lambda kt, s, step=step: step(kt, s, False), state)
        parts = []
        for head in range(2):
            top, total, acc = state[head]
            parts.append(acc / total)
            lse_ref[head : head + 1, q_span] = top + jnp.log(total)
        att = jnp.concatenate(parts, axis=0).T
        att_ref[q_span, :] = att
        o_s[q_span, :] = att.astype(BF16)

    unsort_blocks(order_ref, [o_s], out_ref, blocks, half)


def block_places(order, n_ctx):
    blocks = order.shape[0]
    places = jnp.stack([order // (2 * n_ctx), lax.rem(order // 2, n_ctx), lax.rem(order, 2)]).astype(jnp.int32)
    match = order[:, None] == jnp.arange(blocks)[None, :]
    inverse = jnp.sum(jnp.where(match, jnp.arange(blocks)[:, None], 0), axis=0).astype(jnp.int32)
    return places, inverse


def sort_places(order_ref, source, targets):
    blocks, half = order_ref.shape[1], source.shape[3]

    def body(block, carry):
        row = source[order_ref[0, block], order_ref[1, block], order_ref[2, block]]
        start = pl.multiple_of(block * half, half)
        for k, target in enumerate(targets):
            target[pl.ds(start, half), :] = row[:, k * LANES : (k + 1) * LANES]
        return carry

    lax.fori_loop(0, blocks, body, 0)


def unsort_places(place_ref, sources, target):
    n_ctx = target.shape[1]

    def body(place, carry):
        block = place_ref[place]
        f, c, side = place // (2 * n_ctx), lax.rem(place // 2, n_ctx), lax.rem(place, 2)
        for k, source in enumerate(sources):
            target[f, c, side, :, k * LANES : (k + 1) * LANES] = source[block]
        return carry

    lax.fori_loop(0, place_ref.shape[0], body, 0)


def attend_kernel(
    tile,
    planes,
    seqs,
    order_ref,
    place_ref,
    h1_hbm,
    w_hbm,
    shift_ref,
    out_w_ref,
    qkv_ref,
    att_ref,
    lse_ref,
    tok_ref,
    out_ws_ref,
    h1_ref,
    w_ref,
    load_sem,
    heads,
    a_send,
    a_recv,
    a_local,
    w_send,
    w_recv,
    w_local,
    q_s,
    k_s,
    v_s,
    o_s,
    s_s,
    p_s,
):
    me, others = other_planes(planes)
    pairs = planes // seqs
    n_ctx, half = qkv_ref.shape[1], qkv_ref.shape[3]
    length = att_ref.shape[0]
    tiles, step = length // tile, tile // half
    rows = length // planes
    loads = [pltpu.make_async_copy(w_hbm, w_ref, load_sem.at[planes])]
    for j in range(planes):
        span = pl.ds(j * rows, rows)
        loads.append(pltpu.make_async_copy(h1_hbm.at[span], h1_ref.at[span], load_sem.at[j]))
    for load in loads:
        load.start()
    greet((), others)
    moved = [
        send(out_w_ref, out_ws_ref.at[me], w_send.at[k], w_recv.at[k], "fsdp", peer) for k, peer in enumerate(others)
    ]
    moved.append(pltpu.make_async_copy(out_w_ref, out_ws_ref.at[me], w_local))
    moved[-1].start()

    loads[0].wait()
    for j in range(planes):
        loads[1 + j].wait()
        values = nn(h1_ref[j * rows : (j + 1) * rows, :], w_ref[...]) + shift_ref[...]
        qkv_ref[j] = values.astype(BF16).reshape(n_ctx, 2, half, values.shape[1])

    sort_places(order_ref, qkv_ref, [q_s, k_s, v_s])
    scale = HD ** (-0.5)
    rows_iota = lax.broadcasted_iota(jnp.int32, (tile, tile), 0)
    cols_iota = lax.broadcasted_iota(jnp.int32, (tile, tile), 1)
    allowed = cols_iota <= rows_iota
    masks = [lane_mask(tile, head) for head in range(2)]
    for qt in range(tiles):
        q_span = slice(qt * tile, (qt + 1) * tile)
        query = q_s[q_span, :] * jnp.asarray(scale, BF16)
        parts = []
        for head in range(2):
            one = jnp.where(masks[head], query, jnp.zeros_like(query))
            top = jnp.full((tile, LANES), NEG_BIG, F32)
            for kt in range(qt + 1):
                k_span = slice(kt * tile, (kt + 1) * tile)
                scores = nt(one, k_s[k_span, :])
                if kt == qt:
                    scores = jnp.where(allowed, scores, NEG_BIG)
                s_s[head, :, k_span] = scores
                for lane in range(0, tile, LANES):
                    top = jnp.maximum(top, scores[:, lane : lane + LANES])
            top = jnp.max(top, axis=1, keepdims=True)
            total = jnp.zeros((tile, LANES), F32)
            for kt in range(qt + 1):
                k_span = slice(kt * tile, (kt + 1) * tile)
                soft = jnp.exp(s_s[head, :, k_span] - top)
                for lane in range(0, tile, LANES):
                    total = total + soft[:, lane : lane + LANES]
                p_s[head, :, k_span] = soft.astype(BF16)
            total = jnp.sum(total, axis=1, keepdims=True)
            span = slice(0, (qt + 1) * tile)
            parts.append(nn(p_s[head, :, span], v_s[span, :]) / total)
            lse = jnp.broadcast_to(top + jnp.log(total), (tile, LANES))
            lse_ref[head : head + 1, q_span] = lse.T[0:1, :]
        att = jnp.where(masks[0], parts[0], parts[1])
        att_ref[q_span, :] = att
        o_s[qt * step : (qt + 1) * step] = att.astype(BF16).reshape(step, half, LANES)
    unsort_places(place_ref, [o_s], heads)

    start = pl.multiple_of(lax.rem(me, pairs) * LANES, LANES)
    target = tok_ref.at[:, me // pairs, :, :, pl.ds(start, LANES)]
    moved += [
        send(heads.at[peer], target, a_send.at[k], a_recv.at[k], "fsdp", peer) for k, peer in enumerate(others)
    ]
    moved.append(pltpu.make_async_copy(heads.at[me], target, a_local))
    moved[-1].start()
    for copy in moved:
        copy.wait()


def attend(places, inverse, h1, weight, shift, out_own, n_ctx, planes, seqs, half, tile):
    length = h1.shape[0]
    lanes = weight.shape[1]
    blocks = length // half
    width = (planes // seqs) * LANES
    rows_s = pltpu.VMEM((length, LANES), BF16)
    sems = [DMA((planes - 1,)), DMA((planes - 1,)), DMA]
    return pl.pallas_call(
        functools.partial(attend_kernel, tile, planes, seqs),
        out_shape=(
            jax.ShapeDtypeStruct((planes, n_ctx, 2, half, lanes), BF16),
            jax.ShapeDtypeStruct((length, LANES), F32),
            jax.ShapeDtypeStruct((2, length), F32),
            jax.ShapeDtypeStruct((n_ctx, seqs, 2, half, width), BF16),
            jax.ShapeDtypeStruct((planes,) + out_own.shape, BF16),
        ),
        in_specs=[SMEM, SMEM, ANY, ANY, VMEM, ANY],
        out_specs=(VMEM, VMEM, VMEM, ANY, ANY),
        scratch_shapes=[
            pltpu.VMEM(h1.shape, BF16),
            pltpu.VMEM(weight.shape, BF16),
            DMA((planes + 1,)),
            pltpu.VMEM((planes, n_ctx, 2, half, LANES), BF16),
        ]
        + sems
        + sems
        + [rows_s, rows_s, rows_s, pltpu.VMEM((blocks, half, LANES), BF16)]
        + [pltpu.VMEM((2, tile, length), F32), pltpu.VMEM((2, tile, length), BF16)],
        compiler_params=params(5),
        cost_estimate=SMALL,
        name="attend",
    )(places, inverse, h1, weight, shift, out_own)


SMEM = pl.BlockSpec(memory_space=pltpu.SMEM)
SHORT = 2048


def attend_forward(order, qkv, tile):
    blocks, half, lanes = qkv.shape
    length = blocks * half
    rows = pltpu.VMEM((length, LANES), BF16)
    return pl.pallas_call(
        functools.partial(long_forward_kernel, tile),
        out_shape=(
            jax.ShapeDtypeStruct((blocks, half, LANES), BF16),
            jax.ShapeDtypeStruct((length, LANES), F32),
            jax.ShapeDtypeStruct((2, length), F32),
        ),
        in_specs=[SMEM, VMEM],
        out_specs=(VMEM, VMEM, VMEM),
        scratch_shapes=[rows, rows, rows, pltpu.VMEM((LANES, length), BF16), rows],
        compiler_params=params(),
        cost_estimate=SMALL,
        name="attend_forward",
    )(order, qkv)


def long_backward_kernel(
    tile, order_ref, qkv_ref, grad_ref, att_ref, lse_ref, out_ref, sum_ref, q_s, k_s, v_s, g_s, kt_s, dq_s, dk_s, dv_s
):
    blocks, half = grad_ref.shape[0], grad_ref.shape[1]
    length = blocks * half
    tiles = length // tile
    sort_blocks(order_ref, qkv_ref, [q_s, k_s, v_s], blocks, half)
    sort_blocks(order_ref, grad_ref, [g_s], blocks, half)
    for t in range(tiles):
        span = slice(t * tile, (t + 1) * tile)
        kt_s[:, span] = k_s[span, :].T
    scale = HD ** (-0.5)
    rows_iota = lax.broadcasted_iota(jnp.int32, (tile, tile), 0)
    cols_iota = lax.broadcasted_iota(jnp.int32, (tile, tile), 1)
    allowed = rows_iota <= cols_iota
    masks = [lane_mask(tile, head) for head in range(2)]
    dk_s[...] = jnp.zeros_like(dk_s)
    dv_s[...] = jnp.zeros_like(dv_s)

    for qt in range(tiles):
        q_span = slice(qt * tile, (qt + 1) * tile)
        query = q_s[q_span, :] * jnp.asarray(scale, BF16)
        grad = g_s[q_span, :]
        queries = [jnp.where(masks[head], query, jnp.zeros_like(query)) for head in range(2)]
        grads = [jnp.where(masks[head], grad, jnp.zeros_like(grad)) for head in range(2)]
        product = (grad.astype(F32) * att_ref[q_span, :]).T
        dots = [jnp.sum(product[head * HD : (head + 1) * HD], axis=0, keepdims=True) for head in range(2)]
        totals = [lse_ref[head : head + 1, q_span] for head in range(2)]

        def step(kt, state, masked, queries=queries, grads=grads, dots=dots, totals=totals):
            start = pl.multiple_of(kt * tile, tile)
            rows = pl.ds(start, tile)
            keys = k_s[rows, :]
            values = v_s[rows, :]
            dk = dk_s[rows, :]
            dv = dv_s[rows, :]
            new = []
            for head in range(2):
                scores = nt(keys, queries[head])
                if masked:
                    scores = jnp.where(allowed, scores, NEG_BIG)
                soft = jnp.exp(scores - totals[head])
                dsoft = nt(values, grads[head])
                dscore = (soft * (dsoft - dots[head])).astype(BF16)
                dv = dv + nn(soft.astype(BF16), grads[head])
                dk = dk + nn(dscore, queries[head])
                new.append(state[head] + nn(kt_s[head * HD : (head + 1) * HD, rows], dscore))
            dk_s[rows, :] = dk
            dv_s[rows, :] = dv
            return tuple(new)

        state = (jnp.zeros((HD, tile), F32), jnp.zeros((HD, tile), F32))
        state = step(qt, state, True)
        if qt > 0:
            state = lax.fori_loop(0, qt, lambda kt, s, step=step: step(kt, s, False), state)
        dq = jnp.concatenate(state, axis=0) * scale
        dq_s[q_span, :] = dq.T.astype(BF16)

    unsort_blocks(order_ref, [dq_s, dk_s, dv_s], out_ref, blocks, half)
    for k, source in enumerate([dq_s, dk_s, dv_s]):
        values = source[...].astype(BF16).astype(F32)
        sum_ref[:, k * LANES : (k + 1) * LANES] = jnp.sum(values, axis=0, keepdims=True)


def branch_back_kernel(
    tile,
    planes,
    seqs,
    chips,
    order_ref,
    place_ref,
    db_hbm,
    w_hbm,
    at_hbm,
    qkv_hbm,
    att_hbm,
    down_ref,
    out_part_ref,
    mixed_ref,
    vec_ref,
    lse_ref,
    out_ref,
    sum_ref,
    out_w_ref,
    block_ref,
    down_all,
    db_ref,
    w_ref,
    at_ref,
    qkv_ref,
    att_ref,
    load_sem,
    d_att,
    heads,
    h_send,
    h_recv,
    h_local,
    q_s,
    k_s,
    v_s,
    g_s,
    kt_s,
    dq_s,
    dk_s,
    dv_s,
    qh_s,
    gh_s,
    dot_s,
    p_s,
    ds_s,
    *scratch,
):
    n_ctx = 2 * chips
    ctx_me, core, chip, sibling, to, come = plane_peers(chips)
    me, others = other_planes(planes)
    pairs = planes // seqs
    out_scatter, down_sems = scratch[:8], scratch[8:]
    loads = [
        pltpu.make_async_copy(source, target, load_sem.at[k])
        for k, (source, target) in enumerate(
            [(db_hbm, db_ref), (w_hbm, w_ref), (qkv_hbm, qkv_ref), (at_hbm, at_ref), (att_hbm, att_ref)]
        )
    ]
    for load in loads:
        load.start()
    greet(to + [sibling], others)
    down_started = plane_gather_start([down_ref], [down_all], down_sems, chips)
    out_total = []
    out_stages = plane_scatter_stages(
        lambda c: out_part_ref.at[c], *out_scatter[:3], out_scatter[3:], chips, out_total
    )
    next(out_stages)

    loads[0].wait()
    loads[1].wait()
    d_att[...] = nt(db_ref[...], w_ref[...]).astype(BF16).reshape(d_att.shape)

    def source(unit):
        start = pl.multiple_of(lax.rem(unit, pairs) * LANES, LANES)
        return d_att.at[:, unit // pairs, :, :, pl.ds(start, LANES)]

    moved = [
        send(source(unit), heads.at[me], h_send.at[k], h_recv.at[k], "fsdp", unit) for k, unit in enumerate(others)
    ]
    moved.append(pltpu.make_async_copy(source(me), heads.at[me], h_local))
    moved[-1].start()
    for load in loads[2:]:
        load.wait()
    out_w_ref[...] = tn(at_ref[...], db_ref[...]).astype(BF16)

    blocks, half = dq_s.shape[0], dq_s.shape[1]
    length = blocks * half
    tiles, step = length // tile, tile // half

    sort_places(order_ref, qkv_ref, [q_s, k_s, v_s])
    scale = HD ** (-0.5)
    rows_iota = lax.broadcasted_iota(jnp.int32, (tile, tile), 0)
    cols_iota = lax.broadcasted_iota(jnp.int32, (tile, tile), 1)
    allowed = rows_iota <= cols_iota
    masks = [lane_mask(tile, head) for head in range(2)]
    for t in range(tiles):
        span = slice(t * tile, (t + 1) * tile)
        kt_s[:, span] = k_s[span, :].T
        query = q_s[span, :] * jnp.asarray(scale, BF16)
        for head in range(2):
            qh_s[head, span, :] = jnp.where(masks[head], query, jnp.zeros_like(query))
    next(out_stages)
    for copy in moved:
        copy.wait()
    sort_places(order_ref, heads, [g_s])
    for t in range(tiles):
        span = slice(t * tile, (t + 1) * tile)
        grad = g_s[span, :]
        product = (grad.astype(F32) * att_ref[span, :]).T
        for head in range(2):
            gh_s[head, span, :] = jnp.where(masks[head], grad, jnp.zeros_like(grad))
            dot_s[head : head + 1, span] = jnp.sum(product[head * HD : (head + 1) * HD], axis=0, keepdims=True)
    plane_gather_middle(down_started, [down_all], down_sems, chips)

    def keep(target, index, values):
        target[index * step : (index + 1) * step] = values.astype(BF16).reshape(step, half, LANES)

    for kt in range(tiles):
        k_span = slice(kt * tile, (kt + 1) * tile)
        rest = slice(kt * tile, length)
        keys, values = k_s[k_span, :], v_s[k_span, :]
        dk, dv = None, None
        for head in range(2):
            for qt in range(kt, tiles):
                span = slice(qt * tile, (qt + 1) * tile)
                scores = nt(keys, qh_s[head, span, :])
                if kt == qt:
                    scores = jnp.where(allowed, scores, NEG_BIG)
                soft = jnp.exp(scores - lse_ref[head : head + 1, span])
                p_s[head, :, span] = soft.astype(BF16)
                dsoft = nt(values, gh_s[head, span, :])
                ds_s[head, k_span, span] = (soft * (dsoft - dot_s[head : head + 1, span])).astype(BF16)
            dv_one = nn(p_s[head, :, rest], gh_s[head, rest, :])
            dk_one = nn(ds_s[head, k_span, rest], qh_s[head, rest, :])
            dv = dv_one if dv is None else dv + dv_one
            dk = dk_one if dk is None else dk + dk_one
        keep(dk_s, kt, dk)
        keep(dv_s, kt, dv)
        if kt == 0:
            next(out_stages, None)
    for qt in range(tiles):
        span = slice(qt * tile, (qt + 1) * tile)
        upto = slice(0, (qt + 1) * tile)
        dq = [nn(kt_s[head * HD : (head + 1) * HD, upto], ds_s[head, upto, span]) for head in range(2)]
        keep(dq_s, qt, (jnp.concatenate(dq, axis=0) * scale).T)
    for unused in out_stages:
        pass
    block_ref[...] = (mixed_ref[...] + out_total[0] + vec_ref[...]).astype(BF16)

    unsort_places(place_ref, [dq_s, dk_s, dv_s], out_ref)
    for k, ref in enumerate([dq_s, dk_s, dv_s]):
        values = ref[...].astype(F32)
        sum_ref[:, k * LANES : (k + 1) * LANES] = jnp.sum(jnp.sum(values, axis=0), axis=0, keepdims=True)
    plane_gather_end(down_started, [down_all], down_sems, chips)


def branch_back(places, inverse, d_branch, weight, att, qkv, att_exact, lse, down_own, out_part, mixed, vec, planes, tile):
    shape = qkv.shape
    half, lanes = shape[3:]
    n_ctx, rows, width = out_part.shape
    blocks = 2 * planes * n_ctx
    length = blocks * half
    seqs = rows * n_ctx * planes // length
    chips = n_ctx // 2
    rows_s = pltpu.VMEM((length, LANES), BF16)
    blocks_s = pltpu.VMEM((blocks, half, LANES), BF16)
    return pl.pallas_call(
        functools.partial(branch_back_kernel, tile, planes, seqs, chips),
        out_shape=(
            jax.ShapeDtypeStruct(shape, BF16),
            jax.ShapeDtypeStruct((1, lanes), F32),
            jax.ShapeDtypeStruct(weight.shape, BF16),
            jax.ShapeDtypeStruct((rows, width), BF16),
            jax.ShapeDtypeStruct((n_ctx,) + down_own.shape, BF16),
        ),
        in_specs=[SMEM, SMEM] + [ANY] * 7 + [VMEM] * 3,
        out_specs=(VMEM, VMEM, VMEM, VMEM, ANY),
        scratch_shapes=[
            pltpu.VMEM(d_branch.shape, BF16),
            pltpu.VMEM(weight.shape, BF16),
            pltpu.VMEM(att.shape, BF16),
            pltpu.VMEM(shape, BF16),
            pltpu.VMEM(att_exact.shape, F32),
            DMA((5,)),
            pltpu.VMEM((n_ctx, seqs, 2, half, weight.shape[0]), BF16),
            pltpu.VMEM((planes, n_ctx, 2, half, LANES), BF16),
            DMA((planes - 1,)),
            DMA((planes - 1,)),
            DMA,
            rows_s,
            rows_s,
            rows_s,
            rows_s,
            pltpu.VMEM((LANES, length), BF16),
            blocks_s,
            blocks_s,
            blocks_s,
            pltpu.VMEM((2, length, LANES), BF16),
            pltpu.VMEM((2, length, LANES), BF16),
            pltpu.VMEM((2, length), F32),
            pltpu.VMEM((2, tile, length), BF16),
            pltpu.VMEM((2, length, length), BF16),
        ]
        + scatter_scratch(chips, rows, width)
        + gather_sems(chips),
        compiler_params=params(10),
        cost_estimate=SMALL,
        name="branch_back",
    )(places, inverse, d_branch, weight, att, qkv, att_exact, down_own, out_part, mixed, vec, lse)


def attend_backward(order, qkv, grad, att, lse, tile):
    blocks, half, lanes = qkv.shape
    length = blocks * half
    rows = pltpu.VMEM((length, LANES), BF16)
    flipped = pltpu.VMEM((LANES, length), BF16)
    return pl.pallas_call(
        functools.partial(long_backward_kernel, tile),
        out_shape=(
            jax.ShapeDtypeStruct((blocks, half, 3 * LANES), BF16),
            jax.ShapeDtypeStruct((1, 3 * LANES), F32),
        ),
        in_specs=[SMEM, VMEM, VMEM, VMEM, VMEM],
        out_specs=(VMEM, VMEM),
        scratch_shapes=[rows, rows, rows, rows, flipped, rows] + [pltpu.VMEM((length, LANES), F32)] * 2,
        compiler_params=params(),
        cost_estimate=SMALL,
        name="attend_backward",
    )(order, qkv, grad, att, lse)


def assemble_kernel(pieces, part_ref, out_ref):
    for start, source, first, size in pieces:
        out_ref[:, start : start + size] = part_ref[source, :, first : first + size].astype(F32)


def assemble(parts, pieces, width, block):
    n_ctx, rows, columns = parts.shape
    return pl.pallas_call(
        functools.partial(assemble_kernel, pieces),
        grid=(rows // block,),
        out_shape=jax.ShapeDtypeStruct((rows, width), F32),
        in_specs=[pl.BlockSpec((n_ctx, block, columns), lambda i: (0, i, 0))],
        out_specs=pl.BlockSpec((block, width), lambda i: (i, 0)),
        compiler_params=params(),
        name="assemble",
    )(parts)


def tn(left, right):
    return nn(left.T, right)


def rows_block(rows, most):
    return math.gcd(rows, most)


def whole_block(shape):
    return pl.BlockSpec(shape, lambda i: (0,) * len(shape), pipeline_mode=pl.Buffered(1))


def row_spec(block, width):
    return pl.BlockSpec((block, width), lambda i: (i, 0))


def product_kernel(left_ref, right_ref, shift_ref, out_ref):
    out_ref[...] = (nn(left_ref[...], right_ref[...]) + shift_ref[...]).astype(BF16)


def product(left, right, shift=None):
    rows, depth = left.shape
    width = right.shape[1]
    block = rows_block(rows, 512)
    if shift is None:
        shift = jnp.zeros((width,), F32)
    return pl.pallas_call(
        product_kernel,
        grid=(rows // block,),
        out_shape=jax.ShapeDtypeStruct((rows, width), BF16),
        in_specs=[row_spec(block, depth), whole_block((depth, width)), whole_block((1, width))],
        out_specs=row_spec(block, width),
        compiler_params=params(),
        cost_estimate=SMALL,
        name="product",
    )(left, right, shift[None, :])


def back_kernel(left_ref, grad_ref, weight_ref, grad_left_ref, grad_weight_ref, sum_ref, total):
    step = pl.program_id(0)
    grad = grad_ref[...]
    grad_left_ref[...] = nt(grad, weight_ref[...]).astype(BF16)
    term = tn(grad, left_ref[...])
    sums = jnp.sum(grad.astype(F32), axis=0, keepdims=True)

    @pl.when(step == 0)
    def _():
        total[...] = term
        sum_ref[...] = sums

    @pl.when(step > 0)
    def _():
        total[...] += term
        sum_ref[...] += sums

    @pl.when(step == pl.num_programs(0) - 1)
    def _():
        grad_weight_ref[...] = total[...].T.astype(BF16)


def product_back(left, grad, weight):
    rows, depth = left.shape
    width = grad.shape[1]
    block = rows_block(rows, 512)
    return pl.pallas_call(
        back_kernel,
        grid=(rows // block,),
        out_shape=(
            jax.ShapeDtypeStruct((rows, depth), BF16),
            jax.ShapeDtypeStruct((depth, width), BF16),
            jax.ShapeDtypeStruct((1, width), F32),
        ),
        in_specs=[row_spec(block, depth), row_spec(block, width), whole_block((depth, width))],
        out_specs=(
            row_spec(block, depth),
            pl.BlockSpec((depth, width), lambda i: (0, 0)),
            pl.BlockSpec((1, width), lambda i: (0, 0)),
        ),
        scratch_shapes=[pltpu.VMEM((width, depth), F32)],
        compiler_params=params(),
        cost_estimate=SMALL,
        name="product_back",
    )(left, grad, weight)


def out_back_kernel(att_ref, grad_ref, weight_ref, grad_att_ref, grad_weight_ref, total):
    step = pl.program_id(0)
    grad = grad_ref[...]
    grad_att_ref[...] = nt(grad, weight_ref[...]).astype(BF16)
    term = tn(att_ref[...], grad)

    @pl.when(step == 0)
    def _():
        total[...] = term

    @pl.when(step > 0)
    def _():
        total[...] += term

    @pl.when(step == pl.num_programs(0) - 1)
    def _():
        grad_weight_ref[...] = total[...].astype(BF16)


def out_back(att, grad, weight):
    rows, depth = att.shape
    width = grad.shape[1]
    block = rows_block(rows, 512)
    return pl.pallas_call(
        out_back_kernel,
        grid=(rows // block,),
        out_shape=(jax.ShapeDtypeStruct((rows, depth), BF16), jax.ShapeDtypeStruct((depth, width), BF16)),
        in_specs=[row_spec(block, depth), row_spec(block, width), whole_block((depth, width))],
        out_specs=(row_spec(block, depth), pl.BlockSpec((depth, width), lambda i: (0, 0))),
        scratch_shapes=[pltpu.VMEM((depth, width), F32)],
        compiler_params=params(),
        cost_estimate=SMALL,
        name="out_back",
    )(att, grad, weight)


GELU_A = math.sqrt(2.0 / math.pi)
GELU_B = 0.044715


def up_kernel(h_ref, og_ref, weight_ref, shift_ref, act_ref, slope_ref, grad_ref, total):
    step = pl.program_id(0)
    up = nn(h_ref[...], weight_ref[...]) + shift_ref[...]
    square = up * up
    soft = jnp.tanh(GELU_A * up * (1.0 + GELU_B * square))
    half = 0.5 * (1.0 + soft)
    act = (up * half).astype(BF16)
    act_ref[...] = act
    slope_ref[...] = half + 0.5 * up * (1.0 - soft * soft) * (GELU_A * (1.0 + 3.0 * GELU_B * square))
    term = tn(act, og_ref[...])

    @pl.when(step == 0)
    def _():
        total[...] = term

    @pl.when(step > 0)
    def _():
        total[...] += term

    @pl.when(step == pl.num_programs(0) - 1)
    def _():
        grad_ref[...] = total[...].astype(BF16)


def feed_up(values, out_grad, weight, shift):
    rows, width = values.shape
    hidden = weight.shape[1]
    block = rows_block(rows, 512)
    return pl.pallas_call(
        up_kernel,
        grid=(rows // block,),
        out_shape=(
            jax.ShapeDtypeStruct((rows, hidden), BF16),
            jax.ShapeDtypeStruct((rows, hidden), F32),
            jax.ShapeDtypeStruct((hidden, width), BF16),
        ),
        in_specs=[
            row_spec(block, width),
            row_spec(block, width),
            whole_block((width, hidden)),
            whole_block((1, hidden)),
        ],
        out_specs=(
            row_spec(block, hidden),
            row_spec(block, hidden),
            pl.BlockSpec((hidden, width), lambda i: (0, 0)),
        ),
        scratch_shapes=[pltpu.VMEM((hidden, width), F32)],
        compiler_params=params(),
        cost_estimate=SMALL,
        name="feed_up",
    )(values, out_grad, weight, shift[None, :])


def local(
    tokens,
    block_pairs,
    out_grad,
    ln1_gain,
    ln1_bias,
    qkv_weight,
    query_bias,
    value_bias,
    out_weight,
    out_bias,
    ln2_gain,
    ln2_bias,
    up_weight,
    up_bias,
    down_weight,
    down_bias,
):
    n_ctx, planes = lax.axis_size("ctx"), lax.axis_size("fsdp")
    c, f = lax.axis_index("ctx"), lax.axis_index("fsdp")
    local_rows, seqs, width = tokens.shape
    half = local_rows // 2
    devices = n_ctx * planes
    blocks = 2 * devices
    length = devices * local_rows
    heads = width // HD
    slots = planes * (-(-heads // devices))
    assert slots == planes and planes % seqs == 0
    span = slots * HD
    rows = local_rows * seqs
    plane_rows = n_ctx * rows
    quarter = width // planes
    ff = up_weight.shape[1]
    ff_quarter = ff // planes
    ff_piece = ff_quarter // n_ctx
    ff_span = ff_piece * planes
    tile = 256

    device_ids = jnp.arange(devices, dtype=jnp.int32)
    device_of_block = jnp.sum(
        jnp.where(block_pairs[None, :] == device_ids[:, None], device_ids[None, :], 0), axis=1
    )
    place_of_block = lax.rem(device_of_block, planes) * n_ctx + device_of_block // planes
    order = jnp.concatenate([place_of_block * 2, place_of_block[::-1] * 2 + 1]).astype(jnp.int32)

    first = [-(-quarter * j // HD) for j in range(planes)] + [heads]
    counts = [first[j + 1] - first[j] for j in range(planes)]
    assert max(counts) <= n_ctx
    slot_head = [jnp.minimum(first[j] + c, heads - 1) for j in range(planes)]
    first_own = jnp.asarray(first, jnp.int32)[f]
    count_own = jnp.asarray(counts, jnp.int32)[f]

    pairs = planes // seqs
    pair, pair_span = lax.rem(f, pairs), 2 * HD
    qkv_own = jnp.stack(
        [
            jnp.concatenate(
                [
                    lax.dynamic_slice(qkv_weight, (0, k * width + slot_head[j] * HD), (quarter, HD))
                    for k in range(3)
                    for j in (2 * p, 2 * p + 1)
                ],
                axis=1,
            )
            for p in range(pairs)
        ]
    )
    down_own = lax.dynamic_slice(down_weight, (c * ff_piece, 0), (ff_piece, width))


    tok = jnp.swapaxes(tokens, 0, 1).reshape(rows, width)
    og = jnp.swapaxes(out_grad, 0, 1).reshape(rows, width)

    short = -quarter % LANES
    vector_list = [ln1_gain, ln1_bias, ln2_gain, ln2_bias, query_bias, value_bias, out_bias, down_bias]
    vector_list += [up_bias[k * quarter : (k + 1) * quarter] for k in range(ff // width)]
    packed = jnp.concatenate([jnp.pad(v, (0, short)) for v in vector_list])
    packed = jnp.pad(packed, (0, -packed.size % (16 * LANES))).reshape(-1, LANES)
    up_own = jnp.concatenate(
        [
            lax.dynamic_slice(up_weight, (0, k * ff_quarter + c * ff_piece), (quarter, ff_piece))
            for k in range(planes)
        ],
        axis=1,
    )
    tok_first, up_own = lax.optimization_barrier((tok, up_own))
    vectors, og_all, h1, qkv_slice, next_rows = first_norm_gather(
        tok_first, og, packed, qkv_own, out_weight, n_ctx, planes, seqs
    )
    out_own = lax.dynamic_slice(
        jnp.concatenate([out_weight, next_rows]), ((first_own + c) * HD - f * quarter, 0), (HD, width)
    )
    out_own = jnp.where(c < count_own, out_own, jnp.zeros_like(out_own))
    h1 = h1.reshape(length, width)
    qkv_slice = qkv_slice.reshape(width, 3 * pair_span)
    h1, up_own, down_own = lax.optimization_barrier((h1, up_own, down_own))
    down_slice = lax.all_gather(down_own, "fsdp", axis=0, tiled=True)
    up_slice = lax.all_gather(up_own, "fsdp", axis=0, tiled=True)
    og_all = og_all.reshape(plane_rows, width)
    vectors = vectors.reshape(planes, -1)[:, : len(vector_list) * (quarter + short)]
    vectors = vectors.reshape(planes, len(vector_list), quarter + short)[:, :, :quarter].astype(F32)
    gain1, bias1, gain2, bias2, bias_q, bias_v, bias_o, bias_d = [
        vectors[:, k].reshape(width) for k in range(8)
    ]
    bias_up = lax.dynamic_slice(
        vectors[:, 8 : 8 + ff // width].reshape(planes, ff_quarter), (0, c * ff_piece), (planes, ff_piece)
    ).reshape(ff_span)

    pair_heads = [jnp.minimum(jnp.asarray(first, jnp.int32)[2 * pair + i] + c, heads - 1) for i in range(2)]

    def head_part(vector):
        return [lax.dynamic_slice(vector, (head * HD,), (HD,)) for head in pair_heads]

    qkv_shift = jnp.concatenate(head_part(bias_q) + [jnp.zeros((pair_span,), F32)] + head_part(bias_v))

    if length <= SHORT:
        places, inverse = block_places(order, n_ctx)
        qkv, att_exact, lse, att, out_slice = attend(
            places, inverse, h1, qkv_slice, qkv_shift[None, :], out_own, n_ctx, planes, seqs, half, tile
        )
    else:
        qkv = product(h1, qkv_slice, qkv_shift).reshape(blocks, half, 3 * pair_span)
        att_heads, att_exact, lse = attend_forward(order, qkv, tile)
        att, out_slice = to_tokens(att_heads.reshape(planes, n_ctx, local_rows, LANES), seqs, 6, out_own)
    out_slice = out_slice.reshape(span, width)
    att = att.reshape(plane_rows, span)
    mixed, h2 = second_norm_gather(att, out_slice, tok, jnp.stack([gain2, bias2, bias_o]), n_ctx)
    h2 = h2.reshape(plane_rows, width)
    def reduce_own(part):
        return lax.psum_scatter(part, "fsdp", scatter_dimension=0, tiled=True)

    act, slope, down_part = feed_up(h2, og_all, up_slice, bias_up)
    down_own_grad = reduce_own(down_part)
    d_mixed, sums2, d_branch, out_part, up_part, d_up_sum = feed_back(
        h2, og_all, act, slope, up_slice, down_slice, mixed, og, gain2[None, :]
    )
    up_own_grad = reduce_own(up_part)
    out_part = out_part.reshape(n_ctx, rows, width)
    d_branch = d_branch.reshape(plane_rows, width)
    if length <= SHORT:
        d_qkv, d_qkv_sum, out_w_part, block_out, down_parts = branch_back(
            places,
            inverse,
            d_branch,
            out_slice,
            att,
            qkv,
            att_exact,
            lse,
            down_own_grad,
            out_part,
            mixed,
            bias_d[None, :],
            planes,
            tile,
        )
    else:
        d_att, out_w_part = out_back(att, d_branch, out_slice)
        d_att_heads, down_parts = to_heads(
            d_att.reshape(n_ctx, seqs, local_rows, span), planes, 7, down_own_grad
        )
        d_qkv, d_qkv_sum = attend_backward(
            order, qkv, d_att_heads.reshape(blocks, half, LANES), att_exact, lse, tile
        )
        total = lax.psum_scatter(out_part.reshape(plane_rows, width), "ctx", scatter_dimension=0, tiled=True)
        block_out = (mixed + total.astype(F32) + bias_d).astype(BF16)
    d_qkv, d_qkv_sum = d_qkv.reshape(length, 3 * pair_span), d_qkv_sum[0]
    down_parts, unused = lax.optimization_barrier((down_parts, d_qkv))
    down_grad = down_parts.reshape(ff_quarter, width).astype(F32)
    up_own_grad, down_grad = lax.optimization_barrier((up_own_grad, down_grad))

    d_up_sum = d_up_sum.reshape(planes, ff_piece)
    up_spread = lax.dynamic_update_slice(jnp.zeros((planes, ff_quarter), F32), d_up_sum, (0, c * ff_piece))

    def spread(values):
        full = jnp.zeros((width + HD,), F32)
        for i in range(2):
            slot = 2 * pair + i
            real = c < jnp.asarray(counts, jnp.int32)[slot]
            place = jnp.where(real, pair_heads[i] * HD, width)
            full = lax.dynamic_update_slice(full, values[i * HD : (i + 1) * HD], (place,))
        return full[None, :width]

    wide = jnp.concatenate([sums2, spread(d_qkv_sum[:pair_span]), spread(d_qkv_sum[2 * pair_span :])])
    wide = wide.reshape(6, planes, quarter).transpose(1, 0, 2).reshape(planes, 6 * quarter)
    flat = jnp.concatenate([wide, up_spread], axis=1)
    size = flat.shape[1]
    flat = jnp.pad(flat, ((0, 0), (0, -size % (8 * LANES)))).reshape(planes, -1, LANES)

    if length <= SHORT:
        grad_tok, qkv_parts, up_parts, out_parts, sums1, totals = finish(
            h1,
            d_qkv,
            qkv_slice,
            up_own_grad,
            out_w_part.reshape(planes, HD, width),
            flat,
            tok,
            d_mixed,
            gain1[None, :],
        )
    else:
        d_h1, qkv_part, unused = product_back(h1, d_qkv, qkv_slice)
        grad_tok, qkv_parts, out_parts, sums1, totals = first_norm_back(
            d_h1.reshape(planes, n_ctx, local_rows, width),
            qkv_part.reshape(planes, quarter, 3 * pair_span),
            reduce_own(out_w_part),
            flat,
            tok,
            d_mixed,
            gain1[None, :],
        )
        up_parts = lax.all_gather(up_own_grad, "ctx", axis=0)
    sums1 = sums1[:2, :quarter]
    totals = totals.reshape(-1)
    sums = totals[: 6 * quarter].reshape(6, quarter)
    up_bias_grad = totals[6 * quarter : size]

    block = quarter // 5
    up_pieces = [
        (j * ff_quarter + d * ff_piece, d, j * ff_piece, ff_piece) for j in range(planes) for d in range(n_ctx)
    ]
    up_grad = assemble(up_parts, up_pieces, ff, block)
    qkv_pieces = [
        (k * width + (first[j] + d) * HD, d * pairs + j // 2, k * pair_span + j % 2 * HD, HD)
        for k in range(3)
        for j in range(planes)
        for d in range(counts[j])
    ]
    qkv_grad = assemble(qkv_parts.reshape(n_ctx * pairs, quarter, 3 * pair_span), qkv_pieces, 3 * width, block)
    out_rows = out_parts.reshape(n_ctx * HD, width)
    tail = (f + 1) * quarter - first_own * HD
    tail_rows = lax.dynamic_slice(out_rows, (tail, 0), (HD, width))
    tail_rows = lax.ppermute(tail_rows, "fsdp", [(j, j + 1) for j in range(planes - 1)])
    lead = first_own * HD - f * quarter
    shifted = lax.dynamic_slice(
        jnp.concatenate([jnp.zeros((HD, width), BF16), out_rows]), (HD - lead, 0), (quarter, width)
    )
    from_tail = jnp.concatenate([tail_rows, jnp.zeros((quarter - HD, width), BF16)])
    row_ids = lax.broadcasted_iota(jnp.int32, (quarter, width), 0)
    out_grad_own = jnp.where(row_ids < lead, from_tail, shifted).astype(F32)

    def back(values):
        return jnp.swapaxes(values.reshape(seqs, local_rows, width), 0, 1)

    return (
        back(block_out),
        back(grad_tok),
        sums1[0],
        sums1[1],
        qkv_grad,
        sums[4],
        sums[5],
        out_grad_own,
        sums[2],
        sums[0],
        sums[1],
        up_grad,
        up_bias_grad,
        down_grad,
        sums[3],
    )


def solution(mesh):
    both, row, vec, mat = P(("ctx", "fsdp"), None, None), P(), P("fsdp"), P("fsdp", None)
    in_specs = (both, row, both, vec, vec, mat, vec, vec, mat, vec, vec, vec, mat, vec, mat, vec)
    out_specs = (both, both, vec, vec, mat, vec, vec, mat, vec, vec, vec, mat, vec, mat, vec)
    return jax.shard_map(local, mesh=mesh, in_specs=in_specs, out_specs=out_specs, check_vma=False)
```

```python
import functools
import math

import jax
import jax.numpy as jnp
from jax import lax
from jax.experimental import pallas as pl
from jax.experimental.pallas import tpu as pltpu
from jax.sharding import PartitionSpec as P

HD = 64
LANES = 128
NORM_EPS = 1e-05
NEG_BIG = -1e30
MESH = pl.DeviceIdType.MESH
F32 = jnp.float32
BF16 = jnp.bfloat16
ANY = pl.BlockSpec(memory_space=pl.ANY)
VMEM = pl.BlockSpec(memory_space=pltpu.VMEM)
DMA = pltpu.SemaphoreType.DMA
VMEM_LIMIT = 56 * 1024 * 1024
SMALL = pl.CostEstimate(flops=1, bytes_accessed=1, transcendentals=0)


def params(cid=None):
    if cid is None:
        return pltpu.CompilerParams(vmem_limit_bytes=VMEM_LIMIT)
    return pltpu.CompilerParams(
        collective_id=cid, has_side_effects=True, vmem_limit_bytes=VMEM_LIMIT
    )


def plane_peers(chips):
    me = lax.axis_index("ctx")
    core = lax.rem(me, 2)
    chip = me // 2
    sibling = chip * 2 + 1 - core
    if chips == 4:
        across_x = chip + 1 - 2 * lax.rem(chip, 2)
        across_y = lax.rem(chip + 2, 4)
        corner = lax.rem(across_x + 2, 4)
        first = across_x * (1 - core) + across_y * core
        second = across_y * (1 - core) + across_x * core
        to = come = [first * 2 + core, second * 2 + core, corner * 2 + core]
    else:
        to = [lax.rem(chip + k, chips) * 2 + core for k in range(1, chips)]
        come = [lax.rem(chip + chips - k, chips) * 2 + core for k in range(1, chips)]
    return me, core, chip, sibling, to, come


def greet(plane=(), across=()):
    barrier = pltpu.get_barrier_semaphore()
    for peer in plane:
        pl.semaphore_signal(barrier, inc=1, device_id={"ctx": peer}, device_id_type=MESH)
    for peer in across:
        pl.semaphore_signal(barrier, inc=1, device_id={"fsdp": peer}, device_id_type=MESH)
    pl.semaphore_wait(barrier, len(plane) + len(across))


def other_planes(planes):
    me = lax.axis_index("fsdp")
    return me, [lax.rem(me + k, planes) for k in range(1, planes)]


def send(src, dst, send_sem, recv_sem, axis, peer):
    copy = pltpu.make_async_remote_copy(
        src_ref=src,
        dst_ref=dst,
        send_sem=send_sem,
        recv_sem=recv_sem,
        device_id={axis: peer},
        device_id_type=MESH,
    )
    copy.start()
    return copy


def plane_gather_start(owns, alls, sems, chips):
    far_send, far_recv, near_send, near_recv, local_sem = sems
    me, core, chip, sibling, to, come = plane_peers(chips)
    direct = 2 if chips == 4 else chips - 1
    last = chips - 1
    far, near, local = [], [], []
    for i, (own_ref, all_ref) in enumerate(zip(owns, alls)):
        far.append(
            [
                send(own_ref, all_ref.at[me], far_send.at[i, k], far_recv.at[i, k], "ctx", to[k])
                for k in range(direct)
            ]
        )
        near.append(send(own_ref, all_ref.at[me], near_send.at[i, last], near_recv.at[i, last], "ctx", sibling))
        copy = pltpu.make_async_copy(own_ref, all_ref.at[me], local_sem.at[i])
        copy.start()
        local.append(copy)
    return far, near, local


def plane_gather_pass(started, alls, sems, chips, turns):
    far_send, far_recv, near_send, near_recv, local_sem = sems
    me, core, chip, sibling, to, come = plane_peers(chips)
    far, near, local = started
    for i, all_ref in enumerate(alls):
        for k in turns:
            far[i][k].wait_recv()
            block = all_ref.at[come[k]]
            if chips == 4 and k == 0:
                far[i].append(send(block, block, far_send.at[i, 2], far_recv.at[i, 2], "ctx", to[1]))
            near.append(send(block, block, near_send.at[i, k], near_recv.at[i, k], "ctx", sibling))


def plane_gather_middle(started, alls, sems, chips):
    plane_gather_pass(started, alls, sems, chips, range(2 if chips == 4 else chips - 1))


def plane_gather_end(started, alls, sems, chips):
    plane_gather_pass(started, alls, sems, chips, range(2, chips - 1) if chips == 4 else ())
    far, near, local = started
    for group in far:
        for copy in group:
            copy.wait_send()
    for copy in near + local:
        copy.wait()


def plane_gather_finish(started, alls, sems, chips):
    plane_gather_middle(started, alls, sems, chips)
    plane_gather_end(started, alls, sems, chips)


def plane_gather(owns, alls, sems, chips):
    plane_gather_finish(plane_gather_start(owns, alls, sems, chips), alls, sems, chips)


def plane_scatter_stages(block_of, mine, paired, arrived, sems, chips, result):
    far_send, far_recv, near_send, near_recv, local_sem = sems
    me, core, chip, sibling, to, come = plane_peers(chips)
    targets = to + [me]
    order = [2, 1, 0, 3] if chips == 4 else list(range(chips))
    near, local = [None] * chips, [None] * chips
    crossed = [1, 0, 2, 3] if chips == 4 else list(range(chips))
    for k in order:
        other = targets[crossed[k]] + 1 - 2 * core
        near[k] = send(block_of(other), paired.at[k], near_send.at[k], near_recv.at[k], "ctx", sibling)
        local[k] = pltpu.make_async_copy(block_of(targets[k]), mine.at[k], local_sem.at[k])
        local[k].start()
    yield

    def both(k):
        local[k].wait()
        near[k].wait_recv()
        return mine[k].astype(F32) + paired[k].astype(F32)

    def dispatch(k, target):
        return send(mine.at[k], arrived.at[k], far_send.at[k], far_recv.at[k], "ctx", target)

    far = [None] * (chips - 1)
    if chips == 4:
        mine[2] = both(2).astype(BF16)
        far[2] = dispatch(2, to[0])
        mine[0] = both(0).astype(BF16)
        far[0] = dispatch(0, to[0])
        partial = both(1)
        yield
        far[2].wait_recv()
        mine[1] = (partial + arrived[2].astype(F32)).astype(BF16)
        far[1] = dispatch(1, to[1])
        total = both(3)
        arriving = [0, 1]
    else:
        for k in range(chips - 1):
            mine[k] = both(k).astype(BF16)
            far[k] = dispatch(k, to[k])
        total = both(chips - 1)
        arriving = range(chips - 1)
    yield
    for k in arriving:
        far[k].wait_recv()
        total = total + arrived[k].astype(F32)
    for copy in far + near:
        copy.wait_send()
    result.append(total)


def plane_scatter(block_of, mine, paired, arrived, sems, chips):
    result = []
    for unused in plane_scatter_stages(block_of, mine, paired, arrived, sems, chips, result):
        pass
    return result[0]


def gather_sems(chips, count=1):
    return [DMA((count, chips - 1))] * 2 + [DMA((count, chips))] * 2 + [DMA((count,))]


def scatter_orders(chips):
    if chips == 4:
        return [2, 0, 1, 3], [1, 0, 2, 3]
    return list(range(chips)), list(range(chips))


def plane_scatter_made(make, part, paired, arrived, sems, chips, meanwhile):
    far_send, far_recv, near_send, near_recv = sems
    me, core, chip, sibling, to, come = plane_peers(chips)
    targets = to + [me]
    order, crossed = scatter_orders(chips)
    near, far = [None] * chips, [None] * (chips - 1)

    def produce(k):
        make(k, targets[k] // 2)
        place = crossed[k]
        near[place] = send(
            part.at[k, 1 - core], paired.at[place], near_send.at[place], near_recv.at[place], "ctx", sibling
        )

    def both(k):
        near[k].wait_recv()
        return part[k, core].astype(F32) + paired[k].astype(F32)

    def dispatch(k, values, target):
        paired[k] = values.astype(BF16)
        far[k] = send(paired.at[k], arrived.at[k], far_send.at[k], far_recv.at[k], "ctx", target)

    if chips == 4:
        produce(2)
        produce(0)
        dispatch(2, both(2), to[0])
        produce(1)
        dispatch(0, both(0), to[0])
        produce(3)
        partial = both(1)
        far[2].wait_recv()
        dispatch(1, partial + arrived[2].astype(F32), to[1])
        arriving = [0, 1]
    else:
        for k in order:
            produce(k)
        for k in range(chips - 1):
            dispatch(k, both(k), to[k])
        arriving = range(chips - 1)
    meanwhile()
    total = both(chips - 1)
    for k in arriving:
        far[k].wait_recv()
        total = total + arrived[k].astype(F32)
    for copy in far + near:
        copy.wait_send()
    return total


def made_scratch(chips, *block):
    return [
        pltpu.VMEM((chips, 2) + block, BF16),
        pltpu.VMEM((chips,) + block, BF16),
        pltpu.VMEM((chips - 1,) + block, BF16),
        DMA((chips - 1,)),
        DMA((chips - 1,)),
        DMA((chips,)),
        DMA((chips,)),
    ]


def scatter_scratch(chips, *block):
    return [
        pltpu.VMEM((chips,) + block, BF16),
        pltpu.VMEM((chips,) + block, BF16),
        pltpu.VMEM((chips - 1,) + block, BF16),
        DMA((chips - 1,)),
        DMA((chips - 1,)),
        DMA((chips,)),
        DMA((chips,)),
        DMA((chips,)),
    ]


def normalize(values):
    average = jnp.mean(values, axis=-1, keepdims=True)
    centered = values - average
    variance = jnp.mean(centered * centered, axis=-1, keepdims=True)
    inverse = lax.rsqrt(variance + NORM_EPS)
    return centered * inverse, inverse


def norm_backward(grad, gain, unit, inverse):
    scaled = grad * gain
    first = jnp.mean(scaled, axis=-1, keepdims=True)
    second = jnp.mean(scaled * unit, axis=-1, keepdims=True)
    return (scaled - first - unit * second) * inverse


def first_kernel(
    chips,
    planes,
    seqs,
    quarter,
    tok_ref,
    og_ref,
    vec_ref,
    weight_ref,
    out_w_ref,
    vecs_ref,
    ogs_ref,
    h1_ref,
    weights_ref,
    next_ref,
    own,
    column,
    v_send,
    v_recv,
    v_local,
    h_send,
    h_recv,
    w_send,
    w_recv,
    w_local,
    n_send,
    n_recv,
    n_local,
    *sems,
):
    me, core, chip, sibling, to, come = plane_peers(chips)
    plane, others = other_planes(planes)
    pairs = planes // seqs
    rows = own.shape[0] // seqs
    greet(to + [sibling], others)
    og_sems, h1_sems = sems[:5], [sems[5 + 5 * k : 10 + 5 * k] for k in range(planes)]
    copies = [
        send(vec_ref, vecs_ref.at[plane], v_send.at[k], v_recv.at[k], "fsdp", peer) for k, peer in enumerate(others)
    ]
    local = pltpu.make_async_copy(vec_ref, vecs_ref.at[plane], v_local)
    local.start()
    lead = out_w_ref.at[pl.ds(0, HD)]
    last = plane == planes - 1

    def lead_copy():
        return pltpu.make_async_remote_copy(
            src_ref=lead,
            dst_ref=next_ref,
            send_sem=n_send,
            recv_sem=n_recv,
            device_id={"fsdp": lax.rem(plane + planes - 1, planes)},
            device_id_type=MESH,
        )

    @pl.when(plane > 0)
    def _():
        lead_copy().start()

    @pl.when(last)
    def _():
        pltpu.make_async_copy(lead, next_ref, n_local).start()

    og_started = plane_gather_start([og_ref], [ogs_ref], og_sems, chips)
    unit, inverse = normalize(tok_ref[...].astype(F32))
    for copy in copies + [local]:
        copy.wait()
    lines = quarter // LANES + 1

    def vector(k):
        pieces = []
        for j in range(planes):
            for line in range(lines):
                size = min(LANES, quarter - line * LANES)
                if size:
                    row = k * lines + line
                    pieces.append(vecs_ref[j, row : row + 1, :size].astype(F32))
        return jnp.concatenate(pieces, axis=1)

    own[...] = (unit * vector(0) + vector(1)).astype(BF16)

    def half_of(peer):
        return own.at[pl.ds(pl.multiple_of(peer // pairs * rows, rows), rows)]

    halves = [
        send(half_of(peer), column.at[k], h_send.at[k], h_recv.at[k], "fsdp", peer) for k, peer in enumerate(others)
    ]
    weights = [
        send(weight_ref.at[lax.rem(peer, pairs)], weights_ref.at[plane], w_send.at[k], w_recv.at[k], "fsdp", peer)
        for k, peer in enumerate(others)
    ]
    weights.append(pltpu.make_async_copy(weight_ref.at[lax.rem(plane, pairs)], weights_ref.at[plane], w_local))
    weights[-1].start()
    sources = [plane] + [lax.rem(plane + planes - k, planes) for k in range(1, planes)]
    blocks = [half_of(plane)] + [column.at[k] for k in range(planes - 1)]
    started = [plane_gather_start([blocks[0]], [h1_ref.at[sources[0]]], h1_sems[0], chips)]
    plane_gather_middle(og_started, [ogs_ref], og_sems, chips)
    for k in range(1, planes):
        halves[k - 1].wait_recv()
        started.append(plane_gather_start([blocks[k]], [h1_ref.at[sources[k]]], h1_sems[k], chips))
        plane_gather_middle(started[k - 1], [h1_ref.at[sources[k - 1]]], h1_sems[k - 1], chips)
    plane_gather_middle(started[-1], [h1_ref.at[sources[-1]]], h1_sems[-1], chips)
    plane_gather_end(og_started, [ogs_ref], og_sems, chips)
    for k in range(planes):
        plane_gather_end(started[k], [h1_ref.at[sources[k]]], h1_sems[k], chips)
    @pl.when(plane > 0)
    def _():
        lead_copy().wait_send()

    @pl.when(last)
    def _():
        pltpu.make_async_copy(lead, next_ref, n_local).wait()

    @pl.when(plane < planes - 1)
    def _():
        lead_copy().wait_recv()

    for copy in halves:
        copy.wait_send()
    for copy in weights:
        copy.wait()


def first_norm_gather(tok, og, vec, weight, out_weight, n_ctx, planes, seqs):
    rows, width = tok.shape
    chips, half = n_ctx // 2, rows // seqs
    return pl.pallas_call(
        functools.partial(first_kernel, chips, planes, seqs, width // planes),
        out_shape=(
            jax.ShapeDtypeStruct((planes,) + vec.shape, BF16),
            jax.ShapeDtypeStruct((n_ctx, rows, width), BF16),
            jax.ShapeDtypeStruct((planes, n_ctx, half, width), BF16),
            jax.ShapeDtypeStruct((planes,) + weight.shape[1:], BF16),
            jax.ShapeDtypeStruct((HD, width), BF16),
        ),
        in_specs=[VMEM, ANY, VMEM, ANY, ANY],
        out_specs=(VMEM, ANY, ANY, ANY, ANY),
        scratch_shapes=[
            pltpu.VMEM((rows, width), BF16),
            pltpu.VMEM((planes - 1, half, width), BF16),
            DMA((planes - 1,)),
            DMA((planes - 1,)),
            DMA,
            DMA((planes - 1,)),
            DMA((planes - 1,)),
            DMA((planes - 1,)),
            DMA((planes - 1,)),
            DMA,
            DMA,
            DMA,
            DMA,
        ]
        + gather_sems(chips)
        + gather_sems(chips) * planes,
        compiler_params=params(0),
        cost_estimate=SMALL,
        name="norm_gather",
    )(tok, og, vec, weight, out_weight)


def second_kernel(chips, att_ref, weight_ref, tok_ref, vec_ref, mixed_ref, all_ref, own, *scratch):
    me, core, chip, sibling, to, come = plane_peers(chips)
    greet(to + [sibling])
    rows = tok_ref.shape[0]
    part = scratch[0]

    def make(k, target):
        span = pl.ds(pl.multiple_of(target * 2 * rows, 2 * rows), 2 * rows)
        branch = nn(att_ref[span, :], weight_ref[...]).astype(BF16)
        part[k, 0] = branch[:rows]
        part[k, 1] = branch[rows:]

    total = plane_scatter_made(make, *scratch[:3], scratch[3:7], chips, lambda: None)
    mixed = tok_ref[...].astype(F32) + total + vec_ref[2:3, :]
    mixed_ref[...] = mixed
    unit, inverse = normalize(mixed)
    own[...] = (unit * vec_ref[0:1, :] + vec_ref[1:2, :]).astype(BF16)
    plane_gather([own], [all_ref], scratch[7:], chips)


def second_norm_gather(att, weight, tok, vecs, n_ctx):
    rows, width = tok.shape
    chips = n_ctx // 2
    return pl.pallas_call(
        functools.partial(second_kernel, chips),
        out_shape=(
            jax.ShapeDtypeStruct((rows, width), F32),
            jax.ShapeDtypeStruct((n_ctx, rows, width), BF16),
        ),
        in_specs=[VMEM] * 4,
        out_specs=(VMEM, ANY),
        scratch_shapes=[pltpu.VMEM((rows, width), BF16)]
        + made_scratch(chips, rows, width)
        + gather_sems(chips),
        compiler_params=params(1),
        cost_estimate=SMALL,
        name="scatter_norm_gather",
    )(att, weight, tok, vecs)


def third_kernel(
    chips,
    h_hbm,
    og_hbm,
    act_hbm,
    slope_hbm,
    up_w_hbm,
    down_w_hbm,
    mixed_ref,
    og_ref,
    vec_ref,
    dmixed_ref,
    sums_ref,
    all_ref,
    out_hbm,
    up_grad_ref,
    up_sum_ref,
    h_ref,
    ogs_ref,
    act_ref,
    slope_ref,
    up_w_ref,
    down_w_ref,
    d_up_ref,
    out_ref,
    load_sem,
    out_sem,
    own,
    *scratch,
):
    me, core, chip, sibling, to, come = plane_peers(chips)
    made, gather = scratch[:7], scratch[7:]
    loads = [
        pltpu.make_async_copy(source, target, load_sem.at[k])
        for k, (source, target) in enumerate(
            [
                (down_w_hbm, down_w_ref),
                (og_hbm, ogs_ref),
                (slope_hbm, slope_ref),
                (up_w_hbm, up_w_ref),
                (h_hbm, h_ref),
                (act_hbm, act_ref),
            ]
        )
    ]
    for load in loads:
        load.start()
    greet(to + [sibling])
    unit, inverse = normalize(mixed_ref[...])
    rows = mixed_ref.shape[0]
    for load in loads[:4]:
        load.wait()
    part = made[0]

    def make(k, target):
        span = pl.ds(pl.multiple_of(target * 2 * rows, 2 * rows), 2 * rows)
        d_up = (nt(ogs_ref[span, :], down_w_ref[...]) * slope_ref[span, :]).astype(BF16)
        d_up_ref[span, :] = d_up
        d_h = nt(d_up, up_w_ref[...]).astype(BF16)
        part[k, 0] = d_h[:rows]
        part[k, 1] = d_h[rows:]

    def meanwhile():
        for load in loads[4:]:
            load.wait()
        d_up = d_up_ref[...]
        up_sum_ref[...] = jnp.sum(d_up.astype(F32), axis=0, keepdims=True)
        up_grad_ref[...] = tn(d_up, h_ref[...]).T.astype(BF16)
        out_ref[...] = nn(act_ref[...], down_w_ref[...]).astype(BF16)
        pltpu.make_async_copy(out_ref, out_hbm, out_sem).start()

    grad = plane_scatter_made(make, *made[:3], made[3:], chips, meanwhile)
    out_grad = og_ref[...].astype(F32)
    dmixed = out_grad + norm_backward(grad, vec_ref[0:1, :], unit, inverse)
    low = dmixed.astype(BF16)
    own[...] = low
    started = plane_gather_start([own], [all_ref], gather, chips)
    dmixed_ref[...] = dmixed
    sums_ref[0:1, :] = jnp.sum(grad * unit, axis=0, keepdims=True)
    sums_ref[1:2, :] = jnp.sum(grad, axis=0, keepdims=True)
    sums_ref[2:3, :] = jnp.sum(low.astype(F32), axis=0, keepdims=True)
    sums_ref[3:4, :] = jnp.sum(out_grad, axis=0, keepdims=True)
    plane_gather_finish(started, [all_ref], gather, chips)
    pltpu.make_async_copy(out_ref, out_hbm, out_sem).wait()


def feed_back(values, out_grads, act, slope, up_weight, down_weight, mixed, og, vecs):
    rows, width = mixed.shape
    total_rows, hidden = act.shape
    n_ctx = total_rows // rows
    chips = n_ctx // 2
    return pl.pallas_call(
        functools.partial(third_kernel, chips),
        out_shape=(
            jax.ShapeDtypeStruct((rows, width), F32),
            jax.ShapeDtypeStruct((4, width), F32),
            jax.ShapeDtypeStruct((n_ctx, rows, width), BF16),
            jax.ShapeDtypeStruct((total_rows, width), BF16),
            jax.ShapeDtypeStruct((width, hidden), BF16),
            jax.ShapeDtypeStruct((1, hidden), F32),
        ),
        in_specs=[ANY] * 6 + [VMEM] * 3,
        out_specs=(VMEM, VMEM, ANY, ANY, VMEM, VMEM),
        scratch_shapes=[
            pltpu.VMEM((total_rows, width), BF16),
            pltpu.VMEM((total_rows, width), BF16),
            pltpu.VMEM((total_rows, hidden), BF16),
            pltpu.VMEM((total_rows, hidden), F32),
            pltpu.VMEM((width, hidden), BF16),
            pltpu.VMEM((hidden, width), BF16),
            pltpu.VMEM((total_rows, hidden), BF16),
            pltpu.VMEM((total_rows, width), BF16),
            DMA((6,)),
            DMA,
            pltpu.VMEM((rows, width), BF16),
        ]
        + made_scratch(chips, rows, width)
        + gather_sems(chips),
        compiler_params=params(2),
        cost_estimate=SMALL,
        name="feed_back",
    )(values, out_grads, act, slope, up_weight, down_weight, mixed, og, vecs)


def fourth_kernel(
    chips,
    planes,
    seqs,
    part_ref,
    qkv_ref,
    outw_ref,
    flat_ref,
    tok_ref,
    dmixed_ref,
    vec_ref,
    grad_ref,
    qkv_all,
    outw_all,
    sums_ref,
    flat_out,
    q_arrived,
    q_own,
    q_send,
    q_recv,
    q_local,
    rows_own,
    rows_arrived,
    r_send,
    r_recv,
    small,
    small_own,
    small_z,
    small_c,
    flat_own,
    flat_z,
    flat_c,
    z_send,
    z_recv,
    c_send,
    c_recv,
    *scratch,
):
    n_ctx = 2 * chips
    pairs = planes // seqs
    me, core, chip, sibling, to, come = plane_peers(chips)
    plane, others = other_planes(planes)
    around = [lax.rem(me + k, n_ctx) for k in range(1, n_ctx)]
    greet(around, others)
    scatter, rest_sems, qkv_sems = scratch[:8], scratch[8:13], scratch[13:]

    pushed = [
        send(qkv_ref.at[peer], q_arrived.at[plane], q_send.at[k], q_recv.at[k], "fsdp", peer)
        for k, peer in enumerate(others)
    ]
    held = pltpu.make_async_copy(qkv_ref.at[plane], q_arrived.at[plane], q_local)
    held.start()
    flat_sent = [
        send(flat_ref.at[peer], flat_z.at[k], z_send.at[0, k], z_recv.at[0, k], "fsdp", peer)
        for k, peer in enumerate(others)
    ]
    unit, inverse = normalize(tok_ref[...].astype(F32))
    total = plane_scatter(lambda c: part_ref.at[:, c], *scatter[:3], scatter[3:], chips)
    rows_own[...] = total.astype(BF16)
    rows_sent = [
        send(rows_own.at[peer], rows_arrived.at[plane], r_send.at[k], r_recv.at[k], "fsdp", peer)
        for k, peer in enumerate(others)
    ]
    rows_arrived[plane] = rows_own[plane]
    rest_started = plane_gather_start([outw_ref], [outw_all], rest_sems, chips)
    for copy in pushed + [held]:
        copy.wait()
    for pair in range(pairs):
        terms = [q_arrived[seq * pairs + pair].astype(F32) for seq in range(seqs)]
        q_own[pair] = sum(terms[1:], terms[0]).astype(BF16)
    qkv_started = plane_gather_start([q_own], [qkv_all], qkv_sems, chips)
    plane_gather_finish(rest_started, [outw_all], rest_sems, chips)

    for copy in rows_sent:
        copy.wait()
    halves = []
    for seq in range(seqs):
        terms = [rows_arrived[seq * pairs + pair].astype(F32) for pair in range(pairs)]
        halves.append(sum(terms[1:], terms[0]))
    grad = jnp.concatenate(halves, axis=0)
    sums = jnp.concatenate(
        [jnp.sum(grad * unit, axis=0, keepdims=True), jnp.sum(grad, axis=0, keepdims=True)], axis=0
    )
    quarter = sums.shape[1] // planes
    small[...] = jnp.zeros_like(small)
    for j in range(planes):
        small[j, 0:2, 0:quarter] = sums[:, j * quarter : (j + 1) * quarter]
    small_sent = [
        send(small.at[peer], small_z.at[k], z_send.at[1, k], z_recv.at[1, k], "fsdp", peer)
        for k, peer in enumerate(others)
    ]
    grad_ref[...] = dmixed_ref[...] + norm_backward(grad, vec_ref[0:1, :], unit, inverse)
    small_total = small[plane]
    flat_total = flat_ref[plane]
    for k in range(planes - 1):
        flat_sent[k].wait()
        small_sent[k].wait()
        small_total = small_total + small_z[k]
        flat_total = flat_total + flat_z[k]
    small_own[...] = small_total
    flat_own[...] = flat_total
    sent = []
    for k, peer in enumerate(around):
        sent.append(send(small_own, small_c.at[k], c_send.at[0, k], c_recv.at[0, k], "ctx", peer))
        sent.append(send(flat_own, flat_c.at[k], c_send.at[1, k], c_recv.at[1, k], "ctx", peer))
    plane_gather_finish(qkv_started, [qkv_all], qkv_sems, chips)
    for copy in sent:
        copy.wait()
    for k in range(n_ctx - 1):
        small_total = small_total + small_c[k]
        flat_total = flat_total + flat_c[k]
    sums_ref[...] = small_total
    flat_out[...] = flat_total


def first_norm_back(part, qkv_part, outw_own, flat, tok, dmixed, vecs):
    planes, n_ctx, half, width = part.shape
    rows = tok.shape[0]
    seqs = rows // half
    quarter, columns = qkv_part.shape[1:]
    chips, pairs = n_ctx // 2, planes // seqs
    size = (8, quarter + -quarter % LANES)
    return pl.pallas_call(
        functools.partial(fourth_kernel, chips, planes, seqs),
        out_shape=(
            jax.ShapeDtypeStruct((rows, width), F32),
            jax.ShapeDtypeStruct((n_ctx, pairs, quarter, columns), BF16),
            jax.ShapeDtypeStruct((n_ctx,) + outw_own.shape, BF16),
            jax.ShapeDtypeStruct(size, F32),
            jax.ShapeDtypeStruct(flat.shape[1:], F32),
        ),
        in_specs=[ANY, ANY, ANY, VMEM, VMEM, VMEM, VMEM],
        out_specs=(VMEM, ANY, ANY, VMEM, VMEM),
        scratch_shapes=[
            pltpu.VMEM((planes, quarter, columns), BF16),
            pltpu.VMEM((pairs, quarter, columns), BF16),
            DMA((planes - 1,)),
            DMA((planes - 1,)),
            DMA,
            pltpu.VMEM((planes, half, width), BF16),
            pltpu.VMEM((planes, half, width), BF16),
            DMA((planes - 1,)),
            DMA((planes - 1,)),
            pltpu.VMEM((planes,) + size, F32),
            pltpu.VMEM(size, F32),
            pltpu.VMEM((planes - 1,) + size, F32),
            pltpu.VMEM((n_ctx - 1,) + size, F32),
            pltpu.VMEM(flat.shape[1:], F32),
            pltpu.VMEM((planes - 1,) + flat.shape[1:], F32),
            pltpu.VMEM((n_ctx - 1,) + flat.shape[1:], F32),
            DMA((2, planes - 1)),
            DMA((2, planes - 1)),
            DMA((2, n_ctx - 1)),
            DMA((2, n_ctx - 1)),
        ]
        + scatter_scratch(chips, planes, half, width)
        + gather_sems(chips)
        + gather_sems(chips),
        compiler_params=params(3),
        cost_estimate=SMALL,
        name="scatter_back",
    )(part, qkv_part, outw_own, flat, tok, dmixed, vecs)


def finish_kernel(
    chips,
    planes,
    seqs,
    counts,
    h1_hbm,
    d_hbm,
    w_hbm,
    up_ref,
    outw_ref,
    flat_ref,
    tok_ref,
    dmixed_ref,
    vec_ref,
    grad_ref,
    qkv_all,
    up_all,
    outw_all,
    tail_ref,
    sums_ref,
    flat_out,
    h1_ref,
    d_ref,
    w_ref,
    load_sem,
    dw_ref,
    q_arrived,
    q_own,
    q_send,
    q_recv,
    outw_arrived,
    outw_own,
    o_send,
    o_recv,
    rows_own,
    rows_arrived,
    r_send,
    r_recv,
    small,
    small_own,
    small_z,
    small_c,
    flat_own,
    flat_z,
    flat_c,
    z_send,
    z_recv,
    c_send,
    c_recv,
    t_send,
    t_recv,
    *scratch,
):
    n_ctx = 2 * chips
    pairs = planes // seqs
    me, core, chip, sibling, to, come = plane_peers(chips)
    plane, others = other_planes(planes)
    around = [lax.rem(me + k, n_ctx) for k in range(1, n_ctx)]
    made, outw_sems, qkv_sems, up_sems = scratch[:7], scratch[7:12], scratch[12:17], scratch[17:]
    loads = [
        pltpu.make_async_copy(source, target, load_sem.at[k])
        for k, (source, target) in enumerate([(d_hbm, d_ref), (h1_hbm, h1_ref), (w_hbm, w_ref)])
    ]
    for load in loads:
        load.start()
    greet(around, others)
    up_started = plane_gather_start([up_ref], [up_all], up_sems, chips)
    outw_sent = [
        send(outw_ref.at[peer], outw_arrived.at[k], o_send.at[k], o_recv.at[k], "fsdp", peer)
        for k, peer in enumerate(others)
    ]
    flat_sent = [
        send(flat_ref.at[peer], flat_z.at[k], z_send.at[0, k], z_recv.at[0, k], "fsdp", peer)
        for k, peer in enumerate(others)
    ]
    unit, inverse = normalize(tok_ref[...].astype(F32))

    for load in loads:
        load.wait()
    quarter = dw_ref.shape[1]
    dw = tn(d_ref[...], h1_ref[...]).T.astype(BF16)
    for j in range(planes):
        dw_ref[j] = dw[j * quarter : (j + 1) * quarter]
    pushed = [
        send(dw_ref.at[peer], q_arrived.at[plane], q_send.at[k], q_recv.at[k], "fsdp", peer)
        for k, peer in enumerate(others)
    ]
    q_arrived[plane] = dw_ref[plane]

    part = made[0]
    half = part.shape[3]

    calls = []

    def make(k, target):
        calls.append(k)
        if len(calls) == chips - 1:
            plane_gather_middle(up_started, [up_all], up_sems, chips)
        blocks = []
        for j in range(planes):
            start = pl.multiple_of(j * n_ctx * half + target * 2 * half, 2 * half)
            blocks.append(d_ref[pl.ds(start, 2 * half), :])
        d_h = nt(jnp.concatenate(blocks, axis=0), w_ref[...]).astype(BF16)
        for j in range(planes):
            for side in range(2):
                start = (2 * j + side) * half
                part[k, side, j] = d_h[start : start + half]

    total = plane_scatter_made(make, *made[:3], made[3:], chips, lambda: None)
    rows_own[...] = total.astype(BF16)
    rows_sent = [
        send(rows_own.at[peer], rows_arrived.at[plane], r_send.at[k], r_recv.at[k], "fsdp", peer)
        for k, peer in enumerate(others)
    ]
    rows_arrived[plane] = rows_own[plane]

    total = outw_ref[plane].astype(F32)
    for k, copy in enumerate(outw_sent):
        copy.wait()
        total = total + outw_arrived[k].astype(F32)
    outw_own[...] = total.astype(BF16)
    outw_started = plane_gather_start([outw_own], [outw_all], outw_sems, chips)
    for copy in pushed:
        copy.wait()
    for pair in range(pairs):
        terms = [q_arrived[seq * pairs + pair].astype(F32) for seq in range(seqs)]
        q_own[pair] = sum(terms[1:], terms[0]).astype(BF16)
    qkv_started = plane_gather_start([q_own], [qkv_all], qkv_sems, chips)
    plane_gather_middle(outw_started, [outw_all], outw_sems, chips)
    plane_gather_middle(qkv_started, [qkv_all], qkv_sems, chips)

    for copy in rows_sent:
        copy.wait()
    halves = []
    for seq in range(seqs):
        terms = [rows_arrived[seq * pairs + pair].astype(F32) for pair in range(pairs)]
        halves.append(sum(terms[1:], terms[0]))
    grad = jnp.concatenate(halves, axis=0)
    sums = jnp.concatenate(
        [jnp.sum(grad * unit, axis=0, keepdims=True), jnp.sum(grad, axis=0, keepdims=True)], axis=0
    )
    small[...] = jnp.zeros_like(small)
    for j in range(planes):
        small[j, 0:2, 0:quarter] = sums[:, j * quarter : (j + 1) * quarter]
    small_sent = [
        send(small.at[peer], small_z.at[k], z_send.at[1, k], z_recv.at[1, k], "fsdp", peer)
        for k, peer in enumerate(others)
    ]
    grad_ref[...] = dmixed_ref[...] + norm_backward(grad, vec_ref[0:1, :], unit, inverse)
    small_total = small[plane]
    flat_total = flat_ref[plane]
    for k in range(planes - 1):
        flat_sent[k].wait()
        small_sent[k].wait()
        small_total = small_total + small_z[k]
        flat_total = flat_total + flat_z[k]
    small_own[...] = small_total
    flat_own[...] = flat_total
    sent = []
    for k, peer in enumerate(around):
        sent.append(send(small_own, small_c.at[k], c_send.at[0, k], c_recv.at[0, k], "ctx", peer))
        sent.append(send(flat_own, flat_c.at[k], c_send.at[1, k], c_recv.at[1, k], "ctx", peer))
    plane_gather_end(outw_started, [outw_all], outw_sems, chips)
    last_head = sum((plane == j).astype(jnp.int32) * (counts[j] - 1) for j in range(planes))

    def tail_copy():
        return pltpu.make_async_remote_copy(
            src_ref=outw_all.at[last_head],
            dst_ref=tail_ref,
            send_sem=t_send,
            recv_sem=t_recv,
            device_id={"fsdp": lax.rem(plane + 1, planes)},
            device_id_type=MESH,
        )

    @pl.when(plane < planes - 1)
    def _():
        tail_copy().start()

    plane_gather_end(qkv_started, [qkv_all], qkv_sems, chips)
    plane_gather_end(up_started, [up_all], up_sems, chips)
    for copy in sent:
        copy.wait()
    for k in range(n_ctx - 1):
        small_total = small_total + small_c[k]
        flat_total = flat_total + flat_c[k]
    @pl.when(plane < planes - 1)
    def _():
        tail_copy().wait_send()

    @pl.when(plane > 0)
    def _():
        tail_copy().wait_recv()

    sums_ref[...] = small_total
    flat_out[...] = flat_total


def finish(h1, d_qkv, weight, up_own, outw_part, flat, tok, dmixed, vecs, counts):
    rows, width = tok.shape
    planes = outw_part.shape[0]
    n_ctx = lax.axis_size("ctx")
    half = h1.shape[0] // (planes * n_ctx)
    seqs = rows // half
    quarter, columns = width // planes, weight.shape[1]
    chips, pairs = n_ctx // 2, planes // seqs
    size = (8, quarter + -quarter % LANES)
    piece = outw_part.shape[1:]
    return pl.pallas_call(
        functools.partial(finish_kernel, chips, planes, seqs, counts),
        out_shape=(
            jax.ShapeDtypeStruct((rows, width), F32),
            jax.ShapeDtypeStruct((n_ctx, pairs, quarter, columns), BF16),
            jax.ShapeDtypeStruct((n_ctx,) + up_own.shape, BF16),
            jax.ShapeDtypeStruct((n_ctx,) + piece, BF16),
            jax.ShapeDtypeStruct(piece, BF16),
            jax.ShapeDtypeStruct(size, F32),
            jax.ShapeDtypeStruct(flat.shape[1:], F32),
        ),
        in_specs=[ANY] * 4 + [VMEM] * 5,
        out_specs=(VMEM, ANY, ANY, ANY, ANY, VMEM, VMEM),
        scratch_shapes=[
            pltpu.VMEM(h1.shape, BF16),
            pltpu.VMEM(d_qkv.shape, BF16),
            pltpu.VMEM(weight.shape, BF16),
            DMA((3,)),
            pltpu.VMEM((planes, quarter, columns), BF16),
            pltpu.VMEM((planes, quarter, columns), BF16),
            pltpu.VMEM((pairs, quarter, columns), BF16),
            DMA((planes - 1,)),
            DMA((planes - 1,)),
            pltpu.VMEM((planes - 1,) + piece, BF16),
            pltpu.VMEM(piece, BF16),
            DMA((planes - 1,)),
            DMA((planes - 1,)),
            pltpu.VMEM((planes, half, width), BF16),
            pltpu.VMEM((planes, half, width), BF16),
            DMA((planes - 1,)),
            DMA((planes - 1,)),
            pltpu.VMEM((planes,) + size, F32),
            pltpu.VMEM(size, F32),
            pltpu.VMEM((planes - 1,) + size, F32),
            pltpu.VMEM((n_ctx - 1,) + size, F32),
            pltpu.VMEM(flat.shape[1:], F32),
            pltpu.VMEM((planes - 1,) + flat.shape[1:], F32),
            pltpu.VMEM((n_ctx - 1,) + flat.shape[1:], F32),
            DMA((2, planes - 1)),
            DMA((2, planes - 1)),
            DMA((2, n_ctx - 1)),
            DMA((2, n_ctx - 1)),
            DMA,
            DMA,
        ]
        + made_scratch(chips, planes, half, width)
        + gather_sems(chips)
        + gather_sems(chips)
        + gather_sems(chips),
        compiler_params=params(9),
        cost_estimate=SMALL,
        name="finish",
    )(h1, d_qkv, weight, up_own, outw_part, flat, tok, dmixed, vecs)


def to_heads_kernel(
    planes, seqs, chips, tok_ref, down_ref, head_ref, down_all, send_sems, recv_sems, local_sem, *sems
):
    ctx_me, core, chip, sibling, to, come = plane_peers(chips)
    me, others = other_planes(planes)
    pairs = planes // seqs
    greet(to + [sibling], others)

    def source(unit):
        start = pl.multiple_of(lax.rem(unit, pairs) * LANES, LANES)
        return tok_ref.at[:, unit // pairs, :, pl.ds(start, LANES)]

    copies = [
        send(source(unit), head_ref.at[me], send_sems.at[k], recv_sems.at[k], "fsdp", unit)
        for k, unit in enumerate(others)
    ]
    copies.append(pltpu.make_async_copy(source(me), head_ref.at[me], local_sem))
    copies[-1].start()
    plane_gather([down_ref], [down_all], sems, chips)
    for copy in copies:
        copy.wait()


def to_heads(tok, planes, cid, down_own):
    n_ctx, seqs, local_rows, width = tok.shape
    chips = n_ctx // 2
    return pl.pallas_call(
        functools.partial(to_heads_kernel, planes, seqs, chips),
        out_shape=(
            jax.ShapeDtypeStruct((planes, n_ctx, local_rows, LANES), BF16),
            jax.ShapeDtypeStruct((n_ctx,) + down_own.shape, BF16),
        ),
        in_specs=[ANY, ANY],
        out_specs=(ANY, ANY),
        scratch_shapes=[DMA((planes - 1,)), DMA((planes - 1,)), DMA] + gather_sems(chips),
        compiler_params=params(cid),
        cost_estimate=SMALL,
        name="to_heads",
    )(tok, down_own)


def to_tokens_kernel(
    planes, seqs, head_ref, weight_ref, tok_ref, weights_ref, send_sems, recv_sems, local_sem, w_send, w_recv, w_local
):
    me, others = other_planes(planes)
    pairs = planes // seqs
    greet((), others)
    start = pl.multiple_of(lax.rem(me, pairs) * LANES, LANES)
    target = tok_ref.at[:, me // pairs, :, pl.ds(start, LANES)]
    copies = [
        send(head_ref.at[peer], target, send_sems.at[k], recv_sems.at[k], "fsdp", peer) for k, peer in enumerate(others)
    ]
    copies += [
        send(weight_ref, weights_ref.at[me], w_send.at[k], w_recv.at[k], "fsdp", peer) for k, peer in enumerate(others)
    ]
    for copy in (
        pltpu.make_async_copy(head_ref.at[me], target, local_sem),
        pltpu.make_async_copy(weight_ref, weights_ref.at[me], w_local),
    ):
        copy.start()
        copies.append(copy)
    for copy in copies:
        copy.wait()


def to_tokens(heads, seqs, cid, weight):
    planes, n_ctx, rows, lanes = heads.shape
    width = (planes // seqs) * LANES
    return pl.pallas_call(
        functools.partial(to_tokens_kernel, planes, seqs),
        out_shape=(
            jax.ShapeDtypeStruct((n_ctx, seqs, rows, width), heads.dtype),
            jax.ShapeDtypeStruct((planes,) + weight.shape, BF16),
        ),
        in_specs=[ANY] * 2,
        out_specs=(ANY,) * 2,
        scratch_shapes=[DMA((planes - 1,)), DMA((planes - 1,)), DMA] * 2,
        compiler_params=params(cid),
        cost_estimate=SMALL,
        name="to_tokens",
    )(heads, weight)


def nt(left, right):
    return lax.dot_general(left, right, (((1,), (1,)), ((), ())), preferred_element_type=F32)


def nn(left, right):
    return lax.dot_general(left, right, (((1,), (0,)), ((), ())), preferred_element_type=F32)


def sort_blocks(order_ref, qkv_ref, targets, blocks, half):
    def body(block, carry):
        row = qkv_ref[order_ref[block]]
        start = pl.multiple_of(block * half, half)
        for k, target in enumerate(targets):
            target[pl.ds(start, half), :] = row[:, k * LANES : (k + 1) * LANES]
        return carry

    lax.fori_loop(0, blocks, body, 0)


def lane_mask(rows, head):
    lane = lax.broadcasted_iota(jnp.int32, (rows, LANES), 1)
    return (lane < HD) if head == 0 else (lane >= HD)


def unsort_blocks(order_ref, sorted_refs, target_ref, blocks, half):
    def body(block, carry):
        start = pl.multiple_of(block * half, half)
        place = order_ref[block]
        for k, source in enumerate(sorted_refs):
            target_ref[place, :, k * LANES : (k + 1) * LANES] = source[pl.ds(start, half), :].astype(BF16)
        return carry

    lax.fori_loop(0, blocks, body, 0)


def long_forward_kernel(tile, order_ref, qkv_ref, out_ref, att_ref, lse_ref, q_s, k_s, v_s, vt_s, o_s):
    blocks, half = out_ref.shape[0], out_ref.shape[1]
    length = blocks * half
    tiles = length // tile
    sort_blocks(order_ref, qkv_ref, [q_s, k_s, v_s], blocks, half)
    for t in range(tiles):
        span = slice(t * tile, (t + 1) * tile)
        vt_s[:, span] = v_s[span, :].T
    scale = HD ** (-0.5)
    rows_iota = lax.broadcasted_iota(jnp.int32, (tile, tile), 0)
    cols_iota = lax.broadcasted_iota(jnp.int32, (tile, tile), 1)
    allowed = rows_iota <= cols_iota
    masks = [lane_mask(tile, head) for head in range(2)]

    for qt in range(tiles):
        q_span = slice(qt * tile, (qt + 1) * tile)
        query = q_s[q_span, :] * jnp.asarray(scale, BF16)
        queries = [jnp.where(masks[head], query, jnp.zeros_like(query)) for head in range(2)]

        def step(kt, state, masked, queries=queries):
            start = pl.multiple_of(kt * tile, tile)
            keys = k_s[pl.ds(start, tile), :]
            new = []
            for head in range(2):
                top, total, acc = state[head]
                scores = nt(keys, queries[head])
                if masked:
                    scores = jnp.where(allowed, scores, NEG_BIG)
                new_top = jnp.maximum(top, jnp.max(scores, axis=0, keepdims=True))
                soft = jnp.exp(scores - new_top)
                factor = jnp.exp(top - new_top)
                total = total * factor + jnp.sum(soft, axis=0, keepdims=True)
                values = vt_s[head * HD : (head + 1) * HD, pl.ds(start, tile)]
                acc = acc * factor + nn(values, soft.astype(BF16))
                new.append((new_top, total, acc))
            return tuple(new)

        state = tuple(
            (jnp.full((1, tile), NEG_BIG, F32), jnp.zeros((1, tile), F32), jnp.zeros((HD, tile), F32))
            for head in range(2)
        )
        state = step(qt, state, True)
        if qt > 0:
            state = lax.fori_loop(0, qt, lambda kt, s, step=step: step(kt, s, False), state)
        parts = []
        for head in range(2):
            top, total, acc = state[head]
            parts.append(acc / total)
            lse_ref[head : head + 1, q_span] = top + jnp.log(total)
        att = jnp.concatenate(parts, axis=0).T
        att_ref[q_span, :] = att
        o_s[q_span, :] = att.astype(BF16)

    unsort_blocks(order_ref, [o_s], out_ref, blocks, half)


def block_places(order, n_ctx):
    blocks = order.shape[0]
    places = jnp.stack([order // (2 * n_ctx), lax.rem(order // 2, n_ctx), lax.rem(order, 2)]).astype(jnp.int32)
    match = order[:, None] == jnp.arange(blocks)[None, :]
    inverse = jnp.sum(jnp.where(match, jnp.arange(blocks)[:, None], 0), axis=0).astype(jnp.int32)
    return places, inverse


def sort_places(order_ref, source, targets):
    blocks, half = order_ref.shape[1], source.shape[3]

    def body(block, carry):
        row = source[order_ref[0, block], order_ref[1, block], order_ref[2, block]]
        start = pl.multiple_of(block * half, half)
        for k, target in enumerate(targets):
            target[pl.ds(start, half), :] = row[:, k * LANES : (k + 1) * LANES]
        return carry

    lax.fori_loop(0, blocks, body, 0)


def unsort_places(place_ref, sources, target):
    n_ctx = target.shape[1]

    def body(place, carry):
        block = place_ref[place]
        f, c, side = place // (2 * n_ctx), lax.rem(place // 2, n_ctx), lax.rem(place, 2)
        for k, source in enumerate(sources):
            target[f, c, side, :, k * LANES : (k + 1) * LANES] = source[block]
        return carry

    lax.fori_loop(0, place_ref.shape[0], body, 0)


def attend_kernel(
    tile,
    planes,
    seqs,
    order_ref,
    place_ref,
    h1_hbm,
    w_hbm,
    shift_ref,
    out_w_ref,
    qkv_ref,
    att_ref,
    lse_ref,
    tok_ref,
    out_ws_ref,
    h1_ref,
    w_ref,
    load_sem,
    heads,
    a_send,
    a_recv,
    a_local,
    w_send,
    w_recv,
    w_local,
    q_s,
    k_s,
    v_s,
    o_s,
    s_s,
    p_s,
):
    me, others = other_planes(planes)
    pairs = planes // seqs
    n_ctx, half = qkv_ref.shape[1], qkv_ref.shape[3]
    length = att_ref.shape[0]
    tiles, step = length // tile, tile // half
    rows = length // planes
    loads = [pltpu.make_async_copy(w_hbm, w_ref, load_sem.at[planes])]
    for j in range(planes):
        span = pl.ds(j * rows, rows)
        loads.append(pltpu.make_async_copy(h1_hbm.at[span], h1_ref.at[span], load_sem.at[j]))
    for load in loads:
        load.start()
    greet((), others)
    moved = [
        send(out_w_ref, out_ws_ref.at[me], w_send.at[k], w_recv.at[k], "fsdp", peer) for k, peer in enumerate(others)
    ]
    moved.append(pltpu.make_async_copy(out_w_ref, out_ws_ref.at[me], w_local))
    moved[-1].start()

    loads[0].wait()
    for j in range(planes):
        loads[1 + j].wait()
        values = nn(h1_ref[j * rows : (j + 1) * rows, :], w_ref[...]) + shift_ref[...]
        qkv_ref[j] = values.astype(BF16).reshape(n_ctx, 2, half, values.shape[1])

    sort_places(order_ref, qkv_ref, [q_s, k_s, v_s])
    scale = HD ** (-0.5)
    rows_iota = lax.broadcasted_iota(jnp.int32, (tile, tile), 0)
    cols_iota = lax.broadcasted_iota(jnp.int32, (tile, tile), 1)
    allowed = cols_iota <= rows_iota
    masks = [lane_mask(tile, head) for head in range(2)]
    for qt in range(tiles):
        q_span = slice(qt * tile, (qt + 1) * tile)
        query = q_s[q_span, :] * jnp.asarray(scale, BF16)
        parts = []
        for head in range(2):
            one = jnp.where(masks[head], query, jnp.zeros_like(query))
            top = jnp.full((tile, LANES), NEG_BIG, F32)
            for kt in range(qt + 1):
                k_span = slice(kt * tile, (kt + 1) * tile)
                scores = nt(one, k_s[k_span, :])
                if kt == qt:
                    scores = jnp.where(allowed, scores, NEG_BIG)
                s_s[head, :, k_span] = scores
                for lane in range(0, tile, LANES):
                    top = jnp.maximum(top, scores[:, lane : lane + LANES])
            top = jnp.max(top, axis=1, keepdims=True)
            total = jnp.zeros((tile, LANES), F32)
            for kt in range(qt + 1):
                k_span = slice(kt * tile, (kt + 1) * tile)
                soft = jnp.exp(s_s[head, :, k_span] - top)
                for lane in range(0, tile, LANES):
                    total = total + soft[:, lane : lane + LANES]
                p_s[head, :, k_span] = soft.astype(BF16)
            total = jnp.sum(total, axis=1, keepdims=True)
            span = slice(0, (qt + 1) * tile)
            parts.append(nn(p_s[head, :, span], v_s[span, :]) / total)
            lse = jnp.broadcast_to(top + jnp.log(total), (tile, LANES))
            lse_ref[head : head + 1, q_span] = lse.T[0:1, :]
        att = jnp.where(masks[0], parts[0], parts[1])
        att_ref[q_span, :] = att
        o_s[qt * step : (qt + 1) * step] = att.astype(BF16).reshape(step, half, LANES)
    unsort_places(place_ref, [o_s], heads)

    start = pl.multiple_of(lax.rem(me, pairs) * LANES, LANES)
    target = tok_ref.at[:, me // pairs, :, :, pl.ds(start, LANES)]
    moved += [
        send(heads.at[peer], target, a_send.at[k], a_recv.at[k], "fsdp", peer) for k, peer in enumerate(others)
    ]
    moved.append(pltpu.make_async_copy(heads.at[me], target, a_local))
    moved[-1].start()
    for copy in moved:
        copy.wait()


def attend(places, inverse, h1, weight, shift, out_own, n_ctx, planes, seqs, half, tile):
    length = h1.shape[0]
    lanes = weight.shape[1]
    blocks = length // half
    width = (planes // seqs) * LANES
    rows_s = pltpu.VMEM((length, LANES), BF16)
    sems = [DMA((planes - 1,)), DMA((planes - 1,)), DMA]
    return pl.pallas_call(
        functools.partial(attend_kernel, tile, planes, seqs),
        out_shape=(
            jax.ShapeDtypeStruct((planes, n_ctx, 2, half, lanes), BF16),
            jax.ShapeDtypeStruct((length, LANES), F32),
            jax.ShapeDtypeStruct((2, length), F32),
            jax.ShapeDtypeStruct((n_ctx, seqs, 2, half, width), BF16),
            jax.ShapeDtypeStruct((planes,) + out_own.shape, BF16),
        ),
        in_specs=[SMEM, SMEM, ANY, ANY, VMEM, ANY],
        out_specs=(VMEM, VMEM, VMEM, ANY, ANY),
        scratch_shapes=[
            pltpu.VMEM(h1.shape, BF16),
            pltpu.VMEM(weight.shape, BF16),
            DMA((planes + 1,)),
            pltpu.VMEM((planes, n_ctx, 2, half, LANES), BF16),
        ]
        + sems
        + sems
        + [rows_s, rows_s, rows_s, pltpu.VMEM((blocks, half, LANES), BF16)]
        + [pltpu.VMEM((2, tile, length), F32), pltpu.VMEM((2, tile, length), BF16)],
        compiler_params=params(5),
        cost_estimate=SMALL,
        name="attend",
    )(places, inverse, h1, weight, shift, out_own)


SMEM = pl.BlockSpec(memory_space=pltpu.SMEM)
SHORT = 2048


def attend_forward(order, qkv, tile):
    blocks, half, lanes = qkv.shape
    length = blocks * half
    rows = pltpu.VMEM((length, LANES), BF16)
    return pl.pallas_call(
        functools.partial(long_forward_kernel, tile),
        out_shape=(
            jax.ShapeDtypeStruct((blocks, half, LANES), BF16),
            jax.ShapeDtypeStruct((length, LANES), F32),
            jax.ShapeDtypeStruct((2, length), F32),
        ),
        in_specs=[SMEM, VMEM],
        out_specs=(VMEM, VMEM, VMEM),
        scratch_shapes=[rows, rows, rows, pltpu.VMEM((LANES, length), BF16), rows],
        compiler_params=params(),
        cost_estimate=SMALL,
        name="attend_forward",
    )(order, qkv)


def long_backward_kernel(
    tile, order_ref, qkv_ref, grad_ref, att_ref, lse_ref, out_ref, sum_ref, q_s, k_s, v_s, g_s, kt_s, dq_s, dk_s, dv_s
):
    blocks, half = grad_ref.shape[0], grad_ref.shape[1]
    length = blocks * half
    tiles = length // tile
    sort_blocks(order_ref, qkv_ref, [q_s, k_s, v_s], blocks, half)
    sort_blocks(order_ref, grad_ref, [g_s], blocks, half)
    for t in range(tiles):
        span = slice(t * tile, (t + 1) * tile)
        kt_s[:, span] = k_s[span, :].T
    scale = HD ** (-0.5)
    rows_iota = lax.broadcasted_iota(jnp.int32, (tile, tile), 0)
    cols_iota = lax.broadcasted_iota(jnp.int32, (tile, tile), 1)
    allowed = rows_iota <= cols_iota
    masks = [lane_mask(tile, head) for head in range(2)]
    dk_s[...] = jnp.zeros_like(dk_s)
    dv_s[...] = jnp.zeros_like(dv_s)

    for qt in range(tiles):
        q_span = slice(qt * tile, (qt + 1) * tile)
        query = q_s[q_span, :] * jnp.asarray(scale, BF16)
        grad = g_s[q_span, :]
        queries = [jnp.where(masks[head], query, jnp.zeros_like(query)) for head in range(2)]
        grads = [jnp.where(masks[head], grad, jnp.zeros_like(grad)) for head in range(2)]
        product = (grad.astype(F32) * att_ref[q_span, :]).T
        dots = [jnp.sum(product[head * HD : (head + 1) * HD], axis=0, keepdims=True) for head in range(2)]
        totals = [lse_ref[head : head + 1, q_span] for head in range(2)]

        def step(kt, state, masked, queries=queries, grads=grads, dots=dots, totals=totals):
            start = pl.multiple_of(kt * tile, tile)
            rows = pl.ds(start, tile)
            keys = k_s[rows, :]
            values = v_s[rows, :]
            dk = dk_s[rows, :]
            dv = dv_s[rows, :]
            new = []
            for head in range(2):
                scores = nt(keys, queries[head])
                if masked:
                    scores = jnp.where(allowed, scores, NEG_BIG)
                soft = jnp.exp(scores - totals[head])
                dsoft = nt(values, grads[head])
                dscore = (soft * (dsoft - dots[head])).astype(BF16)
                dv = dv + nn(soft.astype(BF16), grads[head])
                dk = dk + nn(dscore, queries[head])
                new.append(state[head] + nn(kt_s[head * HD : (head + 1) * HD, rows], dscore))
            dk_s[rows, :] = dk
            dv_s[rows, :] = dv
            return tuple(new)

        state = (jnp.zeros((HD, tile), F32), jnp.zeros((HD, tile), F32))
        state = step(qt, state, True)
        if qt > 0:
            state = lax.fori_loop(0, qt, lambda kt, s, step=step: step(kt, s, False), state)
        dq = jnp.concatenate(state, axis=0) * scale
        dq_s[q_span, :] = dq.T.astype(BF16)

    unsort_blocks(order_ref, [dq_s, dk_s, dv_s], out_ref, blocks, half)
    for k, source in enumerate([dq_s, dk_s, dv_s]):
        values = source[...].astype(BF16).astype(F32)
        sum_ref[:, k * LANES : (k + 1) * LANES] = jnp.sum(values, axis=0, keepdims=True)


def branch_back_kernel(
    tile,
    planes,
    seqs,
    chips,
    order_ref,
    place_ref,
    db_hbm,
    w_hbm,
    at_hbm,
    qkv_hbm,
    att_hbm,
    down_ref,
    out_part_ref,
    mixed_ref,
    vec_ref,
    lse_ref,
    out_ref,
    sum_ref,
    out_w_ref,
    block_ref,
    down_all,
    db_ref,
    w_ref,
    at_ref,
    qkv_ref,
    att_ref,
    load_sem,
    d_att,
    heads,
    h_send,
    h_recv,
    h_local,
    q_s,
    k_s,
    v_s,
    g_s,
    kt_s,
    dq_s,
    dk_s,
    dv_s,
    qh_s,
    gh_s,
    dot_s,
    p_s,
    ds_s,
    *scratch,
):
    n_ctx = 2 * chips
    ctx_me, core, chip, sibling, to, come = plane_peers(chips)
    me, others = other_planes(planes)
    pairs = planes // seqs
    out_scatter, down_sems = scratch[:8], scratch[8:]
    loads = [
        pltpu.make_async_copy(source, target, load_sem.at[k])
        for k, (source, target) in enumerate(
            [(db_hbm, db_ref), (w_hbm, w_ref), (qkv_hbm, qkv_ref), (at_hbm, at_ref), (att_hbm, att_ref)]
        )
    ]
    for load in loads:
        load.start()
    greet(to + [sibling], others)
    down_started = plane_gather_start([down_ref], [down_all], down_sems, chips)
    out_total = []
    out_stages = plane_scatter_stages(
        lambda c: out_part_ref.at[c], *out_scatter[:3], out_scatter[3:], chips, out_total
    )
    next(out_stages)

    loads[0].wait()
    loads[1].wait()
    d_att[...] = nt(db_ref[...], w_ref[...]).astype(BF16).reshape(d_att.shape)

    def source(unit):
        start = pl.multiple_of(lax.rem(unit, pairs) * LANES, LANES)
        return d_att.at[:, unit // pairs, :, :, pl.ds(start, LANES)]

    moved = [
        send(source(unit), heads.at[me], h_send.at[k], h_recv.at[k], "fsdp", unit) for k, unit in enumerate(others)
    ]
    moved.append(pltpu.make_async_copy(source(me), heads.at[me], h_local))
    moved[-1].start()
    for load in loads[2:]:
        load.wait()
    out_w_ref[...] = tn(at_ref[...], db_ref[...]).astype(BF16)

    blocks, half = dq_s.shape[0], dq_s.shape[1]
    length = blocks * half
    tiles, step = length // tile, tile // half

    sort_places(order_ref, qkv_ref, [q_s, k_s, v_s])
    scale = HD ** (-0.5)
    rows_iota = lax.broadcasted_iota(jnp.int32, (tile, tile), 0)
    cols_iota = lax.broadcasted_iota(jnp.int32, (tile, tile), 1)
    allowed = rows_iota <= cols_iota
    masks = [lane_mask(tile, head) for head in range(2)]
    for t in range(tiles):
        span = slice(t * tile, (t + 1) * tile)
        kt_s[:, span] = k_s[span, :].T
        query = q_s[span, :] * jnp.asarray(scale, BF16)
        for head in range(2):
            qh_s[head, span, :] = jnp.where(masks[head], query, jnp.zeros_like(query))
    next(out_stages)
    for copy in moved:
        copy.wait()
    sort_places(order_ref, heads, [g_s])
    for t in range(tiles):
        span = slice(t * tile, (t + 1) * tile)
        grad = g_s[span, :]
        product = (grad.astype(F32) * att_ref[span, :]).T
        for head in range(2):
            gh_s[head, span, :] = jnp.where(masks[head], grad, jnp.zeros_like(grad))
            dot_s[head : head + 1, span] = jnp.sum(product[head * HD : (head + 1) * HD], axis=0, keepdims=True)
    plane_gather_middle(down_started, [down_all], down_sems, chips)

    def keep(target, index, values):
        target[index * step : (index + 1) * step] = values.astype(BF16).reshape(step, half, LANES)

    for kt in range(tiles):
        k_span = slice(kt * tile, (kt + 1) * tile)
        rest = slice(kt * tile, length)
        keys, values = k_s[k_span, :], v_s[k_span, :]
        dk, dv = None, None
        for head in range(2):
            for qt in range(kt, tiles):
                span = slice(qt * tile, (qt + 1) * tile)
                scores = nt(keys, qh_s[head, span, :])
                if kt == qt:
                    scores = jnp.where(allowed, scores, NEG_BIG)
                soft = jnp.exp(scores - lse_ref[head : head + 1, span])
                p_s[head, :, span] = soft.astype(BF16)
                dsoft = nt(values, gh_s[head, span, :])
                ds_s[head, k_span, span] = (soft * (dsoft - dot_s[head : head + 1, span])).astype(BF16)
            dv_one = nn(p_s[head, :, rest], gh_s[head, rest, :])
            dk_one = nn(ds_s[head, k_span, rest], qh_s[head, rest, :])
            dv = dv_one if dv is None else dv + dv_one
            dk = dk_one if dk is None else dk + dk_one
        keep(dk_s, kt, dk)
        keep(dv_s, kt, dv)
        if kt == 0:
            next(out_stages, None)
    for qt in range(tiles):
        span = slice(qt * tile, (qt + 1) * tile)
        upto = slice(0, (qt + 1) * tile)
        dq = [nn(kt_s[head * HD : (head + 1) * HD, upto], ds_s[head, upto, span]) for head in range(2)]
        keep(dq_s, qt, (jnp.concatenate(dq, axis=0) * scale).T)
    for unused in out_stages:
        pass
    block_ref[...] = (mixed_ref[...] + out_total[0] + vec_ref[...]).astype(BF16)

    unsort_places(place_ref, [dq_s, dk_s, dv_s], out_ref)
    for k, ref in enumerate([dq_s, dk_s, dv_s]):
        values = ref[...].astype(F32)
        sum_ref[:, k * LANES : (k + 1) * LANES] = jnp.sum(jnp.sum(values, axis=0), axis=0, keepdims=True)
    plane_gather_end(down_started, [down_all], down_sems, chips)


def branch_back(places, inverse, d_branch, weight, att, qkv, att_exact, lse, down_own, out_part, mixed, vec, planes, tile):
    shape = qkv.shape
    half, lanes = shape[3:]
    n_ctx, rows, width = out_part.shape
    blocks = 2 * planes * n_ctx
    length = blocks * half
    seqs = rows * n_ctx * planes // length
    chips = n_ctx // 2
    rows_s = pltpu.VMEM((length, LANES), BF16)
    blocks_s = pltpu.VMEM((blocks, half, LANES), BF16)
    return pl.pallas_call(
        functools.partial(branch_back_kernel, tile, planes, seqs, chips),
        out_shape=(
            jax.ShapeDtypeStruct(shape, BF16),
            jax.ShapeDtypeStruct((1, lanes), F32),
            jax.ShapeDtypeStruct(weight.shape, BF16),
            jax.ShapeDtypeStruct((rows, width), BF16),
            jax.ShapeDtypeStruct((n_ctx,) + down_own.shape, BF16),
        ),
        in_specs=[SMEM, SMEM] + [ANY] * 7 + [VMEM] * 3,
        out_specs=(VMEM, VMEM, VMEM, VMEM, ANY),
        scratch_shapes=[
            pltpu.VMEM(d_branch.shape, BF16),
            pltpu.VMEM(weight.shape, BF16),
            pltpu.VMEM(att.shape, BF16),
            pltpu.VMEM(shape, BF16),
            pltpu.VMEM(att_exact.shape, F32),
            DMA((5,)),
            pltpu.VMEM((n_ctx, seqs, 2, half, weight.shape[0]), BF16),
            pltpu.VMEM((planes, n_ctx, 2, half, LANES), BF16),
            DMA((planes - 1,)),
            DMA((planes - 1,)),
            DMA,
            rows_s,
            rows_s,
            rows_s,
            rows_s,
            pltpu.VMEM((LANES, length), BF16),
            blocks_s,
            blocks_s,
            blocks_s,
            pltpu.VMEM((2, length, LANES), BF16),
            pltpu.VMEM((2, length, LANES), BF16),
            pltpu.VMEM((2, length), F32),
            pltpu.VMEM((2, tile, length), BF16),
            pltpu.VMEM((2, length, length), BF16),
        ]
        + scatter_scratch(chips, rows, width)
        + gather_sems(chips),
        compiler_params=params(10),
        cost_estimate=SMALL,
        name="branch_back",
    )(places, inverse, d_branch, weight, att, qkv, att_exact, down_own, out_part, mixed, vec, lse)


def attend_backward(order, qkv, grad, att, lse, tile):
    blocks, half, lanes = qkv.shape
    length = blocks * half
    rows = pltpu.VMEM((length, LANES), BF16)
    flipped = pltpu.VMEM((LANES, length), BF16)
    return pl.pallas_call(
        functools.partial(long_backward_kernel, tile),
        out_shape=(
            jax.ShapeDtypeStruct((blocks, half, 3 * LANES), BF16),
            jax.ShapeDtypeStruct((1, 3 * LANES), F32),
        ),
        in_specs=[SMEM, VMEM, VMEM, VMEM, VMEM],
        out_specs=(VMEM, VMEM),
        scratch_shapes=[rows, rows, rows, rows, flipped, rows] + [pltpu.VMEM((length, LANES), F32)] * 2,
        compiler_params=params(),
        cost_estimate=SMALL,
        name="attend_backward",
    )(order, qkv, grad, att, lse)


def assemble_kernel(pieces, part_ref, out_ref):
    for start, source, first, size in pieces:
        out_ref[:, start : start + size] = part_ref[source, :, first : first + size].astype(F32)


def assemble(parts, pieces, width):
    n_ctx, rows, columns = parts.shape
    block = -(-rows // 32) * 16
    return pl.pallas_call(
        functools.partial(assemble_kernel, pieces),
        grid=(-(-rows // block),),
        out_shape=jax.ShapeDtypeStruct((rows, width), F32),
        in_specs=[pl.BlockSpec((n_ctx, block, columns), lambda i: (0, i, 0))],
        out_specs=pl.BlockSpec((block, width), lambda i: (i, 0)),
        compiler_params=params(),
        name="assemble",
    )(parts)


def tn(left, right):
    return nn(left.T, right)


def rows_block(rows, most):
    return math.gcd(rows, most)


def whole_block(shape):
    return pl.BlockSpec(shape, lambda i: (0,) * len(shape), pipeline_mode=pl.Buffered(1))


def row_spec(block, width):
    return pl.BlockSpec((block, width), lambda i: (i, 0))


def product_kernel(left_ref, right_ref, shift_ref, out_ref):
    out_ref[...] = (nn(left_ref[...], right_ref[...]) + shift_ref[...]).astype(BF16)


def product(left, right, shift=None):
    rows, depth = left.shape
    width = right.shape[1]
    block = rows_block(rows, 512)
    if shift is None:
        shift = jnp.zeros((width,), F32)
    return pl.pallas_call(
        product_kernel,
        grid=(rows // block,),
        out_shape=jax.ShapeDtypeStruct((rows, width), BF16),
        in_specs=[row_spec(block, depth), whole_block((depth, width)), whole_block((1, width))],
        out_specs=row_spec(block, width),
        compiler_params=params(),
        cost_estimate=SMALL,
        name="product",
    )(left, right, shift[None, :])


def back_kernel(left_ref, grad_ref, weight_ref, grad_left_ref, grad_weight_ref, sum_ref, total):
    step = pl.program_id(0)
    grad = grad_ref[...]
    grad_left_ref[...] = nt(grad, weight_ref[...]).astype(BF16)
    term = tn(grad, left_ref[...])
    sums = jnp.sum(grad.astype(F32), axis=0, keepdims=True)

    @pl.when(step == 0)
    def _():
        total[...] = term
        sum_ref[...] = sums

    @pl.when(step > 0)
    def _():
        total[...] += term
        sum_ref[...] += sums

    @pl.when(step == pl.num_programs(0) - 1)
    def _():
        grad_weight_ref[...] = total[...].T.astype(BF16)


def product_back(left, grad, weight):
    rows, depth = left.shape
    width = grad.shape[1]
    block = rows_block(rows, 512)
    return pl.pallas_call(
        back_kernel,
        grid=(rows // block,),
        out_shape=(
            jax.ShapeDtypeStruct((rows, depth), BF16),
            jax.ShapeDtypeStruct((depth, width), BF16),
            jax.ShapeDtypeStruct((1, width), F32),
        ),
        in_specs=[row_spec(block, depth), row_spec(block, width), whole_block((depth, width))],
        out_specs=(
            row_spec(block, depth),
            pl.BlockSpec((depth, width), lambda i: (0, 0)),
            pl.BlockSpec((1, width), lambda i: (0, 0)),
        ),
        scratch_shapes=[pltpu.VMEM((width, depth), F32)],
        compiler_params=params(),
        cost_estimate=SMALL,
        name="product_back",
    )(left, grad, weight)


def out_back_kernel(att_ref, grad_ref, weight_ref, grad_att_ref, grad_weight_ref, total):
    step = pl.program_id(0)
    grad = grad_ref[...]
    grad_att_ref[...] = nt(grad, weight_ref[...]).astype(BF16)
    term = tn(att_ref[...], grad)

    @pl.when(step == 0)
    def _():
        total[...] = term

    @pl.when(step > 0)
    def _():
        total[...] += term

    @pl.when(step == pl.num_programs(0) - 1)
    def _():
        grad_weight_ref[...] = total[...].astype(BF16)


def out_back(att, grad, weight):
    rows, depth = att.shape
    width = grad.shape[1]
    block = rows_block(rows, 512)
    return pl.pallas_call(
        out_back_kernel,
        grid=(rows // block,),
        out_shape=(jax.ShapeDtypeStruct((rows, depth), BF16), jax.ShapeDtypeStruct((depth, width), BF16)),
        in_specs=[row_spec(block, depth), row_spec(block, width), whole_block((depth, width))],
        out_specs=(row_spec(block, depth), pl.BlockSpec((depth, width), lambda i: (0, 0))),
        scratch_shapes=[pltpu.VMEM((depth, width), F32)],
        compiler_params=params(),
        cost_estimate=SMALL,
        name="out_back",
    )(att, grad, weight)


GELU_A = math.sqrt(2.0 / math.pi)
GELU_B = 0.044715


def up_kernel(h_ref, og_ref, weight_ref, shift_ref, act_ref, slope_ref, grad_ref, total):
    step = pl.program_id(0)
    up = nn(h_ref[...], weight_ref[...]) + shift_ref[...]
    square = up * up
    soft = jnp.tanh(GELU_A * up * (1.0 + GELU_B * square))
    half = 0.5 * (1.0 + soft)
    act = (up * half).astype(BF16)
    act_ref[...] = act
    slope_ref[...] = half + 0.5 * up * (1.0 - soft * soft) * (GELU_A * (1.0 + 3.0 * GELU_B * square))
    term = tn(act, og_ref[...])

    @pl.when(step == 0)
    def _():
        total[...] = term

    @pl.when(step > 0)
    def _():
        total[...] += term

    @pl.when(step == pl.num_programs(0) - 1)
    def _():
        grad_ref[...] = total[...].astype(BF16)


def feed_up(values, out_grad, weight, shift):
    rows, width = values.shape
    hidden = weight.shape[1]
    block = rows_block(rows, 512)
    return pl.pallas_call(
        up_kernel,
        grid=(rows // block,),
        out_shape=(
            jax.ShapeDtypeStruct((rows, hidden), BF16),
            jax.ShapeDtypeStruct((rows, hidden), F32),
            jax.ShapeDtypeStruct((hidden, width), BF16),
        ),
        in_specs=[
            row_spec(block, width),
            row_spec(block, width),
            whole_block((width, hidden)),
            whole_block((1, hidden)),
        ],
        out_specs=(
            row_spec(block, hidden),
            row_spec(block, hidden),
            pl.BlockSpec((hidden, width), lambda i: (0, 0)),
        ),
        scratch_shapes=[pltpu.VMEM((hidden, width), F32)],
        compiler_params=params(),
        cost_estimate=SMALL,
        name="feed_up",
    )(values, out_grad, weight, shift[None, :])


def local(
    tokens,
    block_pairs,
    out_grad,
    ln1_gain,
    ln1_bias,
    qkv_weight,
    query_bias,
    value_bias,
    out_weight,
    out_bias,
    ln2_gain,
    ln2_bias,
    up_weight,
    up_bias,
    down_weight,
    down_bias,
):
    n_ctx, planes = lax.axis_size("ctx"), lax.axis_size("fsdp")
    c, f = lax.axis_index("ctx"), lax.axis_index("fsdp")
    local_rows, seqs, width = tokens.shape
    half = local_rows // 2
    devices = n_ctx * planes
    blocks = 2 * devices
    length = devices * local_rows
    heads = width // HD
    slots = planes * (-(-heads // devices))
    assert slots == planes and planes % seqs == 0
    span = slots * HD
    rows = local_rows * seqs
    plane_rows = n_ctx * rows
    quarter = width // planes
    ff = up_weight.shape[1]
    ff_quarter = ff // planes
    ff_piece = ff_quarter // n_ctx
    ff_span = ff_piece * planes
    tile = 256

    device_ids = jnp.arange(devices, dtype=jnp.int32)
    device_of_block = jnp.sum(
        jnp.where(block_pairs[None, :] == device_ids[:, None], device_ids[None, :], 0), axis=1
    )
    place_of_block = lax.rem(device_of_block, planes) * n_ctx + device_of_block // planes
    order = jnp.concatenate([place_of_block * 2, place_of_block[::-1] * 2 + 1]).astype(jnp.int32)

    first = [-(-quarter * j // HD) for j in range(planes)] + [heads]
    counts = [first[j + 1] - first[j] for j in range(planes)]
    assert max(counts) <= n_ctx
    slot_head = [jnp.minimum(first[j] + c, heads - 1) for j in range(planes)]
    first_own = jnp.asarray(first, jnp.int32)[f]
    count_own = jnp.asarray(counts, jnp.int32)[f]

    pairs = planes // seqs
    pair, pair_span = lax.rem(f, pairs), 2 * HD
    qkv_own = jnp.stack(
        [
            jnp.concatenate(
                [
                    lax.dynamic_slice(qkv_weight, (0, k * width + slot_head[j] * HD), (quarter, HD))
                    for k in range(3)
                    for j in (2 * p, 2 * p + 1)
                ],
                axis=1,
            )
            for p in range(pairs)
        ]
    )
    down_own = lax.dynamic_slice(down_weight, (c * ff_piece, 0), (ff_piece, width))


    tok = jnp.swapaxes(tokens, 0, 1).reshape(rows, width)
    og = jnp.swapaxes(out_grad, 0, 1).reshape(rows, width)

    short = -quarter % LANES
    vector_list = [ln1_gain, ln1_bias, ln2_gain, ln2_bias, query_bias, value_bias, out_bias, down_bias]
    vector_list += [up_bias[k * quarter : (k + 1) * quarter] for k in range(ff // width)]
    packed = jnp.concatenate([jnp.pad(v, (0, short)) for v in vector_list])
    packed = jnp.pad(packed, (0, -packed.size % (16 * LANES))).reshape(-1, LANES)
    up_own = jnp.concatenate(
        [
            lax.dynamic_slice(up_weight, (0, k * ff_quarter + c * ff_piece), (quarter, ff_piece))
            for k in range(planes)
        ],
        axis=1,
    )
    tok_first, up_own = lax.optimization_barrier((tok, up_own))
    vectors, og_all, h1, qkv_slice, next_rows = first_norm_gather(
        tok_first, og, packed, qkv_own, out_weight, n_ctx, planes, seqs
    )
    out_own = lax.dynamic_slice(
        jnp.concatenate([out_weight, next_rows]), ((first_own + c) * HD - f * quarter, 0), (HD, width)
    )
    out_own = jnp.where(c < count_own, out_own, jnp.zeros_like(out_own))
    h1 = h1.reshape(length, width)
    qkv_slice = qkv_slice.reshape(width, 3 * pair_span)
    h1, up_own, down_own = lax.optimization_barrier((h1, up_own, down_own))
    down_slice = lax.all_gather(down_own, "fsdp", axis=0, tiled=True)
    up_slice = lax.all_gather(up_own, "fsdp", axis=0, tiled=True)
    og_all = og_all.reshape(plane_rows, width)
    vectors = vectors.reshape(planes, -1)[:, : len(vector_list) * (quarter + short)]
    vectors = vectors.reshape(planes, len(vector_list), quarter + short)[:, :, :quarter].astype(F32)
    gain1, bias1, gain2, bias2, bias_q, bias_v, bias_o, bias_d = [
        vectors[:, k].reshape(width) for k in range(8)
    ]
    bias_up = lax.dynamic_slice(
        vectors[:, 8 : 8 + ff // width].reshape(planes, ff_quarter), (0, c * ff_piece), (planes, ff_piece)
    ).reshape(ff_span)

    pair_heads = [jnp.minimum(jnp.asarray(first, jnp.int32)[2 * pair + i] + c, heads - 1) for i in range(2)]

    def head_part(vector):
        return [lax.dynamic_slice(vector, (head * HD,), (HD,)) for head in pair_heads]

    qkv_shift = jnp.concatenate(head_part(bias_q) + [jnp.zeros((pair_span,), F32)] + head_part(bias_v))

    if length <= SHORT:
        places, inverse = block_places(order, n_ctx)
        qkv, att_exact, lse, att, out_slice = attend(
            places, inverse, h1, qkv_slice, qkv_shift[None, :], out_own, n_ctx, planes, seqs, half, tile
        )
    else:
        qkv = product(h1, qkv_slice, qkv_shift).reshape(blocks, half, 3 * pair_span)
        att_heads, att_exact, lse = attend_forward(order, qkv, tile)
        att, out_slice = to_tokens(att_heads.reshape(planes, n_ctx, local_rows, LANES), seqs, 6, out_own)
    out_slice = out_slice.reshape(span, width)
    att = att.reshape(plane_rows, span)
    mixed, h2 = second_norm_gather(att, out_slice, tok, jnp.stack([gain2, bias2, bias_o]), n_ctx)
    h2 = h2.reshape(plane_rows, width)
    def reduce_own(part):
        return lax.psum_scatter(part, "fsdp", scatter_dimension=0, tiled=True)

    act, slope, down_part = feed_up(h2, og_all, up_slice, bias_up)
    down_own_grad = reduce_own(down_part)
    d_mixed, sums2, d_branch, out_part, up_part, d_up_sum = feed_back(
        h2, og_all, act, slope, up_slice, down_slice, mixed, og, gain2[None, :]
    )
    up_own_grad = reduce_own(up_part)
    out_part = out_part.reshape(n_ctx, rows, width)
    d_branch = d_branch.reshape(plane_rows, width)
    if length <= SHORT:
        d_qkv, d_qkv_sum, out_w_part, block_out, down_parts = branch_back(
            places,
            inverse,
            d_branch,
            out_slice,
            att,
            qkv,
            att_exact,
            lse,
            down_own_grad,
            out_part,
            mixed,
            bias_d[None, :],
            planes,
            tile,
        )
    else:
        d_att, out_w_part = out_back(att, d_branch, out_slice)
        d_att_heads, down_parts = to_heads(
            d_att.reshape(n_ctx, seqs, local_rows, span), planes, 7, down_own_grad
        )
        d_qkv, d_qkv_sum = attend_backward(
            order, qkv, d_att_heads.reshape(blocks, half, LANES), att_exact, lse, tile
        )
        total = lax.psum_scatter(out_part.reshape(plane_rows, width), "ctx", scatter_dimension=0, tiled=True)
        block_out = (mixed + total.astype(F32) + bias_d).astype(BF16)
    d_qkv, d_qkv_sum = d_qkv.reshape(length, 3 * pair_span), d_qkv_sum[0]
    down_parts, unused = lax.optimization_barrier((down_parts, d_qkv))
    down_grad = down_parts.reshape(ff_quarter, width).astype(F32)
    up_own_grad, down_grad = lax.optimization_barrier((up_own_grad, down_grad))

    d_up_sum = d_up_sum.reshape(planes, ff_piece)
    up_spread = lax.dynamic_update_slice(jnp.zeros((planes, ff_quarter), F32), d_up_sum, (0, c * ff_piece))

    def spread(values):
        full = jnp.zeros((width + HD,), F32)
        for i in range(2):
            slot = 2 * pair + i
            real = c < jnp.asarray(counts, jnp.int32)[slot]
            place = jnp.where(real, pair_heads[i] * HD, width)
            full = lax.dynamic_update_slice(full, values[i * HD : (i + 1) * HD], (place,))
        return full[None, :width]

    wide = jnp.concatenate([sums2, spread(d_qkv_sum[:pair_span]), spread(d_qkv_sum[2 * pair_span :])])
    wide = wide.reshape(6, planes, quarter).transpose(1, 0, 2).reshape(planes, 6 * quarter)
    flat = jnp.concatenate([wide, up_spread], axis=1)
    size = flat.shape[1]
    flat = jnp.pad(flat, ((0, 0), (0, -size % (8 * LANES)))).reshape(planes, -1, LANES)

    if length <= SHORT:
        grad_tok, qkv_parts, up_parts, out_parts, tail_rows, sums1, totals = finish(
            h1,
            d_qkv,
            qkv_slice,
            up_own_grad,
            out_w_part.reshape(planes, HD, width),
            flat,
            tok,
            d_mixed,
            gain1[None, :],
            counts,
        )
    else:
        d_h1, qkv_part, unused = product_back(h1, d_qkv, qkv_slice)
        grad_tok, qkv_parts, out_parts, sums1, totals = first_norm_back(
            d_h1.reshape(planes, n_ctx, local_rows, width),
            qkv_part.reshape(planes, quarter, 3 * pair_span),
            reduce_own(out_w_part),
            flat,
            tok,
            d_mixed,
            gain1[None, :],
        )
        up_parts = lax.all_gather(up_own_grad, "ctx", axis=0)
        tail_rows = lax.dynamic_index_in_dim(out_parts, count_own - 1, 0, keepdims=False)
        tail_rows = lax.ppermute(tail_rows, "fsdp", [(j, j + 1) for j in range(planes - 1)])
    sums1 = sums1[:2, :quarter]
    totals = totals.reshape(-1)
    sums = totals[: 6 * quarter].reshape(6, quarter)
    up_bias_grad = totals[6 * quarter : size]

    up_pieces = [
        (j * ff_quarter + d * ff_piece, d, j * ff_piece, ff_piece) for j in range(planes) for d in range(n_ctx)
    ]
    up_grad = assemble(up_parts, up_pieces, ff)
    qkv_pieces = [
        (k * width + (first[j] + d) * HD, d * pairs + j // 2, k * pair_span + j % 2 * HD, HD)
        for k in range(3)
        for j in range(planes)
        for d in range(counts[j])
    ]
    qkv_grad = assemble(qkv_parts.reshape(n_ctx * pairs, quarter, 3 * pair_span), qkv_pieces, 3 * width)
    out_rows = out_parts.reshape(n_ctx * HD, width)
    lead = first_own * HD - f * quarter
    shifted = lax.dynamic_slice(
        jnp.concatenate([jnp.zeros((HD, width), BF16), out_rows]), (HD - lead, 0), (quarter, width)
    )
    from_tail = lax.dynamic_slice(
        jnp.concatenate([tail_rows, jnp.zeros((quarter, width), BF16)]), (HD - lead, 0), (quarter, width)
    )
    row_ids = lax.broadcasted_iota(jnp.int32, (quarter, width), 0)
    out_grad_own = jnp.where(row_ids < lead, from_tail, shifted).astype(F32)

    def back(values):
        return jnp.swapaxes(values.reshape(seqs, local_rows, width), 0, 1)

    return (
        back(block_out),
        back(grad_tok),
        sums1[0],
        sums1[1],
        qkv_grad,
        sums[4],
        sums[5],
        out_grad_own,
        sums[2],
        sums[0],
        sums[1],
        up_grad,
        up_bias_grad,
        down_grad,
        sums[3],
    )


def solution(mesh):
    both, row, vec, mat = P(("ctx", "fsdp"), None, None), P(), P("fsdp"), P("fsdp", None)
    in_specs = (both, row, both, vec, vec, mat, vec, vec, mat, vec, vec, vec, mat, vec, mat, vec)
    out_specs = (both, both, vec, vec, mat, vec, vec, mat, vec, vec, vec, mat, vec, mat, vec)
    return jax.shard_map(local, mesh=mesh, in_specs=in_specs, out_specs=out_specs, check_vma=False)
```

```python
import functools
import math

import jax
import jax.numpy as jnp
from jax import lax
from jax.experimental import pallas as pl
from jax.experimental.pallas import tpu as pltpu
from jax.sharding import PartitionSpec as P

HD = 64
LANES = 128
NORM_EPS = 1e-05
NEG_BIG = -1e30
MESH = pl.DeviceIdType.MESH
F32 = jnp.float32
BF16 = jnp.bfloat16
ANY = pl.BlockSpec(memory_space=pl.ANY)
VMEM = pl.BlockSpec(memory_space=pltpu.VMEM)
DMA = pltpu.SemaphoreType.DMA
VMEM_LIMIT = 56 * 1024 * 1024
SMALL = pl.CostEstimate(flops=1, bytes_accessed=1, transcendentals=0)


def params(cid=None):
    if cid is None:
        return pltpu.CompilerParams(vmem_limit_bytes=VMEM_LIMIT)
    return pltpu.CompilerParams(
        collective_id=cid, has_side_effects=True, vmem_limit_bytes=VMEM_LIMIT
    )


def plane_peers(chips):
    me = lax.axis_index("ctx")
    core = lax.rem(me, 2)
    chip = me // 2
    sibling = chip * 2 + 1 - core
    if chips == 4:
        across_x = chip + 1 - 2 * lax.rem(chip, 2)
        across_y = lax.rem(chip + 2, 4)
        corner = lax.rem(across_x + 2, 4)
        first = across_x * (1 - core) + across_y * core
        second = across_y * (1 - core) + across_x * core
        to = come = [first * 2 + core, second * 2 + core, corner * 2 + core]
    else:
        to = [lax.rem(chip + k, chips) * 2 + core for k in range(1, chips)]
        come = [lax.rem(chip + chips - k, chips) * 2 + core for k in range(1, chips)]
    return me, core, chip, sibling, to, come


def greet(plane=(), across=()):
    barrier = pltpu.get_barrier_semaphore()
    for peer in plane:
        pl.semaphore_signal(barrier, inc=1, device_id={"ctx": peer}, device_id_type=MESH)
    for peer in across:
        pl.semaphore_signal(barrier, inc=1, device_id={"fsdp": peer}, device_id_type=MESH)
    pl.semaphore_wait(barrier, len(plane) + len(across))


def other_planes(planes):
    me = lax.axis_index("fsdp")
    return me, [lax.rem(me + k, planes) for k in range(1, planes)]


def send(src, dst, send_sem, recv_sem, axis, peer):
    copy = pltpu.make_async_remote_copy(
        src_ref=src,
        dst_ref=dst,
        send_sem=send_sem,
        recv_sem=recv_sem,
        device_id={axis: peer},
        device_id_type=MESH,
    )
    copy.start()
    return copy


def plane_gather_start(owns, alls, sems, chips):
    far_send, far_recv, near_send, near_recv, local_sem = sems
    me, core, chip, sibling, to, come = plane_peers(chips)
    direct = 2 if chips == 4 else chips - 1
    last = chips - 1
    far, near, local = [], [], []
    for i, (own_ref, all_ref) in enumerate(zip(owns, alls)):
        far.append(
            [
                send(own_ref, all_ref.at[me], far_send.at[i, k], far_recv.at[i, k], "ctx", to[k])
                for k in range(direct)
            ]
        )
        near.append(send(own_ref, all_ref.at[me], near_send.at[i, last], near_recv.at[i, last], "ctx", sibling))
        copy = pltpu.make_async_copy(own_ref, all_ref.at[me], local_sem.at[i])
        copy.start()
        local.append(copy)
    return far, near, local


def plane_gather_pass(started, alls, sems, chips, turns):
    far_send, far_recv, near_send, near_recv, local_sem = sems
    me, core, chip, sibling, to, come = plane_peers(chips)
    far, near, local = started
    for i, all_ref in enumerate(alls):
        for k in turns:
            far[i][k].wait_recv()
            block = all_ref.at[come[k]]
            if chips == 4 and k == 0:
                far[i].append(send(block, block, far_send.at[i, 2], far_recv.at[i, 2], "ctx", to[1]))
            near.append(send(block, block, near_send.at[i, k], near_recv.at[i, k], "ctx", sibling))


def plane_gather_middle(started, alls, sems, chips):
    plane_gather_pass(started, alls, sems, chips, range(2 if chips == 4 else chips - 1))


def plane_gather_end(started, alls, sems, chips):
    plane_gather_pass(started, alls, sems, chips, range(2, chips - 1) if chips == 4 else ())
    far, near, local = started
    for group in far:
        for copy in group:
            copy.wait_send()
    for copy in near + local:
        copy.wait()


def plane_gather_finish(started, alls, sems, chips):
    plane_gather_middle(started, alls, sems, chips)
    plane_gather_end(started, alls, sems, chips)


def plane_gather(owns, alls, sems, chips):
    plane_gather_finish(plane_gather_start(owns, alls, sems, chips), alls, sems, chips)


def plane_scatter_stages(block_of, mine, paired, arrived, sems, chips, result):
    far_send, far_recv, near_send, near_recv, local_sem = sems
    me, core, chip, sibling, to, come = plane_peers(chips)
    targets = to + [me]
    order = [2, 1, 0, 3] if chips == 4 else list(range(chips))
    near, local = [None] * chips, [None] * chips
    crossed = [1, 0, 2, 3] if chips == 4 else list(range(chips))
    for k in order:
        other = targets[crossed[k]] + 1 - 2 * core
        near[k] = send(block_of(other), paired.at[k], near_send.at[k], near_recv.at[k], "ctx", sibling)
        local[k] = pltpu.make_async_copy(block_of(targets[k]), mine.at[k], local_sem.at[k])
        local[k].start()
    yield

    def both(k):
        local[k].wait()
        near[k].wait_recv()
        return mine[k].astype(F32) + paired[k].astype(F32)

    def dispatch(k, target):
        return send(mine.at[k], arrived.at[k], far_send.at[k], far_recv.at[k], "ctx", target)

    far = [None] * (chips - 1)
    if chips == 4:
        mine[2] = both(2).astype(BF16)
        far[2] = dispatch(2, to[0])
        mine[0] = both(0).astype(BF16)
        far[0] = dispatch(0, to[0])
        partial = both(1)
        yield
        far[2].wait_recv()
        mine[1] = (partial + arrived[2].astype(F32)).astype(BF16)
        far[1] = dispatch(1, to[1])
        total = both(3)
        arriving = [0, 1]
    else:
        for k in range(chips - 1):
            mine[k] = both(k).astype(BF16)
            far[k] = dispatch(k, to[k])
        total = both(chips - 1)
        arriving = range(chips - 1)
    yield
    for k in arriving:
        far[k].wait_recv()
        total = total + arrived[k].astype(F32)
    for copy in far + near:
        copy.wait_send()
    result.append(total)


def plane_scatter(block_of, mine, paired, arrived, sems, chips):
    result = []
    for unused in plane_scatter_stages(block_of, mine, paired, arrived, sems, chips, result):
        pass
    return result[0]


def gather_sems(chips, count=1):
    return [DMA((count, chips - 1))] * 2 + [DMA((count, chips))] * 2 + [DMA((count,))]


def scatter_orders(chips):
    if chips == 4:
        return [2, 0, 1, 3], [1, 0, 2, 3]
    return list(range(chips)), list(range(chips))


def plane_scatter_made(make, part, paired, arrived, sems, chips, meanwhile):
    far_send, far_recv, near_send, near_recv = sems
    me, core, chip, sibling, to, come = plane_peers(chips)
    targets = to + [me]
    order, crossed = scatter_orders(chips)
    near, far = [None] * chips, [None] * (chips - 1)

    def produce(k):
        make(k, targets[k] // 2)
        place = crossed[k]
        near[place] = send(
            part.at[k, 1 - core], paired.at[place], near_send.at[place], near_recv.at[place], "ctx", sibling
        )

    def both(k):
        near[k].wait_recv()
        return part[k, core].astype(F32) + paired[k].astype(F32)

    def dispatch(k, values, target):
        paired[k] = values.astype(BF16)
        far[k] = send(paired.at[k], arrived.at[k], far_send.at[k], far_recv.at[k], "ctx", target)

    if chips == 4:
        produce(2)
        produce(0)
        dispatch(2, both(2), to[0])
        produce(1)
        dispatch(0, both(0), to[0])
        produce(3)
        partial = both(1)
        far[2].wait_recv()
        dispatch(1, partial + arrived[2].astype(F32), to[1])
        arriving = [0, 1]
    else:
        for k in order:
            produce(k)
        for k in range(chips - 1):
            dispatch(k, both(k), to[k])
        arriving = range(chips - 1)
    meanwhile()
    total = both(chips - 1)
    for k in arriving:
        far[k].wait_recv()
        total = total + arrived[k].astype(F32)
    for copy in far + near:
        copy.wait_send()
    return total


def made_scratch(chips, *block):
    return [
        pltpu.VMEM((chips, 2) + block, BF16),
        pltpu.VMEM((chips,) + block, BF16),
        pltpu.VMEM((chips - 1,) + block, BF16),
        DMA((chips - 1,)),
        DMA((chips - 1,)),
        DMA((chips,)),
        DMA((chips,)),
    ]


def scatter_scratch(chips, *block):
    return [
        pltpu.VMEM((chips,) + block, BF16),
        pltpu.VMEM((chips,) + block, BF16),
        pltpu.VMEM((chips - 1,) + block, BF16),
        DMA((chips - 1,)),
        DMA((chips - 1,)),
        DMA((chips,)),
        DMA((chips,)),
        DMA((chips,)),
    ]


def normalize(values):
    average = jnp.mean(values, axis=-1, keepdims=True)
    centered = values - average
    variance = jnp.mean(centered * centered, axis=-1, keepdims=True)
    inverse = lax.rsqrt(variance + NORM_EPS)
    return centered * inverse, inverse


def norm_backward(grad, gain, unit, inverse):
    scaled = grad * gain
    first = jnp.mean(scaled, axis=-1, keepdims=True)
    second = jnp.mean(scaled * unit, axis=-1, keepdims=True)
    return (scaled - first - unit * second) * inverse


def first_kernel(
    chips,
    planes,
    seqs,
    quarter,
    tok_ref,
    og_ref,
    vec_ref,
    weight_ref,
    out_w_ref,
    vecs_ref,
    ogs_ref,
    h1_ref,
    weights_ref,
    next_ref,
    own,
    column,
    v_send,
    v_recv,
    v_local,
    h_send,
    h_recv,
    w_send,
    w_recv,
    w_local,
    n_send,
    n_recv,
    n_local,
    *sems,
):
    me, core, chip, sibling, to, come = plane_peers(chips)
    plane, others = other_planes(planes)
    pairs = planes // seqs
    rows = own.shape[0] // seqs
    greet(to + [sibling], others)
    og_sems, h1_sems = sems[:5], [sems[5 + 5 * k : 10 + 5 * k] for k in range(planes)]
    copies = [
        send(vec_ref, vecs_ref.at[plane], v_send.at[k], v_recv.at[k], "fsdp", peer) for k, peer in enumerate(others)
    ]
    local = pltpu.make_async_copy(vec_ref, vecs_ref.at[plane], v_local)
    local.start()
    lead = out_w_ref.at[pl.ds(0, HD)]
    last = plane == planes - 1

    def lead_copy():
        return pltpu.make_async_remote_copy(
            src_ref=lead,
            dst_ref=next_ref,
            send_sem=n_send,
            recv_sem=n_recv,
            device_id={"fsdp": lax.rem(plane + planes - 1, planes)},
            device_id_type=MESH,
        )

    @pl.when(plane > 0)
    def _():
        lead_copy().start()

    @pl.when(last)
    def _():
        pltpu.make_async_copy(lead, next_ref, n_local).start()

    og_started = plane_gather_start([og_ref], [ogs_ref], og_sems, chips)
    unit, inverse = normalize(tok_ref[...].astype(F32))
    for copy in copies + [local]:
        copy.wait()
    lines = quarter // LANES + 1

    def vector(k):
        pieces = []
        for j in range(planes):
            for line in range(lines):
                size = min(LANES, quarter - line * LANES)
                if size:
                    row = k * lines + line
                    pieces.append(vecs_ref[j, row : row + 1, :size].astype(F32))
        return jnp.concatenate(pieces, axis=1)

    own[...] = (unit * vector(0) + vector(1)).astype(BF16)

    def half_of(peer):
        return own.at[pl.ds(pl.multiple_of(peer // pairs * rows, rows), rows)]

    halves = [
        send(half_of(peer), column.at[k], h_send.at[k], h_recv.at[k], "fsdp", peer) for k, peer in enumerate(others)
    ]
    weights = [
        send(weight_ref.at[lax.rem(peer, pairs)], weights_ref.at[plane], w_send.at[k], w_recv.at[k], "fsdp", peer)
        for k, peer in enumerate(others)
    ]
    weights.append(pltpu.make_async_copy(weight_ref.at[lax.rem(plane, pairs)], weights_ref.at[plane], w_local))
    weights[-1].start()
    sources = [plane] + [lax.rem(plane + planes - k, planes) for k in range(1, planes)]
    blocks = [half_of(plane)] + [column.at[k] for k in range(planes - 1)]
    started = [plane_gather_start([blocks[0]], [h1_ref.at[sources[0]]], h1_sems[0], chips)]
    plane_gather_middle(og_started, [ogs_ref], og_sems, chips)
    for k in range(1, planes):
        halves[k - 1].wait_recv()
        started.append(plane_gather_start([blocks[k]], [h1_ref.at[sources[k]]], h1_sems[k], chips))
        plane_gather_middle(started[k - 1], [h1_ref.at[sources[k - 1]]], h1_sems[k - 1], chips)
    plane_gather_middle(started[-1], [h1_ref.at[sources[-1]]], h1_sems[-1], chips)
    plane_gather_end(og_started, [ogs_ref], og_sems, chips)
    for k in range(planes):
        plane_gather_end(started[k], [h1_ref.at[sources[k]]], h1_sems[k], chips)
    @pl.when(plane > 0)
    def _():
        lead_copy().wait_send()

    @pl.when(last)
    def _():
        pltpu.make_async_copy(lead, next_ref, n_local).wait()

    @pl.when(plane < planes - 1)
    def _():
        lead_copy().wait_recv()

    for copy in halves:
        copy.wait_send()
    for copy in weights:
        copy.wait()


def first_norm_gather(tok, og, vec, weight, out_weight, n_ctx, planes, seqs):
    rows, width = tok.shape
    chips, half = n_ctx // 2, rows // seqs
    return pl.pallas_call(
        functools.partial(first_kernel, chips, planes, seqs, width // planes),
        out_shape=(
            jax.ShapeDtypeStruct((planes,) + vec.shape, BF16),
            jax.ShapeDtypeStruct((n_ctx, rows, width), BF16),
            jax.ShapeDtypeStruct((planes, n_ctx, half, width), BF16),
            jax.ShapeDtypeStruct((planes,) + weight.shape[1:], BF16),
            jax.ShapeDtypeStruct((HD, width), BF16),
        ),
        in_specs=[VMEM, ANY, VMEM, ANY, ANY],
        out_specs=(VMEM, ANY, ANY, ANY, ANY),
        scratch_shapes=[
            pltpu.VMEM((rows, width), BF16),
            pltpu.VMEM((planes - 1, half, width), BF16),
            DMA((planes - 1,)),
            DMA((planes - 1,)),
            DMA,
            DMA((planes - 1,)),
            DMA((planes - 1,)),
            DMA((planes - 1,)),
            DMA((planes - 1,)),
            DMA,
            DMA,
            DMA,
            DMA,
        ]
        + gather_sems(chips)
        + gather_sems(chips) * planes,
        compiler_params=params(0),
        cost_estimate=SMALL,
        name="norm_gather",
    )(tok, og, vec, weight, out_weight)


def second_kernel(chips, att_ref, weight_ref, tok_ref, vec_ref, mixed_ref, all_ref, own, *scratch):
    me, core, chip, sibling, to, come = plane_peers(chips)
    greet(to + [sibling])
    rows = tok_ref.shape[0]
    part = scratch[0]

    def make(k, target):
        span = pl.ds(pl.multiple_of(target * 2 * rows, 2 * rows), 2 * rows)
        branch = nn(att_ref[span, :], weight_ref[...]).astype(BF16)
        part[k, 0] = branch[:rows]
        part[k, 1] = branch[rows:]

    total = plane_scatter_made(make, *scratch[:3], scratch[3:7], chips, lambda: None)
    mixed = tok_ref[...].astype(F32) + total + vec_ref[2:3, :]
    mixed_ref[...] = mixed
    unit, inverse = normalize(mixed)
    own[...] = (unit * vec_ref[0:1, :] + vec_ref[1:2, :]).astype(BF16)
    plane_gather([own], [all_ref], scratch[7:], chips)


def second_norm_gather(att, weight, tok, vecs, n_ctx):
    rows, width = tok.shape
    chips = n_ctx // 2
    return pl.pallas_call(
        functools.partial(second_kernel, chips),
        out_shape=(
            jax.ShapeDtypeStruct((rows, width), F32),
            jax.ShapeDtypeStruct((n_ctx, rows, width), BF16),
        ),
        in_specs=[VMEM] * 4,
        out_specs=(VMEM, ANY),
        scratch_shapes=[pltpu.VMEM((rows, width), BF16)]
        + made_scratch(chips, rows, width)
        + gather_sems(chips),
        compiler_params=params(1),
        cost_estimate=SMALL,
        name="scatter_norm_gather",
    )(att, weight, tok, vecs)


def third_kernel(
    chips,
    planes,
    packed,
    h_hbm,
    og_hbm,
    act_hbm,
    slope_hbm,
    up_w_hbm,
    down_w_hbm,
    mixed_ref,
    og_ref,
    vec_ref,
    dmixed_ref,
    sums_ref,
    all_ref,
    out_hbm,
    up_grad_ref,
    up_sum_ref,
    h_ref,
    ogs_ref,
    act_ref,
    slope_ref,
    up_w_ref,
    down_w_ref,
    d_up_ref,
    out_ref,
    load_sem,
    out_sem,
    own,
    *scratch,
):
    me, core, chip, sibling, to, come = plane_peers(chips)
    made, gather = scratch[:7], scratch[7:]
    loads = [
        pltpu.make_async_copy(source, target, load_sem.at[k])
        for k, (source, target) in enumerate(
            [
                (down_w_hbm, down_w_ref),
                (og_hbm, ogs_ref),
                (slope_hbm, slope_ref),
                (up_w_hbm, up_w_ref),
                (h_hbm, h_ref),
                (act_hbm, act_ref),
            ]
        )
    ]
    for load in loads:
        load.start()
    greet(to + [sibling])
    unit, inverse = normalize(mixed_ref[...])
    rows = mixed_ref.shape[0]
    waiting = loads[:4]
    part = made[0]

    def make(k, target):
        span = pl.ds(pl.multiple_of(target * 2 * rows, 2 * rows), 2 * rows)
        while len(waiting) > 2:
            waiting.pop(0).wait()
        d_act = nt(ogs_ref[span, :], down_w_ref[...])
        while waiting:
            waiting.pop(0).wait()
        d_up = (d_act * slope_ref[span, :]).astype(BF16)
        d_up_ref[span, :] = d_up
        d_h = nt(d_up, up_w_ref[...]).astype(BF16)
        part[k, 0] = d_h[:rows]
        part[k, 1] = d_h[rows:]

    def meanwhile():
        for load in loads[4:]:
            load.wait()
        d_up = d_up_ref[...]
        up_sum_ref[...] = jnp.sum(d_up.astype(F32), axis=0, keepdims=True)
        up_grad = tn(d_up, h_ref[...]).T
        if packed:
            hidden = up_grad.shape[1]
            lines = up_grad.shape[0] // planes // 2
            for j in range(2 * planes):
                rows_at, lanes_at = j // 2 * lines, j % 2 * hidden
                up_grad_ref[rows_at : rows_at + lines, lanes_at : lanes_at + hidden] = up_grad[
                    j * lines : (j + 1) * lines
                ].astype(BF16)
        else:
            up_grad_ref[...] = up_grad.astype(BF16)
        out_ref[...] = nn(act_ref[...], down_w_ref[...]).astype(BF16)
        pltpu.make_async_copy(out_ref, out_hbm, out_sem).start()

    grad = plane_scatter_made(make, *made[:3], made[3:], chips, meanwhile)
    out_grad = og_ref[...].astype(F32)
    dmixed = out_grad + norm_backward(grad, vec_ref[0:1, :], unit, inverse)
    low = dmixed.astype(BF16)
    own[...] = low
    started = plane_gather_start([own], [all_ref], gather, chips)
    dmixed_ref[...] = dmixed
    sums_ref[0:1, :] = jnp.sum(grad * unit, axis=0, keepdims=True)
    sums_ref[1:2, :] = jnp.sum(grad, axis=0, keepdims=True)
    sums_ref[2:3, :] = jnp.sum(low.astype(F32), axis=0, keepdims=True)
    sums_ref[3:4, :] = jnp.sum(out_grad, axis=0, keepdims=True)
    plane_gather_finish(started, [all_ref], gather, chips)
    pltpu.make_async_copy(out_ref, out_hbm, out_sem).wait()


def feed_back(values, out_grads, act, slope, up_weight, down_weight, mixed, og, vecs, planes, packed):
    rows, width = mixed.shape
    total_rows, hidden = act.shape
    n_ctx = total_rows // rows
    chips = n_ctx // 2
    return pl.pallas_call(
        functools.partial(third_kernel, chips, planes, packed),
        out_shape=(
            jax.ShapeDtypeStruct((rows, width), F32),
            jax.ShapeDtypeStruct((4, width), F32),
            jax.ShapeDtypeStruct((n_ctx, rows, width), BF16),
            jax.ShapeDtypeStruct((total_rows, width), BF16),
            jax.ShapeDtypeStruct((width // 2, 2 * hidden) if packed else (width, hidden), BF16),
            jax.ShapeDtypeStruct((1, hidden), F32),
        ),
        in_specs=[ANY] * 6 + [VMEM] * 3,
        out_specs=(VMEM, VMEM, ANY, ANY, VMEM, VMEM),
        scratch_shapes=[
            pltpu.VMEM((total_rows, width), BF16),
            pltpu.VMEM((total_rows, width), BF16),
            pltpu.VMEM((total_rows, hidden), BF16),
            pltpu.VMEM((total_rows, hidden), F32),
            pltpu.VMEM((width, hidden), BF16),
            pltpu.VMEM((hidden, width), BF16),
            pltpu.VMEM((total_rows, hidden), BF16),
            pltpu.VMEM((total_rows, width), BF16),
            DMA((6,)),
            DMA,
            pltpu.VMEM((rows, width), BF16),
        ]
        + made_scratch(chips, rows, width)
        + gather_sems(chips),
        compiler_params=params(2),
        cost_estimate=SMALL,
        name="feed_back",
    )(values, out_grads, act, slope, up_weight, down_weight, mixed, og, vecs)


def fourth_kernel(
    chips,
    planes,
    seqs,
    part_ref,
    qkv_ref,
    outw_ref,
    flat_ref,
    tok_ref,
    dmixed_ref,
    vec_ref,
    grad_ref,
    qkv_all,
    outw_all,
    sums_ref,
    flat_out,
    q_arrived,
    q_own,
    q_send,
    q_recv,
    q_local,
    rows_own,
    rows_arrived,
    r_send,
    r_recv,
    small,
    small_own,
    small_z,
    small_c,
    flat_own,
    flat_z,
    flat_c,
    z_send,
    z_recv,
    c_send,
    c_recv,
    *scratch,
):
    n_ctx = 2 * chips
    pairs = planes // seqs
    me, core, chip, sibling, to, come = plane_peers(chips)
    plane, others = other_planes(planes)
    around = [lax.rem(me + k, n_ctx) for k in range(1, n_ctx)]
    greet(around, others)
    scatter, rest_sems, qkv_sems = scratch[:8], scratch[8:13], scratch[13:]

    pushed = [
        send(qkv_ref.at[peer], q_arrived.at[plane], q_send.at[k], q_recv.at[k], "fsdp", peer)
        for k, peer in enumerate(others)
    ]
    held = pltpu.make_async_copy(qkv_ref.at[plane], q_arrived.at[plane], q_local)
    held.start()
    flat_sent = [
        send(flat_ref.at[peer], flat_z.at[k], z_send.at[0, k], z_recv.at[0, k], "fsdp", peer)
        for k, peer in enumerate(others)
    ]
    unit, inverse = normalize(tok_ref[...].astype(F32))
    total = plane_scatter(lambda c: part_ref.at[:, c], *scatter[:3], scatter[3:], chips)
    rows_own[...] = total.astype(BF16)
    rows_sent = [
        send(rows_own.at[peer], rows_arrived.at[plane], r_send.at[k], r_recv.at[k], "fsdp", peer)
        for k, peer in enumerate(others)
    ]
    rows_arrived[plane] = rows_own[plane]
    rest_started = plane_gather_start([outw_ref], [outw_all], rest_sems, chips)
    for copy in pushed + [held]:
        copy.wait()
    for pair in range(pairs):
        terms = [q_arrived[seq * pairs + pair].astype(F32) for seq in range(seqs)]
        q_own[pair] = sum(terms[1:], terms[0]).astype(BF16)
    qkv_started = plane_gather_start([q_own], [qkv_all], qkv_sems, chips)
    plane_gather_finish(rest_started, [outw_all], rest_sems, chips)

    for copy in rows_sent:
        copy.wait()
    halves = []
    for seq in range(seqs):
        terms = [rows_arrived[seq * pairs + pair].astype(F32) for pair in range(pairs)]
        halves.append(sum(terms[1:], terms[0]))
    grad = jnp.concatenate(halves, axis=0)
    sums = jnp.concatenate(
        [jnp.sum(grad * unit, axis=0, keepdims=True), jnp.sum(grad, axis=0, keepdims=True)], axis=0
    )
    quarter = sums.shape[1] // planes
    small[...] = jnp.zeros_like(small)
    for j in range(planes):
        small[j, 0:2, 0:quarter] = sums[:, j * quarter : (j + 1) * quarter]
    small_sent = [
        send(small.at[peer], small_z.at[k], z_send.at[1, k], z_recv.at[1, k], "fsdp", peer)
        for k, peer in enumerate(others)
    ]
    grad_ref[...] = dmixed_ref[...] + norm_backward(grad, vec_ref[0:1, :], unit, inverse)
    small_total = small[plane]
    flat_total = flat_ref[plane]
    for k in range(planes - 1):
        flat_sent[k].wait()
        small_sent[k].wait()
        small_total = small_total + small_z[k]
        flat_total = flat_total + flat_z[k]
    small_own[...] = small_total
    flat_own[...] = flat_total
    sent = []
    for k, peer in enumerate(around):
        sent.append(send(small_own, small_c.at[k], c_send.at[0, k], c_recv.at[0, k], "ctx", peer))
        sent.append(send(flat_own, flat_c.at[k], c_send.at[1, k], c_recv.at[1, k], "ctx", peer))
    plane_gather_finish(qkv_started, [qkv_all], qkv_sems, chips)
    for copy in sent:
        copy.wait()
    for k in range(n_ctx - 1):
        small_total = small_total + small_c[k]
        flat_total = flat_total + flat_c[k]
    sums_ref[...] = small_total
    flat_out[...] = flat_total


def first_norm_back(part, qkv_part, outw_own, flat, tok, dmixed, vecs):
    planes, n_ctx, half, width = part.shape
    rows = tok.shape[0]
    seqs = rows // half
    quarter, columns = qkv_part.shape[1:]
    chips, pairs = n_ctx // 2, planes // seqs
    size = (8, quarter + -quarter % LANES)
    return pl.pallas_call(
        functools.partial(fourth_kernel, chips, planes, seqs),
        out_shape=(
            jax.ShapeDtypeStruct((rows, width), F32),
            jax.ShapeDtypeStruct((n_ctx, pairs, quarter, columns), BF16),
            jax.ShapeDtypeStruct((n_ctx,) + outw_own.shape, BF16),
            jax.ShapeDtypeStruct(size, F32),
            jax.ShapeDtypeStruct(flat.shape[1:], F32),
        ),
        in_specs=[ANY, ANY, ANY, VMEM, VMEM, VMEM, VMEM],
        out_specs=(VMEM, ANY, ANY, VMEM, VMEM),
        scratch_shapes=[
            pltpu.VMEM((planes, quarter, columns), BF16),
            pltpu.VMEM((pairs, quarter, columns), BF16),
            DMA((planes - 1,)),
            DMA((planes - 1,)),
            DMA,
            pltpu.VMEM((planes, half, width), BF16),
            pltpu.VMEM((planes, half, width), BF16),
            DMA((planes - 1,)),
            DMA((planes - 1,)),
            pltpu.VMEM((planes,) + size, F32),
            pltpu.VMEM(size, F32),
            pltpu.VMEM((planes - 1,) + size, F32),
            pltpu.VMEM((n_ctx - 1,) + size, F32),
            pltpu.VMEM(flat.shape[1:], F32),
            pltpu.VMEM((planes - 1,) + flat.shape[1:], F32),
            pltpu.VMEM((n_ctx - 1,) + flat.shape[1:], F32),
            DMA((2, planes - 1)),
            DMA((2, planes - 1)),
            DMA((2, n_ctx - 1)),
            DMA((2, n_ctx - 1)),
        ]
        + scatter_scratch(chips, planes, half, width)
        + gather_sems(chips)
        + gather_sems(chips),
        compiler_params=params(3),
        cost_estimate=SMALL,
        name="scatter_back",
    )(part, qkv_part, outw_own, flat, tok, dmixed, vecs)


def finish_kernel(
    chips,
    planes,
    seqs,
    counts,
    h1_hbm,
    d_hbm,
    w_hbm,
    up_ref,
    outw_ref,
    flat_ref,
    tok_ref,
    dmixed_ref,
    vec_ref,
    grad_ref,
    qkv_all,
    up_all,
    outw_all,
    tail_ref,
    sums_ref,
    flat_out,
    h1_ref,
    d_ref,
    w_ref,
    load_sem,
    dw_ref,
    q_arrived,
    q_own,
    q_send,
    q_recv,
    outw_arrived,
    outw_own,
    o_send,
    o_recv,
    rows_own,
    rows_arrived,
    r_send,
    r_recv,
    small,
    small_own,
    small_z,
    small_c,
    flat_own,
    flat_z,
    flat_c,
    z_send,
    z_recv,
    c_send,
    c_recv,
    t_send,
    t_recv,
    *scratch,
):
    n_ctx = 2 * chips
    pairs = planes // seqs
    me, core, chip, sibling, to, come = plane_peers(chips)
    plane, others = other_planes(planes)
    around = [lax.rem(me + k, n_ctx) for k in range(1, n_ctx)]
    made, outw_sems, qkv_sems, up_sems = scratch[:7], scratch[7:12], scratch[12:17], scratch[17:]
    loads = [
        pltpu.make_async_copy(source, target, load_sem.at[k])
        for k, (source, target) in enumerate([(d_hbm, d_ref), (h1_hbm, h1_ref), (w_hbm, w_ref)])
    ]
    for load in loads:
        load.start()
    greet(around, others)
    up_started = plane_gather_start([up_ref], [up_all], up_sems, chips)
    outw_sent = [
        send(outw_ref.at[peer], outw_arrived.at[k], o_send.at[k], o_recv.at[k], "fsdp", peer)
        for k, peer in enumerate(others)
    ]
    flat_sent = [
        send(flat_ref.at[peer], flat_z.at[k], z_send.at[0, k], z_recv.at[0, k], "fsdp", peer)
        for k, peer in enumerate(others)
    ]
    unit, inverse = normalize(tok_ref[...].astype(F32))

    for load in loads:
        load.wait()
    quarter = dw_ref.shape[1]
    dw = tn(d_ref[...], h1_ref[...]).T.astype(BF16)
    for j in range(planes):
        dw_ref[j] = dw[j * quarter : (j + 1) * quarter]
    pushed = [
        send(dw_ref.at[peer], q_arrived.at[plane], q_send.at[k], q_recv.at[k], "fsdp", peer)
        for k, peer in enumerate(others)
    ]
    q_arrived[plane] = dw_ref[plane]

    part = made[0]
    half = part.shape[3]

    calls = []

    def make(k, target):
        calls.append(k)
        if len(calls) == chips - 1:
            plane_gather_middle(up_started, [up_all], up_sems, chips)
        blocks = []
        for j in range(planes):
            start = pl.multiple_of(j * n_ctx * half + target * 2 * half, 2 * half)
            blocks.append(d_ref[pl.ds(start, 2 * half), :])
        d_h = nt(jnp.concatenate(blocks, axis=0), w_ref[...]).astype(BF16)
        for j in range(planes):
            for side in range(2):
                start = (2 * j + side) * half
                part[k, side, j] = d_h[start : start + half]

    total = plane_scatter_made(make, *made[:3], made[3:], chips, lambda: None)
    rows_own[...] = total.astype(BF16)
    rows_sent = [
        send(rows_own.at[peer], rows_arrived.at[plane], r_send.at[k], r_recv.at[k], "fsdp", peer)
        for k, peer in enumerate(others)
    ]
    rows_arrived[plane] = rows_own[plane]

    total = outw_ref[plane].astype(F32)
    for k, copy in enumerate(outw_sent):
        copy.wait()
        total = total + outw_arrived[k].astype(F32)
    outw_own[...] = total.astype(BF16)
    outw_started = plane_gather_start([outw_own], [outw_all], outw_sems, chips)
    plane_gather_end(up_started, [up_all], up_sems, chips)
    for copy in pushed:
        copy.wait()
    for pair in range(pairs):
        terms = [q_arrived[seq * pairs + pair].astype(F32) for seq in range(seqs)]
        q_own[pair] = sum(terms[1:], terms[0]).astype(BF16)
    qkv_started = plane_gather_start([q_own], [qkv_all], qkv_sems, chips)
    plane_gather_middle(outw_started, [outw_all], outw_sems, chips)
    plane_gather_middle(qkv_started, [qkv_all], qkv_sems, chips)

    for copy in rows_sent:
        copy.wait()
    halves = []
    for seq in range(seqs):
        terms = [rows_arrived[seq * pairs + pair].astype(F32) for pair in range(pairs)]
        halves.append(sum(terms[1:], terms[0]))
    grad = jnp.concatenate(halves, axis=0)
    sums = jnp.concatenate(
        [jnp.sum(grad * unit, axis=0, keepdims=True), jnp.sum(grad, axis=0, keepdims=True)], axis=0
    )
    small[...] = jnp.zeros_like(small)
    for j in range(planes):
        small[j, 0:2, 0:quarter] = sums[:, j * quarter : (j + 1) * quarter]
    small_sent = [
        send(small.at[peer], small_z.at[k], z_send.at[1, k], z_recv.at[1, k], "fsdp", peer)
        for k, peer in enumerate(others)
    ]
    grad_ref[...] = dmixed_ref[...] + norm_backward(grad, vec_ref[0:1, :], unit, inverse)
    small_total = small[plane]
    flat_total = flat_ref[plane]
    for k in range(planes - 1):
        flat_sent[k].wait()
        small_sent[k].wait()
        small_total = small_total + small_z[k]
        flat_total = flat_total + flat_z[k]
    small_own[...] = small_total
    flat_own[...] = flat_total
    sent = []
    for k, peer in enumerate(around):
        sent.append(send(small_own, small_c.at[k], c_send.at[0, k], c_recv.at[0, k], "ctx", peer))
        sent.append(send(flat_own, flat_c.at[k], c_send.at[1, k], c_recv.at[1, k], "ctx", peer))
    plane_gather_end(outw_started, [outw_all], outw_sems, chips)
    last_head = sum((plane == j).astype(jnp.int32) * (counts[j] - 1) for j in range(planes))

    def tail_copy():
        return pltpu.make_async_remote_copy(
            src_ref=outw_all.at[last_head],
            dst_ref=tail_ref,
            send_sem=t_send,
            recv_sem=t_recv,
            device_id={"fsdp": lax.rem(plane + 1, planes)},
            device_id_type=MESH,
        )

    @pl.when(plane < planes - 1)
    def _():
        tail_copy().start()

    plane_gather_end(qkv_started, [qkv_all], qkv_sems, chips)
    for copy in sent:
        copy.wait()
    for k in range(n_ctx - 1):
        small_total = small_total + small_c[k]
        flat_total = flat_total + flat_c[k]
    @pl.when(plane < planes - 1)
    def _():
        tail_copy().wait_send()

    @pl.when(plane > 0)
    def _():
        tail_copy().wait_recv()

    sums_ref[...] = small_total
    flat_out[...] = flat_total


def finish(h1, d_qkv, weight, up_own, outw_part, flat, tok, dmixed, vecs, counts):
    rows, width = tok.shape
    planes = outw_part.shape[0]
    n_ctx = lax.axis_size("ctx")
    half = h1.shape[0] // (planes * n_ctx)
    seqs = rows // half
    quarter, columns = width // planes, weight.shape[1]
    chips, pairs = n_ctx // 2, planes // seqs
    size = (8, quarter + -quarter % LANES)
    piece = outw_part.shape[1:]
    return pl.pallas_call(
        functools.partial(finish_kernel, chips, planes, seqs, counts),
        out_shape=(
            jax.ShapeDtypeStruct((rows, width), F32),
            jax.ShapeDtypeStruct((n_ctx, pairs, quarter, columns), BF16),
            jax.ShapeDtypeStruct((n_ctx,) + up_own.shape, BF16),
            jax.ShapeDtypeStruct((n_ctx,) + piece, BF16),
            jax.ShapeDtypeStruct(piece, BF16),
            jax.ShapeDtypeStruct(size, F32),
            jax.ShapeDtypeStruct(flat.shape[1:], F32),
        ),
        in_specs=[ANY] * 4 + [VMEM] * 5,
        out_specs=(VMEM, ANY, ANY, ANY, ANY, VMEM, VMEM),
        scratch_shapes=[
            pltpu.VMEM(h1.shape, BF16),
            pltpu.VMEM(d_qkv.shape, BF16),
            pltpu.VMEM(weight.shape, BF16),
            DMA((3,)),
            pltpu.VMEM((planes, quarter, columns), BF16),
            pltpu.VMEM((planes, quarter, columns), BF16),
            pltpu.VMEM((pairs, quarter, columns), BF16),
            DMA((planes - 1,)),
            DMA((planes - 1,)),
            pltpu.VMEM((planes - 1,) + piece, BF16),
            pltpu.VMEM(piece, BF16),
            DMA((planes - 1,)),
            DMA((planes - 1,)),
            pltpu.VMEM((planes, half, width), BF16),
            pltpu.VMEM((planes, half, width), BF16),
            DMA((planes - 1,)),
            DMA((planes - 1,)),
            pltpu.VMEM((planes,) + size, F32),
            pltpu.VMEM(size, F32),
            pltpu.VMEM((planes - 1,) + size, F32),
            pltpu.VMEM((n_ctx - 1,) + size, F32),
            pltpu.VMEM(flat.shape[1:], F32),
            pltpu.VMEM((planes - 1,) + flat.shape[1:], F32),
            pltpu.VMEM((n_ctx - 1,) + flat.shape[1:], F32),
            DMA((2, planes - 1)),
            DMA((2, planes - 1)),
            DMA((2, n_ctx - 1)),
            DMA((2, n_ctx - 1)),
            DMA,
            DMA,
        ]
        + made_scratch(chips, planes, half, width)
        + gather_sems(chips)
        + gather_sems(chips)
        + gather_sems(chips),
        compiler_params=params(9),
        cost_estimate=SMALL,
        name="finish",
    )(h1, d_qkv, weight, up_own, outw_part, flat, tok, dmixed, vecs)


def to_heads_kernel(
    planes, seqs, chips, tok_ref, down_ref, head_ref, down_all, send_sems, recv_sems, local_sem, *sems
):
    ctx_me, core, chip, sibling, to, come = plane_peers(chips)
    me, others = other_planes(planes)
    pairs = planes // seqs
    greet(to + [sibling], others)

    def source(unit):
        start = pl.multiple_of(lax.rem(unit, pairs) * LANES, LANES)
        return tok_ref.at[:, unit // pairs, :, pl.ds(start, LANES)]

    copies = [
        send(source(unit), head_ref.at[me], send_sems.at[k], recv_sems.at[k], "fsdp", unit)
        for k, unit in enumerate(others)
    ]
    copies.append(pltpu.make_async_copy(source(me), head_ref.at[me], local_sem))
    copies[-1].start()
    plane_gather([down_ref], [down_all], sems, chips)
    for copy in copies:
        copy.wait()


def to_heads(tok, planes, cid, down_own):
    n_ctx, seqs, local_rows, width = tok.shape
    chips = n_ctx // 2
    return pl.pallas_call(
        functools.partial(to_heads_kernel, planes, seqs, chips),
        out_shape=(
            jax.ShapeDtypeStruct((planes, n_ctx, local_rows, LANES), BF16),
            jax.ShapeDtypeStruct((n_ctx,) + down_own.shape, BF16),
        ),
        in_specs=[ANY, ANY],
        out_specs=(ANY, ANY),
        scratch_shapes=[DMA((planes - 1,)), DMA((planes - 1,)), DMA] + gather_sems(chips),
        compiler_params=params(cid),
        cost_estimate=SMALL,
        name="to_heads",
    )(tok, down_own)


def to_tokens_kernel(
    planes, seqs, head_ref, weight_ref, tok_ref, weights_ref, send_sems, recv_sems, local_sem, w_send, w_recv, w_local
):
    me, others = other_planes(planes)
    pairs = planes // seqs
    greet((), others)
    start = pl.multiple_of(lax.rem(me, pairs) * LANES, LANES)
    target = tok_ref.at[:, me // pairs, :, pl.ds(start, LANES)]
    copies = [
        send(head_ref.at[peer], target, send_sems.at[k], recv_sems.at[k], "fsdp", peer) for k, peer in enumerate(others)
    ]
    copies += [
        send(weight_ref, weights_ref.at[me], w_send.at[k], w_recv.at[k], "fsdp", peer) for k, peer in enumerate(others)
    ]
    for copy in (
        pltpu.make_async_copy(head_ref.at[me], target, local_sem),
        pltpu.make_async_copy(weight_ref, weights_ref.at[me], w_local),
    ):
        copy.start()
        copies.append(copy)
    for copy in copies:
        copy.wait()


def to_tokens(heads, seqs, cid, weight):
    planes, n_ctx, rows, lanes = heads.shape
    width = (planes // seqs) * LANES
    return pl.pallas_call(
        functools.partial(to_tokens_kernel, planes, seqs),
        out_shape=(
            jax.ShapeDtypeStruct((n_ctx, seqs, rows, width), heads.dtype),
            jax.ShapeDtypeStruct((planes,) + weight.shape, BF16),
        ),
        in_specs=[ANY] * 2,
        out_specs=(ANY,) * 2,
        scratch_shapes=[DMA((planes - 1,)), DMA((planes - 1,)), DMA] * 2,
        compiler_params=params(cid),
        cost_estimate=SMALL,
        name="to_tokens",
    )(heads, weight)


def nt(left, right):
    return lax.dot_general(left, right, (((1,), (1,)), ((), ())), preferred_element_type=F32)


def nn(left, right):
    return lax.dot_general(left, right, (((1,), (0,)), ((), ())), preferred_element_type=F32)


def sort_blocks(order_ref, qkv_ref, targets, blocks, half):
    def body(block, carry):
        row = qkv_ref[order_ref[block]]
        start = pl.multiple_of(block * half, half)
        for k, target in enumerate(targets):
            target[pl.ds(start, half), :] = row[:, k * LANES : (k + 1) * LANES]
        return carry

    lax.fori_loop(0, blocks, body, 0)


def lane_mask(rows, head):
    lane = lax.broadcasted_iota(jnp.int32, (rows, LANES), 1)
    return (lane < HD) if head == 0 else (lane >= HD)


def unsort_blocks(order_ref, sorted_refs, target_ref, blocks, half):
    def body(block, carry):
        start = pl.multiple_of(block * half, half)
        place = order_ref[block]
        for k, source in enumerate(sorted_refs):
            target_ref[place, :, k * LANES : (k + 1) * LANES] = source[pl.ds(start, half), :].astype(BF16)
        return carry

    lax.fori_loop(0, blocks, body, 0)


def long_forward_kernel(tile, order_ref, qkv_ref, out_ref, att_ref, lse_ref, q_s, k_s, v_s, vt_s, o_s):
    blocks, half = out_ref.shape[0], out_ref.shape[1]
    length = blocks * half
    tiles = length // tile
    sort_blocks(order_ref, qkv_ref, [q_s, k_s, v_s], blocks, half)
    for t in range(tiles):
        span = slice(t * tile, (t + 1) * tile)
        vt_s[:, span] = v_s[span, :].T
    scale = HD ** (-0.5)
    rows_iota = lax.broadcasted_iota(jnp.int32, (tile, tile), 0)
    cols_iota = lax.broadcasted_iota(jnp.int32, (tile, tile), 1)
    allowed = rows_iota <= cols_iota
    masks = [lane_mask(tile, head) for head in range(2)]

    for qt in range(tiles):
        q_span = slice(qt * tile, (qt + 1) * tile)
        query = q_s[q_span, :] * jnp.asarray(scale, BF16)
        queries = [jnp.where(masks[head], query, jnp.zeros_like(query)) for head in range(2)]

        def step(kt, state, masked, queries=queries):
            start = pl.multiple_of(kt * tile, tile)
            keys = k_s[pl.ds(start, tile), :]
            new = []
            for head in range(2):
                top, total, acc = state[head]
                scores = nt(keys, queries[head])
                if masked:
                    scores = jnp.where(allowed, scores, NEG_BIG)
                new_top = jnp.maximum(top, jnp.max(scores, axis=0, keepdims=True))
                soft = jnp.exp(scores - new_top)
                factor = jnp.exp(top - new_top)
                total = total * factor + jnp.sum(soft, axis=0, keepdims=True)
                values = vt_s[head * HD : (head + 1) * HD, pl.ds(start, tile)]
                acc = acc * factor + nn(values, soft.astype(BF16))
                new.append((new_top, total, acc))
            return tuple(new)

        state = tuple(
            (jnp.full((1, tile), NEG_BIG, F32), jnp.zeros((1, tile), F32), jnp.zeros((HD, tile), F32))
            for head in range(2)
        )
        state = step(qt, state, True)
        if qt > 0:
            state = lax.fori_loop(0, qt, lambda kt, s, step=step: step(kt, s, False), state)
        parts = []
        for head in range(2):
            top, total, acc = state[head]
            parts.append(acc / total)
            lse_ref[head : head + 1, q_span] = top + jnp.log(total)
        att = jnp.concatenate(parts, axis=0).T
        att_ref[q_span, :] = att
        o_s[q_span, :] = att.astype(BF16)

    unsort_blocks(order_ref, [o_s], out_ref, blocks, half)


def block_places(order, n_ctx):
    blocks = order.shape[0]
    places = jnp.stack([order // (2 * n_ctx), lax.rem(order // 2, n_ctx), lax.rem(order, 2)]).astype(jnp.int32)
    match = order[:, None] == jnp.arange(blocks)[None, :]
    inverse = jnp.sum(jnp.where(match, jnp.arange(blocks)[:, None], 0), axis=0).astype(jnp.int32)
    return places, inverse


def sort_places(order_ref, source, targets):
    blocks, half = order_ref.shape[1], source.shape[3]

    def body(block, carry):
        row = source[order_ref[0, block], order_ref[1, block], order_ref[2, block]]
        start = pl.multiple_of(block * half, half)
        for k, target in enumerate(targets):
            target[pl.ds(start, half), :] = row[:, k * LANES : (k + 1) * LANES]
        return carry

    lax.fori_loop(0, blocks, body, 0)


def unsort_places(place_ref, sources, target):
    n_ctx = target.shape[1]

    def body(place, carry):
        block = place_ref[place]
        f, c, side = place // (2 * n_ctx), lax.rem(place // 2, n_ctx), lax.rem(place, 2)
        for k, source in enumerate(sources):
            target[f, c, side, :, k * LANES : (k + 1) * LANES] = source[block]
        return carry

    lax.fori_loop(0, place_ref.shape[0], body, 0)


def attend_kernel(
    tile,
    planes,
    seqs,
    order_ref,
    place_ref,
    h1_hbm,
    w_hbm,
    shift_ref,
    out_w_ref,
    qkv_ref,
    att_ref,
    lse_ref,
    tok_ref,
    out_ws_ref,
    h1_ref,
    w_ref,
    load_sem,
    heads,
    a_send,
    a_recv,
    a_local,
    w_send,
    w_recv,
    w_local,
    q_s,
    k_s,
    v_s,
    o_s,
    s_s,
    p_s,
):
    me, others = other_planes(planes)
    pairs = planes // seqs
    n_ctx, half = qkv_ref.shape[1], qkv_ref.shape[3]
    length = att_ref.shape[0]
    tiles, step = length // tile, tile // half
    rows = length // planes
    loads = [pltpu.make_async_copy(w_hbm, w_ref, load_sem.at[planes])]
    for j in range(planes):
        span = pl.ds(j * rows, rows)
        loads.append(pltpu.make_async_copy(h1_hbm.at[span], h1_ref.at[span], load_sem.at[j]))
    for load in loads:
        load.start()
    greet((), others)
    moved = [
        send(out_w_ref, out_ws_ref.at[me], w_send.at[k], w_recv.at[k], "fsdp", peer) for k, peer in enumerate(others)
    ]
    moved.append(pltpu.make_async_copy(out_w_ref, out_ws_ref.at[me], w_local))
    moved[-1].start()

    loads[0].wait()
    for j in range(planes):
        loads[1 + j].wait()
        values = nn(h1_ref[j * rows : (j + 1) * rows, :], w_ref[...]) + shift_ref[...]
        qkv_ref[j] = values.astype(BF16).reshape(n_ctx, 2, half, values.shape[1])

    sort_places(order_ref, qkv_ref, [q_s, k_s, v_s])
    scale = HD ** (-0.5)
    rows_iota = lax.broadcasted_iota(jnp.int32, (tile, tile), 0)
    cols_iota = lax.broadcasted_iota(jnp.int32, (tile, tile), 1)
    allowed = cols_iota <= rows_iota
    masks = [lane_mask(tile, head) for head in range(2)]
    for qt in range(tiles):
        q_span = slice(qt * tile, (qt + 1) * tile)
        query = q_s[q_span, :] * jnp.asarray(scale, BF16)
        parts = []
        for head in range(2):
            one = jnp.where(masks[head], query, jnp.zeros_like(query))
            top = jnp.full((tile, LANES), NEG_BIG, F32)
            for kt in range(qt + 1):
                k_span = slice(kt * tile, (kt + 1) * tile)
                scores = nt(one, k_s[k_span, :])
                if kt == qt:
                    scores = jnp.where(allowed, scores, NEG_BIG)
                s_s[head, :, k_span] = scores
                for lane in range(0, tile, LANES):
                    top = jnp.maximum(top, scores[:, lane : lane + LANES])
            top = jnp.max(top, axis=1, keepdims=True)
            total = jnp.zeros((tile, LANES), F32)
            for kt in range(qt + 1):
                k_span = slice(kt * tile, (kt + 1) * tile)
                soft = jnp.exp(s_s[head, :, k_span] - top)
                for lane in range(0, tile, LANES):
                    total = total + soft[:, lane : lane + LANES]
                p_s[head, :, k_span] = soft.astype(BF16)
            total = jnp.sum(total, axis=1, keepdims=True)
            span = slice(0, (qt + 1) * tile)
            parts.append(nn(p_s[head, :, span], v_s[span, :]) / total)
            lse = jnp.broadcast_to(top + jnp.log(total), (tile, LANES))
            lse_ref[head : head + 1, q_span] = lse.T[0:1, :]
        att = jnp.where(masks[0], parts[0], parts[1])
        att_ref[q_span, :] = att
        o_s[qt * step : (qt + 1) * step] = att.astype(BF16).reshape(step, half, LANES)
    unsort_places(place_ref, [o_s], heads)

    start = pl.multiple_of(lax.rem(me, pairs) * LANES, LANES)
    target = tok_ref.at[:, me // pairs, :, :, pl.ds(start, LANES)]
    moved += [
        send(heads.at[peer], target, a_send.at[k], a_recv.at[k], "fsdp", peer) for k, peer in enumerate(others)
    ]
    moved.append(pltpu.make_async_copy(heads.at[me], target, a_local))
    moved[-1].start()
    for copy in moved:
        copy.wait()


def attend(places, inverse, h1, weight, shift, out_own, n_ctx, planes, seqs, half, tile):
    length = h1.shape[0]
    lanes = weight.shape[1]
    blocks = length // half
    width = (planes // seqs) * LANES
    rows_s = pltpu.VMEM((length, LANES), BF16)
    sems = [DMA((planes - 1,)), DMA((planes - 1,)), DMA]
    return pl.pallas_call(
        functools.partial(attend_kernel, tile, planes, seqs),
        out_shape=(
            jax.ShapeDtypeStruct((planes, n_ctx, 2, half, lanes), BF16),
            jax.ShapeDtypeStruct((length, LANES), F32),
            jax.ShapeDtypeStruct((2, length), F32),
            jax.ShapeDtypeStruct((n_ctx, seqs, 2, half, width), BF16),
            jax.ShapeDtypeStruct((planes,) + out_own.shape, BF16),
        ),
        in_specs=[SMEM, SMEM, ANY, ANY, VMEM, ANY],
        out_specs=(VMEM, VMEM, VMEM, ANY, ANY),
        scratch_shapes=[
            pltpu.VMEM(h1.shape, BF16),
            pltpu.VMEM(weight.shape, BF16),
            DMA((planes + 1,)),
            pltpu.VMEM((planes, n_ctx, 2, half, LANES), BF16),
        ]
        + sems
        + sems
        + [rows_s, rows_s, rows_s, pltpu.VMEM((blocks, half, LANES), BF16)]
        + [pltpu.VMEM((2, tile, length), F32), pltpu.VMEM((2, tile, length), BF16)],
        compiler_params=params(5),
        cost_estimate=SMALL,
        name="attend",
    )(places, inverse, h1, weight, shift, out_own)


SMEM = pl.BlockSpec(memory_space=pltpu.SMEM)
SHORT = 2048


def attend_forward(order, qkv, tile):
    blocks, half, lanes = qkv.shape
    length = blocks * half
    rows = pltpu.VMEM((length, LANES), BF16)
    return pl.pallas_call(
        functools.partial(long_forward_kernel, tile),
        out_shape=(
            jax.ShapeDtypeStruct((blocks, half, LANES), BF16),
            jax.ShapeDtypeStruct((length, LANES), F32),
            jax.ShapeDtypeStruct((2, length), F32),
        ),
        in_specs=[SMEM, VMEM],
        out_specs=(VMEM, VMEM, VMEM),
        scratch_shapes=[rows, rows, rows, pltpu.VMEM((LANES, length), BF16), rows],
        compiler_params=params(),
        cost_estimate=SMALL,
        name="attend_forward",
    )(order, qkv)


def long_backward_kernel(
    tile, order_ref, qkv_ref, grad_ref, att_ref, lse_ref, out_ref, sum_ref, q_s, k_s, v_s, g_s, kt_s, dq_s, dk_s, dv_s
):
    blocks, half = grad_ref.shape[0], grad_ref.shape[1]
    length = blocks * half
    tiles = length // tile
    sort_blocks(order_ref, qkv_ref, [q_s, k_s, v_s], blocks, half)
    sort_blocks(order_ref, grad_ref, [g_s], blocks, half)
    for t in range(tiles):
        span = slice(t * tile, (t + 1) * tile)
        kt_s[:, span] = k_s[span, :].T
    scale = HD ** (-0.5)
    rows_iota = lax.broadcasted_iota(jnp.int32, (tile, tile), 0)
    cols_iota = lax.broadcasted_iota(jnp.int32, (tile, tile), 1)
    allowed = rows_iota <= cols_iota
    masks = [lane_mask(tile, head) for head in range(2)]
    dk_s[...] = jnp.zeros_like(dk_s)
    dv_s[...] = jnp.zeros_like(dv_s)

    for qt in range(tiles):
        q_span = slice(qt * tile, (qt + 1) * tile)
        query = q_s[q_span, :] * jnp.asarray(scale, BF16)
        grad = g_s[q_span, :]
        queries = [jnp.where(masks[head], query, jnp.zeros_like(query)) for head in range(2)]
        grads = [jnp.where(masks[head], grad, jnp.zeros_like(grad)) for head in range(2)]
        product = (grad.astype(F32) * att_ref[q_span, :]).T
        dots = [jnp.sum(product[head * HD : (head + 1) * HD], axis=0, keepdims=True) for head in range(2)]
        totals = [lse_ref[head : head + 1, q_span] for head in range(2)]

        def step(kt, state, masked, queries=queries, grads=grads, dots=dots, totals=totals):
            start = pl.multiple_of(kt * tile, tile)
            rows = pl.ds(start, tile)
            keys = k_s[rows, :]
            values = v_s[rows, :]
            dk = dk_s[rows, :]
            dv = dv_s[rows, :]
            new = []
            for head in range(2):
                scores = nt(keys, queries[head])
                if masked:
                    scores = jnp.where(allowed, scores, NEG_BIG)
                soft = jnp.exp(scores - totals[head])
                dsoft = nt(values, grads[head])
                dscore = (soft * (dsoft - dots[head])).astype(BF16)
                dv = dv + nn(soft.astype(BF16), grads[head])
                dk = dk + nn(dscore, queries[head])
                new.append(state[head] + nn(kt_s[head * HD : (head + 1) * HD, rows], dscore))
            dk_s[rows, :] = dk
            dv_s[rows, :] = dv
            return tuple(new)

        state = (jnp.zeros((HD, tile), F32), jnp.zeros((HD, tile), F32))
        state = step(qt, state, True)
        if qt > 0:
            state = lax.fori_loop(0, qt, lambda kt, s, step=step: step(kt, s, False), state)
        dq = jnp.concatenate(state, axis=0) * scale
        dq_s[q_span, :] = dq.T.astype(BF16)

    unsort_blocks(order_ref, [dq_s, dk_s, dv_s], out_ref, blocks, half)
    for k, source in enumerate([dq_s, dk_s, dv_s]):
        values = source[...].astype(BF16).astype(F32)
        sum_ref[:, k * LANES : (k + 1) * LANES] = jnp.sum(values, axis=0, keepdims=True)


def branch_back_kernel(
    tile,
    planes,
    seqs,
    chips,
    order_ref,
    place_ref,
    db_hbm,
    w_hbm,
    at_hbm,
    qkv_hbm,
    att_hbm,
    down_ref,
    out_part_ref,
    mixed_ref,
    vec_ref,
    lse_ref,
    out_ref,
    sum_ref,
    out_w_ref,
    block_ref,
    down_all,
    db_ref,
    w_ref,
    at_ref,
    qkv_ref,
    att_ref,
    load_sem,
    d_att,
    heads,
    h_send,
    h_recv,
    h_local,
    q_s,
    k_s,
    v_s,
    g_s,
    kt_s,
    dq_s,
    dk_s,
    dv_s,
    qh_s,
    gh_s,
    dot_s,
    p_s,
    ds_s,
    *scratch,
):
    n_ctx = 2 * chips
    ctx_me, core, chip, sibling, to, come = plane_peers(chips)
    me, others = other_planes(planes)
    pairs = planes // seqs
    out_scatter, down_sems = scratch[:8], scratch[8:]
    loads = [
        pltpu.make_async_copy(source, target, load_sem.at[k])
        for k, (source, target) in enumerate(
            [(db_hbm, db_ref), (w_hbm, w_ref), (qkv_hbm, qkv_ref), (at_hbm, at_ref), (att_hbm, att_ref)]
        )
    ]
    for load in loads:
        load.start()
    greet(to + [sibling], others)
    down_started = plane_gather_start([down_ref], [down_all], down_sems, chips)
    out_total = []
    out_stages = plane_scatter_stages(
        lambda c: out_part_ref.at[c], *out_scatter[:3], out_scatter[3:], chips, out_total
    )
    next(out_stages)

    loads[0].wait()
    loads[1].wait()
    d_att[...] = nt(db_ref[...], w_ref[...]).astype(BF16).reshape(d_att.shape)

    def source(unit):
        start = pl.multiple_of(lax.rem(unit, pairs) * LANES, LANES)
        return d_att.at[:, unit // pairs, :, :, pl.ds(start, LANES)]

    moved = [
        send(source(unit), heads.at[me], h_send.at[k], h_recv.at[k], "fsdp", unit) for k, unit in enumerate(others)
    ]
    moved.append(pltpu.make_async_copy(source(me), heads.at[me], h_local))
    moved[-1].start()
    for load in loads[2:]:
        load.wait()
    out_w_ref[...] = tn(at_ref[...], db_ref[...]).astype(BF16)

    blocks, half = dq_s.shape[0], dq_s.shape[1]
    length = blocks * half
    tiles, step = length // tile, tile // half

    sort_places(order_ref, qkv_ref, [q_s, k_s, v_s])
    scale = HD ** (-0.5)
    rows_iota = lax.broadcasted_iota(jnp.int32, (tile, tile), 0)
    cols_iota = lax.broadcasted_iota(jnp.int32, (tile, tile), 1)
    allowed = rows_iota <= cols_iota
    masks = [lane_mask(tile, head) for head in range(2)]
    for t in range(tiles):
        span = slice(t * tile, (t + 1) * tile)
        kt_s[:, span] = k_s[span, :].T
        query = q_s[span, :] * jnp.asarray(scale, BF16)
        for head in range(2):
            qh_s[head, span, :] = jnp.where(masks[head], query, jnp.zeros_like(query))
    next(out_stages)
    for copy in moved:
        copy.wait()
    sort_places(order_ref, heads, [g_s])
    for t in range(tiles):
        span = slice(t * tile, (t + 1) * tile)
        grad = g_s[span, :]
        product = (grad.astype(F32) * att_ref[span, :]).T
        for head in range(2):
            gh_s[head, span, :] = jnp.where(masks[head], grad, jnp.zeros_like(grad))
            dot_s[head : head + 1, span] = jnp.sum(product[head * HD : (head + 1) * HD], axis=0, keepdims=True)
    plane_gather_middle(down_started, [down_all], down_sems, chips)

    def keep(target, index, values):
        target[index * step : (index + 1) * step] = values.astype(BF16).reshape(step, half, LANES)

    for kt in range(tiles):
        k_span = slice(kt * tile, (kt + 1) * tile)
        rest = slice(kt * tile, length)
        keys, values = k_s[k_span, :], v_s[k_span, :]
        dk, dv = None, None
        for head in range(2):
            for qt in range(kt, tiles):
                span = slice(qt * tile, (qt + 1) * tile)
                scores = nt(keys, qh_s[head, span, :])
                if kt == qt:
                    scores = jnp.where(allowed, scores, NEG_BIG)
                soft = jnp.exp(scores - lse_ref[head : head + 1, span])
                p_s[head, :, span] = soft.astype(BF16)
                dsoft = nt(values, gh_s[head, span, :])
                ds_s[head, k_span, span] = (soft * (dsoft - dot_s[head : head + 1, span])).astype(BF16)
            dv_one = nn(p_s[head, :, rest], gh_s[head, rest, :])
            dk_one = nn(ds_s[head, k_span, rest], qh_s[head, rest, :])
            dv = dv_one if dv is None else dv + dv_one
            dk = dk_one if dk is None else dk + dk_one
        keep(dk_s, kt, dk)
        keep(dv_s, kt, dv)
        if kt == 0:
            next(out_stages, None)
    for qt in range(tiles):
        span = slice(qt * tile, (qt + 1) * tile)
        upto = slice(0, (qt + 1) * tile)
        dq = [nn(kt_s[head * HD : (head + 1) * HD, upto], ds_s[head, upto, span]) for head in range(2)]
        keep(dq_s, qt, (jnp.concatenate(dq, axis=0) * scale).T)
    for unused in out_stages:
        pass
    block_ref[...] = (mixed_ref[...] + out_total[0] + vec_ref[...]).astype(BF16)

    unsort_places(place_ref, [dq_s, dk_s, dv_s], out_ref)
    for k, ref in enumerate([dq_s, dk_s, dv_s]):
        values = ref[...].astype(F32)
        sum_ref[:, k * LANES : (k + 1) * LANES] = jnp.sum(jnp.sum(values, axis=0), axis=0, keepdims=True)
    plane_gather_end(down_started, [down_all], down_sems, chips)


def branch_back(places, inverse, d_branch, weight, att, qkv, att_exact, lse, down_own, out_part, mixed, vec, planes, tile):
    shape = qkv.shape
    half, lanes = shape[3:]
    n_ctx, rows, width = out_part.shape
    blocks = 2 * planes * n_ctx
    length = blocks * half
    seqs = rows * n_ctx * planes // length
    chips = n_ctx // 2
    rows_s = pltpu.VMEM((length, LANES), BF16)
    blocks_s = pltpu.VMEM((blocks, half, LANES), BF16)
    return pl.pallas_call(
        functools.partial(branch_back_kernel, tile, planes, seqs, chips),
        out_shape=(
            jax.ShapeDtypeStruct(shape, BF16),
            jax.ShapeDtypeStruct((1, lanes), F32),
            jax.ShapeDtypeStruct(weight.shape, BF16),
            jax.ShapeDtypeStruct((rows, width), BF16),
            jax.ShapeDtypeStruct((n_ctx,) + down_own.shape, BF16),
        ),
        in_specs=[SMEM, SMEM] + [ANY] * 7 + [VMEM] * 3,
        out_specs=(VMEM, VMEM, VMEM, VMEM, ANY),
        scratch_shapes=[
            pltpu.VMEM(d_branch.shape, BF16),
            pltpu.VMEM(weight.shape, BF16),
            pltpu.VMEM(att.shape, BF16),
            pltpu.VMEM(shape, BF16),
            pltpu.VMEM(att_exact.shape, F32),
            DMA((5,)),
            pltpu.VMEM((n_ctx, seqs, 2, half, weight.shape[0]), BF16),
            pltpu.VMEM((planes, n_ctx, 2, half, LANES), BF16),
            DMA((planes - 1,)),
            DMA((planes - 1,)),
            DMA,
            rows_s,
            rows_s,
            rows_s,
            rows_s,
            pltpu.VMEM((LANES, length), BF16),
            blocks_s,
            blocks_s,
            blocks_s,
            pltpu.VMEM((2, length, LANES), BF16),
            pltpu.VMEM((2, length, LANES), BF16),
            pltpu.VMEM((2, length), F32),
            pltpu.VMEM((2, tile, length), BF16),
            pltpu.VMEM((2, length, length), BF16),
        ]
        + scatter_scratch(chips, rows, width)
        + gather_sems(chips),
        compiler_params=params(10),
        cost_estimate=SMALL,
        name="branch_back",
    )(places, inverse, d_branch, weight, att, qkv, att_exact, down_own, out_part, mixed, vec, lse)


def attend_backward(order, qkv, grad, att, lse, tile):
    blocks, half, lanes = qkv.shape
    length = blocks * half
    rows = pltpu.VMEM((length, LANES), BF16)
    flipped = pltpu.VMEM((LANES, length), BF16)
    return pl.pallas_call(
        functools.partial(long_backward_kernel, tile),
        out_shape=(
            jax.ShapeDtypeStruct((blocks, half, 3 * LANES), BF16),
            jax.ShapeDtypeStruct((1, 3 * LANES), F32),
        ),
        in_specs=[SMEM, VMEM, VMEM, VMEM, VMEM],
        out_specs=(VMEM, VMEM),
        scratch_shapes=[rows, rows, rows, rows, flipped, rows] + [pltpu.VMEM((length, LANES), F32)] * 2,
        compiler_params=params(),
        cost_estimate=SMALL,
        name="attend_backward",
    )(order, qkv, grad, att, lse)


def assemble_kernel(pieces, part_ref, out_ref):
    for start, source, first, size in pieces:
        out_ref[:, start : start + size] = part_ref[source, :, first : first + size].astype(F32)


def assemble(parts, pieces, width):
    n_ctx, rows, columns = parts.shape
    block = -(-rows // 32) * 16
    return pl.pallas_call(
        functools.partial(assemble_kernel, pieces),
        grid=(-(-rows // block),),
        out_shape=jax.ShapeDtypeStruct((rows, width), F32),
        in_specs=[pl.BlockSpec((n_ctx, block, columns), lambda i: (0, i, 0))],
        out_specs=pl.BlockSpec((block, width), lambda i: (i, 0)),
        compiler_params=params(),
        name="assemble",
    )(parts)


def assemble_packed_kernel(pieces, part_ref, out_ref):
    hidden = part_ref.shape[2] // 2
    for side in range(2):

        @pl.when(pl.program_id(0) == side)
        def _(side=side):
            for start, source, first, size in pieces:
                first = first + side * hidden
                out_ref[:, start : start + size] = part_ref[source, :, first : first + size].astype(F32)


def assemble_packed(parts, pieces, width):
    n_ctx, rows, columns = parts.shape
    return pl.pallas_call(
        functools.partial(assemble_packed_kernel, pieces),
        grid=(2,),
        out_shape=jax.ShapeDtypeStruct((2 * rows, width), F32),
        in_specs=[pl.BlockSpec((n_ctx, rows, columns), lambda i: (0, 0, 0), pipeline_mode=pl.Buffered(1))],
        out_specs=pl.BlockSpec((rows, width), lambda i: (i, 0)),
        compiler_params=params(),
        name="assemble_packed",
    )(parts)


def tn(left, right):
    return nn(left.T, right)


def rows_block(rows, most):
    return math.gcd(rows, most)


def whole_block(shape):
    return pl.BlockSpec(shape, lambda i: (0,) * len(shape), pipeline_mode=pl.Buffered(1))


def row_spec(block, width):
    return pl.BlockSpec((block, width), lambda i: (i, 0))


def product_kernel(left_ref, right_ref, shift_ref, out_ref):
    out_ref[...] = (nn(left_ref[...], right_ref[...]) + shift_ref[...]).astype(BF16)


def product(left, right, shift=None):
    rows, depth = left.shape
    width = right.shape[1]
    block = rows_block(rows, 512)
    if shift is None:
        shift = jnp.zeros((width,), F32)
    return pl.pallas_call(
        product_kernel,
        grid=(rows // block,),
        out_shape=jax.ShapeDtypeStruct((rows, width), BF16),
        in_specs=[row_spec(block, depth), whole_block((depth, width)), whole_block((1, width))],
        out_specs=row_spec(block, width),
        compiler_params=params(),
        cost_estimate=SMALL,
        name="product",
    )(left, right, shift[None, :])


def back_kernel(left_ref, grad_ref, weight_ref, grad_left_ref, grad_weight_ref, sum_ref, total):
    step = pl.program_id(0)
    grad = grad_ref[...]
    grad_left_ref[...] = nt(grad, weight_ref[...]).astype(BF16)
    term = tn(grad, left_ref[...])
    sums = jnp.sum(grad.astype(F32), axis=0, keepdims=True)

    @pl.when(step == 0)
    def _():
        total[...] = term
        sum_ref[...] = sums

    @pl.when(step > 0)
    def _():
        total[...] += term
        sum_ref[...] += sums

    @pl.when(step == pl.num_programs(0) - 1)
    def _():
        grad_weight_ref[...] = total[...].T.astype(BF16)


def product_back(left, grad, weight):
    rows, depth = left.shape
    width = grad.shape[1]
    block = rows_block(rows, 512)
    return pl.pallas_call(
        back_kernel,
        grid=(rows // block,),
        out_shape=(
            jax.ShapeDtypeStruct((rows, depth), BF16),
            jax.ShapeDtypeStruct((depth, width), BF16),
            jax.ShapeDtypeStruct((1, width), F32),
        ),
        in_specs=[row_spec(block, depth), row_spec(block, width), whole_block((depth, width))],
        out_specs=(
            row_spec(block, depth),
            pl.BlockSpec((depth, width), lambda i: (0, 0)),
            pl.BlockSpec((1, width), lambda i: (0, 0)),
        ),
        scratch_shapes=[pltpu.VMEM((width, depth), F32)],
        compiler_params=params(),
        cost_estimate=SMALL,
        name="product_back",
    )(left, grad, weight)


def out_back_kernel(att_ref, grad_ref, weight_ref, grad_att_ref, grad_weight_ref, total):
    step = pl.program_id(0)
    grad = grad_ref[...]
    grad_att_ref[...] = nt(grad, weight_ref[...]).astype(BF16)
    term = tn(att_ref[...], grad)

    @pl.when(step == 0)
    def _():
        total[...] = term

    @pl.when(step > 0)
    def _():
        total[...] += term

    @pl.when(step == pl.num_programs(0) - 1)
    def _():
        grad_weight_ref[...] = total[...].astype(BF16)


def out_back(att, grad, weight):
    rows, depth = att.shape
    width = grad.shape[1]
    block = rows_block(rows, 512)
    return pl.pallas_call(
        out_back_kernel,
        grid=(rows // block,),
        out_shape=(jax.ShapeDtypeStruct((rows, depth), BF16), jax.ShapeDtypeStruct((depth, width), BF16)),
        in_specs=[row_spec(block, depth), row_spec(block, width), whole_block((depth, width))],
        out_specs=(row_spec(block, depth), pl.BlockSpec((depth, width), lambda i: (0, 0))),
        scratch_shapes=[pltpu.VMEM((depth, width), F32)],
        compiler_params=params(),
        cost_estimate=SMALL,
        name="out_back",
    )(att, grad, weight)


GELU_A = math.sqrt(2.0 / math.pi)
GELU_B = 0.044715


def up_kernel(h_ref, og_ref, weight_ref, shift_ref, act_ref, slope_ref, grad_ref, total):
    step = pl.program_id(0)
    up = nn(h_ref[...], weight_ref[...]) + shift_ref[...]
    square = up * up
    soft = jnp.tanh(GELU_A * up * (1.0 + GELU_B * square))
    half = 0.5 * (1.0 + soft)
    act = (up * half).astype(BF16)
    act_ref[...] = act
    slope_ref[...] = half + 0.5 * up * (1.0 - soft * soft) * (GELU_A * (1.0 + 3.0 * GELU_B * square))
    term = tn(act, og_ref[...])

    @pl.when(step == 0)
    def _():
        total[...] = term

    @pl.when(step > 0)
    def _():
        total[...] += term

    @pl.when(step == pl.num_programs(0) - 1)
    def _():
        grad_ref[...] = total[...].astype(BF16)


def feed_up(values, out_grad, weight, shift):
    rows, width = values.shape
    hidden = weight.shape[1]
    block = rows_block(rows, 512)
    return pl.pallas_call(
        up_kernel,
        grid=(rows // block,),
        out_shape=(
            jax.ShapeDtypeStruct((rows, hidden), BF16),
            jax.ShapeDtypeStruct((rows, hidden), F32),
            jax.ShapeDtypeStruct((hidden, width), BF16),
        ),
        in_specs=[
            row_spec(block, width),
            row_spec(block, width),
            whole_block((width, hidden)),
            whole_block((1, hidden)),
        ],
        out_specs=(
            row_spec(block, hidden),
            row_spec(block, hidden),
            pl.BlockSpec((hidden, width), lambda i: (0, 0)),
        ),
        scratch_shapes=[pltpu.VMEM((hidden, width), F32)],
        compiler_params=params(),
        cost_estimate=SMALL,
        name="feed_up",
    )(values, out_grad, weight, shift[None, :])


def local(
    tokens,
    block_pairs,
    out_grad,
    ln1_gain,
    ln1_bias,
    qkv_weight,
    query_bias,
    value_bias,
    out_weight,
    out_bias,
    ln2_gain,
    ln2_bias,
    up_weight,
    up_bias,
    down_weight,
    down_bias,
):
    n_ctx, planes = lax.axis_size("ctx"), lax.axis_size("fsdp")
    c, f = lax.axis_index("ctx"), lax.axis_index("fsdp")
    local_rows, seqs, width = tokens.shape
    half = local_rows // 2
    devices = n_ctx * planes
    blocks = 2 * devices
    length = devices * local_rows
    heads = width // HD
    slots = planes * (-(-heads // devices))
    assert slots == planes and planes % seqs == 0
    span = slots * HD
    rows = local_rows * seqs
    plane_rows = n_ctx * rows
    quarter = width // planes
    ff = up_weight.shape[1]
    ff_quarter = ff // planes
    ff_piece = ff_quarter // n_ctx
    ff_span = ff_piece * planes
    tile = 256
    halved = quarter % 16 == 0

    device_ids = jnp.arange(devices, dtype=jnp.int32)
    device_of_block = jnp.sum(
        jnp.where(block_pairs[None, :] == device_ids[:, None], device_ids[None, :], 0), axis=1
    )
    place_of_block = lax.rem(device_of_block, planes) * n_ctx + device_of_block // planes
    order = jnp.concatenate([place_of_block * 2, place_of_block[::-1] * 2 + 1]).astype(jnp.int32)

    first = [-(-quarter * j // HD) for j in range(planes)] + [heads]
    counts = [first[j + 1] - first[j] for j in range(planes)]
    assert max(counts) <= n_ctx
    slot_head = [jnp.minimum(first[j] + c, heads - 1) for j in range(planes)]
    first_own = jnp.asarray(first, jnp.int32)[f]
    count_own = jnp.asarray(counts, jnp.int32)[f]

    pairs = planes // seqs
    pair, pair_span = lax.rem(f, pairs), 2 * HD
    qkv_own = jnp.stack(
        [
            jnp.concatenate(
                [
                    lax.dynamic_slice(qkv_weight, (0, k * width + slot_head[j] * HD), (quarter, HD))
                    for k in range(3)
                    for j in (2 * p, 2 * p + 1)
                ],
                axis=1,
            )
            for p in range(pairs)
        ]
    )
    down_own = lax.dynamic_slice(down_weight, (c * ff_piece, 0), (ff_piece, width))


    tok = jnp.swapaxes(tokens, 0, 1).reshape(rows, width)
    og = jnp.swapaxes(out_grad, 0, 1).reshape(rows, width)

    short = -quarter % LANES
    vector_list = [ln1_gain, ln1_bias, ln2_gain, ln2_bias, query_bias, value_bias, out_bias, down_bias]
    vector_list += [up_bias[k * quarter : (k + 1) * quarter] for k in range(ff // width)]
    packed = jnp.concatenate([jnp.pad(v, (0, short)) for v in vector_list])
    packed = jnp.pad(packed, (0, -packed.size % (16 * LANES))).reshape(-1, LANES)
    up_own = jnp.concatenate(
        [
            lax.dynamic_slice(up_weight, (0, k * ff_quarter + c * ff_piece), (quarter, ff_piece))
            for k in range(planes)
        ],
        axis=1,
    )
    tok_first, up_own = lax.optimization_barrier((tok, up_own))
    vectors, og_all, h1, qkv_slice, next_rows = first_norm_gather(
        tok_first, og, packed, qkv_own, out_weight, n_ctx, planes, seqs
    )
    out_own = lax.dynamic_slice(
        jnp.concatenate([out_weight, next_rows]), ((first_own + c) * HD - f * quarter, 0), (HD, width)
    )
    out_own = jnp.where(c < count_own, out_own, jnp.zeros_like(out_own))
    h1 = h1.reshape(length, width)
    qkv_slice = qkv_slice.reshape(width, 3 * pair_span)
    h1, up_own, down_own = lax.optimization_barrier((h1, up_own, down_own))
    down_slice = lax.all_gather(down_own, "fsdp", axis=0, tiled=True)
    up_slice = lax.all_gather(up_own, "fsdp", axis=0, tiled=True)
    og_all = og_all.reshape(plane_rows, width)
    vectors = vectors.reshape(planes, -1)[:, : len(vector_list) * (quarter + short)]
    vectors = vectors.reshape(planes, len(vector_list), quarter + short)[:, :, :quarter].astype(F32)
    gain1, bias1, gain2, bias2, bias_q, bias_v, bias_o, bias_d = [
        vectors[:, k].reshape(width) for k in range(8)
    ]
    bias_up = lax.dynamic_slice(
        vectors[:, 8 : 8 + ff // width].reshape(planes, ff_quarter), (0, c * ff_piece), (planes, ff_piece)
    ).reshape(ff_span)

    pair_heads = [jnp.minimum(jnp.asarray(first, jnp.int32)[2 * pair + i] + c, heads - 1) for i in range(2)]

    def head_part(vector):
        return [lax.dynamic_slice(vector, (head * HD,), (HD,)) for head in pair_heads]

    qkv_shift = jnp.concatenate(head_part(bias_q) + [jnp.zeros((pair_span,), F32)] + head_part(bias_v))

    if length <= SHORT:
        places, inverse = block_places(order, n_ctx)
        qkv, att_exact, lse, att, out_slice = attend(
            places, inverse, h1, qkv_slice, qkv_shift[None, :], out_own, n_ctx, planes, seqs, half, tile
        )
    else:
        qkv = product(h1, qkv_slice, qkv_shift).reshape(blocks, half, 3 * pair_span)
        att_heads, att_exact, lse = attend_forward(order, qkv, tile)
        att, out_slice = to_tokens(att_heads.reshape(planes, n_ctx, local_rows, LANES), seqs, 6, out_own)
    out_slice = out_slice.reshape(span, width)
    att = att.reshape(plane_rows, span)
    mixed, h2 = second_norm_gather(att, out_slice, tok, jnp.stack([gain2, bias2, bias_o]), n_ctx)
    h2 = h2.reshape(plane_rows, width)
    def reduce_own(part):
        return lax.psum_scatter(part, "fsdp", scatter_dimension=0, tiled=True)

    act, slope, down_part = feed_up(h2, og_all, up_slice, bias_up)
    down_own_grad = reduce_own(down_part)
    d_mixed, sums2, d_branch, out_part, up_part, d_up_sum = feed_back(
        h2, og_all, act, slope, up_slice, down_slice, mixed, og, gain2[None, :], planes, halved
    )
    up_own_grad = reduce_own(up_part)
    out_part = out_part.reshape(n_ctx, rows, width)
    d_branch = d_branch.reshape(plane_rows, width)
    if length <= SHORT:
        d_qkv, d_qkv_sum, out_w_part, block_out, down_parts = branch_back(
            places,
            inverse,
            d_branch,
            out_slice,
            att,
            qkv,
            att_exact,
            lse,
            down_own_grad,
            out_part,
            mixed,
            bias_d[None, :],
            planes,
            tile,
        )
    else:
        d_att, out_w_part = out_back(att, d_branch, out_slice)
        d_att_heads, down_parts = to_heads(
            d_att.reshape(n_ctx, seqs, local_rows, span), planes, 7, down_own_grad
        )
        d_qkv, d_qkv_sum = attend_backward(
            order, qkv, d_att_heads.reshape(blocks, half, LANES), att_exact, lse, tile
        )
        total = lax.psum_scatter(out_part.reshape(plane_rows, width), "ctx", scatter_dimension=0, tiled=True)
        block_out = (mixed + total.astype(F32) + bias_d).astype(BF16)
    d_qkv, d_qkv_sum = d_qkv.reshape(length, 3 * pair_span), d_qkv_sum[0]
    down_parts, unused = lax.optimization_barrier((down_parts, d_qkv))
    down_grad = down_parts.reshape(ff_quarter, width).astype(F32)
    up_own_grad, down_grad = lax.optimization_barrier((up_own_grad, down_grad))

    d_up_sum = d_up_sum.reshape(planes, ff_piece)
    up_spread = lax.dynamic_update_slice(jnp.zeros((planes, ff_quarter), F32), d_up_sum, (0, c * ff_piece))

    def spread(values):
        full = jnp.zeros((width + HD,), F32)
        for i in range(2):
            slot = 2 * pair + i
            real = c < jnp.asarray(counts, jnp.int32)[slot]
            place = jnp.where(real, pair_heads[i] * HD, width)
            full = lax.dynamic_update_slice(full, values[i * HD : (i + 1) * HD], (place,))
        return full[None, :width]

    wide = jnp.concatenate([sums2, spread(d_qkv_sum[:pair_span]), spread(d_qkv_sum[2 * pair_span :])])
    wide = wide.reshape(6, planes, quarter).transpose(1, 0, 2).reshape(planes, 6 * quarter)
    flat = jnp.concatenate([wide, up_spread], axis=1)
    size = flat.shape[1]
    flat = jnp.pad(flat, ((0, 0), (0, -size % (8 * LANES)))).reshape(planes, -1, LANES)

    if length <= SHORT:
        grad_tok, qkv_parts, up_parts, out_parts, tail_rows, sums1, totals = finish(
            h1,
            d_qkv,
            qkv_slice,
            up_own_grad,
            out_w_part.reshape(planes, HD, width),
            flat,
            tok,
            d_mixed,
            gain1[None, :],
            counts,
        )
    else:
        d_h1, qkv_part, unused = product_back(h1, d_qkv, qkv_slice)
        grad_tok, qkv_parts, out_parts, sums1, totals = first_norm_back(
            d_h1.reshape(planes, n_ctx, local_rows, width),
            qkv_part.reshape(planes, quarter, 3 * pair_span),
            reduce_own(out_w_part),
            flat,
            tok,
            d_mixed,
            gain1[None, :],
        )
        up_parts = lax.all_gather(up_own_grad, "ctx", axis=0)
        tail_rows = lax.dynamic_index_in_dim(out_parts, count_own - 1, 0, keepdims=False)
        tail_rows = lax.ppermute(tail_rows, "fsdp", [(j, j + 1) for j in range(planes - 1)])
    sums1 = sums1[:2, :quarter]
    totals = totals.reshape(-1)
    sums = totals[: 6 * quarter].reshape(6, quarter)
    up_bias_grad = totals[6 * quarter : size]

    up_pieces = [
        (j * ff_quarter + d * ff_piece, d, j * ff_piece, ff_piece) for j in range(planes) for d in range(n_ctx)
    ]
    qkv_pieces = [
        (k * width + (first[j] + d) * HD, d * pairs + j // 2, k * pair_span + j % 2 * HD, HD)
        for k in range(3)
        for j in range(planes)
        for d in range(counts[j])
    ]
    up_grad = (assemble_packed if halved else assemble)(up_parts, up_pieces, ff)
    qkv_grad = assemble(qkv_parts.reshape(n_ctx * pairs, quarter, 3 * pair_span), qkv_pieces, 3 * width)
    out_rows = out_parts.reshape(n_ctx * HD, width)
    lead = first_own * HD - f * quarter
    out_grad_own = lax.dynamic_slice(
        jnp.concatenate([tail_rows, out_rows]), (HD - lead, 0), (quarter, width)
    ).astype(F32)

    def back(values):
        return jnp.swapaxes(values.reshape(seqs, local_rows, width), 0, 1)

    return (
        back(block_out),
        back(grad_tok),
        sums1[0],
        sums1[1],
        qkv_grad,
        sums[4],
        sums[5],
        out_grad_own,
        sums[2],
        sums[0],
        sums[1],
        up_grad,
        up_bias_grad,
        down_grad,
        sums[3],
    )


def solution(mesh):
    both, row, vec, mat = P(("ctx", "fsdp"), None, None), P(), P("fsdp"), P("fsdp", None)
    in_specs = (both, row, both, vec, vec, mat, vec, vec, mat, vec, vec, vec, mat, vec, mat, vec)
    out_specs = (both, both, vec, vec, mat, vec, vec, mat, vec, vec, vec, mat, vec, mat, vec)
    return jax.shard_map(local, mesh=mesh, in_specs=in_specs, out_specs=out_specs, check_vma=False)
```

```python
import functools
import math

import jax
import jax.numpy as jnp
from jax import lax
from jax.experimental import pallas as pl
from jax.experimental.pallas import tpu as pltpu
from jax.sharding import PartitionSpec as P

HD = 64
LANES = 128
NORM_EPS = 1e-05
NEG_BIG = -1e30
MESH = pl.DeviceIdType.MESH
F32 = jnp.float32
BF16 = jnp.bfloat16
ANY = pl.BlockSpec(memory_space=pl.ANY)
VMEM = pl.BlockSpec(memory_space=pltpu.VMEM)
DMA = pltpu.SemaphoreType.DMA
VMEM_LIMIT = 56 * 1024 * 1024
SMALL = pl.CostEstimate(flops=1, bytes_accessed=1, transcendentals=0)


def params(cid=None):
    if cid is None:
        return pltpu.CompilerParams(vmem_limit_bytes=VMEM_LIMIT)
    return pltpu.CompilerParams(
        collective_id=cid, has_side_effects=True, vmem_limit_bytes=VMEM_LIMIT
    )


def plane_peers(chips):
    me = lax.axis_index("ctx")
    core = lax.rem(me, 2)
    chip = me // 2
    sibling = chip * 2 + 1 - core
    if chips == 4:
        across_x = chip + 1 - 2 * lax.rem(chip, 2)
        across_y = lax.rem(chip + 2, 4)
        corner = lax.rem(across_x + 2, 4)
        first = across_x * (1 - core) + across_y * core
        second = across_y * (1 - core) + across_x * core
        to = come = [first * 2 + core, second * 2 + core, corner * 2 + core]
    else:
        to = [lax.rem(chip + k, chips) * 2 + core for k in range(1, chips)]
        come = [lax.rem(chip + chips - k, chips) * 2 + core for k in range(1, chips)]
    return me, core, chip, sibling, to, come


def greet(plane=(), across=()):
    barrier = pltpu.get_barrier_semaphore()
    for peer in plane:
        pl.semaphore_signal(barrier, inc=1, device_id={"ctx": peer}, device_id_type=MESH)
    for peer in across:
        pl.semaphore_signal(barrier, inc=1, device_id={"fsdp": peer}, device_id_type=MESH)
    pl.semaphore_wait(barrier, len(plane) + len(across))


def other_planes(planes):
    me = lax.axis_index("fsdp")
    return me, [lax.rem(me + k, planes) for k in range(1, planes)]


def send(src, dst, send_sem, recv_sem, axis, peer):
    copy = pltpu.make_async_remote_copy(
        src_ref=src,
        dst_ref=dst,
        send_sem=send_sem,
        recv_sem=recv_sem,
        device_id={axis: peer},
        device_id_type=MESH,
    )
    copy.start()
    return copy


def plane_gather_start(owns, alls, sems, chips):
    far_send, far_recv, near_send, near_recv, local_sem = sems
    me, core, chip, sibling, to, come = plane_peers(chips)
    direct = 2 if chips == 4 else chips - 1
    last = chips - 1
    far, near, local = [], [], []
    for i, (own_ref, all_ref) in enumerate(zip(owns, alls)):
        far.append(
            [
                send(own_ref, all_ref.at[me], far_send.at[i, k], far_recv.at[i, k], "ctx", to[k])
                for k in range(direct)
            ]
        )
        near.append(send(own_ref, all_ref.at[me], near_send.at[i, last], near_recv.at[i, last], "ctx", sibling))
        copy = pltpu.make_async_copy(own_ref, all_ref.at[me], local_sem.at[i])
        copy.start()
        local.append(copy)
    return far, near, local


def plane_gather_pass(started, alls, sems, chips, turns):
    far_send, far_recv, near_send, near_recv, local_sem = sems
    me, core, chip, sibling, to, come = plane_peers(chips)
    far, near, local = started
    for i, all_ref in enumerate(alls):
        for k in turns:
            far[i][k].wait_recv()
            block = all_ref.at[come[k]]
            if chips == 4 and k == 0:
                far[i].append(send(block, block, far_send.at[i, 2], far_recv.at[i, 2], "ctx", to[1]))
            near.append(send(block, block, near_send.at[i, k], near_recv.at[i, k], "ctx", sibling))


def plane_gather_middle(started, alls, sems, chips):
    plane_gather_pass(started, alls, sems, chips, range(2 if chips == 4 else chips - 1))


def plane_gather_end(started, alls, sems, chips):
    plane_gather_pass(started, alls, sems, chips, range(2, chips - 1) if chips == 4 else ())
    far, near, local = started
    for group in far:
        for copy in group:
            copy.wait_send()
    for copy in near + local:
        copy.wait()


def plane_gather_finish(started, alls, sems, chips):
    plane_gather_middle(started, alls, sems, chips)
    plane_gather_end(started, alls, sems, chips)


def plane_gather(owns, alls, sems, chips):
    plane_gather_finish(plane_gather_start(owns, alls, sems, chips), alls, sems, chips)


def plane_scatter_stages(block_of, mine, paired, arrived, sems, chips, result):
    far_send, far_recv, near_send, near_recv, local_sem = sems
    me, core, chip, sibling, to, come = plane_peers(chips)
    targets = to + [me]
    order = [2, 1, 0, 3] if chips == 4 else list(range(chips))
    near, local = [None] * chips, [None] * chips
    crossed = [1, 0, 2, 3] if chips == 4 else list(range(chips))
    for k in order:
        other = targets[crossed[k]] + 1 - 2 * core
        near[k] = send(block_of(other), paired.at[k], near_send.at[k], near_recv.at[k], "ctx", sibling)
        local[k] = pltpu.make_async_copy(block_of(targets[k]), mine.at[k], local_sem.at[k])
        local[k].start()
    yield

    def both(k):
        local[k].wait()
        near[k].wait_recv()
        return mine[k].astype(F32) + paired[k].astype(F32)

    def dispatch(k, target):
        return send(mine.at[k], arrived.at[k], far_send.at[k], far_recv.at[k], "ctx", target)

    far = [None] * (chips - 1)
    if chips == 4:
        mine[2] = both(2).astype(BF16)
        far[2] = dispatch(2, to[0])
        mine[0] = both(0).astype(BF16)
        far[0] = dispatch(0, to[0])
        partial = both(1)
        yield
        far[2].wait_recv()
        mine[1] = (partial + arrived[2].astype(F32)).astype(BF16)
        far[1] = dispatch(1, to[1])
        total = both(3)
        arriving = [0, 1]
    else:
        for k in range(chips - 1):
            mine[k] = both(k).astype(BF16)
            far[k] = dispatch(k, to[k])
        total = both(chips - 1)
        arriving = range(chips - 1)
    yield
    for k in arriving:
        far[k].wait_recv()
        total = total + arrived[k].astype(F32)
    for copy in far + near:
        copy.wait_send()
    result.append(total)


def plane_scatter(block_of, mine, paired, arrived, sems, chips):
    result = []
    for unused in plane_scatter_stages(block_of, mine, paired, arrived, sems, chips, result):
        pass
    return result[0]


def gather_sems(chips, count=1):
    return [DMA((count, chips - 1))] * 2 + [DMA((count, chips))] * 2 + [DMA((count,))]


def scatter_orders(chips):
    if chips == 4:
        return [2, 0, 1, 3], [1, 0, 2, 3]
    return list(range(chips)), list(range(chips))


def plane_scatter_made(make, part, paired, arrived, sems, chips, meanwhile):
    far_send, far_recv, near_send, near_recv = sems
    me, core, chip, sibling, to, come = plane_peers(chips)
    targets = to + [me]
    order, crossed = scatter_orders(chips)
    near, far = [None] * chips, [None] * (chips - 1)

    def produce(k):
        make(k, targets[k] // 2)
        place = crossed[k]
        near[place] = send(
            part.at[k, 1 - core], paired.at[place], near_send.at[place], near_recv.at[place], "ctx", sibling
        )

    def both(k):
        near[k].wait_recv()
        return part[k, core].astype(F32) + paired[k].astype(F32)

    def dispatch(k, values, target):
        paired[k] = values.astype(BF16)
        far[k] = send(paired.at[k], arrived.at[k], far_send.at[k], far_recv.at[k], "ctx", target)

    if chips == 4:
        produce(2)
        produce(0)
        dispatch(2, both(2), to[0])
        produce(1)
        dispatch(0, both(0), to[0])
        produce(3)
        partial = both(1)
        far[2].wait_recv()
        dispatch(1, partial + arrived[2].astype(F32), to[1])
        arriving = [0, 1]
    else:
        for k in order:
            produce(k)
        for k in range(chips - 1):
            dispatch(k, both(k), to[k])
        arriving = range(chips - 1)
    meanwhile()
    total = both(chips - 1)
    for k in arriving:
        far[k].wait_recv()
        total = total + arrived[k].astype(F32)
    for copy in far + near:
        copy.wait_send()
    return total


def made_scratch(chips, *block):
    return [
        pltpu.VMEM((chips, 2) + block, BF16),
        pltpu.VMEM((chips,) + block, BF16),
        pltpu.VMEM((chips - 1,) + block, BF16),
        DMA((chips - 1,)),
        DMA((chips - 1,)),
        DMA((chips,)),
        DMA((chips,)),
    ]


def scatter_scratch(chips, *block):
    return [
        pltpu.VMEM((chips,) + block, BF16),
        pltpu.VMEM((chips,) + block, BF16),
        pltpu.VMEM((chips - 1,) + block, BF16),
        DMA((chips - 1,)),
        DMA((chips - 1,)),
        DMA((chips,)),
        DMA((chips,)),
        DMA((chips,)),
    ]


def normalize(values):
    average = jnp.mean(values, axis=-1, keepdims=True)
    centered = values - average
    variance = jnp.mean(centered * centered, axis=-1, keepdims=True)
    inverse = lax.rsqrt(variance + NORM_EPS)
    return centered * inverse, inverse


def norm_backward(grad, gain, unit, inverse):
    scaled = grad * gain
    first = jnp.mean(scaled, axis=-1, keepdims=True)
    second = jnp.mean(scaled * unit, axis=-1, keepdims=True)
    return (scaled - first - unit * second) * inverse


def first_kernel(
    chips,
    planes,
    seqs,
    quarter,
    tok_ref,
    og_ref,
    vec_ref,
    weight_ref,
    out_w_ref,
    vecs_ref,
    ogs_ref,
    h1_ref,
    weights_ref,
    next_ref,
    own,
    column,
    v_send,
    v_recv,
    v_local,
    h_send,
    h_recv,
    w_send,
    w_recv,
    w_local,
    n_send,
    n_recv,
    n_local,
    *sems,
):
    me, core, chip, sibling, to, come = plane_peers(chips)
    plane, others = other_planes(planes)
    pairs = planes // seqs
    rows = own.shape[0] // seqs
    greet(to + [sibling], others)
    og_sems, h1_sems = sems[:5], [sems[5 + 5 * k : 10 + 5 * k] for k in range(planes)]
    copies = [
        send(vec_ref, vecs_ref.at[plane], v_send.at[k], v_recv.at[k], "fsdp", peer) for k, peer in enumerate(others)
    ]
    local = pltpu.make_async_copy(vec_ref, vecs_ref.at[plane], v_local)
    local.start()
    lead = out_w_ref.at[pl.ds(0, HD)]
    last = plane == planes - 1

    def lead_copy():
        return pltpu.make_async_remote_copy(
            src_ref=lead,
            dst_ref=next_ref,
            send_sem=n_send,
            recv_sem=n_recv,
            device_id={"fsdp": lax.rem(plane + planes - 1, planes)},
            device_id_type=MESH,
        )

    @pl.when(plane > 0)
    def _():
        lead_copy().start()

    @pl.when(last)
    def _():
        pltpu.make_async_copy(lead, next_ref, n_local).start()

    og_started = plane_gather_start([og_ref], [ogs_ref], og_sems, chips)
    unit, inverse = normalize(tok_ref[...].astype(F32))
    for copy in copies + [local]:
        copy.wait()
    lines = quarter // LANES + 1

    def vector(k):
        pieces = []
        for j in range(planes):
            for line in range(lines):
                size = min(LANES, quarter - line * LANES)
                if size:
                    row = k * lines + line
                    pieces.append(vecs_ref[j, row : row + 1, :size].astype(F32))
        return jnp.concatenate(pieces, axis=1)

    own[...] = (unit * vector(0) + vector(1)).astype(BF16)

    def half_of(peer):
        return own.at[pl.ds(pl.multiple_of(peer // pairs * rows, rows), rows)]

    halves = [
        send(half_of(peer), column.at[k], h_send.at[k], h_recv.at[k], "fsdp", peer) for k, peer in enumerate(others)
    ]
    weights = [
        send(weight_ref.at[lax.rem(peer, pairs)], weights_ref.at[plane], w_send.at[k], w_recv.at[k], "fsdp", peer)
        for k, peer in enumerate(others)
    ]
    weights.append(pltpu.make_async_copy(weight_ref.at[lax.rem(plane, pairs)], weights_ref.at[plane], w_local))
    weights[-1].start()
    sources = [plane] + [lax.rem(plane + planes - k, planes) for k in range(1, planes)]
    blocks = [half_of(plane)] + [column.at[k] for k in range(planes - 1)]
    started = [plane_gather_start([blocks[0]], [h1_ref.at[sources[0]]], h1_sems[0], chips)]
    plane_gather_middle(og_started, [ogs_ref], og_sems, chips)
    for k in range(1, planes):
        halves[k - 1].wait_recv()
        started.append(plane_gather_start([blocks[k]], [h1_ref.at[sources[k]]], h1_sems[k], chips))
        plane_gather_middle(started[k - 1], [h1_ref.at[sources[k - 1]]], h1_sems[k - 1], chips)
    plane_gather_middle(started[-1], [h1_ref.at[sources[-1]]], h1_sems[-1], chips)
    plane_gather_end(og_started, [ogs_ref], og_sems, chips)
    for k in range(planes):
        plane_gather_end(started[k], [h1_ref.at[sources[k]]], h1_sems[k], chips)
    @pl.when(plane > 0)
    def _():
        lead_copy().wait_send()

    @pl.when(last)
    def _():
        pltpu.make_async_copy(lead, next_ref, n_local).wait()

    @pl.when(plane < planes - 1)
    def _():
        lead_copy().wait_recv()

    for copy in halves:
        copy.wait_send()
    for copy in weights:
        copy.wait()


def first_norm_gather(tok, og, vec, weight, out_weight, n_ctx, planes, seqs):
    rows, width = tok.shape
    chips, half = n_ctx // 2, rows // seqs
    return pl.pallas_call(
        functools.partial(first_kernel, chips, planes, seqs, width // planes),
        out_shape=(
            jax.ShapeDtypeStruct((planes,) + vec.shape, BF16),
            jax.ShapeDtypeStruct((n_ctx, rows, width), BF16),
            jax.ShapeDtypeStruct((planes, n_ctx, half, width), BF16),
            jax.ShapeDtypeStruct((planes,) + weight.shape[1:], BF16),
            jax.ShapeDtypeStruct((HD, width), BF16),
        ),
        in_specs=[VMEM, ANY, VMEM, ANY, ANY],
        out_specs=(VMEM, ANY, ANY, ANY, ANY),
        scratch_shapes=[
            pltpu.VMEM((rows, width), BF16),
            pltpu.VMEM((planes - 1, half, width), BF16),
            DMA((planes - 1,)),
            DMA((planes - 1,)),
            DMA,
            DMA((planes - 1,)),
            DMA((planes - 1,)),
            DMA((planes - 1,)),
            DMA((planes - 1,)),
            DMA,
            DMA,
            DMA,
            DMA,
        ]
        + gather_sems(chips)
        + gather_sems(chips) * planes,
        compiler_params=params(0),
        cost_estimate=SMALL,
        name="norm_gather",
    )(tok, og, vec, weight, out_weight)


def second_kernel(chips, att_ref, weight_ref, tok_ref, vec_ref, mixed_ref, all_ref, own, *scratch):
    me, core, chip, sibling, to, come = plane_peers(chips)
    greet(to + [sibling])
    rows = tok_ref.shape[0]
    part = scratch[0]

    def make(k, target):
        span = pl.ds(pl.multiple_of(target * 2 * rows, 2 * rows), 2 * rows)
        branch = nn(att_ref[span, :], weight_ref[...]).astype(BF16)
        part[k, 0] = branch[:rows]
        part[k, 1] = branch[rows:]

    total = plane_scatter_made(make, *scratch[:3], scratch[3:7], chips, lambda: None)
    mixed = tok_ref[...].astype(F32) + total + vec_ref[2:3, :]
    mixed_ref[...] = mixed
    unit, inverse = normalize(mixed)
    own[...] = (unit * vec_ref[0:1, :] + vec_ref[1:2, :]).astype(BF16)
    plane_gather([own], [all_ref], scratch[7:], chips)


def second_norm_gather(att, weight, tok, vecs, n_ctx):
    rows, width = tok.shape
    chips = n_ctx // 2
    return pl.pallas_call(
        functools.partial(second_kernel, chips),
        out_shape=(
            jax.ShapeDtypeStruct((rows, width), F32),
            jax.ShapeDtypeStruct((n_ctx, rows, width), BF16),
        ),
        in_specs=[VMEM] * 4,
        out_specs=(VMEM, ANY),
        scratch_shapes=[pltpu.VMEM((rows, width), BF16)]
        + made_scratch(chips, rows, width)
        + gather_sems(chips),
        compiler_params=params(1),
        cost_estimate=SMALL,
        name="scatter_norm_gather",
    )(att, weight, tok, vecs)


def third_kernel(
    chips,
    planes,
    packed,
    h_hbm,
    og_hbm,
    act_hbm,
    slope_hbm,
    up_w_hbm,
    down_w_hbm,
    mixed_ref,
    og_ref,
    vec_ref,
    dmixed_ref,
    sums_ref,
    all_ref,
    out_hbm,
    up_grad_ref,
    up_sum_ref,
    h_ref,
    ogs_ref,
    act_ref,
    slope_ref,
    up_w_ref,
    down_w_ref,
    d_up_ref,
    out_ref,
    load_sem,
    out_sem,
    own,
    *scratch,
):
    me, core, chip, sibling, to, come = plane_peers(chips)
    made, gather = scratch[:7], scratch[7:]
    loads = [
        pltpu.make_async_copy(source, target, load_sem.at[k])
        for k, (source, target) in enumerate(
            [
                (down_w_hbm, down_w_ref),
                (og_hbm, ogs_ref),
                (slope_hbm, slope_ref),
                (up_w_hbm, up_w_ref),
                (h_hbm, h_ref),
                (act_hbm, act_ref),
            ]
        )
    ]
    for load in loads:
        load.start()
    greet(to + [sibling])
    unit, inverse = normalize(mixed_ref[...])
    rows = mixed_ref.shape[0]
    waiting = loads[:4]
    part = made[0]

    def make(k, target):
        span = pl.ds(pl.multiple_of(target * 2 * rows, 2 * rows), 2 * rows)
        while len(waiting) > 2:
            waiting.pop(0).wait()
        d_act = nt(ogs_ref[span, :], down_w_ref[...])
        while waiting:
            waiting.pop(0).wait()
        d_up = (d_act * slope_ref[span, :]).astype(BF16)
        d_up_ref[span, :] = d_up
        d_h = nt(d_up, up_w_ref[...]).astype(BF16)
        part[k, 0] = d_h[:rows]
        part[k, 1] = d_h[rows:]

    def meanwhile():
        for load in loads[4:]:
            load.wait()
        d_up = d_up_ref[...]
        up_sum_ref[...] = jnp.sum(d_up.astype(F32), axis=0, keepdims=True)
        up_grad = tn(d_up, h_ref[...]).T
        if packed:
            hidden = up_grad.shape[1]
            lines = up_grad.shape[0] // planes // 2
            for j in range(2 * planes):
                lanes_at = j % 2 * hidden
                up_grad_ref[j // 2, :, lanes_at : lanes_at + hidden] = up_grad[j * lines : (j + 1) * lines].astype(BF16)
        else:
            for j in range(planes):
                lines = up_grad.shape[0] // planes
                up_grad_ref[j] = up_grad[j * lines : (j + 1) * lines].astype(BF16)
        out_ref[...] = nn(act_ref[...], down_w_ref[...]).astype(BF16)
        pltpu.make_async_copy(out_ref, out_hbm, out_sem).start()

    grad = plane_scatter_made(make, *made[:3], made[3:], chips, meanwhile)
    out_grad = og_ref[...].astype(F32)
    dmixed = out_grad + norm_backward(grad, vec_ref[0:1, :], unit, inverse)
    low = dmixed.astype(BF16)
    own[...] = low
    started = plane_gather_start([own], [all_ref], gather, chips)
    dmixed_ref[...] = dmixed
    sums_ref[0:1, :] = jnp.sum(grad * unit, axis=0, keepdims=True)
    sums_ref[1:2, :] = jnp.sum(grad, axis=0, keepdims=True)
    sums_ref[2:3, :] = jnp.sum(low.astype(F32), axis=0, keepdims=True)
    sums_ref[3:4, :] = jnp.sum(out_grad, axis=0, keepdims=True)
    plane_gather_finish(started, [all_ref], gather, chips)
    pltpu.make_async_copy(out_ref, out_hbm, out_sem).wait()


def feed_back(values, out_grads, act, slope, up_weight, down_weight, mixed, og, vecs, planes, packed):
    rows, width = mixed.shape
    total_rows, hidden = act.shape
    n_ctx = total_rows // rows
    chips = n_ctx // 2
    return pl.pallas_call(
        functools.partial(third_kernel, chips, planes, packed),
        out_shape=(
            jax.ShapeDtypeStruct((rows, width), F32),
            jax.ShapeDtypeStruct((4, width), F32),
            jax.ShapeDtypeStruct((n_ctx, rows, width), BF16),
            jax.ShapeDtypeStruct((total_rows, width), BF16),
            jax.ShapeDtypeStruct((planes,) + ((width // planes // 2, 2 * hidden) if packed else (width // planes, hidden)), BF16),
            jax.ShapeDtypeStruct((1, hidden), F32),
        ),
        in_specs=[ANY] * 6 + [VMEM] * 3,
        out_specs=(VMEM, VMEM, ANY, ANY, VMEM, VMEM),
        scratch_shapes=[
            pltpu.VMEM((total_rows, width), BF16),
            pltpu.VMEM((total_rows, width), BF16),
            pltpu.VMEM((total_rows, hidden), BF16),
            pltpu.VMEM((total_rows, hidden), F32),
            pltpu.VMEM((width, hidden), BF16),
            pltpu.VMEM((hidden, width), BF16),
            pltpu.VMEM((total_rows, hidden), BF16),
            pltpu.VMEM((total_rows, width), BF16),
            DMA((6,)),
            DMA,
            pltpu.VMEM((rows, width), BF16),
        ]
        + made_scratch(chips, rows, width)
        + gather_sems(chips),
        compiler_params=params(2),
        cost_estimate=SMALL,
        name="feed_back",
    )(values, out_grads, act, slope, up_weight, down_weight, mixed, og, vecs)


def fourth_kernel(
    chips,
    planes,
    seqs,
    part_ref,
    qkv_ref,
    outw_ref,
    flat_ref,
    tok_ref,
    dmixed_ref,
    vec_ref,
    grad_ref,
    qkv_all,
    outw_all,
    sums_ref,
    flat_out,
    q_arrived,
    q_own,
    q_send,
    q_recv,
    q_local,
    rows_own,
    rows_arrived,
    r_send,
    r_recv,
    small,
    small_own,
    small_z,
    small_c,
    flat_own,
    flat_z,
    flat_c,
    z_send,
    z_recv,
    c_send,
    c_recv,
    *scratch,
):
    n_ctx = 2 * chips
    pairs = planes // seqs
    me, core, chip, sibling, to, come = plane_peers(chips)
    plane, others = other_planes(planes)
    around = [lax.rem(me + k, n_ctx) for k in range(1, n_ctx)]
    greet(around, others)
    scatter, rest_sems, qkv_sems = scratch[:8], scratch[8:13], scratch[13:]

    pushed = [
        send(qkv_ref.at[peer], q_arrived.at[plane], q_send.at[k], q_recv.at[k], "fsdp", peer)
        for k, peer in enumerate(others)
    ]
    held = pltpu.make_async_copy(qkv_ref.at[plane], q_arrived.at[plane], q_local)
    held.start()
    flat_sent = [
        send(flat_ref.at[peer], flat_z.at[k], z_send.at[0, k], z_recv.at[0, k], "fsdp", peer)
        for k, peer in enumerate(others)
    ]
    unit, inverse = normalize(tok_ref[...].astype(F32))
    total = plane_scatter(lambda c: part_ref.at[:, c], *scatter[:3], scatter[3:], chips)
    rows_own[...] = total.astype(BF16)
    rows_sent = [
        send(rows_own.at[peer], rows_arrived.at[plane], r_send.at[k], r_recv.at[k], "fsdp", peer)
        for k, peer in enumerate(others)
    ]
    rows_arrived[plane] = rows_own[plane]
    rest_started = plane_gather_start([outw_ref], [outw_all], rest_sems, chips)
    for copy in pushed + [held]:
        copy.wait()
    for pair in range(pairs):
        terms = [q_arrived[seq * pairs + pair].astype(F32) for seq in range(seqs)]
        q_own[pair] = sum(terms[1:], terms[0]).astype(BF16)
    qkv_started = plane_gather_start([q_own], [qkv_all], qkv_sems, chips)
    plane_gather_finish(rest_started, [outw_all], rest_sems, chips)

    for copy in rows_sent:
        copy.wait()
    halves = []
    for seq in range(seqs):
        terms = [rows_arrived[seq * pairs + pair].astype(F32) for pair in range(pairs)]
        halves.append(sum(terms[1:], terms[0]))
    grad = jnp.concatenate(halves, axis=0)
    sums = jnp.concatenate(
        [jnp.sum(grad * unit, axis=0, keepdims=True), jnp.sum(grad, axis=0, keepdims=True)], axis=0
    )
    quarter = sums.shape[1] // planes
    small[...] = jnp.zeros_like(small)
    for j in range(planes):
        small[j, 0:2, 0:quarter] = sums[:, j * quarter : (j + 1) * quarter]
    small_sent = [
        send(small.at[peer], small_z.at[k], z_send.at[1, k], z_recv.at[1, k], "fsdp", peer)
        for k, peer in enumerate(others)
    ]
    grad_ref[...] = dmixed_ref[...] + norm_backward(grad, vec_ref[0:1, :], unit, inverse)
    small_total = small[plane]
    flat_total = flat_ref[plane]
    for k in range(planes - 1):
        flat_sent[k].wait()
        small_sent[k].wait()
        small_total = small_total + small_z[k]
        flat_total = flat_total + flat_z[k]
    small_own[...] = small_total
    flat_own[...] = flat_total
    sent = []
    for k, peer in enumerate(around):
        sent.append(send(small_own, small_c.at[k], c_send.at[0, k], c_recv.at[0, k], "ctx", peer))
        sent.append(send(flat_own, flat_c.at[k], c_send.at[1, k], c_recv.at[1, k], "ctx", peer))
    plane_gather_finish(qkv_started, [qkv_all], qkv_sems, chips)
    for copy in sent:
        copy.wait()
    for k in range(n_ctx - 1):
        small_total = small_total + small_c[k]
        flat_total = flat_total + flat_c[k]
    sums_ref[...] = small_total
    flat_out[...] = flat_total


def first_norm_back(part, qkv_part, outw_own, flat, tok, dmixed, vecs):
    planes, n_ctx, half, width = part.shape
    rows = tok.shape[0]
    seqs = rows // half
    quarter, columns = qkv_part.shape[1:]
    chips, pairs = n_ctx // 2, planes // seqs
    size = (8, quarter + -quarter % LANES)
    return pl.pallas_call(
        functools.partial(fourth_kernel, chips, planes, seqs),
        out_shape=(
            jax.ShapeDtypeStruct((rows, width), F32),
            jax.ShapeDtypeStruct((n_ctx, pairs, quarter, columns), BF16),
            jax.ShapeDtypeStruct((n_ctx,) + outw_own.shape, BF16),
            jax.ShapeDtypeStruct(size, F32),
            jax.ShapeDtypeStruct(flat.shape[1:], F32),
        ),
        in_specs=[ANY, ANY, ANY, VMEM, VMEM, VMEM, VMEM],
        out_specs=(VMEM, ANY, ANY, VMEM, VMEM),
        scratch_shapes=[
            pltpu.VMEM((planes, quarter, columns), BF16),
            pltpu.VMEM((pairs, quarter, columns), BF16),
            DMA((planes - 1,)),
            DMA((planes - 1,)),
            DMA,
            pltpu.VMEM((planes, half, width), BF16),
            pltpu.VMEM((planes, half, width), BF16),
            DMA((planes - 1,)),
            DMA((planes - 1,)),
            pltpu.VMEM((planes,) + size, F32),
            pltpu.VMEM(size, F32),
            pltpu.VMEM((planes - 1,) + size, F32),
            pltpu.VMEM((n_ctx - 1,) + size, F32),
            pltpu.VMEM(flat.shape[1:], F32),
            pltpu.VMEM((planes - 1,) + flat.shape[1:], F32),
            pltpu.VMEM((n_ctx - 1,) + flat.shape[1:], F32),
            DMA((2, planes - 1)),
            DMA((2, planes - 1)),
            DMA((2, n_ctx - 1)),
            DMA((2, n_ctx - 1)),
        ]
        + scatter_scratch(chips, planes, half, width)
        + gather_sems(chips)
        + gather_sems(chips),
        compiler_params=params(3),
        cost_estimate=SMALL,
        name="scatter_back",
    )(part, qkv_part, outw_own, flat, tok, dmixed, vecs)


def finish_kernel(
    chips,
    planes,
    seqs,
    counts,
    h1_hbm,
    d_hbm,
    w_hbm,
    up_ref,
    outw_ref,
    flat_ref,
    tok_ref,
    dmixed_ref,
    vec_ref,
    grad_ref,
    qkv_all,
    up_all,
    outw_all,
    tail_ref,
    sums_ref,
    flat_out,
    h1_ref,
    d_ref,
    w_ref,
    load_sem,
    dw_ref,
    q_arrived,
    q_own,
    q_send,
    q_recv,
    outw_arrived,
    outw_own,
    o_send,
    o_recv,
    rows_own,
    rows_arrived,
    r_send,
    r_recv,
    small,
    small_own,
    small_z,
    small_c,
    flat_own,
    flat_z,
    flat_c,
    z_send,
    z_recv,
    c_send,
    c_recv,
    t_send,
    t_recv,
    *scratch,
):
    n_ctx = 2 * chips
    pairs = planes // seqs
    me, core, chip, sibling, to, come = plane_peers(chips)
    plane, others = other_planes(planes)
    around = [lax.rem(me + k, n_ctx) for k in range(1, n_ctx)]
    made, outw_sems, qkv_sems, up_sems = scratch[:7], scratch[7:12], scratch[12:17], scratch[17:]
    loads = [
        pltpu.make_async_copy(source, target, load_sem.at[k])
        for k, (source, target) in enumerate([(d_hbm, d_ref), (h1_hbm, h1_ref), (w_hbm, w_ref)])
    ]
    for load in loads:
        load.start()
    greet(around, others)
    up_started = plane_gather_start([up_ref], [up_all], up_sems, chips)
    outw_sent = [
        send(outw_ref.at[peer], outw_arrived.at[k], o_send.at[k], o_recv.at[k], "fsdp", peer)
        for k, peer in enumerate(others)
    ]
    flat_sent = [
        send(flat_ref.at[peer], flat_z.at[k], z_send.at[0, k], z_recv.at[0, k], "fsdp", peer)
        for k, peer in enumerate(others)
    ]
    unit, inverse = normalize(tok_ref[...].astype(F32))

    for load in loads:
        load.wait()
    quarter = dw_ref.shape[1]
    dw = tn(d_ref[...], h1_ref[...]).T.astype(BF16)
    for j in range(planes):
        dw_ref[j] = dw[j * quarter : (j + 1) * quarter]
    pushed = [
        send(dw_ref.at[peer], q_arrived.at[plane], q_send.at[k], q_recv.at[k], "fsdp", peer)
        for k, peer in enumerate(others)
    ]
    q_arrived[plane] = dw_ref[plane]

    part = made[0]
    half = part.shape[3]

    calls = []

    def make(k, target):
        calls.append(k)
        if len(calls) == chips - 1:
            plane_gather_middle(up_started, [up_all], up_sems, chips)
        blocks = []
        for j in range(planes):
            start = pl.multiple_of(j * n_ctx * half + target * 2 * half, 2 * half)
            blocks.append(d_ref[pl.ds(start, 2 * half), :])
        d_h = nt(jnp.concatenate(blocks, axis=0), w_ref[...]).astype(BF16)
        for j in range(planes):
            for side in range(2):
                start = (2 * j + side) * half
                part[k, side, j] = d_h[start : start + half]

    total = plane_scatter_made(make, *made[:3], made[3:], chips, lambda: None)
    rows_own[...] = total.astype(BF16)
    rows_sent = [
        send(rows_own.at[peer], rows_arrived.at[plane], r_send.at[k], r_recv.at[k], "fsdp", peer)
        for k, peer in enumerate(others)
    ]
    rows_arrived[plane] = rows_own[plane]

    total = outw_ref[plane].astype(F32)
    for k, copy in enumerate(outw_sent):
        copy.wait()
        total = total + outw_arrived[k].astype(F32)
    outw_own[...] = total.astype(BF16)
    outw_started = plane_gather_start([outw_own], [outw_all], outw_sems, chips)
    plane_gather_end(up_started, [up_all], up_sems, chips)
    for copy in pushed:
        copy.wait()
    for pair in range(pairs):
        terms = [q_arrived[seq * pairs + pair].astype(F32) for seq in range(seqs)]
        q_own[pair] = sum(terms[1:], terms[0]).astype(BF16)
    qkv_started = plane_gather_start([q_own], [qkv_all], qkv_sems, chips)
    plane_gather_middle(outw_started, [outw_all], outw_sems, chips)
    plane_gather_middle(qkv_started, [qkv_all], qkv_sems, chips)

    for copy in rows_sent:
        copy.wait()
    halves = []
    for seq in range(seqs):
        terms = [rows_arrived[seq * pairs + pair].astype(F32) for pair in range(pairs)]
        halves.append(sum(terms[1:], terms[0]))
    grad = jnp.concatenate(halves, axis=0)
    sums = jnp.concatenate(
        [jnp.sum(grad * unit, axis=0, keepdims=True), jnp.sum(grad, axis=0, keepdims=True)], axis=0
    )
    small[...] = jnp.zeros_like(small)
    for j in range(planes):
        small[j, 0:2, 0:quarter] = sums[:, j * quarter : (j + 1) * quarter]
    small_sent = [
        send(small.at[peer], small_z.at[k], z_send.at[1, k], z_recv.at[1, k], "fsdp", peer)
        for k, peer in enumerate(others)
    ]
    grad_ref[...] = dmixed_ref[...] + norm_backward(grad, vec_ref[0:1, :], unit, inverse)
    small_total = small[plane]
    flat_total = flat_ref[plane]
    for k in range(planes - 1):
        flat_sent[k].wait()
        small_sent[k].wait()
        small_total = small_total + small_z[k]
        flat_total = flat_total + flat_z[k]
    small_own[...] = small_total
    flat_own[...] = flat_total
    sent = []
    for k, peer in enumerate(around):
        sent.append(send(small_own, small_c.at[k], c_send.at[0, k], c_recv.at[0, k], "ctx", peer))
        sent.append(send(flat_own, flat_c.at[k], c_send.at[1, k], c_recv.at[1, k], "ctx", peer))
    plane_gather_end(outw_started, [outw_all], outw_sems, chips)
    last_head = sum((plane == j).astype(jnp.int32) * (counts[j] - 1) for j in range(planes))

    def tail_copy():
        return pltpu.make_async_remote_copy(
            src_ref=outw_all.at[last_head],
            dst_ref=tail_ref,
            send_sem=t_send,
            recv_sem=t_recv,
            device_id={"fsdp": lax.rem(plane + 1, planes)},
            device_id_type=MESH,
        )

    @pl.when(plane < planes - 1)
    def _():
        tail_copy().start()

    plane_gather_end(qkv_started, [qkv_all], qkv_sems, chips)
    for copy in sent:
        copy.wait()
    for k in range(n_ctx - 1):
        small_total = small_total + small_c[k]
        flat_total = flat_total + flat_c[k]
    @pl.when(plane < planes - 1)
    def _():
        tail_copy().wait_send()

    @pl.when(plane > 0)
    def _():
        tail_copy().wait_recv()

    sums_ref[...] = small_total
    flat_out[...] = flat_total


def finish(h1, d_qkv, weight, up_own, outw_part, flat, tok, dmixed, vecs, counts):
    rows, width = tok.shape
    planes = outw_part.shape[0]
    n_ctx = lax.axis_size("ctx")
    half = h1.shape[0] // (planes * n_ctx)
    seqs = rows // half
    quarter, columns = width // planes, weight.shape[1]
    chips, pairs = n_ctx // 2, planes // seqs
    size = (8, quarter + -quarter % LANES)
    piece = outw_part.shape[1:]
    return pl.pallas_call(
        functools.partial(finish_kernel, chips, planes, seqs, counts),
        out_shape=(
            jax.ShapeDtypeStruct((rows, width), F32),
            jax.ShapeDtypeStruct((n_ctx, pairs, quarter, columns), BF16),
            jax.ShapeDtypeStruct((n_ctx,) + up_own.shape, BF16),
            jax.ShapeDtypeStruct((n_ctx,) + piece, BF16),
            jax.ShapeDtypeStruct(piece, BF16),
            jax.ShapeDtypeStruct(size, F32),
            jax.ShapeDtypeStruct(flat.shape[1:], F32),
        ),
        in_specs=[ANY] * 4 + [VMEM] * 5,
        out_specs=(VMEM, ANY, ANY, ANY, ANY, VMEM, VMEM),
        scratch_shapes=[
            pltpu.VMEM(h1.shape, BF16),
            pltpu.VMEM(d_qkv.shape, BF16),
            pltpu.VMEM(weight.shape, BF16),
            DMA((3,)),
            pltpu.VMEM((planes, quarter, columns), BF16),
            pltpu.VMEM((planes, quarter, columns), BF16),
            pltpu.VMEM((pairs, quarter, columns), BF16),
            DMA((planes - 1,)),
            DMA((planes - 1,)),
            pltpu.VMEM((planes - 1,) + piece, BF16),
            pltpu.VMEM(piece, BF16),
            DMA((planes - 1,)),
            DMA((planes - 1,)),
            pltpu.VMEM((planes, half, width), BF16),
            pltpu.VMEM((planes, half, width), BF16),
            DMA((planes - 1,)),
            DMA((planes - 1,)),
            pltpu.VMEM((planes,) + size, F32),
            pltpu.VMEM(size, F32),
            pltpu.VMEM((planes - 1,) + size, F32),
            pltpu.VMEM((n_ctx - 1,) + size, F32),
            pltpu.VMEM(flat.shape[1:], F32),
            pltpu.VMEM((planes - 1,) + flat.shape[1:], F32),
            pltpu.VMEM((n_ctx - 1,) + flat.shape[1:], F32),
            DMA((2, planes - 1)),
            DMA((2, planes - 1)),
            DMA((2, n_ctx - 1)),
            DMA((2, n_ctx - 1)),
            DMA,
            DMA,
        ]
        + made_scratch(chips, planes, half, width)
        + gather_sems(chips)
        + gather_sems(chips)
        + gather_sems(chips),
        compiler_params=params(9),
        cost_estimate=SMALL,
        name="finish",
    )(h1, d_qkv, weight, up_own, outw_part, flat, tok, dmixed, vecs)


def to_heads_kernel(
    planes, seqs, chips, tok_ref, down_ref, head_ref, down_all, send_sems, recv_sems, local_sem, *sems
):
    ctx_me, core, chip, sibling, to, come = plane_peers(chips)
    me, others = other_planes(planes)
    pairs = planes // seqs
    greet(to + [sibling], others)

    def source(unit):
        start = pl.multiple_of(lax.rem(unit, pairs) * LANES, LANES)
        return tok_ref.at[:, unit // pairs, :, pl.ds(start, LANES)]

    copies = [
        send(source(unit), head_ref.at[me], send_sems.at[k], recv_sems.at[k], "fsdp", unit)
        for k, unit in enumerate(others)
    ]
    copies.append(pltpu.make_async_copy(source(me), head_ref.at[me], local_sem))
    copies[-1].start()
    plane_gather([down_ref], [down_all], sems, chips)
    for copy in copies:
        copy.wait()


def to_heads(tok, planes, cid, down_own):
    n_ctx, seqs, local_rows, width = tok.shape
    chips = n_ctx // 2
    return pl.pallas_call(
        functools.partial(to_heads_kernel, planes, seqs, chips),
        out_shape=(
            jax.ShapeDtypeStruct((planes, n_ctx, local_rows, LANES), BF16),
            jax.ShapeDtypeStruct((n_ctx,) + down_own.shape, BF16),
        ),
        in_specs=[ANY, ANY],
        out_specs=(ANY, ANY),
        scratch_shapes=[DMA((planes - 1,)), DMA((planes - 1,)), DMA] + gather_sems(chips),
        compiler_params=params(cid),
        cost_estimate=SMALL,
        name="to_heads",
    )(tok, down_own)


def to_tokens_kernel(
    planes, seqs, head_ref, weight_ref, tok_ref, weights_ref, send_sems, recv_sems, local_sem, w_send, w_recv, w_local
):
    me, others = other_planes(planes)
    pairs = planes // seqs
    greet((), others)
    start = pl.multiple_of(lax.rem(me, pairs) * LANES, LANES)
    target = tok_ref.at[:, me // pairs, :, pl.ds(start, LANES)]
    copies = [
        send(head_ref.at[peer], target, send_sems.at[k], recv_sems.at[k], "fsdp", peer) for k, peer in enumerate(others)
    ]
    copies += [
        send(weight_ref, weights_ref.at[me], w_send.at[k], w_recv.at[k], "fsdp", peer) for k, peer in enumerate(others)
    ]
    for copy in (
        pltpu.make_async_copy(head_ref.at[me], target, local_sem),
        pltpu.make_async_copy(weight_ref, weights_ref.at[me], w_local),
    ):
        copy.start()
        copies.append(copy)
    for copy in copies:
        copy.wait()


def to_tokens(heads, seqs, cid, weight):
    planes, n_ctx, rows, lanes = heads.shape
    width = (planes // seqs) * LANES
    return pl.pallas_call(
        functools.partial(to_tokens_kernel, planes, seqs),
        out_shape=(
            jax.ShapeDtypeStruct((n_ctx, seqs, rows, width), heads.dtype),
            jax.ShapeDtypeStruct((planes,) + weight.shape, BF16),
        ),
        in_specs=[ANY] * 2,
        out_specs=(ANY,) * 2,
        scratch_shapes=[DMA((planes - 1,)), DMA((planes - 1,)), DMA] * 2,
        compiler_params=params(cid),
        cost_estimate=SMALL,
        name="to_tokens",
    )(heads, weight)


def nt(left, right):
    return lax.dot_general(left, right, (((1,), (1,)), ((), ())), preferred_element_type=F32)


def nn(left, right):
    return lax.dot_general(left, right, (((1,), (0,)), ((), ())), preferred_element_type=F32)


def sort_blocks(order_ref, qkv_ref, targets, blocks, half):
    def body(block, carry):
        row = qkv_ref[order_ref[block]]
        start = pl.multiple_of(block * half, half)
        for k, target in enumerate(targets):
            target[pl.ds(start, half), :] = row[:, k * LANES : (k + 1) * LANES]
        return carry

    lax.fori_loop(0, blocks, body, 0)


def lane_mask(rows, head):
    lane = lax.broadcasted_iota(jnp.int32, (rows, LANES), 1)
    return (lane < HD) if head == 0 else (lane >= HD)


def unsort_blocks(order_ref, sorted_refs, target_ref, blocks, half):
    def body(block, carry):
        start = pl.multiple_of(block * half, half)
        place = order_ref[block]
        for k, source in enumerate(sorted_refs):
            target_ref[place, :, k * LANES : (k + 1) * LANES] = source[pl.ds(start, half), :].astype(BF16)
        return carry

    lax.fori_loop(0, blocks, body, 0)


def long_forward_kernel(tile, order_ref, qkv_ref, out_ref, att_ref, lse_ref, q_s, k_s, v_s, vt_s, o_s):
    blocks, half = out_ref.shape[0], out_ref.shape[1]
    length = blocks * half
    tiles = length // tile
    sort_blocks(order_ref, qkv_ref, [q_s, k_s, v_s], blocks, half)
    for t in range(tiles):
        span = slice(t * tile, (t + 1) * tile)
        vt_s[:, span] = v_s[span, :].T
    scale = HD ** (-0.5)
    rows_iota = lax.broadcasted_iota(jnp.int32, (tile, tile), 0)
    cols_iota = lax.broadcasted_iota(jnp.int32, (tile, tile), 1)
    allowed = rows_iota <= cols_iota
    masks = [lane_mask(tile, head) for head in range(2)]

    for qt in range(tiles):
        q_span = slice(qt * tile, (qt + 1) * tile)
        query = q_s[q_span, :] * jnp.asarray(scale, BF16)
        queries = [jnp.where(masks[head], query, jnp.zeros_like(query)) for head in range(2)]

        def step(kt, state, masked, queries=queries):
            start = pl.multiple_of(kt * tile, tile)
            keys = k_s[pl.ds(start, tile), :]
            new = []
            for head in range(2):
                top, total, acc = state[head]
                scores = nt(keys, queries[head])
                if masked:
                    scores = jnp.where(allowed, scores, NEG_BIG)
                new_top = jnp.maximum(top, jnp.max(scores, axis=0, keepdims=True))
                soft = jnp.exp(scores - new_top)
                factor = jnp.exp(top - new_top)
                total = total * factor + jnp.sum(soft, axis=0, keepdims=True)
                values = vt_s[head * HD : (head + 1) * HD, pl.ds(start, tile)]
                acc = acc * factor + nn(values, soft.astype(BF16))
                new.append((new_top, total, acc))
            return tuple(new)

        state = tuple(
            (jnp.full((1, tile), NEG_BIG, F32), jnp.zeros((1, tile), F32), jnp.zeros((HD, tile), F32))
            for head in range(2)
        )
        state = step(qt, state, True)
        if qt > 0:
            state = lax.fori_loop(0, qt, lambda kt, s, step=step: step(kt, s, False), state)
        parts = []
        for head in range(2):
            top, total, acc = state[head]
            parts.append(acc / total)
            lse_ref[head : head + 1, q_span] = top + jnp.log(total)
        att = jnp.concatenate(parts, axis=0).T
        att_ref[q_span, :] = att
        o_s[q_span, :] = att.astype(BF16)

    unsort_blocks(order_ref, [o_s], out_ref, blocks, half)


def block_places(order, n_ctx):
    blocks = order.shape[0]
    places = jnp.stack([order // (2 * n_ctx), lax.rem(order // 2, n_ctx), lax.rem(order, 2)]).astype(jnp.int32)
    match = order[:, None] == jnp.arange(blocks)[None, :]
    inverse = jnp.sum(jnp.where(match, jnp.arange(blocks)[:, None], 0), axis=0).astype(jnp.int32)
    return places, inverse


def sort_places(order_ref, source, targets):
    blocks, half = order_ref.shape[1], source.shape[3]

    def body(block, carry):
        row = source[order_ref[0, block], order_ref[1, block], order_ref[2, block]]
        start = pl.multiple_of(block * half, half)
        for k, target in enumerate(targets):
            target[pl.ds(start, half), :] = row[:, k * LANES : (k + 1) * LANES]
        return carry

    lax.fori_loop(0, blocks, body, 0)


def unsort_places(place_ref, sources, target):
    n_ctx = target.shape[1]

    def body(place, carry):
        block = place_ref[place]
        f, c, side = place // (2 * n_ctx), lax.rem(place // 2, n_ctx), lax.rem(place, 2)
        for k, source in enumerate(sources):
            target[f, c, side, :, k * LANES : (k + 1) * LANES] = source[block]
        return carry

    lax.fori_loop(0, place_ref.shape[0], body, 0)


def attend_kernel(
    tile,
    planes,
    seqs,
    order_ref,
    place_ref,
    h1_hbm,
    w_hbm,
    shift_ref,
    out_w_ref,
    qkv_ref,
    att_ref,
    lse_ref,
    tok_ref,
    out_ws_ref,
    h1_ref,
    w_ref,
    load_sem,
    heads,
    a_send,
    a_recv,
    a_local,
    w_send,
    w_recv,
    w_local,
    q_s,
    k_s,
    v_s,
    o_s,
    s_s,
    p_s,
):
    me, others = other_planes(planes)
    pairs = planes // seqs
    n_ctx, half = qkv_ref.shape[1], qkv_ref.shape[3]
    length = att_ref.shape[0]
    tiles, step = length // tile, tile // half
    rows = length // planes
    loads = [pltpu.make_async_copy(w_hbm, w_ref, load_sem.at[planes])]
    for j in range(planes):
        span = pl.ds(j * rows, rows)
        loads.append(pltpu.make_async_copy(h1_hbm.at[span], h1_ref.at[span], load_sem.at[j]))
    for load in loads:
        load.start()
    greet((), others)
    moved = [
        send(out_w_ref, out_ws_ref.at[me], w_send.at[k], w_recv.at[k], "fsdp", peer) for k, peer in enumerate(others)
    ]
    moved.append(pltpu.make_async_copy(out_w_ref, out_ws_ref.at[me], w_local))
    moved[-1].start()

    loads[0].wait()
    for j in range(planes):
        loads[1 + j].wait()
        values = nn(h1_ref[j * rows : (j + 1) * rows, :], w_ref[...]) + shift_ref[...]
        qkv_ref[j] = values.astype(BF16).reshape(n_ctx, 2, half, values.shape[1])

    sort_places(order_ref, qkv_ref, [q_s, k_s, v_s])
    scale = HD ** (-0.5)
    rows_iota = lax.broadcasted_iota(jnp.int32, (tile, tile), 0)
    cols_iota = lax.broadcasted_iota(jnp.int32, (tile, tile), 1)
    allowed = cols_iota <= rows_iota
    masks = [lane_mask(tile, head) for head in range(2)]
    for qt in range(tiles):
        q_span = slice(qt * tile, (qt + 1) * tile)
        query = q_s[q_span, :] * jnp.asarray(scale, BF16)
        parts = []
        for head in range(2):
            one = jnp.where(masks[head], query, jnp.zeros_like(query))
            top = jnp.full((tile, LANES), NEG_BIG, F32)
            for kt in range(qt + 1):
                k_span = slice(kt * tile, (kt + 1) * tile)
                scores = nt(one, k_s[k_span, :])
                if kt == qt:
                    scores = jnp.where(allowed, scores, NEG_BIG)
                s_s[head, :, k_span] = scores
                for lane in range(0, tile, LANES):
                    top = jnp.maximum(top, scores[:, lane : lane + LANES])
            top = jnp.max(top, axis=1, keepdims=True)
            total = jnp.zeros((tile, LANES), F32)
            for kt in range(qt + 1):
                k_span = slice(kt * tile, (kt + 1) * tile)
                soft = jnp.exp(s_s[head, :, k_span] - top)
                for lane in range(0, tile, LANES):
                    total = total + soft[:, lane : lane + LANES]
                p_s[head, :, k_span] = soft.astype(BF16)
            total = jnp.sum(total, axis=1, keepdims=True)
            span = slice(0, (qt + 1) * tile)
            parts.append(nn(p_s[head, :, span], v_s[span, :]) / total)
            lse = jnp.broadcast_to(top + jnp.log(total), (tile, LANES))
            lse_ref[head : head + 1, q_span] = lse.T[0:1, :]
        att = jnp.where(masks[0], parts[0], parts[1])
        att_ref[q_span, :] = att
        o_s[qt * step : (qt + 1) * step] = att.astype(BF16).reshape(step, half, LANES)
    unsort_places(place_ref, [o_s], heads)

    start = pl.multiple_of(lax.rem(me, pairs) * LANES, LANES)
    target = tok_ref.at[:, me // pairs, :, :, pl.ds(start, LANES)]
    moved += [
        send(heads.at[peer], target, a_send.at[k], a_recv.at[k], "fsdp", peer) for k, peer in enumerate(others)
    ]
    moved.append(pltpu.make_async_copy(heads.at[me], target, a_local))
    moved[-1].start()
    for copy in moved:
        copy.wait()


def attend(places, inverse, h1, weight, shift, out_own, n_ctx, planes, seqs, half, tile):
    length = h1.shape[0]
    lanes = weight.shape[1]
    blocks = length // half
    width = (planes // seqs) * LANES
    rows_s = pltpu.VMEM((length, LANES), BF16)
    sems = [DMA((planes - 1,)), DMA((planes - 1,)), DMA]
    return pl.pallas_call(
        functools.partial(attend_kernel, tile, planes, seqs),
        out_shape=(
            jax.ShapeDtypeStruct((planes, n_ctx, 2, half, lanes), BF16),
            jax.ShapeDtypeStruct((length, LANES), F32),
            jax.ShapeDtypeStruct((2, length), F32),
            jax.ShapeDtypeStruct((n_ctx, seqs, 2, half, width), BF16),
            jax.ShapeDtypeStruct((planes,) + out_own.shape, BF16),
        ),
        in_specs=[SMEM, SMEM, ANY, ANY, VMEM, ANY],
        out_specs=(VMEM, VMEM, VMEM, ANY, ANY),
        scratch_shapes=[
            pltpu.VMEM(h1.shape, BF16),
            pltpu.VMEM(weight.shape, BF16),
            DMA((planes + 1,)),
            pltpu.VMEM((planes, n_ctx, 2, half, LANES), BF16),
        ]
        + sems
        + sems
        + [rows_s, rows_s, rows_s, pltpu.VMEM((blocks, half, LANES), BF16)]
        + [pltpu.VMEM((2, tile, length), F32), pltpu.VMEM((2, tile, length), BF16)],
        compiler_params=params(5),
        cost_estimate=SMALL,
        name="attend",
    )(places, inverse, h1, weight, shift, out_own)


SMEM = pl.BlockSpec(memory_space=pltpu.SMEM)
SHORT = 2048


def attend_forward(order, qkv, tile):
    blocks, half, lanes = qkv.shape
    length = blocks * half
    rows = pltpu.VMEM((length, LANES), BF16)
    return pl.pallas_call(
        functools.partial(long_forward_kernel, tile),
        out_shape=(
            jax.ShapeDtypeStruct((blocks, half, LANES), BF16),
            jax.ShapeDtypeStruct((length, LANES), F32),
            jax.ShapeDtypeStruct((2, length), F32),
        ),
        in_specs=[SMEM, VMEM],
        out_specs=(VMEM, VMEM, VMEM),
        scratch_shapes=[rows, rows, rows, pltpu.VMEM((LANES, length), BF16), rows],
        compiler_params=params(),
        cost_estimate=SMALL,
        name="attend_forward",
    )(order, qkv)


def long_backward_kernel(
    tile, order_ref, qkv_ref, grad_ref, att_ref, lse_ref, out_ref, sum_ref, q_s, k_s, v_s, g_s, kt_s, dq_s, dk_s, dv_s
):
    blocks, half = grad_ref.shape[0], grad_ref.shape[1]
    length = blocks * half
    tiles = length // tile
    sort_blocks(order_ref, qkv_ref, [q_s, k_s, v_s], blocks, half)
    sort_blocks(order_ref, grad_ref, [g_s], blocks, half)
    for t in range(tiles):
        span = slice(t * tile, (t + 1) * tile)
        kt_s[:, span] = k_s[span, :].T
    scale = HD ** (-0.5)
    rows_iota = lax.broadcasted_iota(jnp.int32, (tile, tile), 0)
    cols_iota = lax.broadcasted_iota(jnp.int32, (tile, tile), 1)
    allowed = rows_iota <= cols_iota
    masks = [lane_mask(tile, head) for head in range(2)]
    dk_s[...] = jnp.zeros_like(dk_s)
    dv_s[...] = jnp.zeros_like(dv_s)

    for qt in range(tiles):
        q_span = slice(qt * tile, (qt + 1) * tile)
        query = q_s[q_span, :] * jnp.asarray(scale, BF16)
        grad = g_s[q_span, :]
        queries = [jnp.where(masks[head], query, jnp.zeros_like(query)) for head in range(2)]
        grads = [jnp.where(masks[head], grad, jnp.zeros_like(grad)) for head in range(2)]
        product = (grad.astype(F32) * att_ref[q_span, :]).T
        dots = [jnp.sum(product[head * HD : (head + 1) * HD], axis=0, keepdims=True) for head in range(2)]
        totals = [lse_ref[head : head + 1, q_span] for head in range(2)]

        def step(kt, state, masked, queries=queries, grads=grads, dots=dots, totals=totals):
            start = pl.multiple_of(kt * tile, tile)
            rows = pl.ds(start, tile)
            keys = k_s[rows, :]
            values = v_s[rows, :]
            dk = dk_s[rows, :]
            dv = dv_s[rows, :]
            new = []
            for head in range(2):
                scores = nt(keys, queries[head])
                if masked:
                    scores = jnp.where(allowed, scores, NEG_BIG)
                soft = jnp.exp(scores - totals[head])
                dsoft = nt(values, grads[head])
                dscore = (soft * (dsoft - dots[head])).astype(BF16)
                dv = dv + nn(soft.astype(BF16), grads[head])
                dk = dk + nn(dscore, queries[head])
                new.append(state[head] + nn(kt_s[head * HD : (head + 1) * HD, rows], dscore))
            dk_s[rows, :] = dk
            dv_s[rows, :] = dv
            return tuple(new)

        state = (jnp.zeros((HD, tile), F32), jnp.zeros((HD, tile), F32))
        state = step(qt, state, True)
        if qt > 0:
            state = lax.fori_loop(0, qt, lambda kt, s, step=step: step(kt, s, False), state)
        dq = jnp.concatenate(state, axis=0) * scale
        dq_s[q_span, :] = dq.T.astype(BF16)

    unsort_blocks(order_ref, [dq_s, dk_s, dv_s], out_ref, blocks, half)
    for k, source in enumerate([dq_s, dk_s, dv_s]):
        values = source[...].astype(BF16).astype(F32)
        sum_ref[:, k * LANES : (k + 1) * LANES] = jnp.sum(values, axis=0, keepdims=True)


def branch_back_kernel(
    tile,
    planes,
    seqs,
    chips,
    order_ref,
    place_ref,
    db_hbm,
    w_hbm,
    at_hbm,
    qkv_hbm,
    att_hbm,
    down_ref,
    out_part_ref,
    mixed_ref,
    vec_ref,
    lse_ref,
    out_ref,
    sum_ref,
    out_w_ref,
    block_ref,
    down_all,
    db_ref,
    w_ref,
    at_ref,
    qkv_ref,
    att_ref,
    load_sem,
    d_att,
    heads,
    h_send,
    h_recv,
    h_local,
    q_s,
    k_s,
    v_s,
    g_s,
    kt_s,
    dq_s,
    dk_s,
    dv_s,
    qh_s,
    gh_s,
    dot_s,
    p_s,
    ds_s,
    *scratch,
):
    n_ctx = 2 * chips
    ctx_me, core, chip, sibling, to, come = plane_peers(chips)
    me, others = other_planes(planes)
    pairs = planes // seqs
    out_scatter, down_sems = scratch[:8], scratch[8:]
    loads = [
        pltpu.make_async_copy(source, target, load_sem.at[k])
        for k, (source, target) in enumerate(
            [(db_hbm, db_ref), (w_hbm, w_ref), (qkv_hbm, qkv_ref), (at_hbm, at_ref), (att_hbm, att_ref)]
        )
    ]
    for load in loads:
        load.start()
    greet(to + [sibling], others)
    down_started = plane_gather_start([down_ref], [down_all], down_sems, chips)
    out_total = []
    out_stages = plane_scatter_stages(
        lambda c: out_part_ref.at[c], *out_scatter[:3], out_scatter[3:], chips, out_total
    )
    next(out_stages)

    loads[0].wait()
    loads[1].wait()
    d_att[...] = nt(db_ref[...], w_ref[...]).astype(BF16).reshape(d_att.shape)

    def source(unit):
        start = pl.multiple_of(lax.rem(unit, pairs) * LANES, LANES)
        return d_att.at[:, unit // pairs, :, :, pl.ds(start, LANES)]

    moved = [
        send(source(unit), heads.at[me], h_send.at[k], h_recv.at[k], "fsdp", unit) for k, unit in enumerate(others)
    ]
    moved.append(pltpu.make_async_copy(source(me), heads.at[me], h_local))
    moved[-1].start()
    for load in loads[2:]:
        load.wait()
    out_w_ref[...] = tn(at_ref[...], db_ref[...]).astype(BF16)

    blocks, half = dq_s.shape[0], dq_s.shape[1]
    length = blocks * half
    tiles, step = length // tile, tile // half

    sort_places(order_ref, qkv_ref, [q_s, k_s, v_s])
    scale = HD ** (-0.5)
    rows_iota = lax.broadcasted_iota(jnp.int32, (tile, tile), 0)
    cols_iota = lax.broadcasted_iota(jnp.int32, (tile, tile), 1)
    allowed = rows_iota <= cols_iota
    masks = [lane_mask(tile, head) for head in range(2)]
    for t in range(tiles):
        span = slice(t * tile, (t + 1) * tile)
        kt_s[:, span] = k_s[span, :].T
        query = q_s[span, :] * jnp.asarray(scale, BF16)
        for head in range(2):
            qh_s[head, span, :] = jnp.where(masks[head], query, jnp.zeros_like(query))
    next(out_stages)
    for copy in moved:
        copy.wait()
    sort_places(order_ref, heads, [g_s])
    for t in range(tiles):
        span = slice(t * tile, (t + 1) * tile)
        grad = g_s[span, :]
        product = (grad.astype(F32) * att_ref[span, :]).T
        for head in range(2):
            gh_s[head, span, :] = jnp.where(masks[head], grad, jnp.zeros_like(grad))
            dot_s[head : head + 1, span] = jnp.sum(product[head * HD : (head + 1) * HD], axis=0, keepdims=True)
    plane_gather_middle(down_started, [down_all], down_sems, chips)

    def keep(target, index, values):
        target[index * step : (index + 1) * step] = values.astype(BF16).reshape(step, half, LANES)

    for kt in range(tiles):
        k_span = slice(kt * tile, (kt + 1) * tile)
        rest = slice(kt * tile, length)
        keys, values = k_s[k_span, :], v_s[k_span, :]
        dk, dv = None, None
        for head in range(2):
            for qt in range(kt, tiles):
                span = slice(qt * tile, (qt + 1) * tile)
                scores = nt(keys, qh_s[head, span, :])
                if kt == qt:
                    scores = jnp.where(allowed, scores, NEG_BIG)
                soft = jnp.exp(scores - lse_ref[head : head + 1, span])
                p_s[head, :, span] = soft.astype(BF16)
                dsoft = nt(values, gh_s[head, span, :])
                ds_s[head, k_span, span] = (soft * (dsoft - dot_s[head : head + 1, span])).astype(BF16)
            dv_one = nn(p_s[head, :, rest], gh_s[head, rest, :])
            dk_one = nn(ds_s[head, k_span, rest], qh_s[head, rest, :])
            dv = dv_one if dv is None else dv + dv_one
            dk = dk_one if dk is None else dk + dk_one
        keep(dk_s, kt, dk)
        keep(dv_s, kt, dv)
        if kt == 0:
            next(out_stages, None)
    for qt in range(tiles):
        span = slice(qt * tile, (qt + 1) * tile)
        upto = slice(0, (qt + 1) * tile)
        dq = [nn(kt_s[head * HD : (head + 1) * HD, upto], ds_s[head, upto, span]) for head in range(2)]
        keep(dq_s, qt, (jnp.concatenate(dq, axis=0) * scale).T)
    for unused in out_stages:
        pass
    block_ref[...] = (mixed_ref[...] + out_total[0] + vec_ref[...]).astype(BF16)

    unsort_places(place_ref, [dq_s, dk_s, dv_s], out_ref)
    for k, ref in enumerate([dq_s, dk_s, dv_s]):
        values = ref[...].astype(F32)
        sum_ref[:, k * LANES : (k + 1) * LANES] = jnp.sum(jnp.sum(values, axis=0), axis=0, keepdims=True)
    plane_gather_end(down_started, [down_all], down_sems, chips)


def branch_back(places, inverse, d_branch, weight, att, qkv, att_exact, lse, down_own, out_part, mixed, vec, planes, tile):
    shape = qkv.shape
    half, lanes = shape[3:]
    n_ctx, rows, width = out_part.shape
    blocks = 2 * planes * n_ctx
    length = blocks * half
    seqs = rows * n_ctx * planes // length
    chips = n_ctx // 2
    rows_s = pltpu.VMEM((length, LANES), BF16)
    blocks_s = pltpu.VMEM((blocks, half, LANES), BF16)
    return pl.pallas_call(
        functools.partial(branch_back_kernel, tile, planes, seqs, chips),
        out_shape=(
            jax.ShapeDtypeStruct(shape, BF16),
            jax.ShapeDtypeStruct((1, lanes), F32),
            jax.ShapeDtypeStruct(weight.shape, BF16),
            jax.ShapeDtypeStruct((rows, width), BF16),
            jax.ShapeDtypeStruct((n_ctx,) + down_own.shape, BF16),
        ),
        in_specs=[SMEM, SMEM] + [ANY] * 7 + [VMEM] * 3,
        out_specs=(VMEM, VMEM, VMEM, VMEM, ANY),
        scratch_shapes=[
            pltpu.VMEM(d_branch.shape, BF16),
            pltpu.VMEM(weight.shape, BF16),
            pltpu.VMEM(att.shape, BF16),
            pltpu.VMEM(shape, BF16),
            pltpu.VMEM(att_exact.shape, F32),
            DMA((5,)),
            pltpu.VMEM((n_ctx, seqs, 2, half, weight.shape[0]), BF16),
            pltpu.VMEM((planes, n_ctx, 2, half, LANES), BF16),
            DMA((planes - 1,)),
            DMA((planes - 1,)),
            DMA,
            rows_s,
            rows_s,
            rows_s,
            rows_s,
            pltpu.VMEM((LANES, length), BF16),
            blocks_s,
            blocks_s,
            blocks_s,
            pltpu.VMEM((2, length, LANES), BF16),
            pltpu.VMEM((2, length, LANES), BF16),
            pltpu.VMEM((2, length), F32),
            pltpu.VMEM((2, tile, length), BF16),
            pltpu.VMEM((2, length, length), BF16),
        ]
        + scatter_scratch(chips, rows, width)
        + gather_sems(chips),
        compiler_params=params(10),
        cost_estimate=SMALL,
        name="branch_back",
    )(places, inverse, d_branch, weight, att, qkv, att_exact, down_own, out_part, mixed, vec, lse)


def attend_backward(order, qkv, grad, att, lse, tile):
    blocks, half, lanes = qkv.shape
    length = blocks * half
    rows = pltpu.VMEM((length, LANES), BF16)
    flipped = pltpu.VMEM((LANES, length), BF16)
    return pl.pallas_call(
        functools.partial(long_backward_kernel, tile),
        out_shape=(
            jax.ShapeDtypeStruct((blocks, half, 3 * LANES), BF16),
            jax.ShapeDtypeStruct((1, 3 * LANES), F32),
        ),
        in_specs=[SMEM, VMEM, VMEM, VMEM, VMEM],
        out_specs=(VMEM, VMEM),
        scratch_shapes=[rows, rows, rows, rows, flipped, rows] + [pltpu.VMEM((length, LANES), F32)] * 2,
        compiler_params=params(),
        cost_estimate=SMALL,
        name="attend_backward",
    )(order, qkv, grad, att, lse)


def assemble_kernel(pieces, part_ref, out_ref):
    for start, source, first, size in pieces:
        out_ref[:, start : start + size] = part_ref[source, :, first : first + size].astype(F32)


def assemble(parts, pieces, width):
    n_ctx, rows, columns = parts.shape
    block = -(-rows // 32) * 16
    return pl.pallas_call(
        functools.partial(assemble_kernel, pieces),
        grid=(-(-rows // block),),
        out_shape=jax.ShapeDtypeStruct((rows, width), F32),
        in_specs=[pl.BlockSpec((n_ctx, block, columns), lambda i: (0, i, 0))],
        out_specs=pl.BlockSpec((block, width), lambda i: (i, 0)),
        compiler_params=params(),
        name="assemble",
    )(parts)


def assemble_packed_kernel(pieces, part_ref, out_ref):
    hidden = part_ref.shape[2] // 2
    for side in range(2):

        @pl.when(pl.program_id(0) == side)
        def _(side=side):
            for start, source, first, size in pieces:
                first = first + side * hidden
                out_ref[:, start : start + size] = part_ref[source, :, first : first + size].astype(F32)


def assemble_packed(parts, pieces, width):
    n_ctx, rows, columns = parts.shape
    return pl.pallas_call(
        functools.partial(assemble_packed_kernel, pieces),
        grid=(2,),
        out_shape=jax.ShapeDtypeStruct((2 * rows, width), F32),
        in_specs=[pl.BlockSpec((n_ctx, rows, columns), lambda i: (0, 0, 0), pipeline_mode=pl.Buffered(1))],
        out_specs=pl.BlockSpec((rows, width), lambda i: (i, 0)),
        compiler_params=params(),
        name="assemble_packed",
    )(parts)


def tn(left, right):
    return nn(left.T, right)


def rows_block(rows, most):
    return math.gcd(rows, most)


def whole_block(shape):
    return pl.BlockSpec(shape, lambda i: (0,) * len(shape), pipeline_mode=pl.Buffered(1))


def row_spec(block, width):
    return pl.BlockSpec((block, width), lambda i: (i, 0))


def product_kernel(left_ref, right_ref, shift_ref, out_ref):
    out_ref[...] = (nn(left_ref[...], right_ref[...]) + shift_ref[...]).astype(BF16)


def product(left, right, shift=None):
    rows, depth = left.shape
    width = right.shape[1]
    block = rows_block(rows, 512)
    if shift is None:
        shift = jnp.zeros((width,), F32)
    return pl.pallas_call(
        product_kernel,
        grid=(rows // block,),
        out_shape=jax.ShapeDtypeStruct((rows, width), BF16),
        in_specs=[row_spec(block, depth), whole_block((depth, width)), whole_block((1, width))],
        out_specs=row_spec(block, width),
        compiler_params=params(),
        cost_estimate=SMALL,
        name="product",
    )(left, right, shift[None, :])


def back_kernel(left_ref, grad_ref, weight_ref, grad_left_ref, grad_weight_ref, sum_ref, total):
    step = pl.program_id(0)
    grad = grad_ref[...]
    grad_left_ref[...] = nt(grad, weight_ref[...]).astype(BF16)
    term = tn(grad, left_ref[...])
    sums = jnp.sum(grad.astype(F32), axis=0, keepdims=True)

    @pl.when(step == 0)
    def _():
        total[...] = term
        sum_ref[...] = sums

    @pl.when(step > 0)
    def _():
        total[...] += term
        sum_ref[...] += sums

    @pl.when(step == pl.num_programs(0) - 1)
    def _():
        grad_weight_ref[...] = total[...].T.astype(BF16)


def product_back(left, grad, weight):
    rows, depth = left.shape
    width = grad.shape[1]
    block = rows_block(rows, 512)
    return pl.pallas_call(
        back_kernel,
        grid=(rows // block,),
        out_shape=(
            jax.ShapeDtypeStruct((rows, depth), BF16),
            jax.ShapeDtypeStruct((depth, width), BF16),
            jax.ShapeDtypeStruct((1, width), F32),
        ),
        in_specs=[row_spec(block, depth), row_spec(block, width), whole_block((depth, width))],
        out_specs=(
            row_spec(block, depth),
            pl.BlockSpec((depth, width), lambda i: (0, 0)),
            pl.BlockSpec((1, width), lambda i: (0, 0)),
        ),
        scratch_shapes=[pltpu.VMEM((width, depth), F32)],
        compiler_params=params(),
        cost_estimate=SMALL,
        name="product_back",
    )(left, grad, weight)


def out_back_kernel(att_ref, grad_ref, weight_ref, grad_att_ref, grad_weight_ref, total):
    step = pl.program_id(0)
    grad = grad_ref[...]
    grad_att_ref[...] = nt(grad, weight_ref[...]).astype(BF16)
    term = tn(att_ref[...], grad)

    @pl.when(step == 0)
    def _():
        total[...] = term

    @pl.when(step > 0)
    def _():
        total[...] += term

    @pl.when(step == pl.num_programs(0) - 1)
    def _():
        grad_weight_ref[...] = total[...].astype(BF16)


def out_back(att, grad, weight):
    rows, depth = att.shape
    width = grad.shape[1]
    block = rows_block(rows, 512)
    return pl.pallas_call(
        out_back_kernel,
        grid=(rows // block,),
        out_shape=(jax.ShapeDtypeStruct((rows, depth), BF16), jax.ShapeDtypeStruct((depth, width), BF16)),
        in_specs=[row_spec(block, depth), row_spec(block, width), whole_block((depth, width))],
        out_specs=(row_spec(block, depth), pl.BlockSpec((depth, width), lambda i: (0, 0))),
        scratch_shapes=[pltpu.VMEM((depth, width), F32)],
        compiler_params=params(),
        cost_estimate=SMALL,
        name="out_back",
    )(att, grad, weight)


GELU_A = math.sqrt(2.0 / math.pi)
GELU_B = 0.044715


def up_kernel(h_ref, og_ref, weight_ref, shift_ref, act_ref, slope_ref, grad_ref, total):
    step = pl.program_id(0)
    up = nn(h_ref[...], weight_ref[...]) + shift_ref[...]
    square = up * up
    soft = jnp.tanh(GELU_A * up * (1.0 + GELU_B * square))
    half = 0.5 * (1.0 + soft)
    act = (up * half).astype(BF16)
    act_ref[...] = act
    slope_ref[...] = half + 0.5 * up * (1.0 - soft * soft) * (GELU_A * (1.0 + 3.0 * GELU_B * square))
    term = tn(act, og_ref[...])

    @pl.when(step == 0)
    def _():
        total[...] = term

    @pl.when(step > 0)
    def _():
        total[...] += term

    @pl.when(step == pl.num_programs(0) - 1)
    def _():
        grad_ref[...] = total[...].astype(BF16)


def feed_up(values, out_grad, weight, shift):
    rows, width = values.shape
    hidden = weight.shape[1]
    block = rows_block(rows, 512)
    return pl.pallas_call(
        up_kernel,
        grid=(rows // block,),
        out_shape=(
            jax.ShapeDtypeStruct((rows, hidden), BF16),
            jax.ShapeDtypeStruct((rows, hidden), F32),
            jax.ShapeDtypeStruct((hidden, width), BF16),
        ),
        in_specs=[
            row_spec(block, width),
            row_spec(block, width),
            whole_block((width, hidden)),
            whole_block((1, hidden)),
        ],
        out_specs=(
            row_spec(block, hidden),
            row_spec(block, hidden),
            pl.BlockSpec((hidden, width), lambda i: (0, 0)),
        ),
        scratch_shapes=[pltpu.VMEM((hidden, width), F32)],
        compiler_params=params(),
        cost_estimate=SMALL,
        name="feed_up",
    )(values, out_grad, weight, shift[None, :])


def local(
    tokens,
    block_pairs,
    out_grad,
    ln1_gain,
    ln1_bias,
    qkv_weight,
    query_bias,
    value_bias,
    out_weight,
    out_bias,
    ln2_gain,
    ln2_bias,
    up_weight,
    up_bias,
    down_weight,
    down_bias,
):
    n_ctx, planes = lax.axis_size("ctx"), lax.axis_size("fsdp")
    c, f = lax.axis_index("ctx"), lax.axis_index("fsdp")
    local_rows, seqs, width = tokens.shape
    half = local_rows // 2
    devices = n_ctx * planes
    blocks = 2 * devices
    length = devices * local_rows
    heads = width // HD
    slots = planes * (-(-heads // devices))
    assert slots == planes and planes % seqs == 0
    span = slots * HD
    rows = local_rows * seqs
    plane_rows = n_ctx * rows
    quarter = width // planes
    ff = up_weight.shape[1]
    ff_quarter = ff // planes
    ff_piece = ff_quarter // n_ctx
    ff_span = ff_piece * planes
    tile = 256
    halved = quarter % 16 == 0

    device_ids = jnp.arange(devices, dtype=jnp.int32)
    device_of_block = jnp.sum(
        jnp.where(block_pairs[None, :] == device_ids[:, None], device_ids[None, :], 0), axis=1
    )
    place_of_block = lax.rem(device_of_block, planes) * n_ctx + device_of_block // planes
    order = jnp.concatenate([place_of_block * 2, place_of_block[::-1] * 2 + 1]).astype(jnp.int32)

    first = [-(-quarter * j // HD) for j in range(planes)] + [heads]
    counts = [first[j + 1] - first[j] for j in range(planes)]
    assert max(counts) <= n_ctx
    slot_head = [jnp.minimum(first[j] + c, heads - 1) for j in range(planes)]
    first_own = jnp.asarray(first, jnp.int32)[f]
    count_own = jnp.asarray(counts, jnp.int32)[f]

    pairs = planes // seqs
    pair, pair_span = lax.rem(f, pairs), 2 * HD
    qkv_own = jnp.stack(
        [
            jnp.concatenate(
                [
                    lax.dynamic_slice(qkv_weight, (0, k * width + slot_head[j] * HD), (quarter, HD))
                    for k in range(3)
                    for j in (2 * p, 2 * p + 1)
                ],
                axis=1,
            )
            for p in range(pairs)
        ]
    )
    down_own = lax.dynamic_slice(down_weight, (c * ff_piece, 0), (ff_piece, width))


    tok = jnp.swapaxes(tokens, 0, 1).reshape(rows, width)
    og = jnp.swapaxes(out_grad, 0, 1).reshape(rows, width)

    short = -quarter % LANES
    vector_list = [ln1_gain, ln1_bias, ln2_gain, ln2_bias, query_bias, value_bias, out_bias, down_bias]
    vector_list += [up_bias[k * quarter : (k + 1) * quarter] for k in range(ff // width)]
    packed = jnp.concatenate([jnp.pad(v, (0, short)) for v in vector_list])
    packed = jnp.pad(packed, (0, -packed.size % (16 * LANES))).reshape(-1, LANES)
    up_own = jnp.concatenate(
        [
            lax.dynamic_slice(up_weight, (0, k * ff_quarter + c * ff_piece), (quarter, ff_piece))
            for k in range(planes)
        ],
        axis=1,
    )
    tok_first, up_own = lax.optimization_barrier((tok, up_own))
    vectors, og_all, h1, qkv_slice, next_rows = first_norm_gather(
        tok_first, og, packed, qkv_own, out_weight, n_ctx, planes, seqs
    )
    out_own = lax.dynamic_slice(
        jnp.concatenate([out_weight, next_rows]), ((first_own + c) * HD - f * quarter, 0), (HD, width)
    )
    out_own = jnp.where(c < count_own, out_own, jnp.zeros_like(out_own))
    h1 = h1.reshape(length, width)
    qkv_slice = qkv_slice.reshape(width, 3 * pair_span)
    h1, up_own, down_own = lax.optimization_barrier((h1, up_own, down_own))
    down_slice = lax.all_gather(down_own, "fsdp", axis=0, tiled=True)
    up_slice = lax.all_gather(up_own, "fsdp", axis=0, tiled=True)
    og_all = og_all.reshape(plane_rows, width)
    vectors = vectors.reshape(planes, -1)[:, : len(vector_list) * (quarter + short)]
    vectors = vectors.reshape(planes, len(vector_list), quarter + short)[:, :, :quarter].astype(F32)
    gain1, bias1, gain2, bias2, bias_q, bias_v, bias_o, bias_d = [
        vectors[:, k].reshape(width) for k in range(8)
    ]
    bias_up = lax.dynamic_slice(
        vectors[:, 8 : 8 + ff // width].reshape(planes, ff_quarter), (0, c * ff_piece), (planes, ff_piece)
    ).reshape(ff_span)

    pair_heads = [jnp.minimum(jnp.asarray(first, jnp.int32)[2 * pair + i] + c, heads - 1) for i in range(2)]

    def head_part(vector):
        return [lax.dynamic_slice(vector, (head * HD,), (HD,)) for head in pair_heads]

    qkv_shift = jnp.concatenate(head_part(bias_q) + [jnp.zeros((pair_span,), F32)] + head_part(bias_v))

    if length <= SHORT:
        places, inverse = block_places(order, n_ctx)
        qkv, att_exact, lse, att, out_slice = attend(
            places, inverse, h1, qkv_slice, qkv_shift[None, :], out_own, n_ctx, planes, seqs, half, tile
        )
    else:
        qkv = product(h1, qkv_slice, qkv_shift).reshape(blocks, half, 3 * pair_span)
        att_heads, att_exact, lse = attend_forward(order, qkv, tile)
        att, out_slice = to_tokens(att_heads.reshape(planes, n_ctx, local_rows, LANES), seqs, 6, out_own)
    out_slice = out_slice.reshape(span, width)
    att = att.reshape(plane_rows, span)
    mixed, h2 = second_norm_gather(att, out_slice, tok, jnp.stack([gain2, bias2, bias_o]), n_ctx)
    h2 = h2.reshape(plane_rows, width)
    def reduce_own(part):
        return lax.psum_scatter(part, "fsdp", scatter_dimension=0, tiled=True)

    act, slope, down_part = feed_up(h2, og_all, up_slice, bias_up)
    down_own_grad = reduce_own(down_part)
    d_mixed, sums2, d_branch, out_part, up_part, d_up_sum = feed_back(
        h2, og_all, act, slope, up_slice, down_slice, mixed, og, gain2[None, :], planes, halved
    )
    up_own_grad = lax.psum_scatter(up_part, "fsdp", scatter_dimension=0, tiled=False)
    out_part = out_part.reshape(n_ctx, rows, width)
    d_branch = d_branch.reshape(plane_rows, width)
    if length <= SHORT:
        d_qkv, d_qkv_sum, out_w_part, block_out, down_parts = branch_back(
            places,
            inverse,
            d_branch,
            out_slice,
            att,
            qkv,
            att_exact,
            lse,
            down_own_grad,
            out_part,
            mixed,
            bias_d[None, :],
            planes,
            tile,
        )
    else:
        d_att, out_w_part = out_back(att, d_branch, out_slice)
        d_att_heads, down_parts = to_heads(
            d_att.reshape(n_ctx, seqs, local_rows, span), planes, 7, down_own_grad
        )
        d_qkv, d_qkv_sum = attend_backward(
            order, qkv, d_att_heads.reshape(blocks, half, LANES), att_exact, lse, tile
        )
        total = lax.psum_scatter(out_part.reshape(plane_rows, width), "ctx", scatter_dimension=0, tiled=True)
        block_out = (mixed + total.astype(F32) + bias_d).astype(BF16)
    d_qkv, d_qkv_sum = d_qkv.reshape(length, 3 * pair_span), d_qkv_sum[0]
    down_parts, unused = lax.optimization_barrier((down_parts, d_qkv))
    down_grad = down_parts.reshape(ff_quarter, width).astype(F32)
    up_own_grad, down_grad = lax.optimization_barrier((up_own_grad, down_grad))

    d_up_sum = d_up_sum.reshape(planes, ff_piece)
    up_spread = lax.dynamic_update_slice(jnp.zeros((planes, ff_quarter), F32), d_up_sum, (0, c * ff_piece))

    def spread(values):
        full = jnp.zeros((width + HD,), F32)
        for i in range(2):
            slot = 2 * pair + i
            real = c < jnp.asarray(counts, jnp.int32)[slot]
            place = jnp.where(real, pair_heads[i] * HD, width)
            full = lax.dynamic_update_slice(full, values[i * HD : (i + 1) * HD], (place,))
        return full[None, :width]

    wide = jnp.concatenate([sums2, spread(d_qkv_sum[:pair_span]), spread(d_qkv_sum[2 * pair_span :])])
    wide = wide.reshape(6, planes, quarter).transpose(1, 0, 2).reshape(planes, 6 * quarter)
    flat = jnp.concatenate([wide, up_spread], axis=1)
    size = flat.shape[1]
    flat = jnp.pad(flat, ((0, 0), (0, -size % (8 * LANES)))).reshape(planes, -1, LANES)

    if length <= SHORT:
        grad_tok, qkv_parts, up_parts, out_parts, tail_rows, sums1, totals = finish(
            h1,
            d_qkv,
            qkv_slice,
            up_own_grad,
            out_w_part.reshape(planes, HD, width),
            flat,
            tok,
            d_mixed,
            gain1[None, :],
            counts,
        )
    else:
        d_h1, qkv_part, unused = product_back(h1, d_qkv, qkv_slice)
        grad_tok, qkv_parts, out_parts, sums1, totals = first_norm_back(
            d_h1.reshape(planes, n_ctx, local_rows, width),
            qkv_part.reshape(planes, quarter, 3 * pair_span),
            reduce_own(out_w_part),
            flat,
            tok,
            d_mixed,
            gain1[None, :],
        )
        up_parts = lax.all_gather(up_own_grad, "ctx", axis=0)
        tail_rows = lax.dynamic_index_in_dim(out_parts, count_own - 1, 0, keepdims=False)
        tail_rows = lax.ppermute(tail_rows, "fsdp", [(j, j + 1) for j in range(planes - 1)])
    sums1 = sums1[:2, :quarter]
    totals = totals.reshape(-1)
    sums = totals[: 6 * quarter].reshape(6, quarter)
    up_bias_grad = totals[6 * quarter : size]

    up_pieces = [
        (j * ff_quarter + d * ff_piece, d, j * ff_piece, ff_piece) for j in range(planes) for d in range(n_ctx)
    ]
    qkv_pieces = [
        (k * width + (first[j] + d) * HD, d * pairs + j // 2, k * pair_span + j % 2 * HD, HD)
        for k in range(3)
        for j in range(planes)
        for d in range(counts[j])
    ]
    up_grad = (assemble_packed if halved else assemble)(up_parts, up_pieces, ff)
    qkv_grad = assemble(qkv_parts.reshape(n_ctx * pairs, quarter, 3 * pair_span), qkv_pieces, 3 * width)
    out_rows = out_parts.reshape(n_ctx * HD, width)
    lead = first_own * HD - f * quarter
    out_grad_own = lax.dynamic_slice(
        jnp.concatenate([tail_rows, out_rows]), (HD - lead, 0), (quarter, width)
    ).astype(F32)

    def back(values):
        return jnp.swapaxes(values.reshape(seqs, local_rows, width), 0, 1)

    return (
        back(block_out),
        back(grad_tok),
        sums1[0],
        sums1[1],
        qkv_grad,
        sums[4],
        sums[5],
        out_grad_own,
        sums[2],
        sums[0],
        sums[1],
        up_grad,
        up_bias_grad,
        down_grad,
        sums[3],
    )


def solution(mesh):
    both, row, vec, mat = P(("ctx", "fsdp"), None, None), P(), P("fsdp"), P("fsdp", None)
    in_specs = (both, row, both, vec, vec, mat, vec, vec, mat, vec, vec, vec, mat, vec, mat, vec)
    out_specs = (both, both, vec, vec, mat, vec, vec, mat, vec, vec, vec, mat, vec, mat, vec)
    return jax.shard_map(local, mesh=mesh, in_specs=in_specs, out_specs=out_specs, check_vma=False)
```
